32 devices in a mesh: section: 4 (over y, x), dp: 8 (over z, core).
Axes of the slice: x: 2, y: 2, z: 4, core: 2. Of those that a mesh axis runs over, the one named last changes fastest.
Arguments:
- start: bfloat16 [64, 128, 768], P('dp'), may hold values from -12 to 12
- cotangent: bfloat16 [64, 128, 768], P('dp'), may hold values from -6 to 6
- first_weights: bfloat16 [4, 768, 3072], P('section')
- second_weights: bfloat16 [4, 3072, 768], P('section'), may hold values from -0.109375 to 0.109375
- norm_params: float32 [4, 2, 768], P('section')
- bias_params: float32 [4, 3840], P('section'), may hold values from -1 to 1
- segment_ids: int32 [64, 128], P('dp'), may hold values from 0 to 5, never falling along the last dimension, each value on 1 to 64 neighbouring positions
- valid_mask: int32 [64, 128], P('dp'), may hold values from 0 to 1, as said below
Outputs:
- residual_streams: bfloat16 [4, 64, 128, 768], P('section', 'dp')
- stream_grads: float32 [4, 64, 128, 768], P('section', 'dp')
- first_grad: float32 [4, 768, 3072], P('section')
- second_grad: float32 [4, 3072, 768], P('section')
- norm_grad: float32 [4, 2, 768], P('section')
- bias_grad: float32 [4, 3840], P('section')
- rms_stats: float32 [4, 2], P('section')
The draws below stay inside these ranges and needn't reach their ends.
Inputs may be any that keep to these rules, and one draw needn't show every extreme that they name: `segment_ids`: numbers never fall along a row; a sentence has 1 to 64 tokens. `valid_mask`: in each row the ones come first, at least 8 of them.
All inputs are finite; a program needn't handle non-finite values.
Results may differ from the reference program's by a relative error of at most 0.018.
Values may be sent and summed in bfloat16 or wider, within the bound.
A program may use at most 448 MiB of HBM per device.

```python
import math
import jax
import jax.numpy as jnp
import numpy as np
from jax import lax

D = 768
HEADS = 12
HEAD_DIM = 64
FF = 3072
SEQ = 128
ROWS_DEV = 8
ROWS = 64
N_SECTION = 4


def draw_start(key, part):
    key = jax.random.fold_in(key, 11)
    row_ids = jnp.arange(ROWS, dtype=jnp.float32)
    fraction = (row_ids / max(ROWS - 1, 1))[:, None, None]
    base_draw = jnp.clip(jax.random.normal(key, (ROWS, SEQ, D), jnp.float32), -4.0, 4.0)
    row_scale = 1.0 + 2.0 * fraction
    return (base_draw * row_scale).astype(jnp.bfloat16)


def draw_first_weights(key, part):
    key = jax.random.fold_in(key, 12)
    base_draw = jnp.clip(jax.random.normal(key, (N_SECTION, D, FF), jnp.float32), -4.0, 4.0)
    section_ids = jnp.arange(N_SECTION)[:, None, None]
    column = jnp.arange(FF)[None, None, :]
    attention = section_ids % 2 == 0
    factor = jnp.where(attention & (column < 2 * D), 1.4, 1.0)
    factor = jnp.where(attention & (column >= 3 * D), 4.0, factor)
    return (base_draw * factor / jnp.sqrt(jnp.float32(D))).astype(jnp.bfloat16)


def draw_norm_params(key, part):
    key = jax.random.fold_in(key, 13)
    gain_key, shift_key = jax.random.split(key)
    gain_part = 1.0 + jax.random.uniform(gain_key, (N_SECTION, 1, D), jnp.float32, -0.15, 0.15)
    shift_part = 0.2 * jnp.clip(jax.random.normal(shift_key, (N_SECTION, 1, D), jnp.float32), -4.0, 4.0)
    return jnp.concatenate([gain_part, shift_part], axis=1)


def draw_valid_mask(key, part):
    key = jax.random.fold_in(key, 14)
    row_ids = jnp.arange(ROWS, dtype=jnp.int32)
    row_span = max(ROWS - 1, 1)
    low_end = SEQ // 16 + SEQ * 11 // 16 * row_ids // row_span
    high_end = SEQ // 2 + SEQ // 2 * row_ids // row_span
    lengths = jax.random.randint(key, (ROWS,), low_end, high_end + 1)
    position = jnp.arange(SEQ, dtype=jnp.int32)[None, :]
    return (position < lengths[:, None]).astype(jnp.int32)


def steps_of(stream_key, shape, pieces, least, largest):
    factor_of = 1.0
    for dim, blocks in pieces:
        steps = jax.random.uniform(jax.random.fold_in(jax.random.fold_in(stream_key, 6), dim), (blocks,), jnp.float32, least / len(pieces), largest / len(pieces))
        factor_of = factor_of * jnp.repeat(jnp.exp(steps), shape[dim] // blocks).reshape((-1,) + (1,) * (len(shape) - 1 - dim))
    return factor_of


def profile(number_of, total, limit, slope):
    weights = [(1 << 20) // math.isqrt(grade ** slope) + 1 for grade in range(2, number_of + 1)]
    spare, given = total - limit - (number_of - 1), [1] * (number_of - 1)
    while spare > 0:
        candidates = [i for i in range(number_of - 1) if given[i] < limit]
        pool, budget = sum([weights[i] for i in candidates]), spare
        for i in candidates:
            addition = min(limit - given[i], max(1, budget * weights[i] // pool), spare)
            given[i] = given[i] + addition
            spare = spare - addition
    return np.array([limit] + given)


def ragged_sizes(key, amount, total, reach, lean):
    if amount == 2:
        one = jax.random.randint(key, (), max(1, total - reach), min(reach, total - 1) + 1)
        return jnp.stack([one, total - one])
    sizes = jnp.asarray(profile(amount, total, reach, lean), jnp.int32)
    couples = (amount - 1) // 2
    source_of, receiver = sizes[1:1 + 2 * couples:2], sizes[2:2 + 2 * couples:2]
    margin = jnp.minimum(source_of - 1, reach - receiver)
    shifted = jax.random.randint(jax.random.fold_in(key, 1), (couples,), 0, 1 << 20) % (margin + 1)
    sizes = sizes.at[1:1 + 2 * couples:2].set(source_of - shifted).at[2:2 + 2 * couples:2].set(receiver + shifted)
    return sizes[jax.random.permutation(jax.random.fold_in(key, 2), amount)]


def gaussian(rng, extent, scale, bound, cuts=(), kind=jnp.bfloat16):
    factor_of = steps_of(rng, extent, cuts, -0.22, 0.18) if cuts else 1.0
    drawn = jax.random.normal(rng, extent, jnp.float32) * scale * factor_of
    return jnp.minimum(jnp.maximum(drawn, -bound), bound).astype(kind)


def setup_inputs(seed: int = 0) -> dict:
    splits = jax.random.split(jax.random.key(seed), 9)
    start = draw_start(jax.random.fold_in(splits[8], 71), 0)
    cotangent = gaussian(splits[1], (ROWS, SEQ, D), 1.0, 6.0, ((0, 8),))
    first_weights = draw_first_weights(jax.random.fold_in(splits[8], 71), 0)
    second_weights = gaussian(splits[3], (N_SECTION, FF, D), FF ** -0.5, 0.109375, ((0, 4),))
    norm_params = draw_norm_params(jax.random.fold_in(splits[8], 71), 0)
    bias_params = gaussian(splits[5], (N_SECTION, FF + D), 0.2, 1.0, ((0, 4),), jnp.float32)
    segment_ids = jax.vmap(lambda own: jnp.searchsorted(jnp.cumsum(ragged_sizes(own, 6, SEQ, SEQ // 2, 0)), jnp.arange(SEQ), side="right"))(jax.random.split(splits[6], ROWS)).reshape((ROWS, SEQ)).astype(jnp.int32)
    valid_mask = draw_valid_mask(jax.random.fold_in(splits[8], 71), 0)
    return {"start": start, "cotangent": cotangent, "first_weights": first_weights, "second_weights": second_weights, "norm_params": norm_params, "bias_params": bias_params, "segment_ids": segment_ids, "valid_mask": valid_mask}


@jax.custom_vjp
def low(v):
    return lax.optimization_barrier(v.astype(jnp.bfloat16)).astype(jnp.float32)

@jax.custom_vjp
def low_back(v):
    return v

def low_keep(v):
    return (low(v), None)

def low_pass(kept, grad):
    return (grad,)

def back_keep(v):
    return (v, None)

def back_low(kept, grad):
    return (low(grad),)
low.defvjp(low_keep, low_pass)
low_back.defvjp(back_keep, back_low)
EPS = 1e-05
PRECISE = lax.Precision.HIGHEST

def norm_rows(hidden, norm_gain, norm_shift):
    row_mean = lax.optimization_barrier(jnp.mean(hidden, axis=-1, keepdims=True))
    centered = hidden - row_mean
    variance = lax.optimization_barrier(jnp.mean(centered * centered, axis=-1, keepdims=True))
    return centered * lax.rsqrt(variance + EPS) * norm_gain + norm_shift

def attend_block(qkv_all, segment, validity):
    row_count, seq_len = segment.shape
    packed = qkv_all.reshape(row_count, seq_len, 3, HEADS, HEAD_DIM)
    queries = packed[:, :, 0]
    key_heads = packed[:, :, 1]
    value_heads = packed[:, :, 2]
    scores = jnp.einsum('bqhe,bkhe->bhqk', queries, key_heads, precision=PRECISE) * HEAD_DIM ** (-0.5)
    diagonal = jnp.arange(seq_len)[:, None] == jnp.arange(seq_len)[None, :]
    same_seg = segment[:, :, None] == segment[:, None, :]
    allowed = same_seg & ((validity[:, None, :] > 0) | diagonal[None])
    scores = low_back(jnp.where(allowed[:, None], scores, -1e+30))
    row_max = lax.optimization_barrier(jnp.max(scores, axis=-1, keepdims=True))
    exponent = jnp.exp(scores - row_max)
    attn_prob = low(exponent / lax.optimization_barrier(jnp.sum(exponent, axis=-1, keepdims=True)))
    mixed_out = jnp.einsum('bhqk,bkhe->bqhe', attn_prob, value_heads, precision=PRECISE)
    return mixed_out.reshape(row_count, seq_len, D)

def attend_item(block_item):
    return attend_block(block_item[0], block_item[1], block_item[2])

def attention(entry_h, wide_mat, vectors, norm_values, segment, validity):
    normed = low(norm_rows(entry_h, norm_values[0], norm_values[1]))
    bias_all = jnp.concatenate([vectors[:D], jnp.zeros((D,), jnp.float32), vectors[D:2 * D]])
    qkv_all = low(low_back(jnp.einsum('rtd,df->rtf', normed, wide_mat[:, :3 * D], precision=PRECISE) + bias_all))
    blocks = ROWS // ROWS_DEV
    mixed_out = lax.map(jax.checkpoint(attend_item), (qkv_all.reshape(blocks, ROWS_DEV, SEQ, 3 * D), segment.reshape(blocks, ROWS_DEV, SEQ), validity.reshape(blocks, ROWS_DEV, SEQ)))
    mixed_out = low(low_back(mixed_out.reshape(ROWS, SEQ, D)))
    return jnp.einsum('rtj,ij->rti', mixed_out, wide_mat[:, 3 * D:], precision=PRECISE) + vectors[FF:]

def dense_layer(entry_h, wide_mat, narrow, vectors, norm_values):
    normed = low(norm_rows(entry_h, norm_values[0], norm_values[1]))
    hidden_pre = low_back(jnp.einsum('rtd,df->rtf', normed, wide_mat, precision=PRECISE) + vectors[:FF])
    activation = low(jax.nn.gelu(hidden_pre, approximate=True))
    return jnp.einsum('rtf,fd->rtd', activation, narrow, precision=PRECISE) + vectors[FF:]

def forward(begin_h, first_f, second_f, norm_values, vectors, probes, segment, validity):
    hidden = begin_h
    streams = []
    branches = []
    for section_id in range(N_SECTION):
        entry_h = hidden + probes[section_id]
        if section_id % 2 == 0:
            branch = attention(entry_h, first_f[section_id], vectors[section_id], norm_values[section_id], segment, validity)
        else:
            branch = dense_layer(entry_h, first_f[section_id], second_f[section_id], vectors[section_id], norm_values[section_id])
        residual = entry_h + branch
        if section_id == N_SECTION - 1:
            hidden = low(residual)
        else:
            hidden = low_back(low(residual))
        streams.append(hidden)
        branches.append(branch)
    return (hidden, (jnp.stack(streams), jnp.stack(branches)))

def reference(start, cotangent, first_weights, second_weights, norm_params, bias_params, segment_ids, valid_mask):
    begin_h = start.astype(jnp.float32)
    first_f = first_weights.astype(jnp.float32)
    second_f = second_weights.astype(jnp.float32)
    probes = jnp.zeros((N_SECTION, ROWS, SEQ, D), jnp.float32)

    def wrapped(first_in, second_in, norm_in, vector_in, probe_in):
        return forward(begin_h, first_in, second_in, norm_in, vector_in, probe_in, segment_ids, valid_mask)
    final_h, pullback, extras = jax.vjp(wrapped, first_f, second_f, norm_params, bias_params, probes, has_aux=True)
    streams, branches = extras
    weight = valid_mask.astype(jnp.float32)[None, :, :, None]
    seed_grad = cotangent.astype(jnp.float32) * weight[0]
    grad_first, grad_second, grad_norm, grad_bias, grad_probes = pullback(seed_grad)
    valid_count = jnp.sum(valid_mask.astype(jnp.float32)) * D
    stream_rms = jnp.sqrt(lax.optimization_barrier(jnp.sum(streams * streams * weight, axis=(1, 2, 3))) / valid_count)
    branch_rms = jnp.sqrt(lax.optimization_barrier(jnp.sum(branches * branches * weight, axis=(1, 2, 3))) / valid_count)
    rms_stats = jnp.stack([stream_rms, branch_rms], axis=1)
    return (streams.astype(jnp.bfloat16), grad_probes, grad_first, grad_second, grad_norm, grad_bias, rms_stats)
```

```python
import functools

import jax
import jax.numpy as jnp
from jax import lax
from jax.experimental import pallas as pl
from jax.experimental.pallas import tpu as pltpu
from jax.sharding import PartitionSpec as P

HEAD_DIM = 64
EPS = 1e-05
NEG_FILL = -1e30
MESH = pl.DeviceIdType.MESH
BF16 = jnp.bfloat16
F32 = jnp.float32
NN = (((1,), (0,)), ((), ()))
NT = (((1,), (1,)), ((), ()))
TN = (((0,), (0,)), ((), ()))
PAIR = 2 * HEAD_DIM
TILE = 1536
GELU_C = 0.7978845608028654
GELU_K = 0.044715


def dot(a, b, dims=NN):
    return lax.dot_general(a, b, dims, preferred_element_type=F32)


def gelu_and_slope(x):
    square = x * x
    t = jnp.tanh(GELU_C * (x + GELU_K * (square * x)))
    half = 0.5 * (1.0 + t)
    slope = half + (0.5 * GELU_C) * x * (1.0 - t * t) * (1.0 + (3.0 * GELU_K) * square)
    return x * half, slope


def fold(x):
    return x.reshape(x.shape[0] // 8, 8, x.shape[1]).sum(axis=0)


def normalize(hidden):
    mean = jnp.mean(hidden, axis=-1, keepdims=True)
    centered = hidden - mean
    variance = jnp.mean(centered * centered, axis=-1, keepdims=True)
    inv_std = lax.rsqrt(variance + EPS)
    return centered * inv_std, inv_std


def pipeline_kernel(
    start, cot, first, second, norm, bias, seg, val,
    res_o, sg_o, nrm_o, gin_o, act_o, mid_o, small_o,
    w1, w2, w1t, w2t, hin, hout, gin, gout, nrm, act, mid,
    sq_acc, norm_acc, in_acc, out_acc,
    load_sem, hs_sem, hr_sem, gs_sem, gr_sem, out_sem,
):
    section = lax.axis_index("section")
    dp = lax.axis_index("dp")
    last = lax.axis_size("section") - 1
    rows, seq, dim = start.shape
    ff = first.shape[2]
    pairs = dim // PAIR
    is_attention = section % 2 == 0
    nxt = jnp.minimum(section + 1, last)
    prv = jnp.maximum(section - 1, 0)

    first_load = pltpu.make_async_copy(first.at[0], w1, load_sem.at[0])
    second_load = pltpu.make_async_copy(second.at[0], w2, load_sem.at[1])
    start_load = pltpu.make_async_copy(start, hin, load_sem.at[2])
    cot_load = pltpu.make_async_copy(cot, gin, load_sem.at[3])
    first_load.start()

    @pl.when(section == 0)
    def _():
        start_load.start()

    @pl.when(jnp.logical_not(is_attention))
    def _():
        second_load.start()

    @pl.when(section == last)
    def _():
        cot_load.start()

    barrier = pltpu.get_barrier_semaphore()

    @pl.when(section > 0)
    def _():
        pl.semaphore_signal(barrier, inc=1, device_id=(prv, dp), device_id_type=MESH)

    @pl.when(section < last)
    def _():
        pl.semaphore_signal(barrier, inc=1, device_id=(nxt, dp), device_id_type=MESH)

    pl.semaphore_wait(barrier, jnp.where((section > 0) & (section < last), 2, 1))

    for ref in (sq_acc, norm_acc, in_acc, out_acc):
        ref[...] = jnp.zeros_like(ref)

    def h_copy(i):
        return pltpu.make_async_remote_copy(
            hout.at[i], hin.at[i], hs_sem.at[i], hr_sem.at[i],
            device_id=(nxt, dp), device_id_type=MESH,
        )

    def g_copy(i):
        return pltpu.make_async_remote_copy(
            gout.at[i], gin.at[i], gs_sem.at[i], gr_sem.at[i],
            device_id=(prv, dp), device_id_type=MESH,
        )

    def out_copy(k, i):
        src, dst = (
            (hout, res_o), (gout, sg_o), (nrm, nrm_o), (gin, gin_o), (act, act_o), (mid, mid_o),
        )[k]
        return pltpu.make_async_copy(src.at[i], dst.at[i], out_sem.at[k, i])

    eye = lax.broadcasted_iota(jnp.int32, (seq, seq), 0) == lax.broadcasted_iota(
        jnp.int32, (seq, seq), 1
    )

    def column(row):
        return jnp.sum(jnp.where(eye, row, 0.0), axis=1, keepdims=True)

    def valid_row(i):
        return val[pl.ds(i, 1), :].astype(F32)

    def entry(i):
        @pl.when(section > 0)
        def _():
            h_copy(i).wait_recv()

        hidden = hin[i].astype(F32)
        normal, _ = normalize(hidden)
        low = (normal * norm[0, 0:1, :] + norm[0, 1:2, :]).astype(BF16)
        nrm[i] = low
        return hidden, low

    def leave(i, hidden, branch):
        low = (hidden + branch).astype(BF16)
        hout[i] = low

        @pl.when(section < last)
        def _():
            h_copy(i).start()

        out_copy(0, i).start()
        out_copy(2, i).start()
        weight = column(valid_row(i))
        value = low.astype(F32)
        sq_acc[0] += fold(value * value * weight)
        sq_acc[1] += fold(branch * branch * weight)

    def grad_entry(i):
        @pl.when(section < last)
        def _():
            g_copy(i).wait_recv()

        @pl.when(section == last)
        def _():
            gin[i] = jnp.where(column(valid_row(i)) > 0, gin[i], jnp.zeros((seq, dim), BF16))

        grad = gin[i]
        out_copy(3, i).start()
        return grad

    def grad_leave(i, grad, normed_grad):
        grad_value = grad.astype(F32)
        normal, inv_std = normalize(hin[i].astype(F32))
        scaled = normed_grad * norm[0, 0:1, :]
        mean_one = jnp.mean(scaled, axis=-1, keepdims=True)
        mean_two = jnp.mean(scaled * normal, axis=-1, keepdims=True)
        low = (grad_value + inv_std * (scaled - mean_one - normal * mean_two)).astype(BF16)
        gout[i] = low

        @pl.when(section > 0)
        def _():
            g_copy(i).start()

        out_copy(1, i).start()
        norm_acc[0] += fold(normed_grad * normal)
        norm_acc[1] += fold(normed_grad)
        out_acc[...] += fold(grad_value)


    def dense_forward(i):
        hidden, low = entry(i)
        branch = jnp.zeros((seq, dim), F32)
        for at in range(0, ff, TILE):
            cols = slice(at, at + TILE)
            value, slope = gelu_and_slope(dot(low, w1[:, cols]) + bias[0:1, cols])
            value = value.astype(BF16)
            act[i, :, cols] = value
            mid[i, :, cols] = slope.astype(BF16)
            branch += dot(value, w2[cols, :])
        leave(i, hidden, branch + bias[0:1, ff:])
        out_copy(4, i).start()

    def dense_backward(i):
        grad = grad_entry(i)
        normed_grad = jnp.zeros((seq, dim), F32)
        for at in range(0, ff, TILE):
            cols = slice(at, at + TILE)
            inner = dot(grad, w2t[:, cols]) * mid[i, :, cols].astype(F32)
            low = inner.astype(BF16)
            mid[i, :, cols] = low
            in_acc[:, cols] += fold(low.astype(F32))
            normed_grad += dot(low, w1t[cols, :])
        out_copy(5, i).start()
        grad_leave(i, grad, normed_grad)


    lower = lax.broadcasted_iota(jnp.int32, (seq, PAIR), 1) < HEAD_DIM

    def split_heads(x):
        zero = jnp.zeros_like(x)
        return jnp.concatenate([jnp.where(lower, x, zero), jnp.where(lower, zero, x)], axis=0)

    def join_heads(x):
        return jnp.where(lower, x[:seq], x[seq:])

    def attention_forward(i):
        hidden, low = entry(i)
        projected = dot(low, w1[:, : 3 * dim])
        mid[i, :, :dim] = (projected[:, :dim] + bias[0:1, :dim]).astype(BF16)
        mid[i, :, dim : 2 * dim] = projected[:, dim : 2 * dim].astype(BF16)
        mid[i, :, 2 * dim : 3 * dim] = (
            projected[:, 2 * dim :] + bias[0:1, dim : 2 * dim]
        ).astype(BF16)
        seg_row = seg[pl.ds(i, 1), :].astype(F32)
        allowed = (column(seg_row) == seg_row) & ((valid_row(i) > 0) | eye)
        for p in range(pairs):
            at = p * PAIR
            query = mid[i, :, at : at + PAIR]
            keys = split_heads(mid[i, :, dim + at : dim + at + PAIR])
            values = split_heads(mid[i, :, 2 * dim + at : 2 * dim + at + PAIR])
            scores = dot(query, keys, NT) * HEAD_DIM**-0.5
            probs = []
            for half in (scores[:, :seq], scores[:, seq:]):
                half = jnp.where(allowed, half, NEG_FILL)
                weight = jnp.exp(half - jnp.max(half, axis=-1, keepdims=True))
                probs.append(weight / jnp.sum(weight, axis=-1, keepdims=True))
            prob = jnp.concatenate(probs, axis=1).astype(BF16)
            act[i, :, 2 * seq * p : 2 * seq * (p + 1)] = prob
            mid[i, :, 3 * dim + at : 3 * dim + at + PAIR] = dot(prob, values).astype(BF16)
        branch = dot(mid[i, :, 3 * dim :], w1t[3 * dim :, :]) + bias[0:1, ff:]
        leave(i, hidden, branch)

    def attention_backward(i):
        grad = grad_entry(i)
        mixed_grad = dot(grad, w1[:, 3 * dim :]).astype(BF16)
        for p in range(pairs):
            at = p * PAIR
            query = mid[i, :, at : at + PAIR]
            keys = split_heads(mid[i, :, dim + at : dim + at + PAIR])
            values = split_heads(mid[i, :, 2 * dim + at : 2 * dim + at + PAIR])
            prob = act[i, :, 2 * seq * p : 2 * seq * (p + 1)]
            out_grad = mixed_grad[:, at : at + PAIR]
            prob_grad = dot(out_grad, values, NT)
            prob_value = prob.astype(F32)
            parts = []
            for cols in (slice(0, seq), slice(seq, 2 * seq)):
                pv, pg = prob_value[:, cols], prob_grad[:, cols]
                parts.append(pv * (pg - jnp.sum(pv * pg, axis=-1, keepdims=True)))
            score_grad = jnp.concatenate(parts, axis=1).astype(BF16)
            query_grad = dot(score_grad, keys) * HEAD_DIM**-0.5
            key_grad = join_heads(dot(score_grad, query, TN)) * HEAD_DIM**-0.5
            value_grad = join_heads(dot(prob, out_grad, TN))
            mid[i, :, at : at + PAIR] = query_grad.astype(BF16)
            mid[i, :, dim + at : dim + at + PAIR] = key_grad.astype(BF16)
            mid[i, :, 2 * dim + at : 2 * dim + at + PAIR] = value_grad.astype(BF16)
        out_copy(5, i).start()
        packed = mid[i, :, : 3 * dim]
        normed_grad = dot(packed, w1t[: 3 * dim, :])
        grad_leave(i, grad, normed_grad)
        in_acc[:, :dim] += fold(packed[:, :dim].astype(F32))
        in_acc[:, dim : 2 * dim] += fold(packed[:, 2 * dim :].astype(F32))

    first_load.wait()

    def transpose(src, dst, low, high):
        for at in range(low, high, 2 * PAIR):
            dst[at : at + 2 * PAIR, :] = src[:, at : at + 2 * PAIR].T

    @pl.when(section == 0)
    def _():
        start_load.wait()

    @pl.when(section == last)
    def _():
        cot_load.wait()

    def run(forward, backward, lag, before_last):
        def step(i, carry):
            @pl.when(i == rows - 1)
            def _():
                before_last()

            @pl.when(i < rows)
            def _():
                forward(i)

            @pl.when(i >= lag)
            def _():
                backward(i - lag)

            return carry

        lax.fori_loop(0, rows + lag, step, 0)

    @pl.when(is_attention)
    def _():
        transpose(w1, w1t, 3 * dim, ff)

        def late():
            @pl.when(section == 0)
            def _():
                transpose(w1, w1t, 0, 3 * dim)

        @pl.when(section > 0)
        def _():
            transpose(w1, w1t, 0, 3 * dim)

        lag = jnp.where(section == 0, rows, rows // 2)
        run(attention_forward, attention_backward, lag, late)

    @pl.when(jnp.logical_not(is_attention))
    def _():
        second_load.wait()
        transpose(w1, w1t, 0, ff)
        for at in range(0, ff, 2 * PAIR):
            w2t[:, at : at + 2 * PAIR] = w2[at : at + 2 * PAIR, :].T
        lag = jnp.where(section == last, 0, rows - 1)
        run(dense_forward, dense_backward, lag, lambda: None)


    def total(x):
        return jnp.sum(x, axis=0, keepdims=True)

    lane = lax.broadcasted_iota(jnp.int32, (1, dim), 1)
    counts = jnp.zeros((1, dim), F32)
    for k, x in enumerate((sq_acc[0], sq_acc[1], val[...].astype(F32))):
        amount = jnp.sum(jnp.sum(x, axis=0, keepdims=True), axis=1, keepdims=True)
        counts = jnp.where(lane == k, amount, counts)
    small_o[0:1, :] = total(norm_acc[0])
    small_o[1:2, :] = total(norm_acc[1])
    for k in range(ff // dim):
        small_o[2 + k : 3 + k, :] = total(in_acc[:, k * dim : (k + 1) * dim])
    small_o[2 + ff // dim : 3 + ff // dim, :] = total(out_acc[...])
    small_o[3 + ff // dim : 4 + ff // dim, :] = counts

    def drain(i, carry):
        for k in (0, 1, 2, 3, 5):
            out_copy(k, i).wait()

        @pl.when(jnp.logical_not(is_attention))
        def _():
            out_copy(4, i).wait()

        @pl.when(section < last)
        def _():
            h_copy(i).wait_send()

        @pl.when(section > 0)
        def _():
            g_copy(i).wait_send()

        return carry

    lax.fori_loop(0, rows, drain, 0)


def run_pipeline(start, cot, first, second, norm, bias, seg, val):
    rows, seq, dim = start.shape
    ff = first.shape[2]
    block = (rows, seq, dim)
    wide = (rows, seq, ff)
    any_space = pl.BlockSpec(memory_space=pl.ANY)
    vmem = pl.BlockSpec(memory_space=pltpu.VMEM)
    out = jax.ShapeDtypeStruct
    return pl.pallas_call(
        pipeline_kernel,
        out_shape=(
            out(block, BF16), out(block, BF16), out(block, BF16), out(block, BF16),
            out(wide, BF16), out(wide, BF16), out((4 + ff // dim, dim), F32),
        ),
        in_specs=[any_space] * 4 + [vmem] * 4,
        out_specs=(any_space,) * 6 + (vmem,),
        scratch_shapes=[
            pltpu.VMEM((dim, ff), BF16), pltpu.VMEM((ff, dim), BF16),
            pltpu.VMEM((ff, dim), BF16), pltpu.VMEM((dim, ff), BF16),
            pltpu.VMEM(block, BF16), pltpu.VMEM(block, BF16),
            pltpu.VMEM(block, BF16), pltpu.VMEM(block, BF16),
            pltpu.VMEM(block, BF16), pltpu.VMEM(wide, BF16), pltpu.VMEM(wide, BF16),
            pltpu.VMEM((2, 8, dim), F32), pltpu.VMEM((2, 8, dim), F32),
            pltpu.VMEM((8, ff), F32), pltpu.VMEM((8, dim), F32),
            pltpu.SemaphoreType.DMA((4,)),
            pltpu.SemaphoreType.DMA((rows,)), pltpu.SemaphoreType.DMA((rows,)),
            pltpu.SemaphoreType.DMA((rows,)), pltpu.SemaphoreType.DMA((rows,)),
            pltpu.SemaphoreType.DMA((6, rows)),
        ],
        compiler_params=pltpu.CompilerParams(
            collective_id=0, has_side_effects=True, vmem_limit_bytes=58 * 2**20
        ),
        name="sublayer_pipeline",
    )(start, cot, first, second, norm, bias, seg, val)


def local(start, cot, first, second, norm, bias, seg, val):
    rows, seq, dim = start.shape
    ff = first.shape[2]
    tokens = rows * seq
    is_attention = lax.axis_index("section") % 2 == 0
    res, sg, nrm, gin, act, mid, small = run_pipeline(
        start, cot, first, second, norm, bias, seg, val
    )
    nrm, gin = nrm.reshape(tokens, dim), gin.reshape(tokens, dim)
    act, mid = act.reshape(tokens, ff), mid.reshape(tokens, ff)
    left = dot(nrm, mid[:, : 3 * dim], TN)
    right = dot(jnp.where(is_attention, gin, nrm), mid[:, 3 * dim :], TN)
    wide = jnp.concatenate([left, right], axis=1).astype(BF16)
    narrow = jnp.where(is_attention, 0.0, dot(act, gin, TN)).astype(BF16)
    wide, narrow, small = lax.psum((wide, narrow, small), "dp")
    stat = small[3 + ff // dim]
    rms = jnp.sqrt(stat[:2] / (stat[2] * dim))
    return (
        res[None],
        sg.astype(F32)[None],
        wide.astype(F32)[None],
        narrow.astype(F32)[None],
        small[:2][None],
        small[2 : 3 + ff // dim].reshape(1, -1),
        rms[None],
    )


def solution(mesh):
    in_specs = (
        P("dp", None, None),
        P("dp", None, None),
        P("section", None, None),
        P("section", None, None),
        P("section", None, None),
        P("section", None),
        P("dp", None),
        P("dp", None),
    )
    out_specs = (
        P("section", "dp", None, None),
        P("section", "dp", None, None),
        P("section", None, None),
        P("section", None, None),
        P("section", None, None),
        P("section", None),
        P("section", None),
    )
    return jax.shard_map(local, mesh=mesh, in_specs=in_specs, out_specs=out_specs, check_vma=False)
```

```python
import functools

import jax
import jax.numpy as jnp
from jax import lax
from jax.experimental import pallas as pl
from jax.experimental.pallas import tpu as pltpu
from jax.sharding import PartitionSpec as P

HEAD_DIM = 64
EPS = 1e-05
NEG_FILL = -1e30
MESH = pl.DeviceIdType.MESH
BF16 = jnp.bfloat16
F32 = jnp.float32
NN = (((1,), (0,)), ((), ()))
NT = (((1,), (1,)), ((), ()))
TN = (((0,), (0,)), ((), ()))
PAIR = 2 * HEAD_DIM
TILE = 1536
CHUNK = 256
SUB = 4
HANDED = 10
GELU_C = 0.7978845608028654
GELU_K = 0.044715


def dot(a, b, dims=NN):
    return lax.dot_general(a, b, dims, preferred_element_type=F32)


def gelu_and_slope(x):
    square = x * x
    t = jnp.tanh(GELU_C * (x + GELU_K * (square * x)))
    half = 0.5 * (1.0 + t)
    slope = half + (0.5 * GELU_C) * x * (1.0 - t * t) * (1.0 + (3.0 * GELU_K) * square)
    return x * half, slope


def fold(x):
    return x.reshape(x.shape[0] // 8, 8, x.shape[1]).sum(axis=0)


def normalize(hidden):
    mean = jnp.mean(hidden, axis=-1, keepdims=True)
    centered = hidden - mean
    variance = jnp.mean(centered * centered, axis=-1, keepdims=True)
    inv_std = lax.rsqrt(variance + EPS)
    return centered * inv_std, inv_std


def sublayer_kernel(
    handed,
    start, cot, first, second, norm, bias, seg, val,
    res_o, sg_o, first_o, second_o, small_o,
    w1, w2, w1t, w2t, hin, hout, pair, gout, act, mid,
    sq_acc, norm_acc, in_acc, out_acc, small,
    sum_a1, sum_b1, sum_c1, sum_a2, sum_b2, sum_c2,
    load_sem, hs_sem, hr_sem, gs_sem, gr_sem, out_sem, small_sem,
    part_send, part_recv, given_recv, line_send, line_recv, whole_recv, back_send,
    mate_send, mate_recv, store_sem,
):
    nrm, gin = pair.at[0], pair.at[1]
    section = lax.axis_index("section")
    dp = lax.axis_index("dp")
    last = lax.axis_size("section") - 1
    rows, seq, dim = start.shape
    ff = first.shape[2]
    pairs = dim // PAIR
    is_attention = section % 2 == 0
    nxt = jnp.minimum(section + 1, last)
    prv = jnp.maximum(section - 1, 0)

    first_load = pltpu.make_async_copy(first.at[0], w1, load_sem.at[0])
    second_load = pltpu.make_async_copy(second.at[0], w2, load_sem.at[1])
    start_load = pltpu.make_async_copy(start, hin, load_sem.at[2])
    cot_load = pltpu.make_async_copy(cot, gin, load_sem.at[3])
    first_load.start()

    @pl.when(section == 0)
    def _():
        start_load.start()

    @pl.when(jnp.logical_not(is_attention))
    def _():
        second_load.start()

    @pl.when(section == last)
    def _():
        cot_load.start()

    chips = lax.axis_size("dp") // 2
    chip, core = dp // 2, dp % 2
    mate = dp + 1 - 2 * core
    on_left = chip < chips // 2
    is_middle = (chip == chips // 2 - 1) | (chip == chips // 2)
    has_outer = (chip > 0) & (chip < chips - 1)
    inner = jnp.where(on_left, dp + 2, dp - 2)
    outer = jnp.clip(jnp.where(on_left, dp - 2, dp + 2), 0, 2 * chips - 1)
    helper = section + 1 - 2 * (section % 2)

    barrier = pltpu.get_barrier_semaphore()

    def greet(to_section, to_dp):
        pl.semaphore_signal(
            barrier, inc=1, device_id=(to_section, to_dp), device_id_type=MESH
        )

    greet(section, mate)
    greet(section, inner)

    @pl.when(has_outer)
    def _():
        greet(section, outer)

    @pl.when(section > 0)
    def _():
        greet(prv, dp)

    @pl.when(section < last)
    def _():
        greet(nxt, dp)

    peers = 3 + has_outer.astype(jnp.int32)
    peers += ((section > 0) & (section < last)).astype(jnp.int32)
    pl.semaphore_wait(barrier, peers)

    for ref in (sq_acc, norm_acc, in_acc, out_acc):
        ref[...] = jnp.zeros_like(ref)

    def h_copy(i):
        return pltpu.make_async_remote_copy(
            hout.at[i], hin.at[i], hs_sem.at[i], hr_sem.at[i],
            device_id=(nxt, dp), device_id_type=MESH,
        )

    def g_copy(i):
        return pltpu.make_async_remote_copy(
            gout.at[i], gin.at[i], gs_sem.at[i], gr_sem.at[i],
            device_id=(prv, dp), device_id_type=MESH,
        )

    def out_copy(k, i):
        src, dst = ((hout, res_o), (gout, sg_o))[k]
        return pltpu.make_async_copy(src.at[i], dst.at[i], out_sem.at[k, i])

    eye = lax.broadcasted_iota(jnp.int32, (seq, seq), 0) == lax.broadcasted_iota(
        jnp.int32, (seq, seq), 1
    )

    def column(row):
        return jnp.sum(jnp.where(eye, row, 0.0), axis=1, keepdims=True)

    def valid_row(i):
        return val[pl.ds(i, 1), :].astype(F32)

    def entry(i):
        @pl.when(section > 0)
        def _():
            h_copy(i).wait_recv()

        hidden = hin[i].astype(F32)
        normal, _ = normalize(hidden)
        low = (normal * norm[0, 0:1, :] + norm[0, 1:2, :]).astype(BF16)
        nrm[i] = low
        return hidden, low

    def leave(i, hidden, branch):
        low = (hidden + branch).astype(BF16)
        hout[i] = low

        @pl.when(section < last)
        def _():
            h_copy(i).start()

        out_copy(0, i).start()
        weight = column(valid_row(i))
        value = low.astype(F32)
        sq_acc[0] += fold(value * value * weight)
        sq_acc[1] += fold(branch * branch * weight)

    def grad_entry(i):
        @pl.when(section < last)
        def _():
            g_copy(i).wait_recv()

        @pl.when(section == last)
        def _():
            gin[i] = jnp.where(column(valid_row(i)) > 0, gin[i], jnp.zeros((seq, dim), BF16))

        return gin[i]

    def grad_leave(i, grad, normed_grad):
        grad_value = grad.astype(F32)
        normal, inv_std = normalize(hin[i].astype(F32))
        scaled = normed_grad * norm[0, 0:1, :]
        mean_one = jnp.mean(scaled, axis=-1, keepdims=True)
        mean_two = jnp.mean(scaled * normal, axis=-1, keepdims=True)
        low = (grad_value + inv_std * (scaled - mean_one - normal * mean_two)).astype(BF16)
        gout[i] = low

        @pl.when(section > 0)
        def _():
            g_copy(i).start()

        out_copy(1, i).start()
        norm_acc[0] += fold(normed_grad * normal)
        norm_acc[1] += fold(normed_grad)
        out_acc[...] += fold(grad_value)


    def dense_forward(i):
        hidden, low = entry(i)
        branch = jnp.zeros((seq, dim), F32)
        for at in range(0, ff, TILE):
            cols = slice(at, at + TILE)
            value, slope = gelu_and_slope(dot(low, w1[:, cols]) + bias[0:1, cols])
            value = value.astype(BF16)
            act[i, :, cols] = value
            mid[i, :, cols] = slope.astype(BF16)
            branch += dot(value, w2[cols, :])
        leave(i, hidden, branch + bias[0:1, ff:])

    def dense_backward(i):
        grad = grad_entry(i)
        normed_grad = jnp.zeros((seq, dim), F32)
        for at in range(0, ff, TILE):
            cols = slice(at, at + TILE)
            inner = dot(grad, w2t[:, cols]) * mid[i, :, cols].astype(F32)
            low = inner.astype(BF16)
            mid[i, :, cols] = low
            in_acc[:, cols] += fold(low.astype(F32))
            normed_grad += dot(low, w1t[cols, :])
        grad_leave(i, grad, normed_grad)


    lower = lax.broadcasted_iota(jnp.int32, (seq, PAIR), 1) < HEAD_DIM

    def split_heads(x):
        zero = jnp.zeros_like(x)
        return jnp.concatenate([jnp.where(lower, x, zero), jnp.where(lower, zero, x)], axis=0)

    def join_heads(x):
        return jnp.where(lower, x[:seq], x[seq:])

    def attention_forward(i):
        hidden, low = entry(i)
        projected = dot(low, w1[:, : 3 * dim])
        mid[i, :, :dim] = (projected[:, :dim] + bias[0:1, :dim]).astype(BF16)
        mid[i, :, dim : 2 * dim] = projected[:, dim : 2 * dim].astype(BF16)
        mid[i, :, 2 * dim : 3 * dim] = (
            projected[:, 2 * dim :] + bias[0:1, dim : 2 * dim]
        ).astype(BF16)
        seg_row = seg[pl.ds(i, 1), :].astype(F32)
        allowed = (column(seg_row) == seg_row) & ((valid_row(i) > 0) | eye)
        for p in range(pairs):
            at = p * PAIR
            query = mid[i, :, at : at + PAIR]
            keys = split_heads(mid[i, :, dim + at : dim + at + PAIR])
            values = split_heads(mid[i, :, 2 * dim + at : 2 * dim + at + PAIR])
            scores = dot(query, keys, NT) * HEAD_DIM**-0.5
            probs = []
            for half in (scores[:, :seq], scores[:, seq:]):
                half = jnp.where(allowed, half, NEG_FILL)
                weight = jnp.exp(half - jnp.max(half, axis=-1, keepdims=True))
                probs.append(weight / jnp.sum(weight, axis=-1, keepdims=True))
            prob = jnp.concatenate(probs, axis=1).astype(BF16)
            act[i, :, 2 * seq * p : 2 * seq * (p + 1)] = prob
            mid[i, :, 3 * dim + at : 3 * dim + at + PAIR] = dot(prob, values).astype(BF16)
        branch = dot(mid[i, :, 3 * dim :], w1t[3 * dim :, :]) + bias[0:1, ff:]
        leave(i, hidden, branch)

    def attention_backward(i):
        grad = grad_entry(i)
        mixed_grad = dot(grad, w1[:, 3 * dim :]).astype(BF16)
        for p in range(pairs):
            at = p * PAIR
            query = mid[i, :, at : at + PAIR]
            keys = split_heads(mid[i, :, dim + at : dim + at + PAIR])
            values = split_heads(mid[i, :, 2 * dim + at : 2 * dim + at + PAIR])
            prob = act[i, :, 2 * seq * p : 2 * seq * (p + 1)]
            out_grad = mixed_grad[:, at : at + PAIR]
            prob_grad = dot(out_grad, values, NT)
            prob_value = prob.astype(F32)
            parts = []
            for cols in (slice(0, seq), slice(seq, 2 * seq)):
                pv, pg = prob_value[:, cols], prob_grad[:, cols]
                parts.append(pv * (pg - jnp.sum(pv * pg, axis=-1, keepdims=True)))
            score_grad = jnp.concatenate(parts, axis=1).astype(BF16)
            query_grad = dot(score_grad, keys) * HEAD_DIM**-0.5
            key_grad = join_heads(dot(score_grad, query, TN)) * HEAD_DIM**-0.5
            value_grad = join_heads(dot(prob, out_grad, TN))
            mid[i, :, at : at + PAIR] = query_grad.astype(BF16)
            mid[i, :, dim + at : dim + at + PAIR] = key_grad.astype(BF16)
            mid[i, :, 2 * dim + at : 2 * dim + at + PAIR] = value_grad.astype(BF16)
        packed = mid[i, :, : 3 * dim]
        normed_grad = dot(packed, w1t[: 3 * dim, :])
        grad_leave(i, grad, normed_grad)
        in_acc[:, :dim] += fold(packed[:, :dim].astype(F32))
        in_acc[:, dim : 2 * dim] += fold(packed[:, 2 * dim :].astype(F32))

    first_load.wait()

    def transpose(src, dst, low, high):
        for at in range(low, high, 2 * PAIR):
            dst[at : at + 2 * PAIR, :] = src[:, at : at + 2 * PAIR].T

    @pl.when(section == 0)
    def _():
        start_load.wait()

    @pl.when(section == last)
    def _():
        cot_load.wait()

    def run(forward, backward, lag, before_last):
        def step(i, carry):
            @pl.when(i == rows - 1)
            def _():
                before_last()

            @pl.when(i < rows)
            def _():
                forward(i)

            @pl.when(i >= lag)
            def _():
                backward(i - lag)

            return carry

        lax.fori_loop(0, rows + lag, step, 0)

    @pl.when(is_attention)
    def _():
        transpose(w1, w1t, 3 * dim, ff)

        def late():
            @pl.when(section == 0)
            def _():
                transpose(w1, w1t, 0, 3 * dim)

        @pl.when(section > 0)
        def _():
            transpose(w1, w1t, 0, 3 * dim)

        lag = jnp.where(section == 0, rows, rows // 2)
        run(attention_forward, attention_backward, lag, late)

    @pl.when(jnp.logical_not(is_attention))
    def _():
        second_load.wait()
        transpose(w1, w1t, 0, ff)
        for at in range(0, ff, 2 * PAIR):
            w2t[:, at : at + 2 * PAIR] = w2[at : at + 2 * PAIR, :].T
        lag = jnp.where(section == last, 0, rows - 1)
        run(dense_forward, dense_backward, lag, lambda: None)


    def total(x):
        return jnp.sum(x, axis=0, keepdims=True)

    lane = lax.broadcasted_iota(jnp.int32, (1, dim), 1)
    counts = jnp.zeros((1, dim), F32)
    for k, x in enumerate((sq_acc[0], sq_acc[1], val[...].astype(F32))):
        amount = jnp.sum(jnp.sum(x, axis=0, keepdims=True), axis=1, keepdims=True)
        counts = jnp.where(lane == k, amount, counts)
    small[0, 0:1, :] = total(norm_acc[0])
    small[0, 1:2, :] = total(norm_acc[1])
    for k in range(ff // dim):
        small[0, 2 + k : 3 + k, :] = total(in_acc[:, k * dim : (k + 1) * dim])
    small[0, 2 + ff // dim : 3 + ff // dim, :] = total(out_acc[...])
    small[0, 3 + ff // dim : 4 + ff // dim, :] = counts

    def remote(src, dst, send, recv, to):
        return pltpu.make_async_remote_copy(
            src, dst, send, recv, device_id=to, device_id_type=MESH
        )

    small_mate = remote(
        small.at[0], small.at[1], small_sem.at[0], small_sem.at[1], (section, mate)
    )
    small_line = remote(
        small.at[0], small.at[2], small_sem.at[2], small_sem.at[3], (section, inner)
    )
    small_cross = remote(
        small.at[0], small.at[3], small_sem.at[2], small_sem.at[4], (section, inner)
    )
    small_back = remote(
        small.at[3], small.at[3], small_sem.at[5], small_sem.at[4], (section, outer)
    )
    small_mate.start()


    tokens = rows * seq
    half = ff // 2
    steps = (half // CHUNK) * SUB
    tall, short = dim // SUB, CHUNK // SUB
    mine, theirs = core * half, (1 - core) * half

    def own(k, v):
        if k == 0:
            return w1.at[
                pl.ds(pl.multiple_of((v % SUB) * tall, 16), tall),
                pl.ds(pl.multiple_of(mine + (v // SUB) * CHUNK, CHUNK), CHUNK),
            ]
        return w2.at[pl.ds(pl.multiple_of(mine + v * short, 16), short), :]

    def stored(k, v):
        if k == 0:
            return first_o.at[
                pl.ds(pl.multiple_of((v % SUB) * tall, 16), tall),
                pl.ds(pl.multiple_of(mine + (v // SUB) * CHUNK, CHUNK), CHUNK),
            ]
        return second_o.at[pl.ds(pl.multiple_of(mine + v * short, 16), short), :]

    def slot(ref, k, v):
        if k == 0:
            return ref.at[
                pl.ds(pl.multiple_of((v % SUB) * tall, 16), tall),
                pl.ds(pl.multiple_of((v // SUB) * CHUNK, CHUNK), CHUNK),
            ]
        return ref.at[pl.ds(pl.multiple_of(v * short, 16), short), :]

    near, line, whole = (sum_a1, sum_a2), (sum_b1, sum_b2), (sum_c1, sum_c2)

    def part_copy(k, c):
        at = pl.ds(pl.multiple_of(theirs + c * CHUNK, CHUNK), CHUNK)
        to = pl.ds(pl.multiple_of(c * CHUNK, CHUNK), CHUNK)
        src, dst = (w1.at[:, at], sum_a1.at[:, to]) if k == 0 else (w2.at[at, :], sum_a2.at[to, :])
        return remote(src, dst, part_send.at[k, c], part_recv.at[k, c], (section, mate))

    def line_copy(k, v):
        return remote(
            own(k, v), slot(line[k], k, v), line_send.at[k, v], line_recv.at[k, v], (section, inner)
        )

    def cross_copy(k, v):
        return remote(
            own(k, v), slot(whole[k], k, v), line_send.at[k, v], whole_recv.at[k, v], (section, inner)
        )

    def given_copy(v):
        return remote(
            own(1, v), slot(sum_a2, 1, v), line_send.at[1, v], given_recv.at[v], (helper, dp)
        )

    def return_copy(v):
        ref = slot(sum_c2, 1, v)
        return remote(ref, ref, mate_send.at[1, v], whole_recv.at[1, v], (helper, dp))

    def back_copy(k, v):
        ref = slot(whole[k], k, v)
        return remote(ref, ref, back_send.at[k, v], whole_recv.at[k, v], (section, outer))

    def mate_copy(k, v):
        return remote(
            slot(whole[k], k, v), stored(k, v), mate_send.at[k, v], mate_recv.at[k, v], (section, mate)
        )

    def store_copy(k, v):
        return pltpu.make_async_copy(slot(whole[k], k, v), stored(k, v), store_sem.at[k, v])

    def compute(k, c):
        for base, is_sent in ((theirs, True), (mine, False)):
            at = pl.ds(pl.multiple_of(base + c * CHUNK, CHUNK), CHUNK)
            if k == 0:
                side = is_attention & (base + c * CHUNK >= 3 * dim)
                left = pair[side.astype(jnp.int32)].reshape(tokens, dim)
                right = mid[:, :, at].reshape(tokens, CHUNK)
                w1[:, at] = dot(left, right, TN).astype(BF16)
            else:
                left = act[:, :, at].reshape(tokens, CHUNK)
                w2[at, :] = dot(left, gin[...].reshape(tokens, dim), TN).astype(BF16)
            if is_sent:
                part_copy(k, c).start()

    def combine(dst, *refs):
        value = refs[0][...].astype(F32)
        for ref in refs[1:]:
            value += ref[...].astype(F32)
        dst[...] = value.astype(BF16)

    def send_in(k, v, *refs):
        @pl.when(has_outer)
        def _():
            line_copy(k, v).wait_recv()
            combine(own(k, v), *refs, slot(line[k], k, v))

        @pl.when(jnp.logical_not(has_outer))
        def _():
            combine(own(k, v), *refs)

        @pl.when(is_middle)
        def _():
            cross_copy(k, v).start()

        @pl.when(jnp.logical_not(is_middle))
        def _():
            line_copy(k, v).start()

    def send_first(v):
        @pl.when(v % SUB == 0)
        def _():
            part_copy(0, v // SUB).wait_recv()

        send_in(0, v, own(0, v), slot(sum_a1, 0, v))

    def send_second(v):
        @pl.when(v % SUB == 0)
        def _():
            part_copy(1, v // SUB).wait_recv()

        @pl.when(v < handed)
        def _():
            combine(own(1, v), own(1, v), slot(sum_a2, 1, v))
            given_copy(v).start()

        @pl.when(v >= handed)
        def _():
            send_in(1, v, own(1, v), slot(sum_a2, 1, v))

    def send_given(v):
        given_copy(v).wait_recv()
        send_in(1, v, slot(sum_a2, 1, v))

    def settle(k, v):
        cross_copy(k, v).wait_recv()

        @pl.when(is_middle)
        def _():
            combine(slot(whole[k], k, v), own(k, v), slot(whole[k], k, v))

        @pl.when(has_outer)
        def _():
            back_copy(k, v).start()

    def finish(k, v):
        mate_copy(k, v).start()
        store_copy(k, v).start()

    def settle_second(v):
        @pl.when(v < handed)
        def _():
            cross_copy(1, v).wait_recv()

        @pl.when(v >= handed)
        def _():
            settle(1, v)

        finish(1, v)

    def settle_first(v):
        settle(0, v)
        finish(0, v)

    def settle_given(v):
        settle(1, v)
        return_copy(v).start()

    def small_in():
        small_mate.wait_recv()
        small_mate.wait_send()
        small[0] += small[1]

        @pl.when(has_outer)
        def _():
            small_line.wait_recv()
            small[0] += small[2]

        @pl.when(is_middle)
        def _():
            small_cross.start()

        @pl.when(jnp.logical_not(is_middle))
        def _():
            small_line.start()

    def small_settle():
        small_cross.wait_recv()

        @pl.when(is_middle)
        def _():
            small[3] += small[0]

        @pl.when(has_outer)
        def _():
            small_back.start()

        small_o[...] = small[3]

    gap = jnp.where(on_left, chips // 2 - 1 - chip, chip - chips // 2)
    lag = 2 + 6 * gap
    begin = jnp.where(is_attention, min(steps - handed, steps - SUB), 0)

    @pl.when(jnp.logical_not(is_attention))
    def _():
        compute(1, 0)

    def step(u, carry):
        @pl.when(u < steps)
        def _():
            v = u - (steps - handed)

            @pl.when(jnp.logical_not(is_attention))
            def _():
                send_second(u)

            @pl.when(is_attention & (v >= 0))
            def _():
                send_given(v)

        @pl.when((u >= steps) & (u < 2 * steps))
        def _():
            send_first(u - steps)

        t = u - lag

        @pl.when((t >= begin) & is_attention)
        def _():
            v = t - (steps - handed)

            @pl.when((v >= 0) & (v < handed))
            def _():
                settle_given(v)

            @pl.when((t >= steps) & (t < 2 * steps))
            def _():
                settle_first(t - steps)

        @pl.when((t >= handed) & jnp.logical_not(is_attention))
        def _():
            @pl.when(t < steps)
            def _():
                settle_second(t)

            @pl.when((t >= steps) & (t < 2 * steps))
            def _():
                settle_first(t - steps)

            @pl.when(t >= 2 * steps)
            def _():
                settle_second(t - 2 * steps)

        @pl.when(u % SUB == 0)
        def _():
            c = u // SUB + 1

            @pl.when((c < steps // SUB) & jnp.logical_not(is_attention))
            def _():
                compute(1, c)

            @pl.when((c >= steps // SUB) & (c < 2 * (steps // SUB)))
            def _():
                compute(0, c - steps // SUB)

        @pl.when(u == steps + SUB)
        def _():
            small_in()

        @pl.when(t == steps + SUB)
        def _():
            small_settle()

        return carry

    lax.fori_loop(begin, 2 * steps + handed + lag, step, 0)


    def drain_streams(i, carry):
        out_copy(0, i).wait()
        out_copy(1, i).wait()

        @pl.when(section < last)
        def _():
            h_copy(i).wait_send()

        @pl.when(section > 0)
        def _():
            g_copy(i).wait_send()

        return carry

    lax.fori_loop(0, rows, drain_streams, 0)

    def drain_chunks(c, carry):
        part_copy(0, c).wait_send()

        @pl.when(jnp.logical_not(is_attention))
        def _():
            part_copy(1, c).wait_send()

        return carry

    lax.fori_loop(0, steps // SUB, drain_chunks, 0)

    def drain_sums(v, carry):
        def both(k, there):
            line_copy(k, v).wait_send()

            @pl.when(there & has_outer)
            def _():
                back_copy(k, v).wait_send()

        both(0, True)
        mate_copy(0, v).wait()
        store_copy(0, v).wait()

        @pl.when(jnp.logical_not(is_attention))
        def _():
            both(1, v >= handed)
            mate_copy(1, v).wait()
            store_copy(1, v).wait()

        @pl.when(is_attention & (v < handed))
        def _():
            both(1, True)
            return_copy(v).wait_send()

        return carry

    lax.fori_loop(0, steps, drain_sums, 0)
    small_line.wait_send()

    @pl.when(has_outer)
    def _():
        small_back.wait_send()


def run_sublayers(start, cot, first, second, norm, bias, seg, val):
    rows, seq, dim = start.shape
    ff = first.shape[2]
    half = ff // 2
    steps = (half // CHUNK) * SUB
    block = (rows, seq, dim)
    wide = (rows, seq, ff)
    small = (4 + ff // dim, dim)
    any_space = pl.BlockSpec(memory_space=pl.ANY)
    vmem = pl.BlockSpec(memory_space=pltpu.VMEM)
    out = jax.ShapeDtypeStruct
    dma = pltpu.SemaphoreType.DMA
    return pl.pallas_call(
        functools.partial(sublayer_kernel, HANDED),
        out_shape=(
            out(block, BF16), out(block, BF16), out((dim, ff), BF16), out((ff, dim), BF16),
            out(small, F32),
        ),
        in_specs=[any_space] * 4 + [vmem] * 4,
        out_specs=(any_space,) * 4 + (vmem,),
        scratch_shapes=[
            pltpu.VMEM((dim, ff), BF16), pltpu.VMEM((ff, dim), BF16),
            pltpu.VMEM((ff, dim), BF16), pltpu.VMEM((dim, ff), BF16),
            pltpu.VMEM(block, BF16), pltpu.VMEM(block, BF16),
            pltpu.VMEM((2, *block), BF16), pltpu.VMEM(block, BF16),
            pltpu.VMEM(wide, BF16), pltpu.VMEM(wide, BF16),
            pltpu.VMEM((2, 8, dim), F32), pltpu.VMEM((2, 8, dim), F32),
            pltpu.VMEM((8, ff), F32), pltpu.VMEM((8, dim), F32),
            pltpu.VMEM((4, *small), F32),
            pltpu.VMEM((dim, half), BF16), pltpu.VMEM((dim, half), BF16),
            pltpu.VMEM((dim, half), BF16), pltpu.VMEM((half, dim), BF16),
            pltpu.VMEM((half, dim), BF16), pltpu.VMEM((half, dim), BF16),
            dma((4,)), dma((rows,)), dma((rows,)), dma((rows,)), dma((rows,)),
            dma((2, rows)), dma((6,)),
            dma((2, steps // SUB)), dma((2, steps // SUB)), dma((steps,)),
            dma((2, steps)), dma((2, steps)), dma((2, steps)), dma((2, steps)),
            dma((2, steps)), dma((2, steps)), dma((2, steps)),
        ],
        compiler_params=pltpu.CompilerParams(
            collective_id=0, has_side_effects=True, vmem_limit_bytes=60 * 2**20
        ),
        name="sublayer",
    )(start, cot, first, second, norm, bias, seg, val)


def local(start, cot, first, second, norm, bias, seg, val):
    rows, seq, dim = start.shape
    ff = first.shape[2]
    is_attention = lax.axis_index("section") % 2 == 0
    res, sg, wide, narrow, small = run_sublayers(
        start, cot, first, second, norm, bias, seg, val
    )
    stat = small[3 + ff // dim]
    rms = jnp.sqrt(stat[:2] / (stat[2] * dim))
    return (
        res[None],
        sg.astype(F32)[None],
        wide.astype(F32)[None],
        jnp.where(is_attention, 0.0, narrow.astype(F32))[None],
        small[:2][None],
        small[2 : 3 + ff // dim].reshape(1, -1),
        rms[None],
    )


def solution(mesh):
    in_specs = (
        P("dp", None, None),
        P("dp", None, None),
        P("section", None, None),
        P("section", None, None),
        P("section", None, None),
        P("section", None),
        P("dp", None),
        P("dp", None),
    )
    out_specs = (
        P("section", "dp", None, None),
        P("section", "dp", None, None),
        P("section", None, None),
        P("section", None, None),
        P("section", None, None),
        P("section", None),
        P("section", None),
    )
    return jax.shard_map(local, mesh=mesh, in_specs=in_specs, out_specs=out_specs, check_vma=False)
```

```python
import functools

import jax
import jax.numpy as jnp
from jax import lax
from jax.experimental import pallas as pl
from jax.experimental.pallas import tpu as pltpu
from jax.sharding import PartitionSpec as P

HEAD_DIM = 64
EPS = 1e-05
NEG_FILL = -1e30
MESH = pl.DeviceIdType.MESH
BF16 = jnp.bfloat16
F32 = jnp.float32
NN = (((1,), (0,)), ((), ()))
NT = (((1,), (1,)), ((), ()))
TN = (((0,), (0,)), ((), ()))
PAIR = 2 * HEAD_DIM
TILE = 1536
CHUNK = 256
SUB = 4
HANDED = 10
LOADS = 4
WRITES = 12
SUBLAYER_VMEM = 50 * 2**20
FINISH_VMEM = 40 * 2**20
GELU_C = 0.7978845608028654
GELU_K = 0.044715


def dot(a, b, dims=NN):
    return lax.dot_general(a, b, dims, preferred_element_type=F32)


def gelu_and_slope(x):
    square = x * x
    t = jnp.tanh(GELU_C * (x + GELU_K * (square * x)))
    half = 0.5 * (1.0 + t)
    slope = half + (0.5 * GELU_C) * x * (1.0 - t * t) * (1.0 + (3.0 * GELU_K) * square)
    return x * half, slope


def fold(x):
    return x.reshape(x.shape[0] // 8, 8, x.shape[1]).sum(axis=0)


def normalize(hidden):
    mean = jnp.mean(hidden, axis=-1, keepdims=True)
    centered = hidden - mean
    variance = jnp.mean(centered * centered, axis=-1, keepdims=True)
    inv_std = lax.rsqrt(variance + EPS)
    return centered * inv_std, inv_std


def sublayer_kernel(
    handed,
    start, cot, first, second, norm_in, bias_in, seg_in, val_in,
    hout, gout, first_o, second_o, small_o,
    w1, w2, w1t, w2t, hin, pair, act, mid,
    norm, bias, seg, val, sq_acc, norm_acc, in_acc, out_acc, small,
    sum_a1, sum_b1, sum_a2, sum_b2,
    load_sem, hs_sem, hr_sem, gs_sem, gr_sem, small_sem,
    part_send, part_recv, given_recv, line_send, line_recv, whole_recv, back_send,
    mate_send, mate_recv,
):
    nrm, gin = pair.at[0], pair.at[1]
    section = lax.axis_index("section")
    dp = lax.axis_index("dp")
    last = lax.axis_size("section") - 1
    rows, seq, dim = start.shape
    ff = first.shape[2]
    pairs = dim // PAIR
    is_attention = section % 2 == 0
    nxt = jnp.minimum(section + 1, last)
    prv = jnp.maximum(section - 1, 0)

    first_load = pltpu.make_async_copy(first.at[0], w1, load_sem.at[0])
    second_load = pltpu.make_async_copy(second.at[0], w2, load_sem.at[1])
    start_load = pltpu.make_async_copy(start, hin, load_sem.at[2])
    cot_load = pltpu.make_async_copy(cot, gin, load_sem.at[3])
    small_loads = [
        pltpu.make_async_copy(src, dst, load_sem.at[4 + k])
        for k, (src, dst) in enumerate(
            ((norm_in, norm), (bias_in, bias), (seg_in, seg), (val_in, val))
        )
    ]

    def split_load(src, dst, k):
        count = dst.shape[0] // LOADS
        for at in range(0, dst.shape[0], count):
            pltpu.make_async_copy(
                src.at[0, pl.ds(at, count)], dst.at[pl.ds(at, count)], load_sem.at[k]
            ).start()

    split_load(first, w1, 0)

    @pl.when(section == 0)
    def _():
        start_load.start()

    for load in small_loads:
        load.start()

    @pl.when(jnp.logical_not(is_attention))
    def _():
        split_load(second, w2, 1)

    @pl.when(section == last)
    def _():
        cot_load.start()

    chips = lax.axis_size("dp") // 2
    chip, core = dp // 2, dp % 2
    mate = dp + 1 - 2 * core
    on_left = chip < chips // 2
    is_middle = (chip == chips // 2 - 1) | (chip == chips // 2)
    has_outer = (chip > 0) & (chip < chips - 1)
    inner = jnp.where(on_left, dp + 2, dp - 2)
    outer = jnp.clip(jnp.where(on_left, dp - 2, dp + 2), 0, 2 * chips - 1)
    helper = section + 1 - 2 * (section % 2)

    barrier = pltpu.get_barrier_semaphore()

    def greet(to_section, to_dp):
        pl.semaphore_signal(
            barrier, inc=1, device_id=(to_section, to_dp), device_id_type=MESH
        )

    greet(section, mate)
    greet(section, inner)

    @pl.when(has_outer)
    def _():
        greet(section, outer)

    @pl.when(section > 0)
    def _():
        greet(prv, dp)

    @pl.when(section < last)
    def _():
        greet(nxt, dp)

    peers = 3 + has_outer.astype(jnp.int32)
    peers += ((section > 0) & (section < last)).astype(jnp.int32)

    for ref in (sq_acc, norm_acc, in_acc, out_acc):
        ref[...] = jnp.zeros_like(ref)

    def h_copy(i):
        return pltpu.make_async_remote_copy(
            hout.at[i], hin.at[i], hs_sem, hr_sem.at[i],
            device_id=(nxt, dp), device_id_type=MESH,
        )

    def g_copy(i):
        return pltpu.make_async_remote_copy(
            gout.at[i], gin.at[i], gs_sem, gr_sem.at[i],
            device_id=(prv, dp), device_id_type=MESH,
        )

    eye = lax.broadcasted_iota(jnp.int32, (seq, seq), 0) == lax.broadcasted_iota(
        jnp.int32, (seq, seq), 1
    )

    def column(row):
        return jnp.sum(jnp.where(eye, row, 0.0), axis=1, keepdims=True)

    def valid_row(i):
        return val[pl.ds(i, 1), :].astype(F32)

    def entry(i):
        @pl.when(section > 0)
        def _():
            h_copy(i).wait_recv()

        hidden = hin[i].astype(F32)
        normal, _ = normalize(hidden)
        low = (normal * norm[0, 0:1, :] + norm[0, 1:2, :]).astype(BF16)
        nrm[i] = low
        return hidden, low

    def leave(i, hidden, branch):
        low = (hidden + branch).astype(BF16)
        hout[i] = low

        @pl.when(section < last)
        def _():
            h_copy(i).start()

        weight = column(valid_row(i))
        value = low.astype(F32)
        sq_acc[0] += fold(value * value * weight)
        sq_acc[1] += fold(branch * branch * weight)

    def grad_entry(i):
        @pl.when(section < last)
        def _():
            g_copy(i).wait_recv()

        @pl.when(section == last)
        def _():
            gin[i] = jnp.where(column(valid_row(i)) > 0, gin[i], jnp.zeros((seq, dim), BF16))

        return gin[i]

    def grad_leave(i, grad, normed_grad):
        grad_value = grad.astype(F32)
        normal, inv_std = normalize(hin[i].astype(F32))
        scaled = normed_grad * norm[0, 0:1, :]
        mean_one = jnp.mean(scaled, axis=-1, keepdims=True)
        mean_two = jnp.mean(scaled * normal, axis=-1, keepdims=True)
        low = (grad_value + inv_std * (scaled - mean_one - normal * mean_two)).astype(BF16)
        gout[i] = low

        @pl.when(section > 0)
        def _():
            g_copy(i).start()

        norm_acc[0] += fold(normed_grad * normal)
        norm_acc[1] += fold(normed_grad)
        out_acc[...] += fold(grad_value)


    def dense_forward(i):
        hidden, low = entry(i)
        branch = jnp.zeros((seq, dim), F32)
        for at in range(0, ff, TILE):
            cols = slice(at, at + TILE)
            value, slope = gelu_and_slope(dot(low, w1[:, cols]) + bias[0:1, cols])
            value = value.astype(BF16)
            act[i, :, cols] = value
            mid[i, :, cols] = slope.astype(BF16)
            branch += dot(value, w2[cols, :])
        leave(i, hidden, branch + bias[0:1, ff:])

    def dense_backward(i):
        grad = grad_entry(i)
        normed_grad = jnp.zeros((seq, dim), F32)
        for at in range(0, ff, TILE):
            cols = slice(at, at + TILE)
            inner = dot(grad, w2t[:, cols]) * mid[i, :, cols].astype(F32)
            low = inner.astype(BF16)
            mid[i, :, cols] = low
            in_acc[:, cols] += fold(low.astype(F32))
            normed_grad += dot(low, w1t[cols, :])
        grad_leave(i, grad, normed_grad)


    lower = lax.broadcasted_iota(jnp.int32, (seq, PAIR), 1) < HEAD_DIM

    def split_heads(x):
        zero = jnp.zeros_like(x)
        return jnp.concatenate([jnp.where(lower, x, zero), jnp.where(lower, zero, x)], axis=0)

    def join_heads(x):
        return jnp.where(lower, x[:seq], x[seq:])

    def attention_forward(i):
        hidden, low = entry(i)
        projected = dot(low, w1[:, : 3 * dim])
        mid[i, :, :dim] = (projected[:, :dim] + bias[0:1, :dim]).astype(BF16)
        mid[i, :, dim : 2 * dim] = projected[:, dim : 2 * dim].astype(BF16)
        mid[i, :, 2 * dim : 3 * dim] = (
            projected[:, 2 * dim :] + bias[0:1, dim : 2 * dim]
        ).astype(BF16)
        seg_row = seg[pl.ds(i, 1), :].astype(F32)
        allowed = (column(seg_row) == seg_row) & ((valid_row(i) > 0) | eye)
        for p in range(pairs):
            at = p * PAIR
            query = mid[i, :, at : at + PAIR]
            keys = split_heads(mid[i, :, dim + at : dim + at + PAIR])
            values = split_heads(mid[i, :, 2 * dim + at : 2 * dim + at + PAIR])
            scores = dot(query, keys, NT) * HEAD_DIM**-0.5
            probs = []
            for half in (scores[:, :seq], scores[:, seq:]):
                half = jnp.where(allowed, half, NEG_FILL)
                weight = jnp.exp(half - jnp.max(half, axis=-1, keepdims=True))
                probs.append(weight / jnp.sum(weight, axis=-1, keepdims=True))
            prob = jnp.concatenate(probs, axis=1).astype(BF16)
            act[i, :, 2 * seq * p : 2 * seq * (p + 1)] = prob
            mid[i, :, 3 * dim + at : 3 * dim + at + PAIR] = dot(prob, values).astype(BF16)
        branch = dot(mid[i, :, 3 * dim :], w1t[3 * dim :, :]) + bias[0:1, ff:]
        leave(i, hidden, branch)

    def attention_backward(i):
        grad = grad_entry(i)
        mixed_grad = dot(grad, w1[:, 3 * dim :]).astype(BF16)
        for p in range(pairs):
            at = p * PAIR
            query = mid[i, :, at : at + PAIR]
            keys = split_heads(mid[i, :, dim + at : dim + at + PAIR])
            values = split_heads(mid[i, :, 2 * dim + at : 2 * dim + at + PAIR])
            prob = act[i, :, 2 * seq * p : 2 * seq * (p + 1)]
            out_grad = mixed_grad[:, at : at + PAIR]
            prob_grad = dot(out_grad, values, NT)
            prob_value = prob.astype(F32)
            parts = []
            for cols in (slice(0, seq), slice(seq, 2 * seq)):
                pv, pg = prob_value[:, cols], prob_grad[:, cols]
                parts.append(pv * (pg - jnp.sum(pv * pg, axis=-1, keepdims=True)))
            score_grad = jnp.concatenate(parts, axis=1).astype(BF16)
            query_grad = dot(score_grad, keys) * HEAD_DIM**-0.5
            key_grad = join_heads(dot(score_grad, query, TN)) * HEAD_DIM**-0.5
            value_grad = join_heads(dot(prob, out_grad, TN))
            mid[i, :, at : at + PAIR] = query_grad.astype(BF16)
            mid[i, :, dim + at : dim + at + PAIR] = key_grad.astype(BF16)
            mid[i, :, 2 * dim + at : 2 * dim + at + PAIR] = value_grad.astype(BF16)
        packed = mid[i, :, : 3 * dim]
        normed_grad = dot(packed, w1t[: 3 * dim, :])
        grad_leave(i, grad, normed_grad)
        in_acc[:, :dim] += fold(packed[:, :dim].astype(F32))
        in_acc[:, dim : 2 * dim] += fold(packed[:, 2 * dim :].astype(F32))

    for load in small_loads:
        load.wait()
    first_load.wait()

    def transpose(src, dst, low, high):
        for at in range(low, high, 2 * PAIR):
            dst[at : at + 2 * PAIR, :] = src[:, at : at + 2 * PAIR].T

    @pl.when(section == 0)
    def _():
        start_load.wait()

    @pl.when(section == last)
    def _():
        cot_load.wait()

    def run(forward, backward, lag, before_last):
        pl.semaphore_wait(barrier, peers)

        def step(i, carry):
            @pl.when(i == rows - 1)
            def _():
                before_last()

            @pl.when(i < rows)
            def _():
                forward(i)

            @pl.when(i >= lag)
            def _():
                backward(i - lag)

            return carry

        lax.fori_loop(0, rows + lag, step, 0)

    @pl.when(is_attention)
    def _():
        transpose(w1, w1t, 3 * dim, ff)

        def late():
            @pl.when(section == 0)
            def _():
                transpose(w1, w1t, 0, 3 * dim)

        @pl.when(section > 0)
        def _():
            transpose(w1, w1t, 0, 3 * dim)

        lag = jnp.where(section == 0, rows, rows // 2)
        run(attention_forward, attention_backward, lag, late)

    @pl.when(jnp.logical_not(is_attention))
    def _():
        second_load.wait()
        transpose(w1, w1t, 0, ff)
        for at in range(0, ff, 2 * PAIR):
            w2t[:, at : at + 2 * PAIR] = w2[at : at + 2 * PAIR, :].T
        lag = jnp.where(section == last, 0, rows - 1)
        run(dense_forward, dense_backward, lag, lambda: None)


    def total(x):
        return jnp.sum(x, axis=0, keepdims=True)

    lane = lax.broadcasted_iota(jnp.int32, (1, dim), 1)
    counts = jnp.zeros((1, dim), F32)
    for k, x in enumerate((sq_acc[0], sq_acc[1], val[...].astype(F32))):
        amount = jnp.sum(jnp.sum(x, axis=0, keepdims=True), axis=1, keepdims=True)
        counts = jnp.where(lane == k, amount, counts)
    small[0, 0:1, :] = total(norm_acc[0])
    small[0, 1:2, :] = total(norm_acc[1])
    for k in range(ff // dim):
        small[0, 2 + k : 3 + k, :] = total(in_acc[:, k * dim : (k + 1) * dim])
    small[0, 2 + ff // dim : 3 + ff // dim, :] = total(out_acc[...])
    small[0, 3 + ff // dim : 4 + ff // dim, :] = counts

    def remote(src, dst, send, recv, to):
        return pltpu.make_async_remote_copy(
            src, dst, send, recv, device_id=to, device_id_type=MESH
        )

    small_mate = remote(
        small.at[0], small.at[1], small_sem.at[0], small_sem.at[1], (section, mate)
    )
    small_line = remote(
        small.at[0], small.at[2], small_sem.at[2], small_sem.at[3], (section, inner)
    )
    small_cross = remote(
        small.at[0], small.at[3], small_sem.at[2], small_sem.at[4], (section, inner)
    )
    small_back = remote(
        small.at[3], small.at[3], small_sem.at[5], small_sem.at[4], (section, outer)
    )
    small_mate.start()


    tokens = rows * seq
    half = ff // 2
    steps = (half // CHUNK) * SUB
    tall, short = dim // SUB, CHUNK // SUB
    mine, theirs = core * half, (1 - core) * half

    def own(k, v):
        if k == 0:
            return w1.at[
                pl.ds(pl.multiple_of((v % SUB) * tall, 16), tall),
                pl.ds(pl.multiple_of(mine + (v // SUB) * CHUNK, CHUNK), CHUNK),
            ]
        return w2.at[pl.ds(pl.multiple_of(mine + v * short, 16), short), :]

    def whole(k, v):
        if k == 0:
            return first_o.at[
                pl.ds(pl.multiple_of((v % SUB) * tall, 16), tall),
                pl.ds(pl.multiple_of(mine + (v // SUB) * CHUNK, CHUNK), CHUNK),
            ]
        return second_o.at[pl.ds(pl.multiple_of(mine + v * short, 16), short), :]

    def slot(ref, k, v):
        if k == 0:
            return ref.at[
                pl.ds(pl.multiple_of((v % SUB) * tall, 16), tall),
                pl.ds(pl.multiple_of((v // SUB) * CHUNK, CHUNK), CHUNK),
            ]
        return ref.at[pl.ds(pl.multiple_of(v * short, 16), short), :]

    line = (sum_b1, sum_b2)

    def part_copy(k, c):
        at = pl.ds(pl.multiple_of(theirs + c * CHUNK, CHUNK), CHUNK)
        to = pl.ds(pl.multiple_of(c * CHUNK, CHUNK), CHUNK)
        src, dst = (w1.at[:, at], sum_a1.at[:, to]) if k == 0 else (w2.at[at, :], sum_a2.at[to, :])
        return remote(src, dst, part_send.at[k], part_recv.at[k, c], (section, mate))

    def line_copy(k, v):
        return remote(
            own(k, v), slot(line[k], k, v), line_send.at[k], line_recv.at[k, v], (section, inner)
        )

    def cross_copy(k, v):
        return remote(
            own(k, v), whole(k, v), line_send.at[k], whole_recv.at[k, v], (section, inner)
        )

    def given_copy(v):
        return remote(
            own(1, v), slot(sum_a2, 1, v), line_send.at[1], given_recv.at[v], (helper, dp)
        )

    def return_copy(v):
        ref = whole(1, v)
        return remote(ref, ref, mate_send.at[1], whole_recv.at[1, v], (helper, dp))

    def back_copy(k, v):
        ref = whole(k, v)
        return remote(ref, ref, back_send.at[k], whole_recv.at[k, v], (section, outer))

    def mate_copy(k, v):
        ref = whole(k, v)
        return remote(ref, ref, mate_send.at[k], mate_recv.at[k], (section, mate))

    def compute(k, c):
        for base, is_sent in ((theirs, True), (mine, False)):
            at = pl.ds(pl.multiple_of(base + c * CHUNK, CHUNK), CHUNK)
            if k == 0:
                side = is_attention & (base + c * CHUNK >= 3 * dim)
                left = pair[side.astype(jnp.int32)].reshape(tokens, dim)
                right = mid[:, :, at].reshape(tokens, CHUNK)
                w1[:, at] = dot(left, right, TN).astype(BF16)
            else:
                left = act[:, :, at].reshape(tokens, CHUNK)
                w2[at, :] = dot(left, gin[...].reshape(tokens, dim), TN).astype(BF16)
            if is_sent:
                part_copy(k, c).start()

    def combine(dst, *refs):
        value = refs[0][...].astype(F32)
        for ref in refs[1:]:
            value += ref[...].astype(F32)
        dst[...] = value.astype(BF16)

    def send_in(k, v, *refs):
        @pl.when(has_outer)
        def _():
            line_copy(k, v).wait_recv()
            combine(own(k, v), *refs, slot(line[k], k, v))

        @pl.when(jnp.logical_not(has_outer))
        def _():
            combine(own(k, v), *refs)

        @pl.when(is_middle)
        def _():
            cross_copy(k, v).start()

        @pl.when(jnp.logical_not(is_middle))
        def _():
            line_copy(k, v).start()

    def send_first(v):
        @pl.when(v % SUB == 0)
        def _():
            part_copy(0, v // SUB).wait_recv()

        send_in(0, v, own(0, v), slot(sum_a1, 0, v))

    def send_second(v):
        @pl.when(v % SUB == 0)
        def _():
            part_copy(1, v // SUB).wait_recv()

        @pl.when(v < handed)
        def _():
            combine(own(1, v), own(1, v), slot(sum_a2, 1, v))
            given_copy(v).start()

        @pl.when(v >= handed)
        def _():
            send_in(1, v, own(1, v), slot(sum_a2, 1, v))

    def send_given(v):
        given_copy(v).wait_recv()
        send_in(1, v, slot(sum_a2, 1, v))

    def settle(k, v):
        cross_copy(k, v).wait_recv()

        @pl.when(is_middle)
        def _():
            combine(whole(k, v), own(k, v), whole(k, v))

        @pl.when(has_outer)
        def _():
            back_copy(k, v).start()

    def settle_second(v):
        @pl.when(v < handed)
        def _():
            cross_copy(1, v).wait_recv()

        @pl.when(v >= handed)
        def _():
            settle(1, v)

        mate_copy(1, v).start()

    def settle_first(v):
        settle(0, v)
        mate_copy(0, v).start()

    def settle_given(v):
        settle(1, v)
        return_copy(v).start()

    def small_in():
        small_mate.wait_recv()
        small_mate.wait_send()
        small[0] += small[1]

        @pl.when(has_outer)
        def _():
            small_line.wait_recv()
            small[0] += small[2]

        @pl.when(is_middle)
        def _():
            small_cross.start()

        @pl.when(jnp.logical_not(is_middle))
        def _():
            small_line.start()

    def small_settle():
        small_cross.wait_recv()

        @pl.when(is_middle)
        def _():
            small[3] += small[0]

        @pl.when(has_outer)
        def _():
            small_back.start()

        small_o[...] = small[3]

    gap = jnp.where(on_left, chips // 2 - 1 - chip, chip - chips // 2)
    lag = 2 + 6 * gap
    begin = jnp.where(is_attention, min(steps - handed, steps - SUB), 0)

    @pl.when(jnp.logical_not(is_attention))
    def _():
        compute(1, 0)

    def step(u, carry):
        @pl.when(u < steps)
        def _():
            v = u - (steps - handed)

            @pl.when(jnp.logical_not(is_attention))
            def _():
                send_second(u)

            @pl.when(is_attention & (v >= 0))
            def _():
                send_given(v)

        @pl.when((u >= steps) & (u < 2 * steps))
        def _():
            send_first(u - steps)

        t = u - lag

        @pl.when((t >= begin) & is_attention)
        def _():
            v = t - (steps - handed)

            @pl.when((v >= 0) & (v < handed))
            def _():
                settle_given(v)

            @pl.when((t >= steps) & (t < 2 * steps))
            def _():
                settle_first(t - steps)

        @pl.when((t >= handed) & jnp.logical_not(is_attention))
        def _():
            @pl.when(t < steps)
            def _():
                settle_second(t)

            @pl.when((t >= steps) & (t < 2 * steps))
            def _():
                settle_first(t - steps)

            @pl.when(t >= 2 * steps)
            def _():
                settle_second(t - 2 * steps)

        @pl.when(u % SUB == 0)
        def _():
            c = u // SUB + 1

            @pl.when((c < steps // SUB) & jnp.logical_not(is_attention))
            def _():
                compute(1, c)

            @pl.when((c >= steps // SUB) & (c < 2 * (steps // SUB)))
            def _():
                compute(0, c - steps // SUB)

        @pl.when(u == steps + SUB)
        def _():
            small_in()

        @pl.when(t == steps + SUB)
        def _():
            small_settle()

        return carry

    lax.fori_loop(begin, 2 * steps + handed + lag, step, 0)


    @pl.when(section < last)
    def _():
        remote(hout, hin, hs_sem, hr_sem.at[0], (nxt, dp)).wait_send()

    @pl.when(section > 0)
    def _():
        remote(gout, gin, gs_sem, gr_sem.at[0], (prv, dp)).wait_send()

    def taken(k, sem, count):
        if k == 0:
            ref = w1.at[:, pl.ds(0, (count // SUB) * CHUNK)]
        else:
            ref = w2.at[pl.ds(0, count * short), :]
        pltpu.make_async_copy(ref, ref, sem.at[k]).wait()

    taken(0, part_send, steps)
    taken(0, line_send, steps)
    taken(0, mate_send, steps)
    taken(0, mate_recv, steps)

    @pl.when(has_outer)
    def _():
        taken(0, back_send, steps)
        small_back.wait_send()

    @pl.when(jnp.logical_not(is_attention))
    def _():
        taken(1, part_send, steps)
        taken(1, line_send, steps)
        taken(1, mate_send, steps)
        taken(1, mate_recv, steps)

        @pl.when(has_outer)
        def _():
            taken(1, back_send, steps - handed)

    @pl.when(is_attention)
    def _():
        taken(1, line_send, handed)
        taken(1, mate_send, handed)

        @pl.when(has_outer)
        def _():
            taken(1, back_send, handed)

        second_o[...] = jnp.zeros_like(second_o)

    small_line.wait_send()


def finish_kernel(
    res, sg, first, second, small,
    res_o, sg_o, first_o, second_o, norm_o, bias_o, rms_o,
    sg_wide, first_wide, second_wide, sem, first_sem, second_sem,
):
    rows, _, dim = sg.shape
    ff = first.shape[1]
    copies = [pltpu.make_async_copy(res, res_o.at[0], sem.at[0])]
    copies[0].start()
    for src, wide, dst, sems in (
        (first, first_wide, first_o, first_sem), (second, second_wide, second_o, second_sem),
    ):
        count = src.shape[0] // WRITES
        for k in range(WRITES):
            at = pl.ds(k * count, count)
            wide[at, :] = src[at, :].astype(F32)
            copies.append(pltpu.make_async_copy(wide.at[at], dst.at[0, at], sems.at[k]))
            copies[-1].start()
    sg_wide[...] = sg[...].astype(F32)
    copies.append(pltpu.make_async_copy(sg_wide, sg_o.at[0], sem.at[1]))
    copies[-1].start()
    norm_o[0] = small[0:2, :]
    count = ff // dim + 1
    for k in range(count):
        bias_o[0:1, k * dim : (k + 1) * dim] = small[2 + k : 3 + k, :]
    stat = small[2 + count : 3 + count, :]
    rms_o[...] = jnp.sqrt(stat[:, 0:2] / (stat[:, 2:3] * dim))
    for copy in copies:
        copy.wait()


def run_sublayers(start, cot, first, second, norm, bias, seg, val):
    rows, seq, dim = start.shape
    ff = first.shape[2]
    half = ff // 2
    steps = (half // CHUNK) * SUB
    block = (rows, seq, dim)
    wide = (rows, seq, ff)
    small = (4 + ff // dim, dim)
    any_space = pl.BlockSpec(memory_space=pl.ANY)
    vmem = pl.BlockSpec(memory_space=pltpu.VMEM)
    out = jax.ShapeDtypeStruct
    dma = pltpu.SemaphoreType.DMA
    return pl.pallas_call(
        functools.partial(sublayer_kernel, HANDED),
        out_shape=(
            pltpu.VMEM(block, BF16), pltpu.VMEM(block, BF16),
            pltpu.VMEM((dim, ff), BF16), pltpu.VMEM((ff, dim), BF16), pltpu.VMEM(small, F32),
        ),
        in_specs=[any_space] * 8,
        out_specs=(vmem,) * 5,
        scratch_shapes=[
            pltpu.VMEM((dim, ff), BF16), pltpu.VMEM((ff, dim), BF16),
            pltpu.VMEM((ff, dim), BF16), pltpu.VMEM((dim, ff), BF16),
            pltpu.VMEM(block, BF16), pltpu.VMEM((2, *block), BF16),
            pltpu.VMEM(wide, BF16), pltpu.VMEM(wide, BF16),
            pltpu.VMEM(norm.shape, F32), pltpu.VMEM(bias.shape, F32),
            pltpu.VMEM(seg.shape, jnp.int32), pltpu.VMEM(val.shape, jnp.int32),
            pltpu.VMEM((2, 8, dim), F32), pltpu.VMEM((2, 8, dim), F32),
            pltpu.VMEM((8, ff), F32), pltpu.VMEM((8, dim), F32),
            pltpu.VMEM((4, *small), F32),
            pltpu.VMEM((dim, half), BF16), pltpu.VMEM((dim, half), BF16),
            pltpu.VMEM((half, dim), BF16), pltpu.VMEM((half, dim), BF16),
            dma((8,)), dma, dma((rows,)), dma, dma((rows,)), dma((6,)),
            dma((2,)), dma((2, steps // SUB)), dma((HANDED,)),
            dma((2,)), dma((2, steps)), dma((2, steps)), dma((2,)),
            dma((2,)), dma((2,)),
        ],
        compiler_params=pltpu.CompilerParams(
            collective_id=0, has_side_effects=True, vmem_limit_bytes=SUBLAYER_VMEM
        ),
        name="sublayer",
    )(start, cot, first, second, norm, bias, seg, val)


def run_finish(res, sg, first, second, small):
    rows, seq, dim = res.shape
    ff = first.shape[1]
    any_space = pl.BlockSpec(memory_space=pl.ANY)
    vmem = pl.BlockSpec(memory_space=pltpu.VMEM)
    out = jax.ShapeDtypeStruct
    dma = pltpu.SemaphoreType.DMA
    return pl.pallas_call(
        finish_kernel,
        out_shape=(
            out((1, rows, seq, dim), BF16), out((1, rows, seq, dim), F32),
            out((1, dim, ff), F32), out((1, ff, dim), F32),
            out((1, 2, dim), F32), out((1, ff + dim), F32), out((1, 2), F32),
        ),
        in_specs=[vmem] * 5,
        out_specs=(any_space,) * 4 + (vmem,) * 3,
        scratch_shapes=[
            pltpu.VMEM((rows, seq, dim), F32),
            pltpu.VMEM((dim, ff), F32), pltpu.VMEM((ff, dim), F32),
            dma((2,)), dma((WRITES,)), dma((WRITES,)),
        ],
        compiler_params=pltpu.CompilerParams(vmem_limit_bytes=FINISH_VMEM),
        name="finish",
    )(res, sg, first, second, small)


def local(start, cot, first, second, norm, bias, seg, val):
    return run_finish(*run_sublayers(start, cot, first, second, norm, bias, seg, val))


def solution(mesh):
    in_specs = (
        P("dp", None, None),
        P("dp", None, None),
        P("section", None, None),
        P("section", None, None),
        P("section", None, None),
        P("section", None),
        P("dp", None),
        P("dp", None),
    )
    out_specs = (
        P("section", "dp", None, None),
        P("section", "dp", None, None),
        P("section", None, None),
        P("section", None, None),
        P("section", None, None),
        P("section", None),
        P("section", None),
    )
    return jax.shard_map(local, mesh=mesh, in_specs=in_specs, out_specs=out_specs, check_vma=False)
```

```python
import jax
import jax.numpy as jnp
from jax import lax
from jax.experimental import pallas as pl
from jax.experimental.pallas import tpu as pltpu
from jax.sharding import PartitionSpec as P

HEAD_DIM = 64
EPS = 1e-05
NEG_FILL = -1e30
MESH = pl.DeviceIdType.MESH
BF16 = jnp.bfloat16
F32 = jnp.float32
NN = (((1,), (0,)), ((), ()))
NT = (((1,), (1,)), ((), ()))
TN = (((0,), (0,)), ((), ()))
PAIR = 2 * HEAD_DIM
TILE = 1536
CHUNK = 256
SUB = 4
NEAR = (6, 5)
FAR = 9
LOADS = 4
WRITES = 12
SUBLAYER_VMEM = 50 * 2**20
FINISH_VMEM = 40 * 2**20
GELU_C = 0.7978845608028654
GELU_K = 0.044715


def dot(a, b, dims=NN):
    return lax.dot_general(a, b, dims, preferred_element_type=F32)


def gelu_and_slope(x):
    square = x * x
    t = jnp.tanh(GELU_C * (x + GELU_K * (square * x)))
    half = 0.5 * (1.0 + t)
    slope = half + (0.5 * GELU_C) * x * (1.0 - t * t) * (1.0 + (3.0 * GELU_K) * square)
    return x * half, slope


def fold(x):
    return x.reshape(x.shape[0] // 8, 8, x.shape[1]).sum(axis=0)


def normalize(hidden):
    mean = jnp.mean(hidden, axis=-1, keepdims=True)
    centered = hidden - mean
    variance = jnp.mean(centered * centered, axis=-1, keepdims=True)
    inv_std = lax.rsqrt(variance + EPS)
    return centered * inv_std, inv_std


def sublayer_kernel(
    start, cot, first, second, norm_in, bias_in, seg_in, val_in,
    hout, gout, first_o, second_o, small_o,
    w1, w2, w1t, w2t, hin, pair, act, mid,
    norm, bias, seg, val, sq_acc, norm_acc, in_acc, out_acc, small,
    sum_a1, sum_b1, sum_a2, sum_b2,
    load_sem, hs_sem, hr_sem, gs_sem, gr_sem, small_sem,
    part_send, part_recv, given_recv, line_send, line_recv, whole_recv, back_send,
    mate_send, mate_recv,
):
    nrm, gin = pair.at[0], pair.at[1]
    section = lax.axis_index("section")
    dp = lax.axis_index("dp")
    last = lax.axis_size("section") - 1
    rows, seq, dim = start.shape
    ff = first.shape[2]
    pairs = dim // PAIR
    is_attention = section % 2 == 0
    nxt = jnp.minimum(section + 1, last)
    prv = jnp.maximum(section - 1, 0)

    first_load = pltpu.make_async_copy(first.at[0], w1, load_sem.at[0])
    second_load = pltpu.make_async_copy(second.at[0], w2, load_sem.at[1])
    start_load = pltpu.make_async_copy(start, hin, load_sem.at[2])
    cot_load = pltpu.make_async_copy(cot, gin, load_sem.at[3])
    small_loads = [
        pltpu.make_async_copy(src, dst, load_sem.at[4 + k])
        for k, (src, dst) in enumerate(
            ((norm_in, norm), (bias_in, bias), (seg_in, seg), (val_in, val))
        )
    ]

    def split_load(src, dst, k):
        count = dst.shape[0] // LOADS
        for at in range(0, dst.shape[0], count):
            pltpu.make_async_copy(
                src.at[0, pl.ds(at, count)], dst.at[pl.ds(at, count)], load_sem.at[k]
            ).start()

    split_load(first, w1, 0)

    @pl.when(section == 0)
    def _():
        start_load.start()

    for load in small_loads:
        load.start()

    @pl.when(jnp.logical_not(is_attention))
    def _():
        split_load(second, w2, 1)

    @pl.when(section == last)
    def _():
        cot_load.start()

    chips = lax.axis_size("dp") // 2
    chip, core = dp // 2, dp % 2
    mate = dp + 1 - 2 * core
    on_left = chip < chips // 2
    is_middle = (chip == chips // 2 - 1) | (chip == chips // 2)
    has_outer = (chip > 0) & (chip < chips - 1)
    inner = jnp.where(on_left, dp + 2, dp - 2)
    outer = jnp.clip(jnp.where(on_left, dp - 2, dp + 2), 0, 2 * chips - 1)
    helper = section + 1 - 2 * (section % 2)
    near = jnp.where(section < 2, NEAR[0], NEAR[1])
    far = jnp.where((section == 1) | (section == 2), FAR, 0)
    handed = near + far

    barrier = pltpu.get_barrier_semaphore()

    def greet(to_section, to_dp):
        pl.semaphore_signal(
            barrier, inc=1, device_id=(to_section, to_dp), device_id_type=MESH
        )

    greet(section, mate)
    greet(section, inner)

    @pl.when(has_outer)
    def _():
        greet(section, outer)

    @pl.when(section > 0)
    def _():
        greet(prv, dp)

    @pl.when(section < last)
    def _():
        greet(nxt, dp)

    peers = 3 + has_outer.astype(jnp.int32)
    peers += ((section > 0) & (section < last)).astype(jnp.int32)

    for ref in (sq_acc, norm_acc, in_acc, out_acc):
        ref[...] = jnp.zeros_like(ref)

    def h_copy(i):
        return pltpu.make_async_remote_copy(
            hout.at[i], hin.at[i], hs_sem, hr_sem.at[i],
            device_id=(nxt, dp), device_id_type=MESH,
        )

    def g_copy(i):
        return pltpu.make_async_remote_copy(
            gout.at[i], gin.at[i], gs_sem, gr_sem.at[i],
            device_id=(prv, dp), device_id_type=MESH,
        )

    eye = lax.broadcasted_iota(jnp.int32, (seq, seq), 0) == lax.broadcasted_iota(
        jnp.int32, (seq, seq), 1
    )

    def column(row):
        return jnp.sum(jnp.where(eye, row, 0.0), axis=1, keepdims=True)

    def valid_row(i):
        return val[pl.ds(i, 1), :].astype(F32)

    def entry(i):
        @pl.when(section > 0)
        def _():
            h_copy(i).wait_recv()

        hidden = hin[i].astype(F32)
        normal, _ = normalize(hidden)
        low = (normal * norm[0, 0:1, :] + norm[0, 1:2, :]).astype(BF16)
        nrm[i] = low
        return hidden, low

    def leave(i, hidden, branch):
        low = (hidden + branch).astype(BF16)
        hout[i] = low

        @pl.when(section < last)
        def _():
            h_copy(i).start()

        weight = column(valid_row(i))
        value = low.astype(F32)
        sq_acc[0] += fold(value * value * weight)
        sq_acc[1] += fold(branch * branch * weight)

    def grad_entry(i):
        @pl.when(section < last)
        def _():
            g_copy(i).wait_recv()

        @pl.when(section == last)
        def _():
            gin[i] = jnp.where(column(valid_row(i)) > 0, gin[i], jnp.zeros((seq, dim), BF16))

        return gin[i]

    def grad_leave(i, grad, normed_grad):
        grad_value = grad.astype(F32)
        normal, inv_std = normalize(hin[i].astype(F32))
        scaled = normed_grad * norm[0, 0:1, :]
        mean_one = jnp.mean(scaled, axis=-1, keepdims=True)
        mean_two = jnp.mean(scaled * normal, axis=-1, keepdims=True)
        low = (grad_value + inv_std * (scaled - mean_one - normal * mean_two)).astype(BF16)
        gout[i] = low

        @pl.when(section > 0)
        def _():
            g_copy(i).start()

        norm_acc[0] += fold(normed_grad * normal)
        norm_acc[1] += fold(normed_grad)
        out_acc[...] += fold(grad_value)


    def dense_forward(i):
        hidden, low = entry(i)
        branch = jnp.zeros((seq, dim), F32)
        for at in range(0, ff, TILE):
            cols = slice(at, at + TILE)
            value, slope = gelu_and_slope(dot(low, w1[:, cols]) + bias[0:1, cols])
            value = value.astype(BF16)
            act[i, :, cols] = value
            mid[i, :, cols] = slope.astype(BF16)
            branch += dot(value, w2[cols, :])
        leave(i, hidden, branch + bias[0:1, ff:])

    def dense_backward(i):
        grad = grad_entry(i)
        normed_grad = jnp.zeros((seq, dim), F32)
        for at in range(0, ff, TILE):
            cols = slice(at, at + TILE)
            inner = dot(grad, w2t[:, cols]) * mid[i, :, cols].astype(F32)
            low = inner.astype(BF16)
            mid[i, :, cols] = low
            in_acc[:, cols] += fold(low.astype(F32))
            normed_grad += dot(low, w1t[cols, :])
        grad_leave(i, grad, normed_grad)


    lower = lax.broadcasted_iota(jnp.int32, (seq, PAIR), 1) < HEAD_DIM

    def split_heads(x):
        zero = jnp.zeros_like(x)
        return jnp.concatenate([jnp.where(lower, x, zero), jnp.where(lower, zero, x)], axis=0)

    def join_heads(x):
        return jnp.where(lower, x[:seq], x[seq:])

    def attention_forward(i):
        hidden, low = entry(i)
        projected = dot(low, w1[:, : 3 * dim])
        mid[i, :, :dim] = (projected[:, :dim] + bias[0:1, :dim]).astype(BF16)
        mid[i, :, dim : 2 * dim] = projected[:, dim : 2 * dim].astype(BF16)
        mid[i, :, 2 * dim : 3 * dim] = (
            projected[:, 2 * dim :] + bias[0:1, dim : 2 * dim]
        ).astype(BF16)
        seg_row = seg[pl.ds(i, 1), :].astype(F32)
        allowed = (column(seg_row) == seg_row) & ((valid_row(i) > 0) | eye)
        for p in range(pairs):
            at = p * PAIR
            query = mid[i, :, at : at + PAIR]
            keys = split_heads(mid[i, :, dim + at : dim + at + PAIR])
            values = split_heads(mid[i, :, 2 * dim + at : 2 * dim + at + PAIR])
            scores = dot(query, keys, NT) * HEAD_DIM**-0.5
            probs = []
            for half in (scores[:, :seq], scores[:, seq:]):
                half = jnp.where(allowed, half, NEG_FILL)
                weight = jnp.exp(half - jnp.max(half, axis=-1, keepdims=True))
                probs.append(weight / jnp.sum(weight, axis=-1, keepdims=True))
            prob = jnp.concatenate(probs, axis=1).astype(BF16)
            act[i, :, 2 * seq * p : 2 * seq * (p + 1)] = prob
            mid[i, :, 3 * dim + at : 3 * dim + at + PAIR] = dot(prob, values).astype(BF16)
        branch = dot(mid[i, :, 3 * dim :], w1t[3 * dim :, :]) + bias[0:1, ff:]
        leave(i, hidden, branch)

    def attention_backward(i):
        grad = grad_entry(i)
        mixed_grad = dot(grad, w1[:, 3 * dim :]).astype(BF16)
        for p in range(pairs):
            at = p * PAIR
            query = mid[i, :, at : at + PAIR]
            keys = split_heads(mid[i, :, dim + at : dim + at + PAIR])
            values = split_heads(mid[i, :, 2 * dim + at : 2 * dim + at + PAIR])
            prob = act[i, :, 2 * seq * p : 2 * seq * (p + 1)]
            out_grad = mixed_grad[:, at : at + PAIR]
            prob_grad = dot(out_grad, values, NT)
            prob_value = prob.astype(F32)
            parts = []
            for cols in (slice(0, seq), slice(seq, 2 * seq)):
                pv, pg = prob_value[:, cols], prob_grad[:, cols]
                parts.append(pv * (pg - jnp.sum(pv * pg, axis=-1, keepdims=True)))
            score_grad = jnp.concatenate(parts, axis=1).astype(BF16)
            query_grad = dot(score_grad, keys) * HEAD_DIM**-0.5
            key_grad = join_heads(dot(score_grad, query, TN)) * HEAD_DIM**-0.5
            value_grad = join_heads(dot(prob, out_grad, TN))
            mid[i, :, at : at + PAIR] = query_grad.astype(BF16)
            mid[i, :, dim + at : dim + at + PAIR] = key_grad.astype(BF16)
            mid[i, :, 2 * dim + at : 2 * dim + at + PAIR] = value_grad.astype(BF16)
        packed = mid[i, :, : 3 * dim]
        normed_grad = dot(packed, w1t[: 3 * dim, :])
        grad_leave(i, grad, normed_grad)
        in_acc[:, :dim] += fold(packed[:, :dim].astype(F32))
        in_acc[:, dim : 2 * dim] += fold(packed[:, 2 * dim :].astype(F32))

    for load in small_loads:
        load.wait()
    first_load.wait()

    def transpose(src, dst, low, high):
        for at in range(low, high, 2 * PAIR):
            dst[at : at + 2 * PAIR, :] = src[:, at : at + 2 * PAIR].T

    @pl.when(section == 0)
    def _():
        start_load.wait()

    @pl.when(section == last)
    def _():
        cot_load.wait()

    def run(forward, backward, lag, before_last):
        pl.semaphore_wait(barrier, peers)

        def step(i, carry):
            @pl.when(i == rows - 1)
            def _():
                before_last()

            @pl.when(i < rows)
            def _():
                forward(i)

            @pl.when(i >= lag)
            def _():
                backward(i - lag)

            return carry

        lax.fori_loop(0, rows + lag, step, 0)

    @pl.when(is_attention)
    def _():
        transpose(w1, w1t, 3 * dim, ff)

        def late():
            @pl.when(section == 0)
            def _():
                transpose(w1, w1t, 0, 3 * dim)

        @pl.when(section > 0)
        def _():
            transpose(w1, w1t, 0, 3 * dim)

        lag = jnp.where(section == 0, rows, rows // 2)
        run(attention_forward, attention_backward, lag, late)

    @pl.when(jnp.logical_not(is_attention))
    def _():
        second_load.wait()
        transpose(w1, w1t, 0, ff)
        for at in range(0, ff, 2 * PAIR):
            w2t[:, at : at + 2 * PAIR] = w2[at : at + 2 * PAIR, :].T
        lag = jnp.where(section == last, 0, rows - 1)
        run(dense_forward, dense_backward, lag, lambda: None)


    def total(x):
        return jnp.sum(x, axis=0, keepdims=True)

    lane = lax.broadcasted_iota(jnp.int32, (1, dim), 1)
    counts = jnp.zeros((1, dim), F32)
    for k, x in enumerate((sq_acc[0], sq_acc[1], val[...].astype(F32))):
        amount = jnp.sum(jnp.sum(x, axis=0, keepdims=True), axis=1, keepdims=True)
        counts = jnp.where(lane == k, amount, counts)
    small[0, 0:1, :] = total(norm_acc[0])
    small[0, 1:2, :] = total(norm_acc[1])
    for k in range(ff // dim):
        small[0, 2 + k : 3 + k, :] = total(in_acc[:, k * dim : (k + 1) * dim])
    small[0, 2 + ff // dim : 3 + ff // dim, :] = total(out_acc[...])
    small[0, 3 + ff // dim : 4 + ff // dim, :] = counts

    def remote(src, dst, send, recv, to):
        return pltpu.make_async_remote_copy(
            src, dst, send, recv, device_id=to, device_id_type=MESH
        )

    small_mate = remote(
        small.at[0], small.at[1], small_sem.at[0], small_sem.at[1], (section, mate)
    )
    small_line = remote(
        small.at[0], small.at[2], small_sem.at[2], small_sem.at[3], (section, inner)
    )
    small_cross = remote(
        small.at[0], small.at[3], small_sem.at[2], small_sem.at[4], (section, inner)
    )
    small_back = remote(
        small.at[3], small.at[3], small_sem.at[5], small_sem.at[4], (section, outer)
    )
    small_mate.start()


    tokens = rows * seq
    half = ff // 2
    steps = (half // CHUNK) * SUB
    tall, short = dim // SUB, CHUNK // SUB
    mine, theirs = core * half, (1 - core) * half

    def own(k, v):
        if k == 0:
            return w1.at[
                pl.ds(pl.multiple_of((v % SUB) * tall, 16), tall),
                pl.ds(pl.multiple_of(mine + (v // SUB) * CHUNK, CHUNK), CHUNK),
            ]
        return w2.at[pl.ds(pl.multiple_of(mine + v * short, 16), short), :]

    def whole(k, v):
        if k == 0:
            return first_o.at[
                pl.ds(pl.multiple_of((v % SUB) * tall, 16), tall),
                pl.ds(pl.multiple_of(mine + (v // SUB) * CHUNK, CHUNK), CHUNK),
            ]
        return second_o.at[pl.ds(pl.multiple_of(mine + v * short, 16), short), :]

    def slot(ref, k, v):
        if k == 0:
            return ref.at[
                pl.ds(pl.multiple_of((v % SUB) * tall, 16), tall),
                pl.ds(pl.multiple_of((v // SUB) * CHUNK, CHUNK), CHUNK),
            ]
        return ref.at[pl.ds(pl.multiple_of(v * short, 16), short), :]

    line = (sum_b1, sum_b2)

    def part_copy(k, c):
        at = pl.ds(pl.multiple_of(theirs + c * CHUNK, CHUNK), CHUNK)
        to = pl.ds(pl.multiple_of(c * CHUNK, CHUNK), CHUNK)
        src, dst = (w1.at[:, at], sum_a1.at[:, to]) if k == 0 else (w2.at[at, :], sum_a2.at[to, :])
        return remote(src, dst, part_send.at[k], part_recv.at[k, c], (section, mate))

    def line_copy(k, v):
        return remote(
            own(k, v), slot(line[k], k, v), line_send.at[k], line_recv.at[k, v], (section, inner)
        )

    def cross_copy(k, v):
        return remote(
            own(k, v), whole(k, v), line_send.at[k], whole_recv.at[k, v], (section, inner)
        )

    def given_copy(v):
        to = jnp.where(v < near, helper, nxt)
        return remote(own(1, v), slot(sum_a2, 1, v), line_send.at[1], given_recv.at[v], (to, dp))

    def return_copy(v, to):
        ref = whole(1, v)
        return remote(ref, ref, mate_send.at[1], whole_recv.at[1, v], (to, dp))

    def back_copy(k, v):
        ref = whole(k, v)
        return remote(ref, ref, back_send.at[k], whole_recv.at[k, v], (section, outer))

    def mate_copy(k, v):
        ref = whole(k, v)
        return remote(ref, ref, mate_send.at[k], mate_recv.at[k], (section, mate))

    def compute(k, c):
        for base, is_sent in ((theirs, True), (mine, False)):
            at = pl.ds(pl.multiple_of(base + c * CHUNK, CHUNK), CHUNK)
            if k == 0:
                side = is_attention & (base + c * CHUNK >= 3 * dim)
                left = pair[side.astype(jnp.int32)].reshape(tokens, dim)
                right = mid[:, :, at].reshape(tokens, CHUNK)
                w1[:, at] = dot(left, right, TN).astype(BF16)
            else:
                left = act[:, :, at].reshape(tokens, CHUNK)
                w2[at, :] = dot(left, gin[...].reshape(tokens, dim), TN).astype(BF16)
            if is_sent:
                part_copy(k, c).start()

    def combine(dst, *refs):
        value = refs[0][...].astype(F32)
        for ref in refs[1:]:
            value += ref[...].astype(F32)
        dst[...] = value.astype(BF16)

    def send_in(k, v, *refs):
        @pl.when(has_outer)
        def _():
            line_copy(k, v).wait_recv()
            combine(own(k, v), *refs, slot(line[k], k, v))

        @pl.when(jnp.logical_not(has_outer))
        def _():
            combine(own(k, v), *refs)

        @pl.when(is_middle)
        def _():
            cross_copy(k, v).start()

        @pl.when(jnp.logical_not(is_middle))
        def _():
            line_copy(k, v).start()

    def send_first(v):
        @pl.when(v % SUB == 0)
        def _():
            part_copy(0, v // SUB).wait_recv()

        send_in(0, v, own(0, v), slot(sum_a1, 0, v))

    def send_second(v):
        @pl.when(v % SUB == 0)
        def _():
            part_copy(1, v // SUB).wait_recv()

        @pl.when(v < handed)
        def _():
            combine(own(1, v), own(1, v), slot(sum_a2, 1, v))
            given_copy(v).start()

        @pl.when(v >= handed)
        def _():
            send_in(1, v, own(1, v), slot(sum_a2, 1, v))

    def send_given(v):
        given_copy(v).wait_recv()
        send_in(1, v, slot(sum_a2, 1, v))

    def settle(k, v):
        cross_copy(k, v).wait_recv()

        @pl.when(is_middle)
        def _():
            combine(whole(k, v), own(k, v), whole(k, v))

        @pl.when(has_outer)
        def _():
            back_copy(k, v).start()

    def settle_second(v):
        @pl.when(v < handed)
        def _():
            cross_copy(1, v).wait_recv()

        @pl.when(v >= handed)
        def _():
            settle(1, v)

        mate_copy(1, v).start()

    def settle_first(v):
        settle(0, v)
        mate_copy(0, v).start()

    def settle_given(v, to):
        settle(1, v)
        return_copy(v, to).start()

    def small_in():
        small_mate.wait_recv()
        small_mate.wait_send()
        small[0] += small[1]

        @pl.when(has_outer)
        def _():
            small_line.wait_recv()
            small[0] += small[2]

        @pl.when(is_middle)
        def _():
            small_cross.start()

        @pl.when(jnp.logical_not(is_middle))
        def _():
            small_line.start()

    def small_settle():
        small_cross.wait_recv()

        @pl.when(is_middle)
        def _():
            small[3] += small[0]

        @pl.when(has_outer)
        def _():
            small_back.start()

        small_o[...] = small[3]

    gap = jnp.where(on_left, chips // 2 - 1 - chip, chip - chips // 2)
    lag = 2 + 6 * gap
    begin = jnp.where(is_attention, jnp.minimum(steps - near, steps - SUB), 0)

    @pl.when(jnp.logical_not(is_attention))
    def _():
        compute(1, 0)

    def step(u, carry):
        @pl.when((u < steps) & jnp.logical_not(is_attention))
        def _():
            send_second(u)

        @pl.when((u < steps) & (u >= steps - near) & is_attention)
        def _():
            send_given(u - (steps - near))

        @pl.when((u >= 2 * steps) & (u < 2 * steps + far) & is_attention)
        def _():
            send_given(NEAR[0] + u - 2 * steps)

        @pl.when((u >= steps) & (u < 2 * steps))
        def _():
            send_first(u - steps)

        t = u - lag

        @pl.when((t >= begin) & is_attention)
        def _():
            @pl.when((t >= steps - near) & (t < steps))
            def _():
                settle_given(t - (steps - near), helper)

            @pl.when((t >= 2 * steps) & (t < 2 * steps + far))
            def _():
                settle_given(NEAR[0] + t - 2 * steps, prv)

            @pl.when((t >= steps) & (t < 2 * steps))
            def _():
                settle_first(t - steps)

        @pl.when((t >= handed) & jnp.logical_not(is_attention))
        def _():
            @pl.when(t < steps)
            def _():
                settle_second(t)

            @pl.when((t >= steps) & (t < 2 * steps))
            def _():
                settle_first(t - steps)

            @pl.when(t >= 2 * steps)
            def _():
                settle_second(t - 2 * steps)

        @pl.when(u % SUB == 0)
        def _():
            c = u // SUB + 1

            @pl.when((c < steps // SUB) & jnp.logical_not(is_attention))
            def _():
                compute(1, c)

            @pl.when((c >= steps // SUB) & (c < 2 * (steps // SUB)))
            def _():
                compute(0, c - steps // SUB)

        @pl.when(u == steps + SUB)
        def _():
            small_in()

        @pl.when(t == steps + SUB)
        def _():
            small_settle()

        return carry

    tail = jnp.where(is_attention, far, handed)
    lax.fori_loop(begin, 2 * steps + tail + lag, step, 0)


    @pl.when(section < last)
    def _():
        remote(hout, hin, hs_sem, hr_sem.at[0], (nxt, dp)).wait_send()

    @pl.when(section > 0)
    def _():
        remote(gout, gin, gs_sem, gr_sem.at[0], (prv, dp)).wait_send()

    def taken(k, sem, count):
        if k == 0:
            ref = w1.at[:, pl.ds(0, (count // SUB) * CHUNK)]
        else:
            ref = w2.at[pl.ds(0, count * short), :]
        pltpu.make_async_copy(ref, ref, sem.at[k]).wait()

    taken(0, part_send, steps)
    taken(0, line_send, steps)
    taken(0, mate_send, steps)
    taken(0, mate_recv, steps)

    @pl.when(has_outer)
    def _():
        taken(0, back_send, steps)
        small_back.wait_send()

    @pl.when(jnp.logical_not(is_attention))
    def _():
        taken(1, part_send, steps)
        taken(1, line_send, steps)
        taken(1, mate_send, steps)
        taken(1, mate_recv, steps)

    for which, count in enumerate((NEAR[0], NEAR[0] + FAR, NEAR[1] + FAR, NEAR[1])):
        if which % 2:

            @pl.when((section == which) & has_outer)
            def _(count=count):
                taken(1, back_send, steps - count)

        else:

            @pl.when(section == which)
            def _(count=count):
                taken(1, line_send, count)
                taken(1, mate_send, count)

            @pl.when((section == which) & has_outer)
            def _(count=count):
                taken(1, back_send, count)

    small_line.wait_send()

    @pl.when(is_attention)
    def _():
        second_o[...] = jnp.zeros_like(second_o)


def finish_kernel(
    res, sg, first, second, small,
    res_o, sg_o, first_o, second_o, norm_o, bias_o, rms_o,
    sg_wide, first_wide, second_wide, sem, first_sem, second_sem,
):
    rows, _, dim = sg.shape
    ff = first.shape[1]
    copies = [pltpu.make_async_copy(res, res_o.at[0], sem.at[0])]
    copies[0].start()
    for src, wide, dst, sems in (
        (first, first_wide, first_o, first_sem), (second, second_wide, second_o, second_sem),
    ):
        count = src.shape[0] // WRITES
        for k in range(WRITES):
            at = pl.ds(k * count, count)
            wide[at, :] = src[at, :].astype(F32)
            copies.append(pltpu.make_async_copy(wide.at[at], dst.at[0, at], sems.at[k]))
            copies[-1].start()
    sg_wide[...] = sg[...].astype(F32)
    copies.append(pltpu.make_async_copy(sg_wide, sg_o.at[0], sem.at[1]))
    copies[-1].start()
    norm_o[0] = small[0:2, :]
    count = ff // dim + 1
    for k in range(count):
        bias_o[0:1, k * dim : (k + 1) * dim] = small[2 + k : 3 + k, :]
    stat = small[2 + count : 3 + count, :]
    rms_o[...] = jnp.sqrt(stat[:, 0:2] / (stat[:, 2:3] * dim))
    for copy in copies:
        copy.wait()


def run_sublayers(start, cot, first, second, norm, bias, seg, val):
    rows, seq, dim = start.shape
    ff = first.shape[2]
    half = ff // 2
    steps = (half // CHUNK) * SUB
    block = (rows, seq, dim)
    wide = (rows, seq, ff)
    small = (4 + ff // dim, dim)
    any_space = pl.BlockSpec(memory_space=pl.ANY)
    vmem = pl.BlockSpec(memory_space=pltpu.VMEM)
    out = jax.ShapeDtypeStruct
    dma = pltpu.SemaphoreType.DMA
    return pl.pallas_call(
        sublayer_kernel,
        out_shape=(
            pltpu.VMEM(block, BF16), pltpu.VMEM(block, BF16),
            pltpu.VMEM((dim, ff), BF16), pltpu.VMEM((ff, dim), BF16), pltpu.VMEM(small, F32),
        ),
        in_specs=[any_space] * 8,
        out_specs=(vmem,) * 5,
        scratch_shapes=[
            pltpu.VMEM((dim, ff), BF16), pltpu.VMEM((ff, dim), BF16),
            pltpu.VMEM((ff, dim), BF16), pltpu.VMEM((dim, ff), BF16),
            pltpu.VMEM(block, BF16), pltpu.VMEM((2, *block), BF16),
            pltpu.VMEM(wide, BF16), pltpu.VMEM(wide, BF16),
            pltpu.VMEM(norm.shape, F32), pltpu.VMEM(bias.shape, F32),
            pltpu.VMEM(seg.shape, jnp.int32), pltpu.VMEM(val.shape, jnp.int32),
            pltpu.VMEM((2, 8, dim), F32), pltpu.VMEM((2, 8, dim), F32),
            pltpu.VMEM((8, ff), F32), pltpu.VMEM((8, dim), F32),
            pltpu.VMEM((4, *small), F32),
            pltpu.VMEM((dim, half), BF16), pltpu.VMEM((dim, half), BF16),
            pltpu.VMEM((half, dim), BF16), pltpu.VMEM((half, dim), BF16),
            dma((8,)), dma, dma((rows,)), dma, dma((rows,)), dma((6,)),
            dma((2,)), dma((2, steps // SUB)), dma((NEAR[0] + FAR,)),
            dma((2,)), dma((2, steps)), dma((2, steps)), dma((2,)),
            dma((2,)), dma((2,)),
        ],
        compiler_params=pltpu.CompilerParams(
            collective_id=0, has_side_effects=True, vmem_limit_bytes=SUBLAYER_VMEM
        ),
        name="sublayer",
    )(start, cot, first, second, norm, bias, seg, val)


def run_finish(res, sg, first, second, small):
    rows, seq, dim = res.shape
    ff = first.shape[1]
    any_space = pl.BlockSpec(memory_space=pl.ANY)
    vmem = pl.BlockSpec(memory_space=pltpu.VMEM)
    out = jax.ShapeDtypeStruct
    dma = pltpu.SemaphoreType.DMA
    return pl.pallas_call(
        finish_kernel,
        out_shape=(
            out((1, rows, seq, dim), BF16), out((1, rows, seq, dim), F32),
            out((1, dim, ff), F32), out((1, ff, dim), F32),
            out((1, 2, dim), F32), out((1, ff + dim), F32), out((1, 2), F32),
        ),
        in_specs=[vmem] * 5,
        out_specs=(any_space,) * 4 + (vmem,) * 3,
        scratch_shapes=[
            pltpu.VMEM((rows, seq, dim), F32),
            pltpu.VMEM((dim, ff), F32), pltpu.VMEM((ff, dim), F32),
            dma((2,)), dma((WRITES,)), dma((WRITES,)),
        ],
        compiler_params=pltpu.CompilerParams(vmem_limit_bytes=FINISH_VMEM),
        name="finish",
    )(res, sg, first, second, small)


def local(start, cot, first, second, norm, bias, seg, val):
    return run_finish(*run_sublayers(start, cot, first, second, norm, bias, seg, val))


def solution(mesh):
    in_specs = (
        P("dp", None, None),
        P("dp", None, None),
        P("section", None, None),
        P("section", None, None),
        P("section", None, None),
        P("section", None),
        P("dp", None),
        P("dp", None),
    )
    out_specs = (
        P("section", "dp", None, None),
        P("section", "dp", None, None),
        P("section", None, None),
        P("section", None, None),
        P("section", None, None),
        P("section", None),
        P("section", None),
    )
    return jax.shard_map(local, mesh=mesh, in_specs=in_specs, out_specs=out_specs, check_vma=False)
```

```python
import jax
import jax.numpy as jnp
from jax import lax
from jax.experimental import pallas as pl
from jax.experimental.pallas import tpu as pltpu
from jax.sharding import PartitionSpec as P

HEAD_DIM = 64
EPS = 1e-05
NEG_FILL = -1e30
MESH = pl.DeviceIdType.MESH
BF16 = jnp.bfloat16
F32 = jnp.float32
NN = (((1,), (0,)), ((), ()))
NT = (((1,), (1,)), ((), ()))
TN = (((0,), (0,)), ((), ()))
PAIR = 2 * HEAD_DIM
TILE = 1536
CHUNK = 256
SUB = 4
NEAR = (6, 5)
FAR = 9
LOADS = 4
WRITES = 12
SUBLAYER_VMEM = 50 * 2**20
FINISH_VMEM = 40 * 2**20
GELU_C = 0.7978845608028654
GELU_K = 0.044715


def dot(a, b, dims=NN):
    return lax.dot_general(a, b, dims, preferred_element_type=F32)


def gelu_and_slope(x):
    square = x * x
    t = jnp.tanh(GELU_C * (x + GELU_K * (square * x)))
    half = 0.5 * (1.0 + t)
    slope = half + (0.5 * GELU_C) * x * (1.0 - t * t) * (1.0 + (3.0 * GELU_K) * square)
    return x * half, slope


def fold(x):
    return x.reshape(x.shape[0] // 8, 8, x.shape[1]).sum(axis=0)


def normalize(hidden):
    mean = jnp.mean(hidden, axis=-1, keepdims=True)
    centered = hidden - mean
    variance = jnp.mean(centered * centered, axis=-1, keepdims=True)
    inv_std = lax.rsqrt(variance + EPS)
    return centered * inv_std, inv_std


def sublayer_kernel(
    start, cot, first, second, norm_in, bias_in, seg_in, val_in,
    hout, gout, first_o, second_o, small_o,
    w1, w2, w1t, w2t, hin, pair, act, mid,
    norm, bias, seg, val, sq_acc, norm_acc, in_acc, out_acc, small,
    sum_a1, sum_b1, sum_a2, sum_b2,
    load_sem, hs_sem, hr_sem, gs_sem, gr_sem, small_sem,
    part_send, part_recv, given_recv, line_send, line_recv, whole_recv, back_send,
    mate_send, mate_recv,
):
    nrm, gin = pair.at[0], pair.at[1]
    section = lax.axis_index("section")
    dp = lax.axis_index("dp")
    last = lax.axis_size("section") - 1
    rows, seq, dim = start.shape
    ff = first.shape[2]
    pairs = dim // PAIR
    is_attention = section % 2 == 0
    nxt = jnp.minimum(section + 1, last)
    prv = jnp.maximum(section - 1, 0)

    first_load = pltpu.make_async_copy(first.at[0], w1, load_sem.at[0])
    second_load = pltpu.make_async_copy(second.at[0], w2, load_sem.at[1])
    start_load = pltpu.make_async_copy(start, hin, load_sem.at[2])
    cot_load = pltpu.make_async_copy(cot, gin, load_sem.at[3])
    small_loads = [
        pltpu.make_async_copy(src, dst, load_sem.at[4 + k])
        for k, (src, dst) in enumerate(
            ((norm_in, norm), (bias_in, bias), (seg_in, seg), (val_in, val))
        )
    ]

    def split_load(src, dst, k):
        count = dst.shape[0] // LOADS
        for at in range(0, dst.shape[0], count):
            pltpu.make_async_copy(
                src.at[0, pl.ds(at, count)], dst.at[pl.ds(at, count)], load_sem.at[k]
            ).start()

    split_load(first, w1, 0)

    @pl.when(section == 0)
    def _():
        start_load.start()

    for load in small_loads:
        load.start()

    @pl.when(jnp.logical_not(is_attention))
    def _():
        split_load(second, w2, 1)

    @pl.when(section == last)
    def _():
        cot_load.start()

    chips = lax.axis_size("dp") // 2
    chip, core = dp // 2, dp % 2
    mate = dp + 1 - 2 * core
    on_left = chip < chips // 2
    is_middle = (chip == chips // 2 - 1) | (chip == chips // 2)
    has_outer = (chip > 0) & (chip < chips - 1)
    inner = jnp.where(on_left, dp + 2, dp - 2)
    outer = jnp.clip(jnp.where(on_left, dp - 2, dp + 2), 0, 2 * chips - 1)
    helper = section + 1 - 2 * (section % 2)
    near = jnp.where(section < 2, NEAR[0], NEAR[1])
    far = jnp.where((section == 1) | (section == 2), FAR, 0)
    handed = near + far

    barrier = pltpu.get_barrier_semaphore()

    def greet(to_section, to_dp):
        pl.semaphore_signal(
            barrier, inc=1, device_id=(to_section, to_dp), device_id_type=MESH
        )

    greet(section, mate)
    greet(section, inner)

    @pl.when(has_outer)
    def _():
        greet(section, outer)

    @pl.when(section > 0)
    def _():
        greet(prv, dp)

    @pl.when(section < last)
    def _():
        greet(nxt, dp)

    peers = 3 + has_outer.astype(jnp.int32)
    peers += ((section > 0) & (section < last)).astype(jnp.int32)

    for ref in (sq_acc, norm_acc, in_acc, out_acc):
        ref[...] = jnp.zeros_like(ref)

    def h_copy(i):
        return pltpu.make_async_remote_copy(
            hout.at[i], hin.at[i], hs_sem, hr_sem.at[i],
            device_id=(nxt, dp), device_id_type=MESH,
        )

    def g_copy(i):
        return pltpu.make_async_remote_copy(
            gout.at[i], gin.at[i], gs_sem, gr_sem.at[i],
            device_id=(prv, dp), device_id_type=MESH,
        )

    eye = lax.broadcasted_iota(jnp.int32, (seq, seq), 0) == lax.broadcasted_iota(
        jnp.int32, (seq, seq), 1
    )

    def column(row):
        return jnp.sum(jnp.where(eye, row, 0.0), axis=1, keepdims=True)

    def valid_row(i):
        return val[pl.ds(i, 1), :].astype(F32)

    def entry(i):
        @pl.when(section > 0)
        def _():
            h_copy(i).wait_recv()

        hidden = hin[i].astype(F32)
        normal, _ = normalize(hidden)
        low = (normal * norm[0, 0:1, :] + norm[0, 1:2, :]).astype(BF16)
        nrm[i] = low
        return hidden, low

    def leave(i, hidden, branch):
        low = (hidden + branch).astype(BF16)
        hout[i] = low

        @pl.when(section < last)
        def _():
            h_copy(i).start()

        weight = column(valid_row(i))
        value = low.astype(F32)
        sq_acc[0] += fold(value * value * weight)
        sq_acc[1] += fold(branch * branch * weight)

    def grad_entry(i):
        @pl.when(section < last)
        def _():
            g_copy(i).wait_recv()

        @pl.when(section == last)
        def _():
            gin[i] = jnp.where(column(valid_row(i)) > 0, gin[i], jnp.zeros((seq, dim), BF16))

        return gin[i]

    def grad_leave(i, grad, normed_grad):
        grad_value = grad.astype(F32)
        normal, inv_std = normalize(hin[i].astype(F32))
        scaled = normed_grad * norm[0, 0:1, :]
        mean_one = jnp.mean(scaled, axis=-1, keepdims=True)
        mean_two = jnp.mean(scaled * normal, axis=-1, keepdims=True)
        low = (grad_value + inv_std * (scaled - mean_one - normal * mean_two)).astype(BF16)
        gout[i] = low

        @pl.when(section > 0)
        def _():
            g_copy(i).start()

        norm_acc[0] += fold(normed_grad * normal)
        norm_acc[1] += fold(normed_grad)
        out_acc[...] += fold(grad_value)


    def dense_forward(i):
        hidden, low = entry(i)
        branch = jnp.zeros((seq, dim), F32)
        for at in range(0, ff, TILE):
            cols = slice(at, at + TILE)
            value, slope = gelu_and_slope(dot(low, w1[:, cols]) + bias[0:1, cols])
            value = value.astype(BF16)
            act[i, :, cols] = value
            mid[i, :, cols] = slope.astype(BF16)
            branch += dot(value, w2[cols, :])
        leave(i, hidden, branch + bias[0:1, ff:])

    def dense_backward(i):
        grad = grad_entry(i)
        normed_grad = jnp.zeros((seq, dim), F32)
        for at in range(0, ff, TILE):
            cols = slice(at, at + TILE)
            inner = dot(grad, w2t[:, cols]) * mid[i, :, cols].astype(F32)
            low = inner.astype(BF16)
            mid[i, :, cols] = low
            in_acc[:, cols] += fold(low.astype(F32))
            normed_grad += dot(low, w1t[cols, :])
        grad_leave(i, grad, normed_grad)


    lower = lax.broadcasted_iota(jnp.int32, (seq, PAIR), 1) < HEAD_DIM

    def split_heads(x):
        zero = jnp.zeros_like(x)
        return jnp.concatenate([jnp.where(lower, x, zero), jnp.where(lower, zero, x)], axis=0)

    def join_heads(x):
        return jnp.where(lower, x[:seq], x[seq:])

    def attention_forward(i):
        hidden, low = entry(i)
        projected = dot(low, w1[:, : 3 * dim])
        mid[i, :, :dim] = (projected[:, :dim] + bias[0:1, :dim]).astype(BF16)
        mid[i, :, dim : 2 * dim] = projected[:, dim : 2 * dim].astype(BF16)
        mid[i, :, 2 * dim : 3 * dim] = (
            projected[:, 2 * dim :] + bias[0:1, dim : 2 * dim]
        ).astype(BF16)
        seg_row = seg[pl.ds(i, 1), :].astype(F32)
        allowed = (column(seg_row) == seg_row) & ((column(valid_row(i)) > 0) | eye)
        packed = [mid[i, :, k * PAIR : (k + 1) * PAIR] for k in range(3 * pairs)]
        scores = [
            dot(split_heads(packed[pairs + p]), packed[p], NT) * HEAD_DIM**-0.5
            for p in range(pairs)
        ]
        mixed = []
        for p in range(pairs):
            probs = []
            for half in (scores[p][:seq], scores[p][seq:]):
                half = jnp.where(allowed, half, NEG_FILL)
                weight = jnp.exp(half - jnp.max(half, axis=0, keepdims=True))
                probs.append((weight / jnp.sum(weight, axis=0, keepdims=True)).astype(BF16))
                act[i, :, (2 * p + len(probs) - 1) * seq : (2 * p + len(probs)) * seq] = probs[-1]
            prob = jnp.concatenate(probs, axis=0)
            mixed.append(dot(prob, split_heads(packed[2 * pairs + p]), TN).astype(BF16))
        mixed = jnp.concatenate(mixed, axis=1)
        mid[i, :, 3 * dim :] = mixed
        branch = dot(mixed, w1t[3 * dim :, :]) + bias[0:1, ff:]
        leave(i, hidden, branch)

    def attention_backward(i):
        grad = grad_entry(i)
        mixed_grad = dot(grad, w1[:, 3 * dim :]).astype(BF16)
        packed = [mid[i, :, k * PAIR : (k + 1) * PAIR] for k in range(3 * pairs)]
        probs = [act[i, :, k * seq : (k + 1) * seq] for k in range(2 * pairs)]
        grads = [None] * (3 * pairs)
        for p in range(pairs):
            out_grad = mixed_grad[:, p * PAIR : (p + 1) * PAIR]
            prob_grad = dot(split_heads(packed[2 * pairs + p]), out_grad, NT)
            parts = []
            for k in range(2):
                value, grad_of = probs[2 * p + k].astype(F32), prob_grad[k * seq : (k + 1) * seq]
                inner = jnp.sum(value * grad_of, axis=0, keepdims=True)
                parts.append((value * (grad_of - inner)).astype(BF16))
            score_grad = jnp.concatenate(parts, axis=0)
            prob = jnp.concatenate(probs[2 * p : 2 * p + 2], axis=0)
            query_grad = dot(score_grad, split_heads(packed[pairs + p]), TN) * HEAD_DIM**-0.5
            key_grad = join_heads(dot(score_grad, packed[p])) * HEAD_DIM**-0.5
            grads[p] = query_grad.astype(BF16)
            grads[pairs + p] = key_grad.astype(BF16)
            grads[2 * pairs + p] = join_heads(dot(prob, out_grad)).astype(BF16)
        packed_grad = jnp.concatenate(grads, axis=1)
        mid[i, :, : 3 * dim] = packed_grad
        normed_grad = dot(packed_grad, w1t[: 3 * dim, :])
        grad_leave(i, grad, normed_grad)
        in_acc[:, :dim] += fold(packed_grad[:, :dim].astype(F32))
        in_acc[:, dim : 2 * dim] += fold(packed_grad[:, 2 * dim :].astype(F32))

    for load in small_loads:
        load.wait()
    first_load.wait()

    def transpose(src, dst, low, high):
        for at in range(low, high, 2 * PAIR):
            dst[at : at + 2 * PAIR, :] = src[:, at : at + 2 * PAIR].T

    @pl.when(section == 0)
    def _():
        start_load.wait()

    @pl.when(section == last)
    def _():
        cot_load.wait()

    def run(forward, backward, lag, before_last):
        pl.semaphore_wait(barrier, peers)

        def step(i, carry):
            @pl.when(i == rows - 1)
            def _():
                before_last()

            @pl.when(i < rows)
            def _():
                forward(i)

            @pl.when(i >= lag)
            def _():
                backward(i - lag)

            return carry

        lax.fori_loop(0, rows + lag, step, 0)

    @pl.when(is_attention)
    def _():
        transpose(w1, w1t, 3 * dim, ff)

        def late():
            @pl.when(section == 0)
            def _():
                transpose(w1, w1t, 0, 3 * dim)

        @pl.when(section > 0)
        def _():
            transpose(w1, w1t, 0, 3 * dim)

        lag = jnp.where(section == 0, rows, rows // 2)
        run(attention_forward, attention_backward, lag, late)

    @pl.when(jnp.logical_not(is_attention))
    def _():
        second_load.wait()
        transpose(w1, w1t, 0, ff)
        for at in range(0, ff, 2 * PAIR):
            w2t[:, at : at + 2 * PAIR] = w2[at : at + 2 * PAIR, :].T
        lag = jnp.where(section == last, 0, rows - 1)
        run(dense_forward, dense_backward, lag, lambda: None)


    def total(x):
        return jnp.sum(x, axis=0, keepdims=True)

    lane = lax.broadcasted_iota(jnp.int32, (1, dim), 1)
    counts = jnp.zeros((1, dim), F32)
    for k, x in enumerate((sq_acc[0], sq_acc[1], val[...].astype(F32))):
        amount = jnp.sum(jnp.sum(x, axis=0, keepdims=True), axis=1, keepdims=True)
        counts = jnp.where(lane == k, amount, counts)
    small[0, 0:1, :] = total(norm_acc[0])
    small[0, 1:2, :] = total(norm_acc[1])
    for k in range(ff // dim):
        small[0, 2 + k : 3 + k, :] = total(in_acc[:, k * dim : (k + 1) * dim])
    small[0, 2 + ff // dim : 3 + ff // dim, :] = total(out_acc[...])
    small[0, 3 + ff // dim : 4 + ff // dim, :] = counts

    def remote(src, dst, send, recv, to):
        return pltpu.make_async_remote_copy(
            src, dst, send, recv, device_id=to, device_id_type=MESH
        )

    small_mate = remote(
        small.at[0], small.at[1], small_sem.at[0], small_sem.at[1], (section, mate)
    )
    small_line = remote(
        small.at[0], small.at[2], small_sem.at[2], small_sem.at[3], (section, inner)
    )
    small_cross = remote(
        small.at[0], small.at[3], small_sem.at[2], small_sem.at[4], (section, inner)
    )
    small_back = remote(
        small.at[3], small.at[3], small_sem.at[5], small_sem.at[4], (section, outer)
    )
    small_mate.start()


    tokens = rows * seq
    half = ff // 2
    steps = (half // CHUNK) * SUB
    tall, short = dim // SUB, CHUNK // SUB
    mine, theirs = core * half, (1 - core) * half

    def own(k, v):
        if k == 0:
            return w1.at[
                pl.ds(pl.multiple_of((v % SUB) * tall, 16), tall),
                pl.ds(pl.multiple_of(mine + (v // SUB) * CHUNK, CHUNK), CHUNK),
            ]
        return w2.at[pl.ds(pl.multiple_of(mine + v * short, 16), short), :]

    def whole(k, v):
        if k == 0:
            return first_o.at[
                pl.ds(pl.multiple_of((v % SUB) * tall, 16), tall),
                pl.ds(pl.multiple_of(mine + (v // SUB) * CHUNK, CHUNK), CHUNK),
            ]
        return second_o.at[pl.ds(pl.multiple_of(mine + v * short, 16), short), :]

    def slot(ref, k, v):
        if k == 0:
            return ref.at[
                pl.ds(pl.multiple_of((v % SUB) * tall, 16), tall),
                pl.ds(pl.multiple_of((v // SUB) * CHUNK, CHUNK), CHUNK),
            ]
        return ref.at[pl.ds(pl.multiple_of(v * short, 16), short), :]

    line = (sum_b1, sum_b2)

    def part_copy(k, c):
        at = pl.ds(pl.multiple_of(theirs + c * CHUNK, CHUNK), CHUNK)
        to = pl.ds(pl.multiple_of(c * CHUNK, CHUNK), CHUNK)
        src, dst = (w1.at[:, at], sum_a1.at[:, to]) if k == 0 else (w2.at[at, :], sum_a2.at[to, :])
        return remote(src, dst, part_send.at[k], part_recv.at[k, c], (section, mate))

    def line_copy(k, v):
        return remote(
            own(k, v), slot(line[k], k, v), line_send.at[k], line_recv.at[k, v], (section, inner)
        )

    def cross_copy(k, v):
        return remote(
            own(k, v), whole(k, v), line_send.at[k], whole_recv.at[k, v], (section, inner)
        )

    def given_copy(v):
        to = jnp.where(v < near, helper, nxt)
        return remote(own(1, v), slot(sum_a2, 1, v), line_send.at[1], given_recv.at[v], (to, dp))

    def return_copy(v, to):
        ref = whole(1, v)
        return remote(ref, ref, mate_send.at[1], whole_recv.at[1, v], (to, dp))

    def back_copy(k, v):
        ref = whole(k, v)
        return remote(ref, ref, back_send.at[k], whole_recv.at[k, v], (section, outer))

    def mate_copy(k, v):
        ref = whole(k, v)
        return remote(ref, ref, mate_send.at[k], mate_recv.at[k], (section, mate))

    def compute(k, c):
        for base, is_sent in ((theirs, True), (mine, False)):
            at = pl.ds(pl.multiple_of(base + c * CHUNK, CHUNK), CHUNK)
            if k == 0:
                side = is_attention & (base + c * CHUNK >= 3 * dim)
                left = pair[side.astype(jnp.int32)].reshape(tokens, dim)
                right = mid[:, :, at].reshape(tokens, CHUNK)
                w1[:, at] = dot(left, right, TN).astype(BF16)
            else:
                left = act[:, :, at].reshape(tokens, CHUNK)
                w2[at, :] = dot(left, gin[...].reshape(tokens, dim), TN).astype(BF16)
            if is_sent:
                part_copy(k, c).start()

    def combine(dst, *refs):
        value = refs[0][...].astype(F32)
        for ref in refs[1:]:
            value += ref[...].astype(F32)
        dst[...] = value.astype(BF16)

    def send_in(k, v, *refs):
        @pl.when(has_outer)
        def _():
            line_copy(k, v).wait_recv()
            combine(own(k, v), *refs, slot(line[k], k, v))

        @pl.when(jnp.logical_not(has_outer))
        def _():
            combine(own(k, v), *refs)

        @pl.when(is_middle)
        def _():
            cross_copy(k, v).start()

        @pl.when(jnp.logical_not(is_middle))
        def _():
            line_copy(k, v).start()

    def send_first(v):
        @pl.when(v % SUB == 0)
        def _():
            part_copy(0, v // SUB).wait_recv()

        send_in(0, v, own(0, v), slot(sum_a1, 0, v))

    def send_second(v):
        @pl.when(v % SUB == 0)
        def _():
            part_copy(1, v // SUB).wait_recv()

        @pl.when(v < handed)
        def _():
            combine(own(1, v), own(1, v), slot(sum_a2, 1, v))
            given_copy(v).start()

        @pl.when(v >= handed)
        def _():
            send_in(1, v, own(1, v), slot(sum_a2, 1, v))

    def send_given(v):
        given_copy(v).wait_recv()
        send_in(1, v, slot(sum_a2, 1, v))

    def settle(k, v):
        cross_copy(k, v).wait_recv()

        @pl.when(is_middle)
        def _():
            combine(whole(k, v), own(k, v), whole(k, v))

        @pl.when(has_outer)
        def _():
            back_copy(k, v).start()

    def settle_second(v):
        @pl.when(v < handed)
        def _():
            cross_copy(1, v).wait_recv()

        @pl.when(v >= handed)
        def _():
            settle(1, v)

        mate_copy(1, v).start()

    def settle_first(v):
        settle(0, v)
        mate_copy(0, v).start()

    def settle_given(v, to):
        settle(1, v)
        return_copy(v, to).start()

    def small_in():
        small_mate.wait_recv()
        small_mate.wait_send()
        small[0] += small[1]

        @pl.when(has_outer)
        def _():
            small_line.wait_recv()
            small[0] += small[2]

        @pl.when(is_middle)
        def _():
            small_cross.start()

        @pl.when(jnp.logical_not(is_middle))
        def _():
            small_line.start()

    def small_settle():
        small_cross.wait_recv()

        @pl.when(is_middle)
        def _():
            small[3] += small[0]

        @pl.when(has_outer)
        def _():
            small_back.start()

        small_o[...] = small[3]

    gap = jnp.where(on_left, chips // 2 - 1 - chip, chip - chips // 2)
    lag = 2 + 6 * gap
    begin = jnp.where(is_attention, jnp.minimum(steps - near, steps - SUB), 0)

    @pl.when(jnp.logical_not(is_attention))
    def _():
        compute(1, 0)

    def step(u, carry):
        @pl.when((u < steps) & jnp.logical_not(is_attention))
        def _():
            send_second(u)

        @pl.when((u < steps) & (u >= steps - near) & is_attention)
        def _():
            send_given(u - (steps - near))

        @pl.when((u >= 2 * steps) & (u < 2 * steps + far) & is_attention)
        def _():
            send_given(NEAR[0] + u - 2 * steps)

        @pl.when((u >= steps) & (u < 2 * steps))
        def _():
            send_first(u - steps)

        t = u - lag

        @pl.when((t >= begin) & is_attention)
        def _():
            @pl.when((t >= steps - near) & (t < steps))
            def _():
                settle_given(t - (steps - near), helper)

            @pl.when((t >= 2 * steps) & (t < 2 * steps + far))
            def _():
                settle_given(NEAR[0] + t - 2 * steps, prv)

            @pl.when((t >= steps) & (t < 2 * steps))
            def _():
                settle_first(t - steps)

        @pl.when((t >= handed) & jnp.logical_not(is_attention))
        def _():
            @pl.when(t < steps)
            def _():
                settle_second(t)

            @pl.when((t >= steps) & (t < 2 * steps))
            def _():
                settle_first(t - steps)

            @pl.when(t >= 2 * steps)
            def _():
                settle_second(t - 2 * steps)

        @pl.when(u % SUB == 0)
        def _():
            c = u // SUB + 1

            @pl.when((c < steps // SUB) & jnp.logical_not(is_attention))
            def _():
                compute(1, c)

            @pl.when((c >= steps // SUB) & (c < 2 * (steps // SUB)))
            def _():
                compute(0, c - steps // SUB)

        @pl.when(u == steps + SUB)
        def _():
            small_in()

        @pl.when(t == steps + SUB)
        def _():
            small_settle()

        return carry

    tail = jnp.where(is_attention, far, handed)
    lax.fori_loop(begin, 2 * steps + tail + lag, step, 0)


    @pl.when(section < last)
    def _():
        remote(hout, hin, hs_sem, hr_sem.at[0], (nxt, dp)).wait_send()

    @pl.when(section > 0)
    def _():
        remote(gout, gin, gs_sem, gr_sem.at[0], (prv, dp)).wait_send()

    def taken(k, sem, count):
        if k == 0:
            ref = w1.at[:, pl.ds(0, (count // SUB) * CHUNK)]
        else:
            ref = w2.at[pl.ds(0, count * short), :]
        pltpu.make_async_copy(ref, ref, sem.at[k]).wait()

    taken(0, part_send, steps)
    taken(0, line_send, steps)
    taken(0, mate_send, steps)
    taken(0, mate_recv, steps)

    @pl.when(has_outer)
    def _():
        taken(0, back_send, steps)
        small_back.wait_send()

    @pl.when(jnp.logical_not(is_attention))
    def _():
        taken(1, part_send, steps)
        taken(1, line_send, steps)
        taken(1, mate_send, steps)
        taken(1, mate_recv, steps)

    for which, count in enumerate((NEAR[0], NEAR[0] + FAR, NEAR[1] + FAR, NEAR[1])):
        if which % 2:

            @pl.when((section == which) & has_outer)
            def _(count=count):
                taken(1, back_send, steps - count)

        else:

            @pl.when(section == which)
            def _(count=count):
                taken(1, line_send, count)
                taken(1, mate_send, count)

            @pl.when((section == which) & has_outer)
            def _(count=count):
                taken(1, back_send, count)

    small_line.wait_send()

    @pl.when(is_attention)
    def _():
        second_o[...] = jnp.zeros_like(second_o)


def finish_kernel(
    res, sg, first, second, small,
    res_o, sg_o, first_o, second_o, norm_o, bias_o, rms_o,
    sg_wide, first_wide, second_wide, sem, first_sem, second_sem,
):
    rows, _, dim = sg.shape
    ff = first.shape[1]
    copies = [pltpu.make_async_copy(res, res_o.at[0], sem.at[0])]
    copies[0].start()
    for src, wide, dst, sems in (
        (first, first_wide, first_o, first_sem), (second, second_wide, second_o, second_sem),
    ):
        count = src.shape[0] // WRITES
        for k in range(WRITES):
            at = pl.ds(k * count, count)
            wide[at, :] = src[at, :].astype(F32)
            copies.append(pltpu.make_async_copy(wide.at[at], dst.at[0, at], sems.at[k]))
            copies[-1].start()
    sg_wide[...] = sg[...].astype(F32)
    copies.append(pltpu.make_async_copy(sg_wide, sg_o.at[0], sem.at[1]))
    copies[-1].start()
    norm_o[0] = small[0:2, :]
    count = ff // dim + 1
    for k in range(count):
        bias_o[0:1, k * dim : (k + 1) * dim] = small[2 + k : 3 + k, :]
    stat = small[2 + count : 3 + count, :]
    rms_o[...] = jnp.sqrt(stat[:, 0:2] / (stat[:, 2:3] * dim))
    for copy in copies:
        copy.wait()


def run_sublayers(start, cot, first, second, norm, bias, seg, val):
    rows, seq, dim = start.shape
    ff = first.shape[2]
    half = ff // 2
    steps = (half // CHUNK) * SUB
    block = (rows, seq, dim)
    wide = (rows, seq, ff)
    small = (4 + ff // dim, dim)
    any_space = pl.BlockSpec(memory_space=pl.ANY)
    vmem = pl.BlockSpec(memory_space=pltpu.VMEM)
    out = jax.ShapeDtypeStruct
    dma = pltpu.SemaphoreType.DMA
    return pl.pallas_call(
        sublayer_kernel,
        out_shape=(
            pltpu.VMEM(block, BF16), pltpu.VMEM(block, BF16),
            pltpu.VMEM((dim, ff), BF16), pltpu.VMEM((ff, dim), BF16), pltpu.VMEM(small, F32),
        ),
        in_specs=[any_space] * 8,
        out_specs=(vmem,) * 5,
        scratch_shapes=[
            pltpu.VMEM((dim, ff), BF16), pltpu.VMEM((ff, dim), BF16),
            pltpu.VMEM((ff, dim), BF16), pltpu.VMEM((dim, ff), BF16),
            pltpu.VMEM(block, BF16), pltpu.VMEM((2, *block), BF16),
            pltpu.VMEM(wide, BF16), pltpu.VMEM(wide, BF16),
            pltpu.VMEM(norm.shape, F32), pltpu.VMEM(bias.shape, F32),
            pltpu.VMEM(seg.shape, jnp.int32), pltpu.VMEM(val.shape, jnp.int32),
            pltpu.VMEM((2, 8, dim), F32), pltpu.VMEM((2, 8, dim), F32),
            pltpu.VMEM((8, ff), F32), pltpu.VMEM((8, dim), F32),
            pltpu.VMEM((4, *small), F32),
            pltpu.VMEM((dim, half), BF16), pltpu.VMEM((dim, half), BF16),
            pltpu.VMEM((half, dim), BF16), pltpu.VMEM((half, dim), BF16),
            dma((8,)), dma, dma((rows,)), dma, dma((rows,)), dma((6,)),
            dma((2,)), dma((2, steps // SUB)), dma((NEAR[0] + FAR,)),
            dma((2,)), dma((2, steps)), dma((2, steps)), dma((2,)),
            dma((2,)), dma((2,)),
        ],
        compiler_params=pltpu.CompilerParams(
            collective_id=0, has_side_effects=True, vmem_limit_bytes=SUBLAYER_VMEM
        ),
        name="sublayer",
    )(start, cot, first, second, norm, bias, seg, val)


def run_finish(res, sg, first, second, small):
    rows, seq, dim = res.shape
    ff = first.shape[1]
    any_space = pl.BlockSpec(memory_space=pl.ANY)
    vmem = pl.BlockSpec(memory_space=pltpu.VMEM)
    out = jax.ShapeDtypeStruct
    dma = pltpu.SemaphoreType.DMA
    return pl.pallas_call(
        finish_kernel,
        out_shape=(
            out((1, rows, seq, dim), BF16), out((1, rows, seq, dim), F32),
            out((1, dim, ff), F32), out((1, ff, dim), F32),
            out((1, 2, dim), F32), out((1, ff + dim), F32), out((1, 2), F32),
        ),
        in_specs=[vmem] * 5,
        out_specs=(any_space,) * 4 + (vmem,) * 3,
        scratch_shapes=[
            pltpu.VMEM((rows, seq, dim), F32),
            pltpu.VMEM((dim, ff), F32), pltpu.VMEM((ff, dim), F32),
            dma((2,)), dma((WRITES,)), dma((WRITES,)),
        ],
        compiler_params=pltpu.CompilerParams(vmem_limit_bytes=FINISH_VMEM),
        name="finish",
    )(res, sg, first, second, small)


def local(start, cot, first, second, norm, bias, seg, val):
    return run_finish(*run_sublayers(start, cot, first, second, norm, bias, seg, val))


def solution(mesh):
    in_specs = (
        P("dp", None, None),
        P("dp", None, None),
        P("section", None, None),
        P("section", None, None),
        P("section", None, None),
        P("section", None),
        P("dp", None),
        P("dp", None),
    )
    out_specs = (
        P("section", "dp", None, None),
        P("section", "dp", None, None),
        P("section", None, None),
        P("section", None, None),
        P("section", None, None),
        P("section", None),
        P("section", None),
    )
    return jax.shard_map(local, mesh=mesh, in_specs=in_specs, out_specs=out_specs, check_vma=False)
```

```python
import jax
import jax.numpy as jnp
from jax import lax
from jax.experimental import pallas as pl
from jax.experimental.pallas import tpu as pltpu
from jax.sharding import PartitionSpec as P

HEAD_DIM = 64
EPS = 1e-05
NEG_FILL = -1e30
MESH = pl.DeviceIdType.MESH
BF16 = jnp.bfloat16
F32 = jnp.float32
NN = (((1,), (0,)), ((), ()))
NT = (((1,), (1,)), ((), ()))
TN = (((0,), (0,)), ((), ()))
PAIR = 2 * HEAD_DIM
TILE = 1536
CHUNK = 256
SUB = 4
NEAR = (6, 6)
FAR = 10
RELAYED = 4
LOADS = 4
WRITES = 12
SUBLAYER_VMEM = 50 * 2**20
FINISH_VMEM = 40 * 2**20
GELU_C = 0.7978845608028654
GELU_K = 0.044715


def dot(a, b, dims=NN):
    return lax.dot_general(a, b, dims, preferred_element_type=F32)


def gelu_and_slope(x):
    square = x * x
    t = jnp.tanh(GELU_C * (x + GELU_K * (square * x)))
    half = 0.5 * (1.0 + t)
    slope = half + (0.5 * GELU_C) * x * (1.0 - t * t) * (1.0 + (3.0 * GELU_K) * square)
    return x * half, slope


def fold(x):
    return x.reshape(x.shape[0] // 8, 8, x.shape[1]).sum(axis=0)


def normalize(hidden):
    mean = jnp.mean(hidden, axis=-1, keepdims=True)
    centered = hidden - mean
    variance = jnp.mean(centered * centered, axis=-1, keepdims=True)
    inv_std = lax.rsqrt(variance + EPS)
    return centered * inv_std, inv_std


def sublayer_kernel(
    start, cot, first, second, norm_in, bias_in, seg_in, val_in,
    hout, gout, first_o, second_o, small_o,
    w1, w2, w1t, w2t, hin, pair, act, mid,
    norm, bias, seg, val, sq_acc, norm_acc, in_acc, out_acc, small,
    sum_a1, sum_b1, sum_a2, sum_b2,
    load_sem, hs_sem, hr_sem, gs_sem, gr_sem, relay_send, relay_recv, small_sem,
    part_send, part_recv, given_recv, line_send, line_recv, whole_recv, back_send,
    mate_send, mate_recv,
):
    nrm, gin = pair.at[0], pair.at[1]
    section = lax.axis_index("section")
    dp = lax.axis_index("dp")
    last = lax.axis_size("section") - 1
    rows, seq, dim = start.shape
    ff = first.shape[2]
    pairs = dim // PAIR
    is_attention = section % 2 == 0
    nxt = jnp.minimum(section + 1, last)
    prv = jnp.maximum(section - 1, 0)

    first_load = pltpu.make_async_copy(first.at[0], w1, load_sem.at[0])
    second_load = pltpu.make_async_copy(second.at[0], w2, load_sem.at[1])
    start_load = pltpu.make_async_copy(start, hin, load_sem.at[2])
    cot_load = pltpu.make_async_copy(cot, gin, load_sem.at[3])
    small_loads = [
        pltpu.make_async_copy(src, dst, load_sem.at[4 + k])
        for k, (src, dst) in enumerate(
            ((norm_in, norm), (bias_in, bias), (seg_in, seg), (val_in, val))
        )
    ]

    def split_load(src, dst, k):
        count = dst.shape[0] // LOADS
        for at in range(0, dst.shape[0], count):
            pltpu.make_async_copy(
                src.at[0, pl.ds(at, count)], dst.at[pl.ds(at, count)], load_sem.at[k]
            ).start()

    split_load(first, w1, 0)

    @pl.when(section == 0)
    def _():
        start_load.start()

    for load in small_loads:
        load.start()

    @pl.when(jnp.logical_not(is_attention))
    def _():
        split_load(second, w2, 1)

    @pl.when(section == last)
    def _():
        cot_load.start()

    chips = lax.axis_size("dp") // 2
    chip, core = dp // 2, dp % 2
    mate = dp + 1 - 2 * core
    on_left = chip < chips // 2
    is_middle = (chip == chips // 2 - 1) | (chip == chips // 2)
    has_outer = (chip > 0) & (chip < chips - 1)
    inner = jnp.where(on_left, dp + 2, dp - 2)
    outer = jnp.clip(jnp.where(on_left, dp - 2, dp + 2), 0, 2 * chips - 1)
    helper = section + 1 - 2 * (section % 2)
    near = jnp.where(section < 2, NEAR[0], NEAR[1])
    far = jnp.where((section == 1) | (section == 2), FAR, 0)
    handed = near + far

    barrier = pltpu.get_barrier_semaphore()

    def greet(to_section, to_dp):
        pl.semaphore_signal(
            barrier, inc=1, device_id=(to_section, to_dp), device_id_type=MESH
        )

    greet(section, mate)
    greet(section, inner)

    @pl.when(has_outer)
    def _():
        greet(section, outer)

    @pl.when(section > 0)
    def _():
        greet(prv, dp)

    @pl.when(section < last)
    def _():
        greet(nxt, dp)

    @pl.when((section == 0) | (section == 2))
    def _():
        greet(2 - section, dp)

    peers = 3 + has_outer.astype(jnp.int32)
    peers += ((section == 0) | (section == 2)).astype(jnp.int32)
    peers += ((section > 0) & (section < last)).astype(jnp.int32)

    for ref in (sq_acc, norm_acc, in_acc, out_acc):
        ref[...] = jnp.zeros_like(ref)

    def h_copy(i):
        return pltpu.make_async_remote_copy(
            hout.at[i], hin.at[i], hs_sem, hr_sem.at[i],
            device_id=(nxt, dp), device_id_type=MESH,
        )

    def g_copy(i):
        return pltpu.make_async_remote_copy(
            gout.at[i], gin.at[i], gs_sem, gr_sem.at[i],
            device_id=(prv, dp), device_id_type=MESH,
        )

    def via(i):
        return w2.at[pl.ds(pl.multiple_of(i * seq, seq), seq), :]

    def relay_in(i):
        return pltpu.make_async_remote_copy(
            gout.at[i], via(i), gs_sem, relay_recv.at[i],
            device_id=(0, dp), device_id_type=MESH,
        )

    def relay_out(i):
        return pltpu.make_async_remote_copy(
            via(i), gin.at[i], relay_send, gr_sem.at[i],
            device_id=(nxt, dp), device_id_type=MESH,
        )

    def pass_on(i, carry):
        relay_in(i).wait_recv()
        relay_out(i).start()
        return carry

    eye = lax.broadcasted_iota(jnp.int32, (seq, seq), 0) == lax.broadcasted_iota(
        jnp.int32, (seq, seq), 1
    )

    def column(row):
        return jnp.sum(jnp.where(eye, row, 0.0), axis=1, keepdims=True)

    def valid_row(i):
        return val[pl.ds(i, 1), :].astype(F32)

    def entry(i):
        @pl.when(section > 0)
        def _():
            h_copy(i).wait_recv()

        hidden = hin[i].astype(F32)
        normal, _ = normalize(hidden)
        low = (normal * norm[0, 0:1, :] + norm[0, 1:2, :]).astype(BF16)
        nrm[i] = low
        return hidden, low

    def leave(i, hidden, branch):
        low = (hidden + branch).astype(BF16)
        hout[i] = low

        @pl.when(section < last)
        def _():
            h_copy(i).start()

        weight = column(valid_row(i))
        value = low.astype(F32)
        sq_acc[0] += fold(value * value * weight)
        sq_acc[1] += fold(branch * branch * weight)

    def grad_entry(i):
        @pl.when(section < last)
        def _():
            g_copy(i).wait_recv()

        @pl.when(section == last)
        def _():
            gin[i] = jnp.where(column(valid_row(i)) > 0, gin[i], jnp.zeros((seq, dim), BF16))

        return gin[i]

    def grad_leave(i, grad, normed_grad):
        grad_value = grad.astype(F32)
        normal, inv_std = normalize(hin[i].astype(F32))
        scaled = normed_grad * norm[0, 0:1, :]
        mean_one = jnp.mean(scaled, axis=-1, keepdims=True)
        mean_two = jnp.mean(scaled * normal, axis=-1, keepdims=True)
        low = (grad_value + inv_std * (scaled - mean_one - normal * mean_two)).astype(BF16)
        gout[i] = low

        @pl.when((section == 2) & (i < RELAYED))
        def _():
            relay_in(i).start()

        @pl.when((section > 0) & ((section != 2) | (i >= RELAYED)))
        def _():
            g_copy(i).start()

        norm_acc[0] += fold(normed_grad * normal)
        norm_acc[1] += fold(normed_grad)
        out_acc[...] += fold(grad_value)


    def dense_forward(i):
        hidden, low = entry(i)
        branch = jnp.zeros((seq, dim), F32)
        for at in range(0, ff, TILE):
            cols = slice(at, at + TILE)
            value, slope = gelu_and_slope(dot(low, w1[:, cols]) + bias[0:1, cols])
            value = value.astype(BF16)
            act[i, :, cols] = value
            mid[i, :, cols] = slope.astype(BF16)
            branch += dot(value, w2[cols, :])
        leave(i, hidden, branch + bias[0:1, ff:])

    def dense_backward(i):
        grad = grad_entry(i)
        normed_grad = jnp.zeros((seq, dim), F32)
        for at in range(0, ff, TILE):
            cols = slice(at, at + TILE)
            inner = dot(grad, w2t[:, cols]) * mid[i, :, cols].astype(F32)
            low = inner.astype(BF16)
            mid[i, :, cols] = low
            in_acc[:, cols] += fold(low.astype(F32))
            normed_grad += dot(low, w1t[cols, :])
        grad_leave(i, grad, normed_grad)


    lower = lax.broadcasted_iota(jnp.int32, (seq, PAIR), 1) < HEAD_DIM

    def split_heads(x):
        zero = jnp.zeros_like(x)
        return jnp.concatenate([jnp.where(lower, x, zero), jnp.where(lower, zero, x)], axis=0)

    def join_heads(x):
        return jnp.where(lower, x[:seq], x[seq:])

    def attention_forward(i):
        hidden, low = entry(i)
        projected = dot(low, w1[:, : 3 * dim])
        mid[i, :, :dim] = (projected[:, :dim] + bias[0:1, :dim]).astype(BF16)
        mid[i, :, dim : 2 * dim] = projected[:, dim : 2 * dim].astype(BF16)
        mid[i, :, 2 * dim : 3 * dim] = (
            projected[:, 2 * dim :] + bias[0:1, dim : 2 * dim]
        ).astype(BF16)
        seg_row = seg[pl.ds(i, 1), :].astype(F32)
        allowed = (column(seg_row) == seg_row) & ((column(valid_row(i)) > 0) | eye)
        packed = [mid[i, :, k * PAIR : (k + 1) * PAIR] for k in range(3 * pairs)]
        scores = [
            dot(split_heads(packed[pairs + p]), packed[p], NT) * HEAD_DIM**-0.5
            for p in range(pairs)
        ]
        mixed = []
        for p in range(pairs):
            probs = []
            for half in (scores[p][:seq], scores[p][seq:]):
                half = jnp.where(allowed, half, NEG_FILL)
                weight = jnp.exp(half - jnp.max(half, axis=0, keepdims=True))
                probs.append((weight / jnp.sum(weight, axis=0, keepdims=True)).astype(BF16))
                act[i, :, (2 * p + len(probs) - 1) * seq : (2 * p + len(probs)) * seq] = probs[-1]
            prob = jnp.concatenate(probs, axis=0)
            mixed.append(dot(prob, split_heads(packed[2 * pairs + p]), TN).astype(BF16))
        mixed = jnp.concatenate(mixed, axis=1)
        mid[i, :, 3 * dim :] = mixed
        branch = dot(mixed, w1t[3 * dim :, :]) + bias[0:1, ff:]
        leave(i, hidden, branch)

    def attention_backward(i):
        grad = grad_entry(i)
        mixed_grad = dot(grad, w1[:, 3 * dim :]).astype(BF16)
        packed = [mid[i, :, k * PAIR : (k + 1) * PAIR] for k in range(3 * pairs)]
        probs = [act[i, :, k * seq : (k + 1) * seq] for k in range(2 * pairs)]
        grads = [None] * (3 * pairs)
        for p in range(pairs):
            out_grad = mixed_grad[:, p * PAIR : (p + 1) * PAIR]
            prob_grad = dot(split_heads(packed[2 * pairs + p]), out_grad, NT)
            parts = []
            for k in range(2):
                value, grad_of = probs[2 * p + k].astype(F32), prob_grad[k * seq : (k + 1) * seq]
                inner = jnp.sum(value * grad_of, axis=0, keepdims=True)
                parts.append((value * (grad_of - inner)).astype(BF16))
            score_grad = jnp.concatenate(parts, axis=0)
            prob = jnp.concatenate(probs[2 * p : 2 * p + 2], axis=0)
            query_grad = dot(score_grad, split_heads(packed[pairs + p]), TN) * HEAD_DIM**-0.5
            key_grad = join_heads(dot(score_grad, packed[p])) * HEAD_DIM**-0.5
            grads[p] = query_grad.astype(BF16)
            grads[pairs + p] = key_grad.astype(BF16)
            grads[2 * pairs + p] = join_heads(dot(prob, out_grad)).astype(BF16)
        packed_grad = jnp.concatenate(grads, axis=1)
        mid[i, :, : 3 * dim] = packed_grad
        normed_grad = dot(packed_grad, w1t[: 3 * dim, :])
        grad_leave(i, grad, normed_grad)
        in_acc[:, :dim] += fold(packed_grad[:, :dim].astype(F32))
        in_acc[:, dim : 2 * dim] += fold(packed_grad[:, 2 * dim :].astype(F32))

    for load in small_loads:
        load.wait()
    first_load.wait()

    def transpose(src, dst, low, high):
        for at in range(low, high, 2 * PAIR):
            dst[at : at + 2 * PAIR, :] = src[:, at : at + 2 * PAIR].T

    @pl.when(section == 0)
    def _():
        start_load.wait()

    @pl.when(section == last)
    def _():
        cot_load.wait()

    def run(forward, backward, lag, before_last, after_last):
        pl.semaphore_wait(barrier, peers)

        def step(i, carry):
            @pl.when(i == rows - 1)
            def _():
                before_last()

            @pl.when(i < rows)
            def _():
                forward(i)

            @pl.when(i == rows)
            def _():
                after_last()

            @pl.when(i >= lag)
            def _():
                backward(i - lag)

            return carry

        lax.fori_loop(0, rows + lag, step, 0)

    @pl.when(is_attention)
    def _():
        transpose(w1, w1t, 3 * dim, ff)

        def late():
            @pl.when(section == 0)
            def _():
                transpose(w1, w1t, 0, 3 * dim)

        @pl.when(section > 0)
        def _():
            transpose(w1, w1t, 0, 3 * dim)

        def relay():
            @pl.when(section == 0)
            def _():
                lax.fori_loop(0, RELAYED, pass_on, 0)

        lag = jnp.where(section == 0, rows, rows // 2)
        run(attention_forward, attention_backward, lag, late, relay)

        @pl.when(section == 0)
        def _():
            ref = w2.at[pl.ds(0, RELAYED * seq), :]
            pltpu.make_async_copy(ref, ref, relay_send).wait()


    @pl.when(jnp.logical_not(is_attention))
    def _():
        second_load.wait()
        transpose(w1, w1t, 0, ff)
        for at in range(0, ff, 2 * PAIR):
            w2t[:, at : at + 2 * PAIR] = w2[at : at + 2 * PAIR, :].T
        lag = jnp.where(section == last, 0, rows - 1)
        run(dense_forward, dense_backward, lag, lambda: None, lambda: None)


    def total(x):
        return jnp.sum(x, axis=0, keepdims=True)

    lane = lax.broadcasted_iota(jnp.int32, (1, dim), 1)
    counts = jnp.zeros((1, dim), F32)
    for k, x in enumerate((sq_acc[0], sq_acc[1], val[...].astype(F32))):
        amount = jnp.sum(jnp.sum(x, axis=0, keepdims=True), axis=1, keepdims=True)
        counts = jnp.where(lane == k, amount, counts)
    small[0, 0:1, :] = total(norm_acc[0])
    small[0, 1:2, :] = total(norm_acc[1])
    for k in range(ff // dim):
        small[0, 2 + k : 3 + k, :] = total(in_acc[:, k * dim : (k + 1) * dim])
    small[0, 2 + ff // dim : 3 + ff // dim, :] = total(out_acc[...])
    small[0, 3 + ff // dim : 4 + ff // dim, :] = counts

    def remote(src, dst, send, recv, to):
        return pltpu.make_async_remote_copy(
            src, dst, send, recv, device_id=to, device_id_type=MESH
        )

    small_mate = remote(
        small.at[0], small.at[1], small_sem.at[0], small_sem.at[1], (section, mate)
    )
    small_line = remote(
        small.at[0], small.at[2], small_sem.at[2], small_sem.at[3], (section, inner)
    )
    small_cross = remote(
        small.at[0], small.at[3], small_sem.at[2], small_sem.at[4], (section, inner)
    )
    small_back = remote(
        small.at[3], small.at[3], small_sem.at[5], small_sem.at[4], (section, outer)
    )
    small_mate.start()


    tokens = rows * seq
    half = ff // 2
    steps = (half // CHUNK) * SUB
    tall, short = dim // SUB, CHUNK // SUB
    mine, theirs = core * half, (1 - core) * half

    def own(k, v):
        if k == 0:
            return w1.at[
                pl.ds(pl.multiple_of((v % SUB) * tall, 16), tall),
                pl.ds(pl.multiple_of(mine + (v // SUB) * CHUNK, CHUNK), CHUNK),
            ]
        return w2.at[pl.ds(pl.multiple_of(mine + v * short, 16), short), :]

    def whole(k, v):
        if k == 0:
            return first_o.at[
                pl.ds(pl.multiple_of((v % SUB) * tall, 16), tall),
                pl.ds(pl.multiple_of(mine + (v // SUB) * CHUNK, CHUNK), CHUNK),
            ]
        return second_o.at[pl.ds(pl.multiple_of(mine + v * short, 16), short), :]

    def slot(ref, k, v):
        if k == 0:
            return ref.at[
                pl.ds(pl.multiple_of((v % SUB) * tall, 16), tall),
                pl.ds(pl.multiple_of((v // SUB) * CHUNK, CHUNK), CHUNK),
            ]
        return ref.at[pl.ds(pl.multiple_of(v * short, 16), short), :]

    line = (sum_b1, sum_b2)

    def part_copy(k, c):
        at = pl.ds(pl.multiple_of(theirs + c * CHUNK, CHUNK), CHUNK)
        to = pl.ds(pl.multiple_of(c * CHUNK, CHUNK), CHUNK)
        src, dst = (w1.at[:, at], sum_a1.at[:, to]) if k == 0 else (w2.at[at, :], sum_a2.at[to, :])
        return remote(src, dst, part_send.at[k], part_recv.at[k, c], (section, mate))

    def line_copy(k, v):
        return remote(
            own(k, v), slot(line[k], k, v), line_send.at[k], line_recv.at[k, v], (section, inner)
        )

    def cross_copy(k, v):
        return remote(
            own(k, v), whole(k, v), line_send.at[k], whole_recv.at[k, v], (section, inner)
        )

    def given_copy(v):
        to = jnp.where(v < near, helper, nxt)
        return remote(own(1, v), slot(sum_a2, 1, v), line_send.at[1], given_recv.at[v], (to, dp))

    def return_copy(v, to):
        ref = whole(1, v)
        return remote(ref, ref, mate_send.at[1], whole_recv.at[1, v], (to, dp))

    def back_copy(k, v):
        ref = whole(k, v)
        return remote(ref, ref, back_send.at[k], whole_recv.at[k, v], (section, outer))

    def mate_copy(k, v):
        ref = whole(k, v)
        return remote(ref, ref, mate_send.at[k], mate_recv.at[k], (section, mate))

    def compute(k, c):
        for base, is_sent in ((theirs, True), (mine, False)):
            at = pl.ds(pl.multiple_of(base + c * CHUNK, CHUNK), CHUNK)
            if k == 0:
                side = is_attention & (base + c * CHUNK >= 3 * dim)
                left = pair[side.astype(jnp.int32)].reshape(tokens, dim)
                right = mid[:, :, at].reshape(tokens, CHUNK)
                w1[:, at] = dot(left, right, TN).astype(BF16)
            else:
                left = act[:, :, at].reshape(tokens, CHUNK)
                w2[at, :] = dot(left, gin[...].reshape(tokens, dim), TN).astype(BF16)
            if is_sent:
                part_copy(k, c).start()

    def combine(dst, *refs):
        value = refs[0][...].astype(F32)
        for ref in refs[1:]:
            value += ref[...].astype(F32)
        dst[...] = value.astype(BF16)

    def send_in(k, v, *refs):
        @pl.when(has_outer)
        def _():
            line_copy(k, v).wait_recv()
            combine(own(k, v), *refs, slot(line[k], k, v))

        @pl.when(jnp.logical_not(has_outer))
        def _():
            combine(own(k, v), *refs)

        @pl.when(is_middle)
        def _():
            cross_copy(k, v).start()

        @pl.when(jnp.logical_not(is_middle))
        def _():
            line_copy(k, v).start()

    def send_first(v):
        @pl.when(v % SUB == 0)
        def _():
            part_copy(0, v // SUB).wait_recv()

        send_in(0, v, own(0, v), slot(sum_a1, 0, v))

    def send_second(v):
        @pl.when(v % SUB == 0)
        def _():
            part_copy(1, v // SUB).wait_recv()

        @pl.when(v < handed)
        def _():
            combine(own(1, v), own(1, v), slot(sum_a2, 1, v))
            given_copy(v).start()

        @pl.when(v >= handed)
        def _():
            send_in(1, v, own(1, v), slot(sum_a2, 1, v))

    def send_given(v):
        given_copy(v).wait_recv()
        send_in(1, v, slot(sum_a2, 1, v))

    def settle(k, v):
        cross_copy(k, v).wait_recv()

        @pl.when(is_middle)
        def _():
            combine(whole(k, v), own(k, v), whole(k, v))

        @pl.when(has_outer)
        def _():
            back_copy(k, v).start()

    def settle_second(v):
        @pl.when(v < handed)
        def _():
            cross_copy(1, v).wait_recv()

        @pl.when(v >= handed)
        def _():
            settle(1, v)

        mate_copy(1, v).start()

    def settle_first(v):
        settle(0, v)
        mate_copy(0, v).start()

    def settle_given(v, to):
        settle(1, v)
        return_copy(v, to).start()

    def small_in():
        small_mate.wait_recv()
        small_mate.wait_send()
        small[0] += small[1]

        @pl.when(has_outer)
        def _():
            small_line.wait_recv()
            small[0] += small[2]

        @pl.when(is_middle)
        def _():
            small_cross.start()

        @pl.when(jnp.logical_not(is_middle))
        def _():
            small_line.start()

    def small_settle():
        small_cross.wait_recv()

        @pl.when(is_middle)
        def _():
            small[3] += small[0]

        @pl.when(has_outer)
        def _():
            small_back.start()

        small_o[...] = small[3]

    gap = jnp.where(on_left, chips // 2 - 1 - chip, chip - chips // 2)
    lag = 2 + 6 * gap
    begin = jnp.where(is_attention, jnp.minimum(steps - near, steps - SUB), 0)

    @pl.when(jnp.logical_not(is_attention))
    def _():
        compute(1, 0)

    def step(u, carry):
        @pl.when((u < steps) & jnp.logical_not(is_attention))
        def _():
            send_second(u)

        @pl.when((u < steps) & (u >= steps - near) & is_attention)
        def _():
            send_given(u - (steps - near))

        @pl.when((u >= 2 * steps) & (u < 2 * steps + far) & is_attention)
        def _():
            send_given(NEAR[0] + u - 2 * steps)

        @pl.when((u >= steps) & (u < 2 * steps))
        def _():
            send_first(u - steps)

        t = u - lag

        @pl.when((t >= begin) & is_attention)
        def _():
            @pl.when((t >= steps - near) & (t < steps))
            def _():
                settle_given(t - (steps - near), helper)

            @pl.when((t >= 2 * steps) & (t < 2 * steps + far))
            def _():
                settle_given(NEAR[0] + t - 2 * steps, prv)

            @pl.when((t >= steps) & (t < 2 * steps))
            def _():
                settle_first(t - steps)

        @pl.when((t >= handed) & jnp.logical_not(is_attention))
        def _():
            @pl.when(t < steps)
            def _():
                settle_second(t)

            @pl.when((t >= steps) & (t < 2 * steps))
            def _():
                settle_first(t - steps)

            @pl.when(t >= 2 * steps)
            def _():
                settle_second(t - 2 * steps)

        @pl.when(u % SUB == 0)
        def _():
            c = u // SUB + 1

            @pl.when((c < steps // SUB) & jnp.logical_not(is_attention))
            def _():
                compute(1, c)

            @pl.when((c >= steps // SUB) & (c < 2 * (steps // SUB)))
            def _():
                compute(0, c - steps // SUB)

        @pl.when(u == steps + SUB)
        def _():
            small_in()

        @pl.when(t == steps + SUB)
        def _():
            small_settle()

        return carry

    tail = jnp.where(is_attention, far, handed)
    lax.fori_loop(begin, 2 * steps + tail + lag, step, 0)


    @pl.when(section < last)
    def _():
        remote(hout, hin, hs_sem, hr_sem.at[0], (nxt, dp)).wait_send()

    @pl.when(section > 0)
    def _():
        remote(gout, gin, gs_sem, gr_sem.at[0], (prv, dp)).wait_send()

    def taken(k, sem, count):
        if k == 0:
            ref = w1.at[:, pl.ds(0, (count // SUB) * CHUNK)]
        else:
            ref = w2.at[pl.ds(0, count * short), :]
        pltpu.make_async_copy(ref, ref, sem.at[k]).wait()

    taken(0, part_send, steps)
    taken(0, line_send, steps)
    taken(0, mate_send, steps)
    taken(0, mate_recv, steps)

    @pl.when(has_outer)
    def _():
        taken(0, back_send, steps)
        small_back.wait_send()

    @pl.when(jnp.logical_not(is_attention))
    def _():
        taken(1, part_send, steps)
        taken(1, line_send, steps)
        taken(1, mate_send, steps)
        taken(1, mate_recv, steps)

    for which, count in enumerate((NEAR[0], NEAR[0] + FAR, NEAR[1] + FAR, NEAR[1])):
        if which % 2:

            @pl.when((section == which) & has_outer)
            def _(count=count):
                taken(1, back_send, steps - count)

        else:

            @pl.when(section == which)
            def _(count=count):
                taken(1, line_send, count)
                taken(1, mate_send, count)

            @pl.when((section == which) & has_outer)
            def _(count=count):
                taken(1, back_send, count)

    small_line.wait_send()

    @pl.when(is_attention)
    def _():
        second_o[...] = jnp.zeros_like(second_o)


def finish_kernel(
    res, sg, first, second, small,
    res_o, sg_o, first_o, second_o, norm_o, bias_o, rms_o,
    sg_wide, first_wide, second_wide, sem, first_sem, second_sem,
):
    rows, _, dim = sg.shape
    ff = first.shape[1]
    copies = [pltpu.make_async_copy(res, res_o.at[0], sem.at[0])]
    copies[0].start()
    for src, wide, dst, sems in (
        (first, first_wide, first_o, first_sem), (second, second_wide, second_o, second_sem),
    ):
        count = src.shape[0] // WRITES
        for k in range(WRITES):
            at = pl.ds(k * count, count)
            wide[at, :] = src[at, :].astype(F32)
            copies.append(pltpu.make_async_copy(wide.at[at], dst.at[0, at], sems.at[k]))
            copies[-1].start()
    sg_wide[...] = sg[...].astype(F32)
    copies.append(pltpu.make_async_copy(sg_wide, sg_o.at[0], sem.at[1]))
    copies[-1].start()
    norm_o[0] = small[0:2, :]
    count = ff // dim + 1
    for k in range(count):
        bias_o[0:1, k * dim : (k + 1) * dim] = small[2 + k : 3 + k, :]
    stat = small[2 + count : 3 + count, :]
    rms_o[...] = jnp.sqrt(stat[:, 0:2] / (stat[:, 2:3] * dim))
    for copy in copies:
        copy.wait()


def run_sublayers(start, cot, first, second, norm, bias, seg, val):
    rows, seq, dim = start.shape
    ff = first.shape[2]
    half = ff // 2
    steps = (half // CHUNK) * SUB
    block = (rows, seq, dim)
    wide = (rows, seq, ff)
    small = (4 + ff // dim, dim)
    any_space = pl.BlockSpec(memory_space=pl.ANY)
    vmem = pl.BlockSpec(memory_space=pltpu.VMEM)
    out = jax.ShapeDtypeStruct
    dma = pltpu.SemaphoreType.DMA
    return pl.pallas_call(
        sublayer_kernel,
        out_shape=(
            pltpu.VMEM(block, BF16), pltpu.VMEM(block, BF16),
            pltpu.VMEM((dim, ff), BF16), pltpu.VMEM((ff, dim), BF16), pltpu.VMEM(small, F32),
        ),
        in_specs=[any_space] * 8,
        out_specs=(vmem,) * 5,
        scratch_shapes=[
            pltpu.VMEM((dim, ff), BF16), pltpu.VMEM((ff, dim), BF16),
            pltpu.VMEM((ff, dim), BF16), pltpu.VMEM((dim, ff), BF16),
            pltpu.VMEM(block, BF16), pltpu.VMEM((2, *block), BF16),
            pltpu.VMEM(wide, BF16), pltpu.VMEM(wide, BF16),
            pltpu.VMEM(norm.shape, F32), pltpu.VMEM(bias.shape, F32),
            pltpu.VMEM(seg.shape, jnp.int32), pltpu.VMEM(val.shape, jnp.int32),
            pltpu.VMEM((2, 8, dim), F32), pltpu.VMEM((2, 8, dim), F32),
            pltpu.VMEM((8, ff), F32), pltpu.VMEM((8, dim), F32),
            pltpu.VMEM((4, *small), F32),
            pltpu.VMEM((dim, half), BF16), pltpu.VMEM((dim, half), BF16),
            pltpu.VMEM((half, dim), BF16), pltpu.VMEM((half, dim), BF16),
            dma((8,)), dma, dma((rows,)), dma, dma((rows,)), dma, dma((RELAYED,)), dma((6,)),
            dma((2,)), dma((2, steps // SUB)), dma((NEAR[0] + FAR,)),
            dma((2,)), dma((2, steps)), dma((2, steps)), dma((2,)),
            dma((2,)), dma((2,)),
        ],
        compiler_params=pltpu.CompilerParams(
            collective_id=0, has_side_effects=True, vmem_limit_bytes=SUBLAYER_VMEM
        ),
        name="sublayer",
    )(start, cot, first, second, norm, bias, seg, val)


def run_finish(res, sg, first, second, small):
    rows, seq, dim = res.shape
    ff = first.shape[1]
    any_space = pl.BlockSpec(memory_space=pl.ANY)
    vmem = pl.BlockSpec(memory_space=pltpu.VMEM)
    out = jax.ShapeDtypeStruct
    dma = pltpu.SemaphoreType.DMA
    return pl.pallas_call(
        finish_kernel,
        out_shape=(
            out((1, rows, seq, dim), BF16), out((1, rows, seq, dim), F32),
            out((1, dim, ff), F32), out((1, ff, dim), F32),
            out((1, 2, dim), F32), out((1, ff + dim), F32), out((1, 2), F32),
        ),
        in_specs=[vmem] * 5,
        out_specs=(any_space,) * 4 + (vmem,) * 3,
        scratch_shapes=[
            pltpu.VMEM((rows, seq, dim), F32),
            pltpu.VMEM((dim, ff), F32), pltpu.VMEM((ff, dim), F32),
            dma((2,)), dma((WRITES,)), dma((WRITES,)),
        ],
        compiler_params=pltpu.CompilerParams(vmem_limit_bytes=FINISH_VMEM),
        name="finish",
    )(res, sg, first, second, small)


def local(start, cot, first, second, norm, bias, seg, val):
    return run_finish(*run_sublayers(start, cot, first, second, norm, bias, seg, val))


def solution(mesh):
    in_specs = (
        P("dp", None, None),
        P("dp", None, None),
        P("section", None, None),
        P("section", None, None),
        P("section", None, None),
        P("section", None),
        P("dp", None),
        P("dp", None),
    )
    out_specs = (
        P("section", "dp", None, None),
        P("section", "dp", None, None),
        P("section", None, None),
        P("section", None, None),
        P("section", None, None),
        P("section", None),
        P("section", None),
    )
    return jax.shard_map(local, mesh=mesh, in_specs=in_specs, out_specs=out_specs, check_vma=False)
```

```python
import jax
import jax.numpy as jnp
from jax import lax
from jax.experimental import pallas as pl
from jax.experimental.pallas import tpu as pltpu
from jax.sharding import PartitionSpec as P

HEAD_DIM = 64
EPS = 1e-05
NEG_FILL = -1e30
MESH = pl.DeviceIdType.MESH
BF16 = jnp.bfloat16
F32 = jnp.float32
NN = (((1,), (0,)), ((), ()))
NT = (((1,), (1,)), ((), ()))
TN = (((0,), (0,)), ((), ()))
PAIR = 2 * HEAD_DIM
TILE = 1536
CHUNK = 256
SUB = 4
QUARTER = SUB // 4
NEAR = (5, 5)
FAR = 10
RELAYED = 4
LOADS = 4
WRITES = 12
SUBLAYER_VMEM = 50 * 2**20
FINISH_VMEM = 40 * 2**20
GELU_C = 0.7978845608028654
GELU_K = 0.044715


def dot(a, b, dims=NN):
    return lax.dot_general(a, b, dims, preferred_element_type=F32)


def gelu_and_slope(x):
    square = x * x
    t = jnp.tanh(GELU_C * (x + GELU_K * (square * x)))
    half = 0.5 * (1.0 + t)
    slope = half + (0.5 * GELU_C) * x * (1.0 - t * t) * (1.0 + (3.0 * GELU_K) * square)
    return x * half, slope


def fold(x):
    return x.reshape(x.shape[0] // 8, 8, x.shape[1]).sum(axis=0)


def normalize(hidden):
    mean = jnp.mean(hidden, axis=-1, keepdims=True)
    centered = hidden - mean
    variance = jnp.mean(centered * centered, axis=-1, keepdims=True)
    inv_std = lax.rsqrt(variance + EPS)
    return centered * inv_std, inv_std


def sublayer_kernel(
    start, cot, first, second, norm_in, bias_in, seg_in, val_in,
    hout, gout, first_o, second_o, small_o,
    w1, w2, w1t, w2t, hin, pair, act, mid,
    norm, bias, seg, val, sq_acc, norm_acc, small,
    sum_a1, sum_b1, sum_a2, sum_b2,
    load_sem, turn_sem, hs_sem, hr_sem, gs_sem, gr_sem, relay_send, relay_recv, small_sem,
    part_send, part_recv, given_recv, line_send, line_recv, whole_recv, back_send,
    mate_send, mate_recv,
):
    nrm, gin = pair.at[0], pair.at[1]
    section = lax.axis_index("section")
    dp = lax.axis_index("dp")
    last = lax.axis_size("section") - 1
    rows, seq, dim = start.shape
    ff = first.shape[2]
    pairs = dim // PAIR
    is_attention = section % 2 == 0
    nxt = jnp.minimum(section + 1, last)
    prv = jnp.maximum(section - 1, 0)

    first_load = pltpu.make_async_copy(first.at[0], w1, load_sem.at[0])
    second_load = pltpu.make_async_copy(second.at[0], w2, load_sem.at[1])
    start_load = pltpu.make_async_copy(start, hin, load_sem.at[2])
    cot_load = pltpu.make_async_copy(cot, gin, load_sem.at[3])
    small_loads = [
        pltpu.make_async_copy(src, dst, load_sem.at[4 + k])
        for k, (src, dst) in enumerate(
            ((norm_in, norm), (bias_in, bias), (seg_in, seg), (val_in, val))
        )
    ]

    def split_load(src, dst, k):
        count = dst.shape[0] // LOADS
        for at in range(0, dst.shape[0], count):
            pltpu.make_async_copy(
                src.at[0, pl.ds(at, count)], dst.at[pl.ds(at, count)], load_sem.at[k]
            ).start()

    split_load(first, w1, 0)

    @pl.when(section == 0)
    def _():
        start_load.start()

    for load in small_loads:
        load.start()

    @pl.when(jnp.logical_not(is_attention))
    def _():
        split_load(second, w2, 1)

    @pl.when(section == last)
    def _():
        cot_load.start()

    chips = lax.axis_size("dp") // 2
    chip, core = dp // 2, dp % 2
    mate = dp + 1 - 2 * core
    on_left = chip < chips // 2
    is_middle = (chip == chips // 2 - 1) | (chip == chips // 2)
    has_outer = (chip > 0) & (chip < chips - 1)
    inner = jnp.where(on_left, dp + 2, dp - 2)
    outer = jnp.clip(jnp.where(on_left, dp - 2, dp + 2), 0, 2 * chips - 1)
    helper = section + 1 - 2 * (section % 2)
    near = jnp.where(section < 2, NEAR[0], NEAR[1])
    far = jnp.where((section == 1) | (section == 2), FAR, 0)
    handed = near + far

    barrier = pltpu.get_barrier_semaphore()

    def greet(to_section, to_dp):
        pl.semaphore_signal(
            barrier, inc=1, device_id=(to_section, to_dp), device_id_type=MESH
        )

    greet(section, mate)
    greet(section, inner)

    @pl.when(has_outer)
    def _():
        greet(section, outer)

    @pl.when(section > 0)
    def _():
        greet(prv, dp)

    @pl.when(section < last)
    def _():
        greet(nxt, dp)

    @pl.when((section == 0) | (section == 2))
    def _():
        greet(2 - section, dp)

    peers = 3 + has_outer.astype(jnp.int32)
    peers += ((section == 0) | (section == 2)).astype(jnp.int32)
    peers += ((section > 0) & (section < last)).astype(jnp.int32)

    for ref in (sq_acc, norm_acc, small):
        ref[...] = jnp.zeros_like(ref)

    def h_copy(i):
        return pltpu.make_async_remote_copy(
            hout.at[i], hin.at[i], hs_sem, hr_sem.at[i],
            device_id=(nxt, dp), device_id_type=MESH,
        )

    def g_copy(i):
        return pltpu.make_async_remote_copy(
            gout.at[i], gin.at[i], gs_sem, gr_sem.at[i],
            device_id=(prv, dp), device_id_type=MESH,
        )

    def send_in_turn(i):
        @pl.when((i == 0) & (core == 1))
        def _():
            pl.semaphore_wait(turn_sem, 1)

        h_copy(i).start()

        @pl.when((i == 0) & (core == 0))
        def _():
            pl.semaphore_signal(turn_sem, inc=1, device_id=(section, mate), device_id_type=MESH)

    def via(i):
        return w2.at[pl.ds(pl.multiple_of(i * seq, seq), seq), :]

    def relay_in(i):
        return pltpu.make_async_remote_copy(
            gout.at[i], via(i), gs_sem, relay_recv.at[i],
            device_id=(0, dp), device_id_type=MESH,
        )

    def relay_out(i):
        return pltpu.make_async_remote_copy(
            via(i), gin.at[i], relay_send, gr_sem.at[i],
            device_id=(nxt, dp), device_id_type=MESH,
        )

    def pass_on(i, carry):
        relay_in(i).wait_recv()
        relay_out(i).start()
        return carry

    eye = lax.broadcasted_iota(jnp.int32, (seq, seq), 0) == lax.broadcasted_iota(
        jnp.int32, (seq, seq), 1
    )

    def column(row):
        return jnp.sum(jnp.where(eye, row, 0.0), axis=1, keepdims=True)

    def valid_row(i):
        return val[pl.ds(i, 1), :].astype(F32)

    def entry(i):
        @pl.when(section > 0)
        def _():
            h_copy(i).wait_recv()

        hidden = hin[i].astype(F32)
        normal, _ = normalize(hidden)
        low = (normal * norm[0, 0:1, :] + norm[0, 1:2, :]).astype(BF16)
        nrm[i] = low
        return hidden, low

    def leave(i, hidden, branch):
        low = (hidden + branch).astype(BF16)
        hout[i] = low

        @pl.when((section > 0) & (section < last))
        def _():
            h_copy(i).start()

        @pl.when(section == 0)
        def _():
            send_in_turn(i)

        weight = column(valid_row(i))
        value = low.astype(F32)
        sq_acc[0] += fold(value * value * weight)
        sq_acc[1] += fold(branch * branch * weight)

    def grad_entry(i):
        @pl.when(section < last)
        def _():
            g_copy(i).wait_recv()

        @pl.when(section == last)
        def _():
            gin[i] = jnp.where(column(valid_row(i)) > 0, gin[i], jnp.zeros((seq, dim), BF16))

        return gin[i]

    def grad_leave(i, grad, normed_grad):
        grad_value = grad.astype(F32)
        normal, inv_std = normalize(hin[i].astype(F32))
        scaled = normed_grad * norm[0, 0:1, :]
        mean_one = jnp.mean(scaled, axis=-1, keepdims=True)
        mean_two = jnp.mean(scaled * normal, axis=-1, keepdims=True)
        low = (grad_value + inv_std * (scaled - mean_one - normal * mean_two)).astype(BF16)
        gout[i] = low

        @pl.when((section == 2) & (i < RELAYED))
        def _():
            relay_in(i).start()

        @pl.when((section > 0) & ((section != 2) | (i >= RELAYED)))
        def _():
            g_copy(i).start()

        norm_acc[0] += fold(normed_grad * normal)
        norm_acc[1] += fold(normed_grad)


    def dense_forward(i):
        hidden, low = entry(i)
        branch = jnp.zeros((seq, dim), F32)
        for at in range(0, ff, TILE):
            cols = slice(at, at + TILE)
            value, slope = gelu_and_slope(dot(low, w1[:, cols]) + bias[0:1, cols])
            value = value.astype(BF16)
            act[i, :, cols] = value
            mid[i, :, cols] = slope.astype(BF16)
            branch += dot(value, w2[cols, :])
        leave(i, hidden, branch + bias[0:1, ff:])

    def dense_backward(i):
        grad = grad_entry(i)
        normed_grad = jnp.zeros((seq, dim), F32)
        for at in range(0, ff, TILE):
            cols = slice(at, at + TILE)
            inner = dot(grad, w2t[:, cols]) * mid[i, :, cols].astype(F32)
            low = inner.astype(BF16)
            mid[i, :, cols] = low
            normed_grad += dot(low, w1t[cols, :])
        grad_leave(i, grad, normed_grad)


    lower = lax.broadcasted_iota(jnp.int32, (seq, PAIR), 1) < HEAD_DIM

    def split_heads(x):
        zero = jnp.zeros_like(x)
        return jnp.concatenate([jnp.where(lower, x, zero), jnp.where(lower, zero, x)], axis=0)

    def join_heads(x):
        return jnp.where(lower, x[:seq], x[seq:])

    def attention_forward(i):
        hidden, low = entry(i)
        projected = dot(low, w1[:, : 3 * dim])
        mid[i, :, :dim] = (projected[:, :dim] + bias[0:1, :dim]).astype(BF16)
        mid[i, :, dim : 2 * dim] = projected[:, dim : 2 * dim].astype(BF16)
        mid[i, :, 2 * dim : 3 * dim] = (
            projected[:, 2 * dim :] + bias[0:1, dim : 2 * dim]
        ).astype(BF16)
        seg_row = seg[pl.ds(i, 1), :].astype(F32)
        allowed = (column(seg_row) == seg_row) & ((column(valid_row(i)) > 0) | eye)
        packed = [mid[i, :, k * PAIR : (k + 1) * PAIR] for k in range(3 * pairs)]
        scores = [
            dot(split_heads(packed[pairs + p]), packed[p], NT) * HEAD_DIM**-0.5
            for p in range(pairs)
        ]
        mixed = []
        for p in range(pairs):
            probs = []
            for half in (scores[p][:seq], scores[p][seq:]):
                half = jnp.where(allowed, half, NEG_FILL)
                weight = jnp.exp(half - jnp.max(half, axis=0, keepdims=True))
                probs.append((weight / jnp.sum(weight, axis=0, keepdims=True)).astype(BF16))
                act[i, :, (2 * p + len(probs) - 1) * seq : (2 * p + len(probs)) * seq] = probs[-1]
            prob = jnp.concatenate(probs, axis=0)
            mixed.append(dot(prob, split_heads(packed[2 * pairs + p]), TN).astype(BF16))
        mixed = jnp.concatenate(mixed, axis=1)
        mid[i, :, 3 * dim :] = mixed
        branch = dot(mixed, w1t[3 * dim :, :]) + bias[0:1, ff:]
        leave(i, hidden, branch)

    def attention_backward(i):
        grad = grad_entry(i)
        mixed_grad = dot(grad, w1[:, 3 * dim :]).astype(BF16)
        packed = [mid[i, :, k * PAIR : (k + 1) * PAIR] for k in range(3 * pairs)]
        probs = [act[i, :, k * seq : (k + 1) * seq] for k in range(2 * pairs)]
        grads = [None] * (3 * pairs)
        for p in range(pairs):
            out_grad = mixed_grad[:, p * PAIR : (p + 1) * PAIR]
            prob_grad = dot(split_heads(packed[2 * pairs + p]), out_grad, NT)
            parts = []
            for k in range(2):
                value, grad_of = probs[2 * p + k].astype(F32), prob_grad[k * seq : (k + 1) * seq]
                inner = jnp.sum(value * grad_of, axis=0, keepdims=True)
                parts.append((value * (grad_of - inner)).astype(BF16))
            score_grad = jnp.concatenate(parts, axis=0)
            prob = jnp.concatenate(probs[2 * p : 2 * p + 2], axis=0)
            query_grad = dot(score_grad, split_heads(packed[pairs + p]), TN) * HEAD_DIM**-0.5
            key_grad = join_heads(dot(score_grad, packed[p])) * HEAD_DIM**-0.5
            grads[p] = query_grad.astype(BF16)
            grads[pairs + p] = key_grad.astype(BF16)
            grads[2 * pairs + p] = join_heads(dot(prob, out_grad)).astype(BF16)
        packed_grad = jnp.concatenate(grads, axis=1)
        mid[i, :, : 3 * dim] = packed_grad
        normed_grad = dot(packed_grad, w1t[: 3 * dim, :])
        grad_leave(i, grad, normed_grad)

    for load in small_loads:
        load.wait()
    first_load.wait()

    def transpose(src, dst, low, high):
        for at in range(low, high, 2 * PAIR):
            dst[at : at + 2 * PAIR, :] = src[:, at : at + 2 * PAIR].T

    @pl.when(section == 0)
    def _():
        start_load.wait()

    @pl.when(section == last)
    def _():
        cot_load.wait()

    def run(forward, backward, lag, before_last, after_last):
        pl.semaphore_wait(barrier, peers)

        def step(i, carry):
            @pl.when(i == rows - 1)
            def _():
                before_last()

            @pl.when(i < rows)
            def _():
                forward(i)

            @pl.when(i == rows)
            def _():
                after_last()

            @pl.when(i >= lag)
            def _():
                backward(i - lag)

            return carry

        lax.fori_loop(0, rows + lag, step, 0)

    @pl.when(is_attention)
    def _():
        transpose(w1, w1t, 3 * dim, ff)

        def late():
            @pl.when(section == 0)
            def _():
                transpose(w1, w1t, 0, 3 * dim)

        @pl.when(section > 0)
        def _():
            transpose(w1, w1t, 0, 3 * dim)

        def relay():
            @pl.when(section == 0)
            def _():
                lax.fori_loop(0, RELAYED, pass_on, 0)

        lag = jnp.where(section == 0, rows, rows // 2)
        run(attention_forward, attention_backward, lag, late, relay)

        @pl.when(section == 0)
        def _():
            ref = w2.at[pl.ds(0, RELAYED * seq), :]
            pltpu.make_async_copy(ref, ref, relay_send).wait()


    @pl.when(jnp.logical_not(is_attention))
    def _():
        second_load.wait()
        transpose(w1, w1t, 0, ff)
        for at in range(0, ff, 2 * PAIR):
            w2t[:, at : at + 2 * PAIR] = w2[at : at + 2 * PAIR, :].T
        lag = jnp.where(section == last, 0, rows - 1)
        run(dense_forward, dense_backward, lag, lambda: None, lambda: None)

    def remote(src, dst, send, recv, to):
        return pltpu.make_async_remote_copy(
            src, dst, send, recv, device_id=to, device_id_type=MESH
        )

    small_mate = remote(
        small.at[0], small.at[1], small_sem.at[0], small_sem.at[1], (section, mate)
    )
    small_line = remote(
        small.at[0], small.at[2], small_sem.at[2], small_sem.at[3], (section, inner)
    )
    small_cross = remote(
        small.at[0], small.at[3], small_sem.at[2], small_sem.at[4], (section, inner)
    )
    small_back = remote(
        small.at[3], small.at[3], small_sem.at[5], small_sem.at[4], (section, outer)
    )


    tokens = rows * seq
    half = ff // 2
    steps = (half // CHUNK) * SUB
    tall, short = dim // SUB, CHUNK // SUB
    mine, theirs = core * half, (1 - core) * half

    def own(k, v):
        if k == 0:
            return w1.at[
                pl.ds(pl.multiple_of((v % SUB) * tall, 16), tall),
                pl.ds(pl.multiple_of(mine + (v // SUB) * CHUNK, CHUNK), CHUNK),
            ]
        return w2.at[pl.ds(pl.multiple_of(mine + v * short, 16), short), :]

    def whole(k, v):
        if k == 0:
            return first_o.at[
                pl.ds(pl.multiple_of((v % SUB) * tall, 16), tall),
                pl.ds(pl.multiple_of(mine + (v // SUB) * CHUNK, CHUNK), CHUNK),
            ]
        return second_o.at[pl.ds(pl.multiple_of(mine + v * short, 16), short), :]

    def slot(ref, k, v):
        if k == 0:
            return ref.at[
                pl.ds(pl.multiple_of((v % SUB) * tall, 16), tall),
                pl.ds(pl.multiple_of((v // SUB) * CHUNK, CHUNK), CHUNK),
            ]
        return ref.at[pl.ds(pl.multiple_of(v * short, 16), short), :]

    line = (sum_b1, sum_b2)

    def part_copy(k, c):
        at = pl.ds(pl.multiple_of(theirs + c * CHUNK, CHUNK), CHUNK)
        to = pl.ds(pl.multiple_of(c * CHUNK, CHUNK), CHUNK)
        src, dst = (w1.at[:, at], sum_a1.at[:, to]) if k == 0 else (w2.at[at, :], sum_a2.at[to, :])
        return remote(src, dst, part_send.at[k], part_recv.at[k, c], (section, mate))

    def line_copy(k, v):
        return remote(
            own(k, v), slot(line[k], k, v), line_send.at[k], line_recv.at[k, v], (section, inner)
        )

    def cross_copy(k, v):
        return remote(
            own(k, v), whole(k, v), line_send.at[k], whole_recv.at[k, v], (section, inner)
        )

    def given_copy(v):
        to = jnp.where(v < near, helper, nxt)
        return remote(own(1, v), slot(sum_a2, 1, v), line_send.at[1], given_recv.at[v], (to, dp))

    def return_copy(v, to):
        ref = whole(1, v)
        return remote(ref, ref, mate_send.at[1], whole_recv.at[1, v], (to, dp))

    def back_copy(k, v):
        ref = whole(k, v)
        return remote(ref, ref, back_send.at[k], whole_recv.at[k, v], (section, outer))

    def mate_copy(k, v):
        ref = whole(k, v)
        return remote(ref, ref, mate_send.at[k], mate_recv.at[k], (section, mate))

    def token_sum(matrix):
        return jnp.sum(fold(matrix.astype(F32)), axis=0, keepdims=True)

    def small_start():
        lane = lax.broadcasted_iota(jnp.int32, (1, dim), 1)
        counts = jnp.zeros((1, dim), F32)
        for k, x in enumerate((sq_acc[0], sq_acc[1], val[...].astype(F32))):
            amount = jnp.sum(jnp.sum(x, axis=0, keepdims=True), axis=1, keepdims=True)
            counts = jnp.where(lane == k, amount, counts)
        small[0, 0:1, :] = jnp.sum(norm_acc[0], axis=0, keepdims=True)
        small[0, 1:2, :] = jnp.sum(norm_acc[1], axis=0, keepdims=True)
        small[0, 2 + ff // dim : 3 + ff // dim, :] = token_sum(gin[...].reshape(tokens, dim))
        small[0, 3 + ff // dim : 4 + ff // dim, :] = counts
        small_mate.start()

    def bias_sum(matrix, col):
        third = col // dim
        row = jnp.where(is_attention, third // 2, third) + 2
        at = pl.ds(pl.multiple_of(col - third * dim, CHUNK), CHUNK)

        @pl.when(jnp.logical_not(is_attention) | (third == 0) | (third == 2))
        def _():
            small[0, pl.ds(row, 1), at] = token_sum(matrix)

    def compute(k, c, is_mine):
        base = jnp.where(is_mine, mine, theirs) + c * CHUNK
        at = pl.ds(pl.multiple_of(base, CHUNK), CHUNK)
        if k == 0:
            side = is_attention & (base >= 3 * dim)
            left = pair[side.astype(jnp.int32)].reshape(tokens, dim)
            right = mid[:, :, at].reshape(tokens, CHUNK)
            w1[:, at] = dot(left, right, TN).astype(BF16)
        else:
            left = act[:, :, at].reshape(tokens, CHUNK)
            w2[at, :] = dot(left, gin[...].reshape(tokens, dim), TN).astype(BF16)

        @pl.when(jnp.logical_not(is_mine))
        def _():
            part_copy(k, c).start()

        if k == 0:
            bias_sum(mid[:, :, at].reshape(tokens, CHUNK), base)

    def combine(dst, *refs):
        value = refs[0][...].astype(F32)
        for ref in refs[1:]:
            value += ref[...].astype(F32)
        dst[...] = value.astype(BF16)

    def send_in(k, v, *refs):
        @pl.when(has_outer)
        def _():
            line_copy(k, v).wait_recv()
            combine(own(k, v), *refs, slot(line[k], k, v))

        @pl.when(jnp.logical_not(has_outer))
        def _():
            combine(own(k, v), *refs)

        @pl.when(is_middle)
        def _():
            cross_copy(k, v).start()

        @pl.when(jnp.logical_not(is_middle))
        def _():
            line_copy(k, v).start()

    def send_first(v):
        @pl.when(v % SUB == 0)
        def _():
            part_copy(0, v // SUB).wait_recv()

        send_in(0, v, own(0, v), slot(sum_a1, 0, v))

    def send_second(v):
        @pl.when(v % SUB == 0)
        def _():
            part_copy(1, v // SUB).wait_recv()

        @pl.when(v < handed)
        def _():
            combine(own(1, v), own(1, v), slot(sum_a2, 1, v))
            given_copy(v).start()

        @pl.when(v >= handed)
        def _():
            send_in(1, v, own(1, v), slot(sum_a2, 1, v))

    def send_given(v, to):
        given_copy(v).wait_recv()
        send_in(1, v, slot(sum_a2, 1, v))

    def settle(k, v):
        cross_copy(k, v).wait_recv()

        @pl.when(is_middle)
        def _():
            combine(whole(k, v), own(k, v), whole(k, v))

        @pl.when(has_outer)
        def _():
            back_copy(k, v).start()

    def settle_second(v):
        @pl.when(v < handed)
        def _():
            cross_copy(1, v).wait_recv()

        @pl.when(v >= handed)
        def _():
            settle(1, v)

        mate_copy(1, v).start()

    def settle_first(v):
        settle(0, v)
        mate_copy(0, v).start()

    def settle_given(v, to):
        settle(1, v)
        return_copy(v, to).start()

    def small_in():
        small_mate.wait_recv()
        small_mate.wait_send()
        small[0] += small[1]

        @pl.when(has_outer)
        def _():
            small_line.wait_recv()
            small[0] += small[2]

        @pl.when(is_middle)
        def _():
            small_cross.start()

        @pl.when(jnp.logical_not(is_middle))
        def _():
            small_line.start()

    def small_settle():
        small_cross.wait_recv()

        @pl.when(is_middle)
        def _():
            small[3] += small[0]

        @pl.when(has_outer)
        def _():
            small_back.start()

        small_o[...] = small[3]

    gap = jnp.where(on_left, chips // 2 - 1 - chip, chip - chips // 2)
    lag = 2 + 8 * gap
    blocks = steps // SUB
    is_dense = jnp.logical_not(is_attention)
    length = jnp.where(is_attention, steps + near + far, 2 * steps - handed)

    ahead = jnp.where(is_middle, SUB, 0)

    @pl.when(is_dense)
    def _():
        compute(0, 0, False)
        compute(0, 0, True)

    def in_line(u, first_part, second_part, given_part):
        @pl.when((u >= 0) & (u < length) & is_dense)
        def _():
            @pl.when(u < steps)
            def _():
                first_part(u)

            @pl.when(u >= steps)
            def _():
                second_part(u - steps + handed)

        @pl.when((u >= 0) & (u < length) & is_attention)
        def _():
            @pl.when(u < near)
            def _():
                given_part(u, helper)

            @pl.when((u >= near) & (u < steps + near))
            def _():
                first_part(u - near)

            @pl.when(u >= steps + near)
            def _():
                given_part(NEAR[0] + u - steps - near, prv)

    def step(u, carry):
        in_line(u - ahead, send_first, send_second, send_given)

        @pl.when((u % SUB >= SUB // 2) & is_dense)
        def _():
            for k in range(2):
                v = u // SUB * SUB + 2 * (u % SUB - SUB // 2) + k

                @pl.when(v < handed)
                def _(v=v):
                    send_second(v)

        t = u - ahead - lag

        @pl.when(t == length - 1)
        def _():
            small_settle()

        in_line(t, settle_first, settle_second, settle_given)

        @pl.when((t >= length) & (t < length + handed) & is_dense)
        def _():
            settle_second(t - length)

        c, q = u // SUB, u % SUB // QUARTER
        on_time = (u % QUARTER == 0) & (c < blocks)

        @pl.when(on_time & (q < 2) & is_dense)
        def _():
            compute(1, c, q == 1)

        @pl.when(on_time & jnp.where(is_attention, q < 2, (q >= 2) & (c + 1 < blocks)))
        def _():
            compute(0, jnp.where(is_attention, c, c + 1), q % 2 == 1)

        @pl.when(u == steps - 2)
        def _():
            small_start()

        @pl.when(u - ahead == steps + jnp.where((chip > 0) & (chip < chips - 1), SUB, 0))
        def _():
            small_in()

        return carry

    tail = jnp.where(is_attention, 0, handed)
    lax.fori_loop(0, length + ahead + lag + tail, step, 0)


    @pl.when(section < last)
    def _():
        remote(hout, hin, hs_sem, hr_sem.at[0], (nxt, dp)).wait_send()

    @pl.when(section > 0)
    def _():
        remote(gout, gin, gs_sem, gr_sem.at[0], (prv, dp)).wait_send()

    def taken(k, sem, count):
        if k == 0:
            ref = w1.at[:, pl.ds(0, (count // SUB) * CHUNK)]
        else:
            ref = w2.at[pl.ds(0, count * short), :]
        pltpu.make_async_copy(ref, ref, sem.at[k]).wait()

    taken(0, part_send, steps)
    taken(0, line_send, steps)
    taken(0, mate_send, steps)
    taken(0, mate_recv, steps)

    @pl.when(has_outer)
    def _():
        taken(0, back_send, steps)
        small_back.wait_send()

    @pl.when(jnp.logical_not(is_attention))
    def _():
        taken(1, part_send, steps)
        taken(1, line_send, steps)
        taken(1, mate_send, steps)
        taken(1, mate_recv, steps)

    for which, count in enumerate((NEAR[0], NEAR[0] + FAR, NEAR[1] + FAR, NEAR[1])):
        if which % 2:

            @pl.when((section == which) & has_outer)
            def _(count=count):
                taken(1, back_send, steps - count)

        else:

            @pl.when(section == which)
            def _(count=count):
                taken(1, line_send, count)
                taken(1, mate_send, count)

            @pl.when((section == which) & has_outer)
            def _(count=count):
                taken(1, back_send, count)

    small_line.wait_send()

    @pl.when(is_attention)
    def _():
        second_o[...] = jnp.zeros_like(second_o)


def finish_kernel(
    res, sg, first, second, small,
    res_o, sg_o, first_o, second_o, norm_o, bias_o, rms_o,
    sg_wide, first_wide, second_wide, sem, first_sem, second_sem,
):
    rows, _, dim = sg.shape
    ff = first.shape[1]
    copies = [pltpu.make_async_copy(res, res_o.at[0], sem.at[0])]
    copies[0].start()
    for src, wide, dst, sems in (
        (first, first_wide, first_o, first_sem), (second, second_wide, second_o, second_sem),
    ):
        count = src.shape[0] // WRITES
        for k in range(WRITES):
            at = pl.ds(k * count, count)
            wide[at, :] = src[at, :].astype(F32)
            copies.append(pltpu.make_async_copy(wide.at[at], dst.at[0, at], sems.at[k]))
            copies[-1].start()
    sg_wide[...] = sg[...].astype(F32)
    copies.append(pltpu.make_async_copy(sg_wide, sg_o.at[0], sem.at[1]))
    copies[-1].start()
    norm_o[0] = small[0:2, :]
    count = ff // dim + 1
    for k in range(count):
        bias_o[0:1, k * dim : (k + 1) * dim] = small[2 + k : 3 + k, :]
    stat = small[2 + count : 3 + count, :]
    rms_o[...] = jnp.sqrt(stat[:, 0:2] / (stat[:, 2:3] * dim))
    for copy in copies:
        copy.wait()


def run_sublayers(start, cot, first, second, norm, bias, seg, val):
    rows, seq, dim = start.shape
    ff = first.shape[2]
    half = ff // 2
    steps = (half // CHUNK) * SUB
    block = (rows, seq, dim)
    wide = (rows, seq, ff)
    small = (4 + ff // dim, dim)
    any_space = pl.BlockSpec(memory_space=pl.ANY)
    vmem = pl.BlockSpec(memory_space=pltpu.VMEM)
    out = jax.ShapeDtypeStruct
    dma = pltpu.SemaphoreType.DMA
    return pl.pallas_call(
        sublayer_kernel,
        out_shape=(
            pltpu.VMEM(block, BF16), pltpu.VMEM(block, BF16),
            pltpu.VMEM((dim, ff), BF16), pltpu.VMEM((ff, dim), BF16), pltpu.VMEM(small, F32),
        ),
        in_specs=[any_space] * 8,
        out_specs=(vmem,) * 5,
        scratch_shapes=[
            pltpu.VMEM((dim, ff), BF16), pltpu.VMEM((ff, dim), BF16),
            pltpu.VMEM((ff, dim), BF16), pltpu.VMEM((dim, ff), BF16),
            pltpu.VMEM(block, BF16), pltpu.VMEM((2, *block), BF16),
            pltpu.VMEM(wide, BF16), pltpu.VMEM(wide, BF16),
            pltpu.VMEM(norm.shape, F32), pltpu.VMEM(bias.shape, F32),
            pltpu.VMEM(seg.shape, jnp.int32), pltpu.VMEM(val.shape, jnp.int32),
            pltpu.VMEM((2, 8, dim), F32), pltpu.VMEM((2, 8, dim), F32),
            pltpu.VMEM((4, *small), F32),
            pltpu.VMEM((dim, half), BF16), pltpu.VMEM((dim, half), BF16),
            pltpu.VMEM((half, dim), BF16), pltpu.VMEM((half, dim), BF16),
            dma((8,)), pltpu.SemaphoreType.REGULAR, dma, dma((rows,)), dma, dma((rows,)), dma, dma((RELAYED,)), dma((6,)),
            dma((2,)), dma((2, steps // SUB)), dma((NEAR[0] + FAR,)),
            dma((2,)), dma((2, steps)), dma((2, steps)), dma((2,)),
            dma((2,)), dma((2,)),
        ],
        compiler_params=pltpu.CompilerParams(
            collective_id=0, has_side_effects=True, vmem_limit_bytes=SUBLAYER_VMEM
        ),
        name="sublayer",
    )(start, cot, first, second, norm, bias, seg, val)


def run_finish(res, sg, first, second, small):
    rows, seq, dim = res.shape
    ff = first.shape[1]
    any_space = pl.BlockSpec(memory_space=pl.ANY)
    vmem = pl.BlockSpec(memory_space=pltpu.VMEM)
    out = jax.ShapeDtypeStruct
    dma = pltpu.SemaphoreType.DMA
    return pl.pallas_call(
        finish_kernel,
        out_shape=(
            out((1, rows, seq, dim), BF16), out((1, rows, seq, dim), F32),
            out((1, dim, ff), F32), out((1, ff, dim), F32),
            out((1, 2, dim), F32), out((1, ff + dim), F32), out((1, 2), F32),
        ),
        in_specs=[vmem] * 5,
        out_specs=(any_space,) * 4 + (vmem,) * 3,
        scratch_shapes=[
            pltpu.VMEM((rows, seq, dim), F32),
            pltpu.VMEM((dim, ff), F32), pltpu.VMEM((ff, dim), F32),
            dma((2,)), dma((WRITES,)), dma((WRITES,)),
        ],
        compiler_params=pltpu.CompilerParams(vmem_limit_bytes=FINISH_VMEM),
        name="finish",
    )(res, sg, first, second, small)


def local(start, cot, first, second, norm, bias, seg, val):
    return run_finish(*run_sublayers(start, cot, first, second, norm, bias, seg, val))


def solution(mesh):
    in_specs = (
        P("dp", None, None),
        P("dp", None, None),
        P("section", None, None),
        P("section", None, None),
        P("section", None, None),
        P("section", None),
        P("dp", None),
        P("dp", None),
    )
    out_specs = (
        P("section", "dp", None, None),
        P("section", "dp", None, None),
        P("section", None, None),
        P("section", None, None),
        P("section", None, None),
        P("section", None),
        P("section", None),
    )
    return jax.shard_map(local, mesh=mesh, in_specs=in_specs, out_specs=out_specs, check_vma=False)
```

```python
import jax
import jax.numpy as jnp
from jax import lax
from jax.experimental import pallas as pl
from jax.experimental.pallas import tpu as pltpu
from jax.sharding import PartitionSpec as P

HEAD_DIM = 64
EPS = 1e-05
NEG_FILL = -1e30
MESH = pl.DeviceIdType.MESH
BF16 = jnp.bfloat16
F32 = jnp.float32
NN = (((1,), (0,)), ((), ()))
NT = (((1,), (1,)), ((), ()))
TN = (((0,), (0,)), ((), ()))
PAIR = 2 * HEAD_DIM
TILE = 1536
CHUNK = 256
SUB = 8
QUARTER = SUB // 4
NEAR = (10, 12)
FAR = 19
RELAYED = 4
RING = 32
LOADS = 4
WRITES = 12
SUBLAYER_VMEM = 50 * 2**20
FINISH_VMEM = 40 * 2**20
GELU_C = 0.7978845608028654
GELU_K = 0.044715


def dot(a, b, dims=NN):
    return lax.dot_general(a, b, dims, preferred_element_type=F32)


def gelu_and_slope(x):
    square = x * x
    t = jnp.tanh(GELU_C * (x + GELU_K * (square * x)))
    half = 0.5 * (1.0 + t)
    slope = half + (0.5 * GELU_C) * x * (1.0 - t * t) * (1.0 + (3.0 * GELU_K) * square)
    return x * half, slope


def fold(x):
    return x.reshape(x.shape[0] // 8, 8, x.shape[1]).sum(axis=0)


def normalize(hidden):
    mean = jnp.mean(hidden, axis=-1, keepdims=True)
    centered = hidden - mean
    variance = jnp.mean(centered * centered, axis=-1, keepdims=True)
    inv_std = lax.rsqrt(variance + EPS)
    return centered * inv_std, inv_std


def sublayer_kernel(
    start, cot, first, second, norm_in, bias_in, seg_in, val_in,
    hout, gout, first_o, second_o, small_o,
    w1, w2, w1t, w2t, hin, pair, act, mid,
    norm, bias, seg, val, sq_acc, norm_acc, small,
    sum_a1, sum_b1, sum_a2, sum_b2,
    load_sem, turn_sem, hs_sem, hr_sem, gs_sem, gr_sem, relay_send, relay_recv, small_sem,
    part_send, part_recv, hand_recv, line_send, line_recv, whole_recv, back_send,
    mate_send, mate_recv,
):
    nrm, gin = pair.at[0], pair.at[1]
    section = lax.axis_index("section")
    dp = lax.axis_index("dp")
    last = lax.axis_size("section") - 1
    rows, seq, dim = start.shape
    ff = first.shape[2]
    pairs = dim // PAIR
    is_attention = section % 2 == 0
    nxt = jnp.minimum(section + 1, last)
    prv = jnp.maximum(section - 1, 0)

    first_load = pltpu.make_async_copy(first.at[0], w1, load_sem.at[0])
    second_load = pltpu.make_async_copy(second.at[0], w2, load_sem.at[1])
    start_load = pltpu.make_async_copy(start, hin, load_sem.at[2])
    cot_load = pltpu.make_async_copy(cot, gin, load_sem.at[3])
    small_loads = [
        pltpu.make_async_copy(src, dst, load_sem.at[4 + k])
        for k, (src, dst) in enumerate(
            ((norm_in, norm), (bias_in, bias), (seg_in, seg), (val_in, val))
        )
    ]

    def split_load(src, dst, k):
        count = dst.shape[0] // LOADS
        for at in range(0, dst.shape[0], count):
            pltpu.make_async_copy(
                src.at[0, pl.ds(at, count)], dst.at[pl.ds(at, count)], load_sem.at[k]
            ).start()

    split_load(first, w1, 0)

    @pl.when(section == 0)
    def _():
        start_load.start()

    for load in small_loads:
        load.start()

    @pl.when(jnp.logical_not(is_attention))
    def _():
        split_load(second, w2, 1)

    @pl.when(section == last)
    def _():
        cot_load.start()

    chips = lax.axis_size("dp") // 2
    chip, core = dp // 2, dp % 2
    mate = dp + 1 - 2 * core
    on_left = chip < chips // 2
    is_middle = (chip == chips // 2 - 1) | (chip == chips // 2)
    has_outer = (chip > 0) & (chip < chips - 1)
    inner = jnp.where(on_left, dp + 2, dp - 2)
    outer = jnp.clip(jnp.where(on_left, dp - 2, dp + 2), 0, 2 * chips - 1)
    helper = section + 1 - 2 * (section % 2)
    near = jnp.where(section < 2, NEAR[0], NEAR[1])
    far = jnp.where((section == 1) | (section == 2), FAR, 0)
    handed = near + far

    barrier = pltpu.get_barrier_semaphore()

    def greet(to_section, to_dp):
        pl.semaphore_signal(
            barrier, inc=1, device_id=(to_section, to_dp), device_id_type=MESH
        )

    greet(section, mate)
    greet(section, inner)

    @pl.when(has_outer)
    def _():
        greet(section, outer)

    @pl.when(section > 0)
    def _():
        greet(prv, dp)

    @pl.when(section < last)
    def _():
        greet(nxt, dp)

    @pl.when((section == 0) | (section == 2))
    def _():
        greet(2 - section, dp)

    peers = 3 + has_outer.astype(jnp.int32)
    peers += ((section == 0) | (section == 2)).astype(jnp.int32)
    peers += ((section > 0) & (section < last)).astype(jnp.int32)

    for ref in (sq_acc, norm_acc, small):
        ref[...] = jnp.zeros_like(ref)

    def h_copy(i):
        return pltpu.make_async_remote_copy(
            hout.at[i], hin.at[i], hs_sem, hr_sem.at[i],
            device_id=(nxt, dp), device_id_type=MESH,
        )

    def g_copy(i):
        return pltpu.make_async_remote_copy(
            gout.at[i], gin.at[i], gs_sem, gr_sem.at[i],
            device_id=(prv, dp), device_id_type=MESH,
        )

    def send_in_turn(i):
        @pl.when((i == 0) & (core == 1))
        def _():
            pl.semaphore_wait(turn_sem, 1)

        h_copy(i).start()

        @pl.when((i == 0) & (core == 0))
        def _():
            pl.semaphore_signal(turn_sem, inc=1, device_id=(section, mate), device_id_type=MESH)

    def via(i):
        return w2.at[pl.ds(pl.multiple_of(i * seq, seq), seq), :]

    def relay_in(i):
        return pltpu.make_async_remote_copy(
            gout.at[i], via(i), gs_sem, relay_recv.at[i],
            device_id=(0, dp), device_id_type=MESH,
        )

    def relay_out(i):
        return pltpu.make_async_remote_copy(
            via(i), gin.at[i], relay_send, gr_sem.at[i],
            device_id=(nxt, dp), device_id_type=MESH,
        )

    def pass_on(i, carry):
        relay_in(i).wait_recv()
        relay_out(i).start()
        return carry

    eye = lax.broadcasted_iota(jnp.int32, (seq, seq), 0) == lax.broadcasted_iota(
        jnp.int32, (seq, seq), 1
    )

    def column(row):
        return jnp.sum(jnp.where(eye, row, 0.0), axis=1, keepdims=True)

    def valid_row(i):
        return val[pl.ds(i, 1), :].astype(F32)

    def entry(i):
        @pl.when(section > 0)
        def _():
            h_copy(i).wait_recv()

        hidden = hin[i].astype(F32)
        normal, _ = normalize(hidden)
        low = (normal * norm[0, 0:1, :] + norm[0, 1:2, :]).astype(BF16)
        nrm[i] = low
        return hidden, low

    def leave(i, hidden, branch):
        low = (hidden + branch).astype(BF16)
        hout[i] = low

        @pl.when((section > 0) & (section < last))
        def _():
            h_copy(i).start()

        @pl.when(section == 0)
        def _():
            send_in_turn(i)

        weight = column(valid_row(i))
        value = low.astype(F32)
        sq_acc[0] += fold(value * value * weight)
        sq_acc[1] += fold(branch * branch * weight)

    def grad_entry(i):
        @pl.when(section < last)
        def _():
            g_copy(i).wait_recv()

        @pl.when(section == last)
        def _():
            gin[i] = jnp.where(column(valid_row(i)) > 0, gin[i], jnp.zeros((seq, dim), BF16))

        return gin[i]

    def grad_leave(i, grad, normed_grad):
        grad_value = grad.astype(F32)
        normal, inv_std = normalize(hin[i].astype(F32))
        scaled = normed_grad * norm[0, 0:1, :]
        mean_one = jnp.mean(scaled, axis=-1, keepdims=True)
        mean_two = jnp.mean(scaled * normal, axis=-1, keepdims=True)
        low = (grad_value + inv_std * (scaled - mean_one - normal * mean_two)).astype(BF16)
        gout[i] = low

        @pl.when((section == 2) & (i < RELAYED))
        def _():
            relay_in(i).start()

        @pl.when((section > 0) & ((section != 2) | (i >= RELAYED)))
        def _():
            g_copy(i).start()

        norm_acc[0] += fold(normed_grad * normal)
        norm_acc[1] += fold(normed_grad)


    def dense_forward(i):
        hidden, low = entry(i)
        branch = jnp.zeros((seq, dim), F32)
        for at in range(0, ff, TILE):
            cols = slice(at, at + TILE)
            value, slope = gelu_and_slope(dot(low, w1[:, cols]) + bias[0:1, cols])
            value = value.astype(BF16)
            act[i, :, cols] = value
            mid[i, :, cols] = slope.astype(BF16)
            branch += dot(value, w2[cols, :])
        leave(i, hidden, branch + bias[0:1, ff:])

    def dense_backward(i):
        grad = grad_entry(i)
        normed_grad = jnp.zeros((seq, dim), F32)
        for at in range(0, ff, TILE):
            cols = slice(at, at + TILE)
            inner = dot(grad, w2t[:, cols]) * mid[i, :, cols].astype(F32)
            low = inner.astype(BF16)
            mid[i, :, cols] = low
            normed_grad += dot(low, w1t[cols, :])
        grad_leave(i, grad, normed_grad)


    lower = lax.broadcasted_iota(jnp.int32, (seq, PAIR), 1) < HEAD_DIM

    def split_heads(x):
        zero = jnp.zeros_like(x)
        return jnp.concatenate([jnp.where(lower, x, zero), jnp.where(lower, zero, x)], axis=0)

    def join_heads(x):
        return jnp.where(lower, x[:seq], x[seq:])

    def attention_forward(i):
        hidden, low = entry(i)
        projected = dot(low, w1[:, : 3 * dim])
        mid[i, :, :dim] = (projected[:, :dim] + bias[0:1, :dim]).astype(BF16)
        mid[i, :, dim : 2 * dim] = projected[:, dim : 2 * dim].astype(BF16)
        mid[i, :, 2 * dim : 3 * dim] = (
            projected[:, 2 * dim :] + bias[0:1, dim : 2 * dim]
        ).astype(BF16)
        seg_row = seg[pl.ds(i, 1), :].astype(F32)
        allowed = (column(seg_row) == seg_row) & ((column(valid_row(i)) > 0) | eye)
        packed = [mid[i, :, k * PAIR : (k + 1) * PAIR] for k in range(3 * pairs)]
        scores = [
            dot(split_heads(packed[pairs + p]), packed[p], NT) * HEAD_DIM**-0.5
            for p in range(pairs)
        ]
        mixed = []
        for p in range(pairs):
            probs = []
            for half in (scores[p][:seq], scores[p][seq:]):
                half = jnp.where(allowed, half, NEG_FILL)
                weight = jnp.exp(half - jnp.max(half, axis=0, keepdims=True))
                probs.append((weight / jnp.sum(weight, axis=0, keepdims=True)).astype(BF16))
                act[i, :, (2 * p + len(probs) - 1) * seq : (2 * p + len(probs)) * seq] = probs[-1]
            prob = jnp.concatenate(probs, axis=0)
            mixed.append(dot(prob, split_heads(packed[2 * pairs + p]), TN).astype(BF16))
        mixed = jnp.concatenate(mixed, axis=1)
        mid[i, :, 3 * dim :] = mixed
        branch = dot(mixed, w1t[3 * dim :, :]) + bias[0:1, ff:]
        leave(i, hidden, branch)

    def attention_backward(i):
        grad = grad_entry(i)
        mixed_grad = dot(grad, w1[:, 3 * dim :]).astype(BF16)
        packed = [mid[i, :, k * PAIR : (k + 1) * PAIR] for k in range(3 * pairs)]
        probs = [act[i, :, k * seq : (k + 1) * seq] for k in range(2 * pairs)]
        grads = [None] * (3 * pairs)
        for p in range(pairs):
            out_grad = mixed_grad[:, p * PAIR : (p + 1) * PAIR]
            prob_grad = dot(split_heads(packed[2 * pairs + p]), out_grad, NT)
            parts = []
            for k in range(2):
                value, grad_of = probs[2 * p + k].astype(F32), prob_grad[k * seq : (k + 1) * seq]
                inner = jnp.sum(value * grad_of, axis=0, keepdims=True)
                parts.append((value * (grad_of - inner)).astype(BF16))
            score_grad = jnp.concatenate(parts, axis=0)
            prob = jnp.concatenate(probs[2 * p : 2 * p + 2], axis=0)
            query_grad = dot(score_grad, split_heads(packed[pairs + p]), TN) * HEAD_DIM**-0.5
            key_grad = join_heads(dot(score_grad, packed[p])) * HEAD_DIM**-0.5
            grads[p] = query_grad.astype(BF16)
            grads[pairs + p] = key_grad.astype(BF16)
            grads[2 * pairs + p] = join_heads(dot(prob, out_grad)).astype(BF16)
        packed_grad = jnp.concatenate(grads, axis=1)
        mid[i, :, : 3 * dim] = packed_grad
        normed_grad = dot(packed_grad, w1t[: 3 * dim, :])
        grad_leave(i, grad, normed_grad)

    for load in small_loads:
        load.wait()
    first_load.wait()

    def transpose(src, dst, low, high):
        for at in range(low, high, 2 * PAIR):
            dst[at : at + 2 * PAIR, :] = src[:, at : at + 2 * PAIR].T

    @pl.when(section == 0)
    def _():
        start_load.wait()

    @pl.when(section == last)
    def _():
        cot_load.wait()

    def run(forward, backward, lag, before_last, after_last):
        pl.semaphore_wait(barrier, peers)

        def step(i, carry):
            @pl.when(i == rows - 1)
            def _():
                before_last()

            @pl.when(i < rows)
            def _():
                forward(i)

            @pl.when(i == rows)
            def _():
                after_last()

            @pl.when(i >= lag)
            def _():
                backward(i - lag)

            return carry

        lax.fori_loop(0, rows + lag, step, 0)

    @pl.when(is_attention)
    def _():
        transpose(w1, w1t, 3 * dim, ff)

        def late():
            @pl.when(section == 0)
            def _():
                transpose(w1, w1t, 0, 3 * dim)

        @pl.when(section > 0)
        def _():
            transpose(w1, w1t, 0, 3 * dim)

        def relay():
            @pl.when(section == 0)
            def _():
                lax.fori_loop(0, RELAYED, pass_on, 0)

        lag = jnp.where(section == 0, rows, rows // 2)
        run(attention_forward, attention_backward, lag, late, relay)

        @pl.when(section == 0)
        def _():
            ref = w2.at[pl.ds(0, RELAYED * seq), :]
            pltpu.make_async_copy(ref, ref, relay_send).wait()


    @pl.when(jnp.logical_not(is_attention))
    def _():
        second_load.wait()
        transpose(w1, w1t, 0, ff)
        for at in range(0, ff, 2 * PAIR):
            w2t[:, at : at + 2 * PAIR] = w2[at : at + 2 * PAIR, :].T
        lag = jnp.where(section == last, 0, rows - 1)
        run(dense_forward, dense_backward, lag, lambda: None, lambda: None)

    def remote(src, dst, send, recv, to):
        return pltpu.make_async_remote_copy(
            src, dst, send, recv, device_id=to, device_id_type=MESH
        )

    small_mate = remote(
        small.at[0], small.at[1], small_sem.at[0], small_sem.at[1], (section, mate)
    )
    small_line = remote(
        small.at[0], small.at[2], small_sem.at[2], small_sem.at[3], (section, inner)
    )
    small_cross = remote(
        small.at[0], small.at[3], small_sem.at[2], small_sem.at[4], (section, inner)
    )
    small_back = remote(
        small.at[3], small.at[3], small_sem.at[5], small_sem.at[4], (section, outer)
    )


    tokens = rows * seq
    half = ff // 2
    steps = (half // CHUNK) * SUB
    tall, short = dim // SUB, CHUNK // SUB
    mine, theirs = core * half, (1 - core) * half

    def own(k, v):
        if k == 0:
            return w1.at[
                pl.ds(pl.multiple_of((v % SUB) * tall, 16), tall),
                pl.ds(pl.multiple_of(mine + (v // SUB) * CHUNK, CHUNK), CHUNK),
            ]
        return w2.at[pl.ds(pl.multiple_of(mine + v * short, 16), short), :]

    def whole(k, v):
        if k == 0:
            return first_o.at[
                pl.ds(pl.multiple_of((v % SUB) * tall, 16), tall),
                pl.ds(pl.multiple_of(mine + (v // SUB) * CHUNK, CHUNK), CHUNK),
            ]
        return second_o.at[pl.ds(pl.multiple_of(mine + v * short, 16), short), :]

    def slot(ref, k, v):
        if k == 0:
            return ref.at[
                pl.ds(pl.multiple_of((v % SUB) * tall, 16), tall),
                pl.ds(pl.multiple_of((v // SUB) * CHUNK, CHUNK), CHUNK),
            ]
        return ref.at[pl.ds(pl.multiple_of(v * short, 16), short), :]

    line = (sum_b1, sum_b2)

    def part_copy(k, c):
        at = pl.ds(pl.multiple_of(theirs + c * CHUNK, CHUNK), CHUNK)
        to = pl.ds(pl.multiple_of(c * CHUNK, CHUNK), CHUNK)
        src, dst = (w1.at[:, at], sum_a1.at[:, to]) if k == 0 else (w2.at[at, :], sum_a2.at[to, :])
        return remote(src, dst, part_send.at[k], part_recv.at[k, c], (section, mate))

    ring = line_recv.shape[0]

    def line_copy(k, v, p):
        return remote(
            own(k, v), slot(line[k], k, v), line_send.at[k], line_recv.at[p % ring], (section, inner)
        )

    def cross_copy(k, v, p):
        return remote(
            own(k, v), whole(k, v), line_send.at[k], whole_recv.at[p % ring], (section, inner)
        )

    def back_copy(k, v, p):
        ref = whole(k, v)
        return remote(ref, ref, back_send.at[k], whole_recv.at[p % ring], (section, outer))

    shift = jnp.where(section >= 2, NEAR[0] + FAR, 0)

    def given_copy(v):
        to = jnp.where(v < near, helper, nxt)
        w = jnp.where(v < near, v + shift, v)
        return remote(own(1, v), slot(sum_a2, 1, w), line_send.at[1], hand_recv.at[w], (to, dp))

    def return_copy(w, to, v):
        return remote(whole(1, w), whole(1, v), mate_send.at[1], hand_recv.at[v], (to, dp))

    def mate_copy(k, v):
        ref = whole(k, v)
        return remote(ref, ref, mate_send.at[k], mate_recv.at[k], (section, mate))

    def token_sum(matrix):
        return jnp.sum(fold(matrix.astype(F32)), axis=0, keepdims=True)

    def small_start():
        lane = lax.broadcasted_iota(jnp.int32, (1, dim), 1)
        counts = jnp.zeros((1, dim), F32)
        for k, x in enumerate((sq_acc[0], sq_acc[1], val[...].astype(F32))):
            amount = jnp.sum(jnp.sum(x, axis=0, keepdims=True), axis=1, keepdims=True)
            counts = jnp.where(lane == k, amount, counts)
        small[0, 0:1, :] = jnp.sum(norm_acc[0], axis=0, keepdims=True)
        small[0, 1:2, :] = jnp.sum(norm_acc[1], axis=0, keepdims=True)
        small[0, 2 + ff // dim : 3 + ff // dim, :] = token_sum(gin[...].reshape(tokens, dim))
        small[0, 3 + ff // dim : 4 + ff // dim, :] = counts
        small_mate.start()

    def bias_sum(matrix, col):
        third = col // dim
        row = jnp.where(is_attention, third // 2, third) + 2
        at = pl.ds(pl.multiple_of(col - third * dim, CHUNK), CHUNK)

        @pl.when(jnp.logical_not(is_attention) | (third == 0) | (third == 2))
        def _():
            small[0, pl.ds(row, 1), at] = token_sum(matrix)

    def compute(k, c, is_mine):
        base = jnp.where(is_mine, mine, theirs) + c * CHUNK
        at = pl.ds(pl.multiple_of(base, CHUNK), CHUNK)
        if k == 0:
            side = is_attention & (base >= 3 * dim)
            left = pair[side.astype(jnp.int32)].reshape(tokens, dim)
            right = mid[:, :, at].reshape(tokens, CHUNK)
            w1[:, at] = dot(left, right, TN).astype(BF16)
        else:
            left = act[:, :, at].reshape(tokens, CHUNK)
            w2[at, :] = dot(left, gin[...].reshape(tokens, dim), TN).astype(BF16)

        @pl.when(jnp.logical_not(is_mine))
        def _():
            part_copy(k, c).start()

        if k == 0:
            bias_sum(mid[:, :, at].reshape(tokens, CHUNK), base)

    def combine(dst, *refs):
        value = refs[0][...].astype(F32)
        for ref in refs[1:]:
            value += ref[...].astype(F32)
        dst[...] = value.astype(BF16)

    def send_in(k, v, p, *refs):
        @pl.when(has_outer)
        def _():
            line_copy(k, v, p).wait_recv()
            combine(own(k, v), *refs, slot(line[k], k, v))

        @pl.when(jnp.logical_not(has_outer))
        def _():
            combine(own(k, v), *refs)

        @pl.when(is_middle)
        def _():
            cross_copy(k, v, p).start()

        @pl.when(jnp.logical_not(is_middle))
        def _():
            line_copy(k, v, p).start()

    def part_wait(k, v):
        @pl.when(v % SUB == 0)
        def _():
            part_copy(k, v // SUB).wait_recv()

    def send_first(v, p):
        part_wait(0, v)
        send_in(0, v, p, own(0, v), slot(sum_a1, 0, v))

    def send_second(v, p):
        part_wait(1, v)
        send_in(1, v, p, own(1, v), slot(sum_a2, 1, v))

    def hand_over(v):
        part_wait(1, v)
        combine(own(1, v), own(1, v), slot(sum_a2, 1, v))
        given_copy(v).start()

    def send_given(w, to, v, p):
        return_copy(w, to, w).wait_recv()
        send_in(1, w, p, slot(sum_a2, 1, w))

    def settle(k, v, p):
        cross_copy(k, v, p).wait_recv()

        @pl.when(is_middle)
        def _():
            combine(whole(k, v), own(k, v), whole(k, v))

        @pl.when(has_outer)
        def _():
            back_copy(k, v, p).start()

    def settle_first(v, p):
        settle(0, v, p)
        mate_copy(0, v).start()

    def settle_second(v, p):
        settle(1, v, p)
        mate_copy(1, v).start()

    def settle_handed(v):
        return_copy(v, helper, v).wait_recv()
        mate_copy(1, v).start()

    def settle_given(w, to, v, p):
        settle(1, w, p)
        return_copy(w, to, v).start()

    def small_in():
        small_mate.wait_recv()
        small_mate.wait_send()
        small[0] += small[1]

        @pl.when(has_outer)
        def _():
            small_line.wait_recv()
            small[0] += small[2]

        @pl.when(is_middle)
        def _():
            small_cross.start()

        @pl.when(jnp.logical_not(is_middle))
        def _():
            small_line.start()

    def small_settle():
        small_cross.wait_recv()

        @pl.when(is_middle)
        def _():
            small[3] += small[0]

        @pl.when(has_outer)
        def _():
            small_back.start()

        small_o[...] = small[3]

    gap = jnp.where(on_left, chips // 2 - 1 - chip, chip - chips // 2)
    lag = 4 + 14 * gap
    blocks = steps // SUB
    early = (blocks * 2 // 3) * SUB
    is_dense = jnp.logical_not(is_attention)
    length = jnp.where(is_attention, steps + near + far, 2 * steps - handed)

    ahead = jnp.where(is_middle, SUB, 0)

    @pl.when(is_dense)
    def _():
        compute(0, 0, False)
        compute(0, 0, True)

    def in_line(u, first_part, second_part, given_part):
        @pl.when((u >= 0) & (u < length) & is_dense)
        def _():
            @pl.when(u < steps)
            def _():
                first_part(u, u)

            @pl.when(u >= steps)
            def _():
                second_part(u - steps + handed, u)

        @pl.when((u >= 0) & (u < length) & is_attention)
        def _():
            @pl.when(u < near)
            def _():
                given_part(u + shift, helper, u, u)

            @pl.when((u >= near) & (u < near + early))
            def _():
                first_part(u - near, u)

            @pl.when((u >= near + early) & (u < near + early + far))
            def _():
                v = NEAR[0] + u - near - early
                given_part(v, prv, v, u)

            @pl.when(u >= near + early + far)
            def _():
                first_part(u - near - far, u)

    def step(u, carry):
        in_line(u - ahead, send_first, send_second, send_given)

        @pl.when((u % SUB >= SUB // 2) & is_dense)
        def _():
            for k in range(2):
                v = u // SUB * SUB + 2 * (u % SUB - SUB // 2) + k

                @pl.when(v < handed)
                def _(v=v):
                    hand_over(v)

        t = u - ahead - lag

        @pl.when(t == length - 1)
        def _():
            small_settle()

        in_line(t, settle_first, settle_second, settle_given)

        @pl.when((t >= length) & (t < length + handed) & is_dense)
        def _():
            settle_handed(t - length)

        c, q = u // SUB, u % SUB // QUARTER
        on_time = (u % QUARTER == 0) & (c < blocks)

        @pl.when(on_time & (q < 2) & is_dense)
        def _():
            compute(1, c, q == 1)

        @pl.when(on_time & jnp.where(is_attention, q < 2, (q >= 2) & (c + 1 < blocks)))
        def _():
            compute(0, jnp.where(is_attention, c, c + 1), q % 2 == 1)

        @pl.when(u == steps - 2)
        def _():
            small_start()

        @pl.when(u - ahead == steps + jnp.where((chip > 0) & (chip < chips - 1), SUB, 0))
        def _():
            small_in()

        return carry

    tail = jnp.where(is_attention, 0, handed)
    lax.fori_loop(0, length + ahead + lag + tail, step, 0)


    @pl.when(section < last)
    def _():
        remote(hout, hin, hs_sem, hr_sem.at[0], (nxt, dp)).wait_send()

    @pl.when(section > 0)
    def _():
        remote(gout, gin, gs_sem, gr_sem.at[0], (prv, dp)).wait_send()

    def taken(k, sem, count):
        if k == 0:
            ref = w1.at[:, pl.ds(0, (count // SUB) * CHUNK)]
        else:
            ref = w2.at[pl.ds(0, count * short), :]
        pltpu.make_async_copy(ref, ref, sem.at[k]).wait()

    taken(0, part_send, steps)
    taken(0, line_send, steps)
    taken(0, mate_send, steps)
    taken(0, mate_recv, steps)

    @pl.when(has_outer)
    def _():
        taken(0, back_send, steps)
        small_back.wait_send()

    @pl.when(jnp.logical_not(is_attention))
    def _():
        taken(1, part_send, steps)
        taken(1, line_send, steps)
        taken(1, mate_send, steps)
        taken(1, mate_recv, steps)

    for which, count in enumerate((NEAR[0], NEAR[0] + FAR, NEAR[1] + FAR, NEAR[1])):
        if which % 2:

            @pl.when((section == which) & has_outer)
            def _(count=count):
                taken(1, back_send, steps - count)

        else:

            @pl.when(section == which)
            def _(count=count):
                taken(1, line_send, count)
                taken(1, mate_send, count)

            @pl.when((section == which) & has_outer)
            def _(count=count):
                taken(1, back_send, count)

    small_line.wait_send()

    @pl.when(is_attention)
    def _():
        second_o[...] = jnp.zeros_like(second_o)


def finish_kernel(
    res, sg, first, second, small,
    res_o, sg_o, first_o, second_o, norm_o, bias_o, rms_o,
    sg_wide, first_wide, second_wide, sem, first_sem, second_sem,
):
    rows, _, dim = sg.shape
    ff = first.shape[1]
    copies = [pltpu.make_async_copy(res, res_o.at[0], sem.at[0])]
    copies[0].start()
    for src, wide, dst, sems in (
        (first, first_wide, first_o, first_sem), (second, second_wide, second_o, second_sem),
    ):
        count = src.shape[0] // WRITES
        for k in range(WRITES):
            at = pl.ds(k * count, count)
            wide[at, :] = src[at, :].astype(F32)
            copies.append(pltpu.make_async_copy(wide.at[at], dst.at[0, at], sems.at[k]))
            copies[-1].start()
    sg_wide[...] = sg[...].astype(F32)
    copies.append(pltpu.make_async_copy(sg_wide, sg_o.at[0], sem.at[1]))
    copies[-1].start()
    norm_o[0] = small[0:2, :]
    count = ff // dim + 1
    for k in range(count):
        bias_o[0:1, k * dim : (k + 1) * dim] = small[2 + k : 3 + k, :]
    stat = small[2 + count : 3 + count, :]
    rms_o[...] = jnp.sqrt(stat[:, 0:2] / (stat[:, 2:3] * dim))
    for copy in copies:
        copy.wait()


def run_sublayers(start, cot, first, second, norm, bias, seg, val):
    rows, seq, dim = start.shape
    ff = first.shape[2]
    half = ff // 2
    steps = (half // CHUNK) * SUB
    block = (rows, seq, dim)
    wide = (rows, seq, ff)
    small = (4 + ff // dim, dim)
    ring = RING if lax.axis_size("dp") <= 8 else 2 * steps
    any_space = pl.BlockSpec(memory_space=pl.ANY)
    vmem = pl.BlockSpec(memory_space=pltpu.VMEM)
    out = jax.ShapeDtypeStruct
    dma = pltpu.SemaphoreType.DMA
    return pl.pallas_call(
        sublayer_kernel,
        out_shape=(
            pltpu.VMEM(block, BF16), pltpu.VMEM(block, BF16),
            pltpu.VMEM((dim, ff), BF16), pltpu.VMEM((ff, dim), BF16), pltpu.VMEM(small, F32),
        ),
        in_specs=[any_space] * 8,
        out_specs=(vmem,) * 5,
        scratch_shapes=[
            pltpu.VMEM((dim, ff), BF16), pltpu.VMEM((ff, dim), BF16),
            pltpu.VMEM((ff, dim), BF16), pltpu.VMEM((dim, ff), BF16),
            pltpu.VMEM(block, BF16), pltpu.VMEM((2, *block), BF16),
            pltpu.VMEM(wide, BF16), pltpu.VMEM(wide, BF16),
            pltpu.VMEM(norm.shape, F32), pltpu.VMEM(bias.shape, F32),
            pltpu.VMEM(seg.shape, jnp.int32), pltpu.VMEM(val.shape, jnp.int32),
            pltpu.VMEM((2, 8, dim), F32), pltpu.VMEM((2, 8, dim), F32),
            pltpu.VMEM((4, *small), F32),
            pltpu.VMEM((dim, half), BF16), pltpu.VMEM((dim, half), BF16),
            pltpu.VMEM((half, dim), BF16), pltpu.VMEM((half, dim), BF16),
            dma((8,)), pltpu.SemaphoreType.REGULAR, dma, dma((rows,)), dma, dma((rows,)), dma, dma((RELAYED,)), dma((6,)),
            dma((2,)), dma((2, steps // SUB)), dma((sum(NEAR) + FAR,)),
            dma((2,)), dma((ring,)), dma((ring,)), dma((2,)),
            dma((2,)), dma((2,)),
        ],
        compiler_params=pltpu.CompilerParams(
            collective_id=0, has_side_effects=True, vmem_limit_bytes=SUBLAYER_VMEM
        ),
        name="sublayer",
    )(start, cot, first, second, norm, bias, seg, val)


def run_finish(res, sg, first, second, small):
    rows, seq, dim = res.shape
    ff = first.shape[1]
    any_space = pl.BlockSpec(memory_space=pl.ANY)
    vmem = pl.BlockSpec(memory_space=pltpu.VMEM)
    out = jax.ShapeDtypeStruct
    dma = pltpu.SemaphoreType.DMA
    return pl.pallas_call(
        finish_kernel,
        out_shape=(
            out((1, rows, seq, dim), BF16), out((1, rows, seq, dim), F32),
            out((1, dim, ff), F32), out((1, ff, dim), F32),
            out((1, 2, dim), F32), out((1, ff + dim), F32), out((1, 2), F32),
        ),
        in_specs=[vmem] * 5,
        out_specs=(any_space,) * 4 + (vmem,) * 3,
        scratch_shapes=[
            pltpu.VMEM((rows, seq, dim), F32),
            pltpu.VMEM((dim, ff), F32), pltpu.VMEM((ff, dim), F32),
            dma((2,)), dma((WRITES,)), dma((WRITES,)),
        ],
        compiler_params=pltpu.CompilerParams(vmem_limit_bytes=FINISH_VMEM),
        name="finish",
    )(res, sg, first, second, small)


def local(start, cot, first, second, norm, bias, seg, val):
    return run_finish(*run_sublayers(start, cot, first, second, norm, bias, seg, val))


def solution(mesh):
    in_specs = (
        P("dp", None, None),
        P("dp", None, None),
        P("section", None, None),
        P("section", None, None),
        P("section", None, None),
        P("section", None),
        P("dp", None),
        P("dp", None),
    )
    out_specs = (
        P("section", "dp", None, None),
        P("section", "dp", None, None),
        P("section", None, None),
        P("section", None, None),
        P("section", None, None),
        P("section", None),
        P("section", None),
    )
    return jax.shard_map(local, mesh=mesh, in_specs=in_specs, out_specs=out_specs, check_vma=False)
```

```python
import jax
import jax.numpy as jnp
from jax import lax
from jax.experimental import pallas as pl
from jax.experimental.pallas import tpu as pltpu
from jax.sharding import PartitionSpec as P

HEAD_DIM = 64
EPS = 1e-05
NEG_FILL = -1e30
MESH = pl.DeviceIdType.MESH
BF16 = jnp.bfloat16
F32 = jnp.float32
NN = (((1,), (0,)), ((), ()))
NT = (((1,), (1,)), ((), ()))
TN = (((0,), (0,)), ((), ()))
PAIR = 2 * HEAD_DIM
CHUNK = 256
SUB = 8
QUARTER = SUB // 4
NEAR = (9, 12)
FAR = 20
RELAYED = 4
RING = 32
LOADS = 4
WRITES = 12
SUBLAYER_VMEM = 50 * 2**20
FINISH_VMEM = 40 * 2**20
GELU_C = 0.7978845608028654
GELU_K = 0.044715


def dot(a, b, dims=NN):
    return lax.dot_general(a, b, dims, preferred_element_type=F32)


def gelu_and_slope(x):
    square = x * x
    t = jnp.tanh(GELU_C * (x + GELU_K * (square * x)))
    half = 0.5 * (1.0 + t)
    slope = half + (0.5 * GELU_C) * x * (1.0 - t * t) * (1.0 + (3.0 * GELU_K) * square)
    return x * half, slope


def fold(x):
    return x.reshape(x.shape[0] // 8, 8, x.shape[1]).sum(axis=0)


def normalize(hidden):
    mean = jnp.mean(hidden, axis=-1, keepdims=True)
    centered = hidden - mean
    variance = jnp.mean(centered * centered, axis=-1, keepdims=True)
    inv_std = lax.rsqrt(variance + EPS)
    return centered * inv_std, inv_std


def sublayer_kernel(
    start, cot, first, second, norm_in, bias_in, seg_in, val_in,
    hout, gout, first_o, second_o, small_o,
    w1, w2, w1t, w2t, hin, pair, act, mid,
    norm, bias, seg, val, sq_acc, norm_acc, small,
    sum_a1, sum_b1, sum_a2, sum_b2,
    load_sem, hs_sem, hr_sem, gs_sem, gr_sem, relay_send, relay_recv, small_sem,
    part_send, part_recv, hand_recv, line_send, line_recv, whole_recv, back_send,
    mate_send, mate_recv,
):
    nrm, gin = pair.at[0], pair.at[1]
    section = lax.axis_index("section")
    dp = lax.axis_index("dp")
    last = lax.axis_size("section") - 1
    rows, seq, dim = start.shape
    ff = first.shape[2]
    pairs = dim // PAIR
    is_attention = section % 2 == 0
    nxt = jnp.minimum(section + 1, last)
    prv = jnp.maximum(section - 1, 0)

    wide, out_cols = 3 * dim, pl.ds(3 * dim, ff - 3 * dim)
    first_load = pltpu.make_async_copy(
        first.at[0, :, pl.ds(0, wide)], w1.at[:, pl.ds(0, wide)], load_sem.at[0]
    )
    out_load = pltpu.make_async_copy(first.at[0, :, out_cols], w1.at[:, out_cols], load_sem.at[8])
    second_load = pltpu.make_async_copy(second.at[0], w2, load_sem.at[1])
    start_load = pltpu.make_async_copy(start.at[0], hin.at[0], load_sem.at[2])
    others = pl.ds(1, rows - 1)
    rest_load = pltpu.make_async_copy(start.at[others], hin.at[others], load_sem.at[9])
    cot_load = pltpu.make_async_copy(cot, gin, load_sem.at[3])
    small_loads = [
        pltpu.make_async_copy(src, dst, load_sem.at[4 + k])
        for k, (src, dst) in enumerate(
            ((norm_in, norm), (bias_in, bias), (seg_in, seg), (val_in, val))
        )
    ]

    def split_load(src, dst, cols, k):
        count = dst.shape[0] // LOADS
        for at in range(0, dst.shape[0], count):
            pltpu.make_async_copy(
                src.at[0, pl.ds(at, count), cols], dst.at[pl.ds(at, count), cols], load_sem.at[k]
            ).start()

    for load in small_loads:
        load.start()

    @pl.when(section == 0)
    def _():
        start_load.start()

    out_load.start()
    split_load(first, w1, pl.ds(0, wide), 0)

    @pl.when(section == 0)
    def _():
        rest_load.start()

    @pl.when(jnp.logical_not(is_attention))
    def _():
        split_load(second, w2, pl.ds(0, dim), 1)

    @pl.when(section == last)
    def _():
        cot_load.start()

    chips = lax.axis_size("dp") // 2
    chip, core = dp // 2, dp % 2
    mate = dp + 1 - 2 * core
    on_left = chip < chips // 2
    is_middle = (chip == chips // 2 - 1) | (chip == chips // 2)
    has_outer = (chip > 0) & (chip < chips - 1)
    inner = jnp.where(on_left, dp + 2, dp - 2)
    outer = jnp.clip(jnp.where(on_left, dp - 2, dp + 2), 0, 2 * chips - 1)
    helper = section + 1 - 2 * (section % 2)
    near = jnp.where(section < 2, NEAR[0], NEAR[1])
    far = jnp.where((section == 1) | (section == 2), FAR, 0)
    handed = near + far

    barrier = pltpu.get_barrier_semaphore()

    def greet(to_section, to_dp):
        pl.semaphore_signal(
            barrier, inc=1, device_id=(to_section, to_dp), device_id_type=MESH
        )

    greet(section, mate)
    greet(section, inner)

    @pl.when(has_outer)
    def _():
        greet(section, outer)

    @pl.when(section > 0)
    def _():
        greet(prv, dp)

    @pl.when(section < last)
    def _():
        greet(nxt, dp)

    @pl.when((section == 0) | (section == 2))
    def _():
        greet(2 - section, dp)

    peers = 3 + has_outer.astype(jnp.int32)
    peers += ((section == 0) | (section == 2)).astype(jnp.int32)
    peers += ((section > 0) & (section < last)).astype(jnp.int32)

    for ref in (sq_acc, norm_acc, small):
        ref[...] = jnp.zeros_like(ref)

    def h_copy(i):
        return pltpu.make_async_remote_copy(
            hout.at[i], hin.at[i], hs_sem, hr_sem.at[i],
            device_id=(nxt, dp), device_id_type=MESH,
        )

    def g_copy(i):
        return pltpu.make_async_remote_copy(
            gout.at[i], gin.at[i], gs_sem, gr_sem.at[i],
            device_id=(prv, dp), device_id_type=MESH,
        )

    def via(i):
        return w2.at[pl.ds(pl.multiple_of(i * seq, seq), seq), :]

    def relay_in(i):
        return pltpu.make_async_remote_copy(
            gout.at[i], via(i), gs_sem, relay_recv.at[i],
            device_id=(0, dp), device_id_type=MESH,
        )

    def relay_out(i):
        return pltpu.make_async_remote_copy(
            via(i), gin.at[i], relay_send, gr_sem.at[i],
            device_id=(nxt, dp), device_id_type=MESH,
        )

    def pass_on(i, carry):
        relay_in(i).wait_recv()
        relay_out(i).start()
        return carry

    eye = lax.broadcasted_iota(jnp.int32, (seq, seq), 0) == lax.broadcasted_iota(
        jnp.int32, (seq, seq), 1
    )

    def column(row):
        return jnp.sum(jnp.where(eye, row, 0.0), axis=1, keepdims=True)

    def valid_row(i):
        return val[pl.ds(i, 1), :].astype(F32)

    def entry(i):
        @pl.when(section > 0)
        def _():
            h_copy(i).wait_recv()

        hidden = hin[i].astype(F32)
        normal, _ = normalize(hidden)
        low = (normal * norm[0, 0:1, :] + norm[0, 1:2, :]).astype(BF16)
        nrm[i] = low
        return hidden, low

    def leave(i, hidden, branch):
        low = (hidden + branch).astype(BF16)
        hout[i] = low

        @pl.when(section < last)
        def _():
            h_copy(i).start()

        weight = column(valid_row(i))
        value = low.astype(F32)
        sq_acc[0] += fold(value * value * weight)
        sq_acc[1] += fold(branch * branch * weight)

    def grad_entry(i):
        @pl.when(section < last)
        def _():
            g_copy(i).wait_recv()

        @pl.when(section == last)
        def _():
            gin[i] = jnp.where(column(valid_row(i)) > 0, gin[i], jnp.zeros((seq, dim), BF16))

        return gin[i]

    def grad_leave(i, grad, normed_grad):
        grad_value = grad.astype(F32)
        normal, inv_std = normalize(hin[i].astype(F32))
        scaled = normed_grad * norm[0, 0:1, :]
        mean_one = jnp.mean(scaled, axis=-1, keepdims=True)
        mean_two = jnp.mean(scaled * normal, axis=-1, keepdims=True)
        low = (grad_value + inv_std * (scaled - mean_one - normal * mean_two)).astype(BF16)
        gout[i] = low

        @pl.when((section == 2) & (i < RELAYED))
        def _():
            relay_in(i).start()

        @pl.when((section > 0) & ((section != 2) | (i >= RELAYED)))
        def _():
            g_copy(i).start()

        norm_acc[0] += fold(normed_grad * normal)
        norm_acc[1] += fold(normed_grad)


    def dense_forward(i):
        hidden, low = entry(i)
        value, slope = gelu_and_slope(dot(low, w1[...]) + bias[0:1, :ff])
        value = value.astype(BF16)
        act[i] = value
        mid[i] = slope.astype(BF16)
        leave(i, hidden, dot(value, w2[...]) + bias[0:1, ff:])

    def dense_backward(i):
        grad = grad_entry(i)
        low = (dot(grad, w2t[...]) * mid[i].astype(F32)).astype(BF16)
        mid[i] = low
        grad_leave(i, grad, dot(low, w1t[...]))


    lower = lax.broadcasted_iota(jnp.int32, (seq, PAIR), 1) < HEAD_DIM

    def split_heads(x):
        zero = jnp.zeros_like(x)
        return jnp.concatenate([jnp.where(lower, x, zero), jnp.where(lower, zero, x)], axis=0)

    def join_heads(x):
        return jnp.where(lower, x[:seq], x[seq:])

    def attention_forward(i):
        @pl.when((section == 0) & (i == 1))
        def _():
            rest_load.wait()

        hidden, low = entry(i)
        projected = dot(low, w1[:, : 3 * dim])
        mid[i, :, :dim] = (projected[:, :dim] + bias[0:1, :dim]).astype(BF16)
        mid[i, :, dim : 2 * dim] = projected[:, dim : 2 * dim].astype(BF16)
        mid[i, :, 2 * dim : 3 * dim] = (
            projected[:, 2 * dim :] + bias[0:1, dim : 2 * dim]
        ).astype(BF16)
        seg_row = seg[pl.ds(i, 1), :].astype(F32)
        allowed = (column(seg_row) == seg_row) & ((column(valid_row(i)) > 0) | eye)
        packed = [mid[i, :, k * PAIR : (k + 1) * PAIR] for k in range(3 * pairs)]
        scores = [
            dot(split_heads(packed[pairs + p]), packed[p], NT) * HEAD_DIM**-0.5
            for p in range(pairs)
        ]
        mixed = []
        for p in range(pairs):
            probs = []
            for half in (scores[p][:seq], scores[p][seq:]):
                half = jnp.where(allowed, half, NEG_FILL)
                weight = jnp.exp(half - jnp.max(half, axis=0, keepdims=True))
                probs.append((weight / jnp.sum(weight, axis=0, keepdims=True)).astype(BF16))
                act[i, :, (2 * p + len(probs) - 1) * seq : (2 * p + len(probs)) * seq] = probs[-1]
            prob = jnp.concatenate(probs, axis=0)
            mixed.append(dot(prob, split_heads(packed[2 * pairs + p]), TN).astype(BF16))
        mixed = jnp.concatenate(mixed, axis=1)
        mid[i, :, 3 * dim :] = mixed
        branch = dot(mixed, w1t[3 * dim :, :]) + bias[0:1, ff:]
        leave(i, hidden, branch)

    def attention_backward(i):
        grad = grad_entry(i)
        mixed_grad = dot(grad, w1[:, 3 * dim :]).astype(BF16)
        packed = [mid[i, :, k * PAIR : (k + 1) * PAIR] for k in range(3 * pairs)]
        probs = [act[i, :, k * seq : (k + 1) * seq] for k in range(2 * pairs)]
        grads = [None] * (3 * pairs)
        for p in range(pairs):
            out_grad = mixed_grad[:, p * PAIR : (p + 1) * PAIR]
            prob_grad = dot(split_heads(packed[2 * pairs + p]), out_grad, NT)
            parts = []
            for k in range(2):
                value, grad_of = probs[2 * p + k].astype(F32), prob_grad[k * seq : (k + 1) * seq]
                inner = jnp.sum(value * grad_of, axis=0, keepdims=True)
                parts.append((value * (grad_of - inner)).astype(BF16))
            score_grad = jnp.concatenate(parts, axis=0)
            prob = jnp.concatenate(probs[2 * p : 2 * p + 2], axis=0)
            query_grad = dot(score_grad, split_heads(packed[pairs + p]), TN) * HEAD_DIM**-0.5
            key_grad = join_heads(dot(score_grad, packed[p])) * HEAD_DIM**-0.5
            grads[p] = query_grad.astype(BF16)
            grads[pairs + p] = key_grad.astype(BF16)
            grads[2 * pairs + p] = join_heads(dot(prob, out_grad)).astype(BF16)
        packed_grad = jnp.concatenate(grads, axis=1)
        mid[i, :, : 3 * dim] = packed_grad
        normed_grad = dot(packed_grad, w1t[: 3 * dim, :])
        grad_leave(i, grad, normed_grad)

    for load in small_loads:
        load.wait()

    def transpose(src, dst, low, high):
        for at in range(low, high, 2 * PAIR):
            dst[at : at + 2 * PAIR, :] = src[:, at : at + 2 * PAIR].T

    @pl.when(section == 0)
    def _():
        start_load.wait()

    @pl.when(section == last)
    def _():
        cot_load.wait()

    def run(forward, backward, lag, before_last, after_last):
        pl.semaphore_wait(barrier, peers)

        def step(i, carry):
            @pl.when(i == rows - 1)
            def _():
                before_last()

            @pl.when(i < rows)
            def _():
                forward(i)

            @pl.when(i == rows)
            def _():
                after_last()

            @pl.when(i >= lag)
            def _():
                backward(i - lag)

            return carry

        lax.fori_loop(0, rows + lag, step, 0)

    @pl.when(is_attention)
    def _():
        out_load.wait()
        transpose(w1, w1t, 3 * dim, ff)
        first_load.wait()

        def late():
            @pl.when(section == 0)
            def _():
                transpose(w1, w1t, 0, 3 * dim)

        @pl.when(section > 0)
        def _():
            transpose(w1, w1t, 0, 3 * dim)

        def relay():
            @pl.when(section == 0)
            def _():
                lax.fori_loop(0, RELAYED, pass_on, 0)

        lag = jnp.where(section == 0, rows, rows // 2)
        run(attention_forward, attention_backward, lag, late, relay)

        @pl.when(section == 0)
        def _():
            ref = w2.at[pl.ds(0, RELAYED * seq), :]
            pltpu.make_async_copy(ref, ref, relay_send).wait()


    @pl.when(jnp.logical_not(is_attention))
    def _():
        out_load.wait()
        first_load.wait()
        second_load.wait()
        transpose(w1, w1t, 0, ff)
        for at in range(0, ff, 2 * PAIR):
            w2t[:, at : at + 2 * PAIR] = w2[at : at + 2 * PAIR, :].T
        lag = jnp.where(section == last, 0, rows - 1)
        run(dense_forward, dense_backward, lag, lambda: None, lambda: None)

    def remote(src, dst, send, recv, to):
        return pltpu.make_async_remote_copy(
            src, dst, send, recv, device_id=to, device_id_type=MESH
        )

    small_mate = remote(
        small.at[0], small.at[1], small_sem.at[0], small_sem.at[1], (section, mate)
    )
    small_line = remote(
        small.at[0], small.at[2], small_sem.at[2], small_sem.at[3], (section, inner)
    )
    small_cross = remote(
        small.at[0], small.at[3], small_sem.at[2], small_sem.at[4], (section, inner)
    )
    small_back = remote(
        small.at[3], small.at[3], small_sem.at[5], small_sem.at[4], (section, outer)
    )


    tokens = rows * seq
    half = ff // 2
    steps = (half // CHUNK) * SUB
    tall, short = dim // SUB, CHUNK // SUB
    mine, theirs = core * half, (1 - core) * half

    def own(k, v):
        if k == 0:
            return w1.at[
                pl.ds(pl.multiple_of((v % SUB) * tall, 16), tall),
                pl.ds(pl.multiple_of(mine + (v // SUB) * CHUNK, CHUNK), CHUNK),
            ]
        return w2.at[pl.ds(pl.multiple_of(mine + v * short, 16), short), :]

    def whole(k, v):
        if k == 0:
            return first_o.at[
                pl.ds(pl.multiple_of((v % SUB) * tall, 16), tall),
                pl.ds(pl.multiple_of(mine + (v // SUB) * CHUNK, CHUNK), CHUNK),
            ]
        return second_o.at[pl.ds(pl.multiple_of(mine + v * short, 16), short), :]

    def slot(ref, k, v):
        if k == 0:
            return ref.at[
                pl.ds(pl.multiple_of((v % SUB) * tall, 16), tall),
                pl.ds(pl.multiple_of((v // SUB) * CHUNK, CHUNK), CHUNK),
            ]
        return ref.at[pl.ds(pl.multiple_of(v * short, 16), short), :]

    line = (sum_b1, sum_b2)

    def part_copy(k, c):
        at = pl.ds(pl.multiple_of(theirs + c * CHUNK, CHUNK), CHUNK)
        to = pl.ds(pl.multiple_of(c * CHUNK, CHUNK), CHUNK)
        src, dst = (w1.at[:, at], sum_a1.at[:, to]) if k == 0 else (w2.at[at, :], sum_a2.at[to, :])
        return remote(src, dst, part_send.at[k], part_recv.at[k, c], (section, mate))

    ring = line_recv.shape[0]

    def line_copy(k, v, p):
        return remote(
            own(k, v), slot(line[k], k, v), line_send.at[k], line_recv.at[p % ring], (section, inner)
        )

    def cross_copy(k, v, p):
        return remote(
            own(k, v), whole(k, v), line_send.at[k], whole_recv.at[p % ring], (section, inner)
        )

    def back_copy(k, v, p):
        ref = whole(k, v)
        return remote(ref, ref, back_send.at[k], whole_recv.at[p % ring], (section, outer))

    shift = jnp.where(section >= 2, NEAR[0] + FAR, 0)

    def given_copy(v):
        to = jnp.where(v < near, helper, nxt)
        w = jnp.where(v < near, v + shift, v)
        return remote(own(1, v), slot(sum_a2, 1, w), line_send.at[1], hand_recv.at[w], (to, dp))

    def return_copy(w, to, v):
        return remote(whole(1, w), whole(1, v), mate_send.at[1], hand_recv.at[v], (to, dp))

    def mate_copy(k, v):
        ref = whole(k, v)
        return remote(ref, ref, mate_send.at[k], mate_recv.at[k], (section, mate))

    def token_sum(matrix):
        return jnp.sum(fold(matrix.astype(F32)), axis=0, keepdims=True)

    def small_start():
        lane = lax.broadcasted_iota(jnp.int32, (1, dim), 1)
        counts = jnp.zeros((1, dim), F32)
        for k, x in enumerate((sq_acc[0], sq_acc[1], val[...].astype(F32))):
            amount = jnp.sum(jnp.sum(x, axis=0, keepdims=True), axis=1, keepdims=True)
            counts = jnp.where(lane == k, amount, counts)
        small[0, 0:1, :] = jnp.sum(norm_acc[0], axis=0, keepdims=True)
        small[0, 1:2, :] = jnp.sum(norm_acc[1], axis=0, keepdims=True)
        small[0, 2 + ff // dim : 3 + ff // dim, :] = token_sum(gin[...].reshape(tokens, dim))
        small[0, 3 + ff // dim : 4 + ff // dim, :] = counts
        small_mate.start()

    def bias_sum(matrix, col):
        third = col // dim
        row = jnp.where(is_attention, third // 2, third) + 2
        at = pl.ds(pl.multiple_of(col - third * dim, CHUNK), CHUNK)

        @pl.when(jnp.logical_not(is_attention) | (third == 0) | (third == 2))
        def _():
            small[0, pl.ds(row, 1), at] = token_sum(matrix)

    def compute(k, c, is_mine):
        base = jnp.where(is_mine, mine, theirs) + c * CHUNK
        at = pl.ds(pl.multiple_of(base, CHUNK), CHUNK)
        if k == 0:
            side = is_attention & (base >= 3 * dim)
            left = pair[side.astype(jnp.int32)].reshape(tokens, dim)
            right = mid[:, :, at].reshape(tokens, CHUNK)
            w1[:, at] = dot(left, right, TN).astype(BF16)
        else:
            left = act[:, :, at].reshape(tokens, CHUNK)
            w2[at, :] = dot(left, gin[...].reshape(tokens, dim), TN).astype(BF16)

        @pl.when(jnp.logical_not(is_mine))
        def _():
            part_copy(k, c).start()

        if k == 0:
            bias_sum(mid[:, :, at].reshape(tokens, CHUNK), base)

    def combine(dst, *refs):
        value = refs[0][...].astype(F32)
        for ref in refs[1:]:
            value += ref[...].astype(F32)
        dst[...] = value.astype(BF16)

    def send_in(k, v, p, *refs):
        @pl.when(has_outer)
        def _():
            line_copy(k, v, p).wait_recv()
            combine(own(k, v), *refs, slot(line[k], k, v))

        @pl.when(jnp.logical_not(has_outer))
        def _():
            combine(own(k, v), *refs)

        @pl.when(is_middle)
        def _():
            cross_copy(k, v, p).start()

        @pl.when(jnp.logical_not(is_middle))
        def _():
            line_copy(k, v, p).start()

    def part_wait(k, v):
        @pl.when(v % SUB == 0)
        def _():
            part_copy(k, v // SUB).wait_recv()

    def send_first(v, p):
        part_wait(0, v)
        send_in(0, v, p, own(0, v), slot(sum_a1, 0, v))

    def send_second(v, p):
        part_wait(1, v)
        send_in(1, v, p, own(1, v), slot(sum_a2, 1, v))

    def hand_over(v):
        part_wait(1, v)
        combine(own(1, v), own(1, v), slot(sum_a2, 1, v))
        given_copy(v).start()

    def send_given(w, to, v, p):
        return_copy(w, to, w).wait_recv()
        send_in(1, w, p, slot(sum_a2, 1, w))

    def settle(k, v, p):
        cross_copy(k, v, p).wait_recv()

        @pl.when(is_middle)
        def _():
            combine(whole(k, v), own(k, v), whole(k, v))

        @pl.when(has_outer)
        def _():
            back_copy(k, v, p).start()

    def settle_first(v, p):
        settle(0, v, p)
        mate_copy(0, v).start()

    def settle_second(v, p):
        settle(1, v, p)
        mate_copy(1, v).start()

    def settle_handed(v):
        return_copy(v, helper, v).wait_recv()
        mate_copy(1, v).start()

    def settle_given(w, to, v, p):
        settle(1, w, p)
        return_copy(w, to, v).start()

    def small_in():
        small_mate.wait_recv()
        small_mate.wait_send()
        small[0] += small[1]

        @pl.when(has_outer)
        def _():
            small_line.wait_recv()
            small[0] += small[2]

        @pl.when(is_middle)
        def _():
            small_cross.start()

        @pl.when(jnp.logical_not(is_middle))
        def _():
            small_line.start()

    def small_settle():
        small_cross.wait_recv()

        @pl.when(is_middle)
        def _():
            small[3] += small[0]

        @pl.when(has_outer)
        def _():
            small_back.start()

        small_o[...] = small[3]

    gap = jnp.where(on_left, chips // 2 - 1 - chip, chip - chips // 2)
    lag = 4 + 14 * gap
    blocks = steps // SUB
    early = (blocks * 2 // 3) * SUB
    is_dense = jnp.logical_not(is_attention)
    length = jnp.where(is_attention, steps + near + far, 2 * steps - handed)

    ahead = jnp.where(is_middle, SUB, 0)

    @pl.when(is_dense)
    def _():
        compute(0, 0, False)
        compute(0, 0, True)

    def in_line(u, first_part, second_part, given_part):
        @pl.when((u >= 0) & (u < length) & is_dense)
        def _():
            @pl.when(u < steps)
            def _():
                first_part(u, u)

            @pl.when(u >= steps)
            def _():
                second_part(u - steps + handed, u)

        @pl.when((u >= 0) & (u < length) & is_attention)
        def _():
            @pl.when(u < near)
            def _():
                given_part(u + shift, helper, u, u)

            @pl.when((u >= near) & (u < near + early))
            def _():
                first_part(u - near, u)

            @pl.when((u >= near + early) & (u < near + early + far))
            def _():
                v = NEAR[0] + u - near - early
                given_part(v, prv, v, u)

            @pl.when(u >= near + early + far)
            def _():
                first_part(u - near - far, u)

    def step(u, carry):
        in_line(u - ahead, send_first, send_second, send_given)

        @pl.when((u % SUB >= SUB // 2) & is_dense)
        def _():
            for k in range(2):
                v = u // SUB * SUB + 2 * (u % SUB - SUB // 2) + k

                @pl.when(v < handed)
                def _(v=v):
                    hand_over(v)

        t = u - ahead - lag

        @pl.when(t == length - 1)
        def _():
            small_settle()

        in_line(t, settle_first, settle_second, settle_given)

        @pl.when((t >= length) & (t < length + handed) & is_dense)
        def _():
            settle_handed(t - length)

        c, q = u // SUB, u % SUB // QUARTER
        on_time = (u % QUARTER == 0) & (c < blocks)

        @pl.when(on_time & (q < 2) & is_dense)
        def _():
            compute(1, c, q == 1)

        @pl.when(on_time & jnp.where(is_attention, q < 2, (q >= 2) & (c + 1 < blocks)))
        def _():
            compute(0, jnp.where(is_attention, c, c + 1), q % 2 == 1)

        @pl.when(u == steps - 2)
        def _():
            small_start()

        @pl.when(u - ahead == steps + jnp.where((chip > 0) & (chip < chips - 1), SUB, 0))
        def _():
            small_in()

        return carry

    tail = jnp.where(is_attention, 0, handed)
    lax.fori_loop(0, length + ahead + lag + tail, step, 0)


    @pl.when(section < last)
    def _():
        remote(hout, hin, hs_sem, hr_sem.at[0], (nxt, dp)).wait_send()

    @pl.when(section > 0)
    def _():
        remote(gout, gin, gs_sem, gr_sem.at[0], (prv, dp)).wait_send()

    def taken(k, sem, count):
        if k == 0:
            ref = w1.at[:, pl.ds(0, (count // SUB) * CHUNK)]
        else:
            ref = w2.at[pl.ds(0, count * short), :]
        pltpu.make_async_copy(ref, ref, sem.at[k]).wait()

    taken(0, part_send, steps)
    taken(0, line_send, steps)
    taken(0, mate_send, steps)
    taken(0, mate_recv, steps)

    @pl.when(has_outer)
    def _():
        taken(0, back_send, steps)
        small_back.wait_send()

    @pl.when(jnp.logical_not(is_attention))
    def _():
        taken(1, part_send, steps)
        taken(1, line_send, steps)
        taken(1, mate_send, steps)
        taken(1, mate_recv, steps)

    for which, count in enumerate((NEAR[0], NEAR[0] + FAR, NEAR[1] + FAR, NEAR[1])):
        if which % 2:

            @pl.when((section == which) & has_outer)
            def _(count=count):
                taken(1, back_send, steps - count)

        else:

            @pl.when(section == which)
            def _(count=count):
                taken(1, line_send, count)
                taken(1, mate_send, count)

            @pl.when((section == which) & has_outer)
            def _(count=count):
                taken(1, back_send, count)

    small_line.wait_send()

    @pl.when(is_attention)
    def _():
        second_o[...] = jnp.zeros_like(second_o)


def finish_kernel(
    res, sg, first, second, small,
    res_o, sg_o, first_o, second_o, norm_o, bias_o, rms_o,
    sg_wide, first_wide, second_wide, sem, first_sem, second_sem,
):
    rows, _, dim = sg.shape
    ff = first.shape[1]
    copies = [pltpu.make_async_copy(res, res_o.at[0], sem.at[0])]
    copies[0].start()
    for src, wide, dst, sems in (
        (first, first_wide, first_o, first_sem), (second, second_wide, second_o, second_sem),
    ):
        count = src.shape[0] // WRITES
        for k in range(WRITES):
            at = pl.ds(k * count, count)
            wide[at, :] = src[at, :].astype(F32)
            copies.append(pltpu.make_async_copy(wide.at[at], dst.at[0, at], sems.at[k]))
            copies[-1].start()
    sg_wide[...] = sg[...].astype(F32)
    copies.append(pltpu.make_async_copy(sg_wide, sg_o.at[0], sem.at[1]))
    copies[-1].start()
    norm_o[0] = small[0:2, :]
    count = ff // dim + 1
    for k in range(count):
        bias_o[0:1, k * dim : (k + 1) * dim] = small[2 + k : 3 + k, :]
    stat = small[2 + count : 3 + count, :]
    rms_o[...] = jnp.sqrt(stat[:, 0:2] / (stat[:, 2:3] * dim))
    for copy in copies:
        copy.wait()


def run_sublayers(start, cot, first, second, norm, bias, seg, val):
    rows, seq, dim = start.shape
    ff = first.shape[2]
    half = ff // 2
    steps = (half // CHUNK) * SUB
    block = (rows, seq, dim)
    wide = (rows, seq, ff)
    small = (4 + ff // dim, dim)
    ring = RING if lax.axis_size("dp") <= 8 else 2 * steps
    any_space = pl.BlockSpec(memory_space=pl.ANY)
    vmem = pl.BlockSpec(memory_space=pltpu.VMEM)
    out = jax.ShapeDtypeStruct
    dma = pltpu.SemaphoreType.DMA
    return pl.pallas_call(
        sublayer_kernel,
        out_shape=(
            pltpu.VMEM(block, BF16), pltpu.VMEM(block, BF16),
            pltpu.VMEM((dim, ff), BF16), pltpu.VMEM((ff, dim), BF16), pltpu.VMEM(small, F32),
        ),
        in_specs=[any_space] * 8,
        out_specs=(vmem,) * 5,
        scratch_shapes=[
            pltpu.VMEM((dim, ff), BF16), pltpu.VMEM((ff, dim), BF16),
            pltpu.VMEM((ff, dim), BF16), pltpu.VMEM((dim, ff), BF16),
            pltpu.VMEM(block, BF16), pltpu.VMEM((2, *block), BF16),
            pltpu.VMEM(wide, BF16), pltpu.VMEM(wide, BF16),
            pltpu.VMEM(norm.shape, F32), pltpu.VMEM(bias.shape, F32),
            pltpu.VMEM(seg.shape, jnp.int32), pltpu.VMEM(val.shape, jnp.int32),
            pltpu.VMEM((2, 8, dim), F32), pltpu.VMEM((2, 8, dim), F32),
            pltpu.VMEM((4, *small), F32),
            pltpu.VMEM((dim, half), BF16), pltpu.VMEM((dim, half), BF16),
            pltpu.VMEM((half, dim), BF16), pltpu.VMEM((half, dim), BF16),
            dma((10,)), dma, dma((rows,)), dma, dma((rows,)), dma, dma((RELAYED,)), dma((6,)),
            dma((2,)), dma((2, steps // SUB)), dma((sum(NEAR) + FAR,)),
            dma((2,)), dma((ring,)), dma((ring,)), dma((2,)),
            dma((2,)), dma((2,)),
        ],
        compiler_params=pltpu.CompilerParams(
            collective_id=0, has_side_effects=True, vmem_limit_bytes=SUBLAYER_VMEM
        ),
        name="sublayer",
    )(start, cot, first, second, norm, bias, seg, val)


def run_finish(res, sg, first, second, small):
    rows, seq, dim = res.shape
    ff = first.shape[1]
    any_space = pl.BlockSpec(memory_space=pl.ANY)
    vmem = pl.BlockSpec(memory_space=pltpu.VMEM)
    out = jax.ShapeDtypeStruct
    dma = pltpu.SemaphoreType.DMA
    return pl.pallas_call(
        finish_kernel,
        out_shape=(
            out((1, rows, seq, dim), BF16), out((1, rows, seq, dim), F32),
            out((1, dim, ff), F32), out((1, ff, dim), F32),
            out((1, 2, dim), F32), out((1, ff + dim), F32), out((1, 2), F32),
        ),
        in_specs=[vmem] * 5,
        out_specs=(any_space,) * 4 + (vmem,) * 3,
        scratch_shapes=[
            pltpu.VMEM((rows, seq, dim), F32),
            pltpu.VMEM((dim, ff), F32), pltpu.VMEM((ff, dim), F32),
            dma((2,)), dma((WRITES,)), dma((WRITES,)),
        ],
        compiler_params=pltpu.CompilerParams(vmem_limit_bytes=FINISH_VMEM),
        name="finish",
    )(res, sg, first, second, small)


def local(start, cot, first, second, norm, bias, seg, val):
    return run_finish(*run_sublayers(start, cot, first, second, norm, bias, seg, val))


def solution(mesh):
    in_specs = (
        P("dp", None, None),
        P("dp", None, None),
        P("section", None, None),
        P("section", None, None),
        P("section", None, None),
        P("section", None),
        P("dp", None),
        P("dp", None),
    )
    out_specs = (
        P("section", "dp", None, None),
        P("section", "dp", None, None),
        P("section", None, None),
        P("section", None, None),
        P("section", None, None),
        P("section", None),
        P("section", None),
    )
    return jax.shard_map(local, mesh=mesh, in_specs=in_specs, out_specs=out_specs, check_vma=False)
```

```python
import jax
import jax.numpy as jnp
from jax import lax
from jax.experimental import pallas as pl
from jax.experimental.pallas import tpu as pltpu
from jax.sharding import PartitionSpec as P

HEAD_DIM = 64
EPS = 1e-05
NEG_FILL = -1e30
MESH = pl.DeviceIdType.MESH
BF16 = jnp.bfloat16
F32 = jnp.float32
NN = (((1,), (0,)), ((), ()))
NT = (((1,), (1,)), ((), ()))
TN = (((0,), (0,)), ((), ()))
PAIR = 2 * HEAD_DIM
CHUNK = 256
SUB = 8
QUARTER = SUB // 4
NEAR = (9, 12)
FAR = 20
RELAYED = 4
RING = 32
LOADS = 4
WRITES = 12
SUBLAYER_VMEM = 50 * 2**20
FINISH_VMEM = 40 * 2**20
GELU_C = 0.7978845608028654
GELU_K = 0.044715


def dot(a, b, dims=NN):
    return lax.dot_general(a, b, dims, preferred_element_type=F32)


def gelu_and_slope(x):
    square = x * x
    t = jnp.tanh(GELU_C * (x + GELU_K * (square * x)))
    half = 0.5 * (1.0 + t)
    slope = half + (0.5 * GELU_C) * x * (1.0 - t * t) * (1.0 + (3.0 * GELU_K) * square)
    return x * half, slope


def fold(x):
    return x.reshape(x.shape[0] // 8, 8, x.shape[1]).sum(axis=0)


def normalize(hidden):
    mean = jnp.mean(hidden, axis=-1, keepdims=True)
    centered = hidden - mean
    variance = jnp.mean(centered * centered, axis=-1, keepdims=True)
    inv_std = lax.rsqrt(variance + EPS)
    return centered * inv_std, inv_std


def sublayer_kernel(
    start, cot, first, second, norm_in, bias_in, seg_in, val_in,
    hout, gout, first_o, second_o, small_o,
    w1, w2, w1t, w2t, hin, pair, act, mid,
    norm, bias, seg, val, sq_acc, norm_acc, small,
    sum_a1, sum_b1, sum_a2, sum_b2,
    load_sem, hs_sem, hr_sem, gs_sem, gr_sem, relay_send, relay_recv, small_sem,
    part_send, part_recv, hand_recv, line_send, line_recv, whole_recv, back_send,
    mate_send, mate_recv,
):
    nrm, gin = pair.at[0], pair.at[1]
    section = lax.axis_index("section")
    dp = lax.axis_index("dp")
    last = lax.axis_size("section") - 1
    rows, seq, dim = start.shape
    ff = first.shape[2]
    pairs = dim // PAIR
    is_attention = section % 2 == 0
    nxt = jnp.minimum(section + 1, last)
    prv = jnp.maximum(section - 1, 0)

    wide, out_cols = 3 * dim, pl.ds(3 * dim, ff - 3 * dim)
    first_load = pltpu.make_async_copy(
        first.at[0, :, pl.ds(0, wide)], w1.at[:, pl.ds(0, wide)], load_sem.at[0]
    )
    out_load = pltpu.make_async_copy(first.at[0, :, out_cols], w1.at[:, out_cols], load_sem.at[8])
    second_load = pltpu.make_async_copy(second.at[0], w2, load_sem.at[1])
    start_load = pltpu.make_async_copy(start.at[0], hin.at[0], load_sem.at[2])
    others = pl.ds(1, rows - 1)
    rest_load = pltpu.make_async_copy(start.at[others], hin.at[others], load_sem.at[9])
    cot_load = pltpu.make_async_copy(cot, gin, load_sem.at[3])
    small_loads = [
        pltpu.make_async_copy(src, dst, load_sem.at[4 + k])
        for k, (src, dst) in enumerate(
            ((norm_in, norm), (bias_in, bias), (seg_in, seg), (val_in, val))
        )
    ]

    def split_load(src, dst, cols, k):
        count = dst.shape[0] // LOADS
        for at in range(0, dst.shape[0], count):
            pltpu.make_async_copy(
                src.at[0, pl.ds(at, count), cols], dst.at[pl.ds(at, count), cols], load_sem.at[k]
            ).start()

    for load in small_loads:
        load.start()

    @pl.when(section == 0)
    def _():
        start_load.start()

    out_load.start()
    split_load(first, w1, pl.ds(0, wide), 0)

    @pl.when(section == 0)
    def _():
        rest_load.start()

    @pl.when(jnp.logical_not(is_attention))
    def _():
        split_load(second, w2, pl.ds(0, dim), 1)

    @pl.when(section == last)
    def _():
        cot_load.start()

    chips = lax.axis_size("dp") // 2
    chip, core = dp // 2, dp % 2
    mate = dp + 1 - 2 * core
    on_left = chip < chips // 2
    is_middle = (chip == chips // 2 - 1) | (chip == chips // 2)
    has_outer = (chip > 0) & (chip < chips - 1)
    inner = jnp.where(on_left, dp + 2, dp - 2)
    outer = jnp.clip(jnp.where(on_left, dp - 2, dp + 2), 0, 2 * chips - 1)
    helper = section + 1 - 2 * (section % 2)
    near = jnp.where(section < 2, NEAR[0], NEAR[1])
    far = jnp.where((section == 1) | (section == 2), FAR, 0)
    handed = near + far

    barrier = pltpu.get_barrier_semaphore()

    def greet(to_section, to_dp):
        pl.semaphore_signal(
            barrier, inc=1, device_id=(to_section, to_dp), device_id_type=MESH
        )

    greet(section, mate)
    greet(section, inner)

    @pl.when(has_outer)
    def _():
        greet(section, outer)

    @pl.when(section > 0)
    def _():
        greet(prv, dp)

    @pl.when(section < last)
    def _():
        greet(nxt, dp)

    @pl.when((section == 0) | (section == 2))
    def _():
        greet(2 - section, dp)

    peers = 3 + has_outer.astype(jnp.int32)
    peers += ((section == 0) | (section == 2)).astype(jnp.int32)
    peers += ((section > 0) & (section < last)).astype(jnp.int32)

    for ref in (sq_acc, norm_acc, small):
        ref[...] = jnp.zeros_like(ref)

    def h_copy(i):
        return pltpu.make_async_remote_copy(
            hout.at[i], hin.at[i], hs_sem, hr_sem.at[i],
            device_id=(nxt, dp), device_id_type=MESH,
        )

    def g_copy(i):
        return pltpu.make_async_remote_copy(
            gout.at[i], gin.at[i], gs_sem, gr_sem.at[i],
            device_id=(prv, dp), device_id_type=MESH,
        )

    def via(i):
        return w2.at[pl.ds(pl.multiple_of(i * seq, seq), seq), :]

    def relay_in(i):
        return pltpu.make_async_remote_copy(
            gout.at[i], via(i), gs_sem, relay_recv.at[i],
            device_id=(0, dp), device_id_type=MESH,
        )

    def relay_out(i):
        return pltpu.make_async_remote_copy(
            via(i), gin.at[i], relay_send, gr_sem.at[i],
            device_id=(nxt, dp), device_id_type=MESH,
        )

    def pass_on(i, carry):
        relay_in(i).wait_recv()
        relay_out(i).start()
        return carry

    eye = lax.broadcasted_iota(jnp.int32, (seq, seq), 0) == lax.broadcasted_iota(
        jnp.int32, (seq, seq), 1
    )

    def column(row):
        return jnp.sum(jnp.where(eye, row, 0.0), axis=1, keepdims=True)

    def valid_row(i):
        return val[pl.ds(i, 1), :].astype(F32)

    def entry(i):
        @pl.when(section > 0)
        def _():
            h_copy(i).wait_recv()

        hidden = hin[i].astype(F32)
        normal, _ = normalize(hidden)
        low = (normal * norm[0, 0:1, :] + norm[0, 1:2, :]).astype(BF16)
        nrm[i] = low
        return hidden, low

    def leave(i, hidden, branch):
        low = (hidden + branch).astype(BF16)
        hout[i] = low

        @pl.when(section < last)
        def _():
            h_copy(i).start()

        weight = column(valid_row(i))
        value = low.astype(F32)
        sq_acc[0] += fold(value * value * weight)
        sq_acc[1] += fold(branch * branch * weight)

    def grad_entry(i):
        @pl.when(section < last)
        def _():
            g_copy(i).wait_recv()

        @pl.when(section == last)
        def _():
            gin[i] = jnp.where(column(valid_row(i)) > 0, gin[i], jnp.zeros((seq, dim), BF16))

        return gin[i]

    def grad_leave(i, grad, normed_grad):
        grad_value = grad.astype(F32)
        normal, inv_std = normalize(hin[i].astype(F32))
        scaled = normed_grad * norm[0, 0:1, :]
        mean_one = jnp.mean(scaled, axis=-1, keepdims=True)
        mean_two = jnp.mean(scaled * normal, axis=-1, keepdims=True)
        low = (grad_value + inv_std * (scaled - mean_one - normal * mean_two)).astype(BF16)
        gout[i] = low

        @pl.when((section == 2) & (i < RELAYED))
        def _():
            relay_in(i).start()

        @pl.when((section > 0) & ((section != 2) | (i >= RELAYED)))
        def _():
            g_copy(i).start()

        norm_acc[0] += fold(normed_grad * normal)
        norm_acc[1] += fold(normed_grad)


    def dense_forward(i):
        hidden, low = entry(i)
        value, slope = gelu_and_slope(dot(low, w1[...]) + bias[0:1, :ff])
        value = value.astype(BF16)
        act[i] = value
        mid[i] = slope.astype(BF16)
        leave(i, hidden, dot(value, w2[...]) + bias[0:1, ff:])

    def dense_backward(i):
        grad = grad_entry(i)
        low = (dot(grad, w2t[...]) * mid[i].astype(F32)).astype(BF16)
        mid[i] = low
        grad_leave(i, grad, dot(low, w1t[...]))


    lower = lax.broadcasted_iota(jnp.int32, (seq, PAIR), 1) < HEAD_DIM

    def split_heads(x):
        zero = jnp.zeros_like(x)
        return jnp.concatenate([jnp.where(lower, x, zero), jnp.where(lower, zero, x)], axis=0)

    def join_heads(x):
        return jnp.where(lower, x[:seq], x[seq:])

    def attention_forward(i):
        @pl.when((section == 0) & (i == 1))
        def _():
            rest_load.wait()

        hidden, low = entry(i)
        projected = dot(low, w1[:, : 3 * dim])
        mid[i, :, :dim] = (projected[:, :dim] + bias[0:1, :dim]).astype(BF16)
        mid[i, :, dim : 2 * dim] = projected[:, dim : 2 * dim].astype(BF16)
        mid[i, :, 2 * dim : 3 * dim] = (
            projected[:, 2 * dim :] + bias[0:1, dim : 2 * dim]
        ).astype(BF16)
        seg_row = seg[pl.ds(i, 1), :].astype(F32)
        allowed = (column(seg_row) == seg_row) & ((column(valid_row(i)) > 0) | eye)
        packed = [mid[i, :, k * PAIR : (k + 1) * PAIR] for k in range(3 * pairs)]
        scores = [
            dot(split_heads(packed[pairs + p]), packed[p], NT) * HEAD_DIM**-0.5
            for p in range(pairs)
        ]
        mixed = []
        for p in range(pairs):
            probs = []
            for half in (scores[p][:seq], scores[p][seq:]):
                half = jnp.where(allowed, half, NEG_FILL)
                weight = jnp.exp(half - jnp.max(half, axis=0, keepdims=True))
                probs.append((weight / jnp.sum(weight, axis=0, keepdims=True)).astype(BF16))
                act[i, :, (2 * p + len(probs) - 1) * seq : (2 * p + len(probs)) * seq] = probs[-1]
            prob = jnp.concatenate(probs, axis=0)
            mixed.append(dot(prob, split_heads(packed[2 * pairs + p]), TN).astype(BF16))
        mixed = jnp.concatenate(mixed, axis=1)
        mid[i, :, 3 * dim :] = mixed
        branch = dot(mixed, w1t[3 * dim :, :]) + bias[0:1, ff:]
        leave(i, hidden, branch)

    def attention_backward(i):
        grad = grad_entry(i)
        mixed_grad = dot(grad, w1[:, 3 * dim :]).astype(BF16)
        packed = [mid[i, :, k * PAIR : (k + 1) * PAIR] for k in range(3 * pairs)]
        probs = [act[i, :, k * seq : (k + 1) * seq] for k in range(2 * pairs)]
        grads = [None] * (3 * pairs)
        for p in range(pairs):
            out_grad = mixed_grad[:, p * PAIR : (p + 1) * PAIR]
            prob_grad = dot(split_heads(packed[2 * pairs + p]), out_grad, NT)
            parts = []
            for k in range(2):
                value, grad_of = probs[2 * p + k].astype(F32), prob_grad[k * seq : (k + 1) * seq]
                inner = jnp.sum(value * grad_of, axis=0, keepdims=True)
                parts.append((value * (grad_of - inner)).astype(BF16))
            score_grad = jnp.concatenate(parts, axis=0)
            prob = jnp.concatenate(probs[2 * p : 2 * p + 2], axis=0)
            query_grad = dot(score_grad, split_heads(packed[pairs + p]), TN) * HEAD_DIM**-0.5
            key_grad = join_heads(dot(score_grad, packed[p])) * HEAD_DIM**-0.5
            grads[p] = query_grad.astype(BF16)
            grads[pairs + p] = key_grad.astype(BF16)
            grads[2 * pairs + p] = join_heads(dot(prob, out_grad)).astype(BF16)
        packed_grad = jnp.concatenate(grads, axis=1)
        mid[i, :, : 3 * dim] = packed_grad
        normed_grad = dot(packed_grad, w1t[: 3 * dim, :])
        grad_leave(i, grad, normed_grad)

    for load in small_loads:
        load.wait()

    def transpose(src, dst, low, high):
        for at in range(low, high, 2 * PAIR):
            dst[at : at + 2 * PAIR, :] = src[:, at : at + 2 * PAIR].T

    @pl.when(section == 0)
    def _():
        start_load.wait()

    @pl.when(section == last)
    def _():
        cot_load.wait()

    def run(forward, backward, lag, before_last, after_last):
        pl.semaphore_wait(barrier, peers)

        def step(i, carry):
            @pl.when(i == rows - 1)
            def _():
                before_last()

            @pl.when(i < rows)
            def _():
                forward(i)

            @pl.when(i == rows)
            def _():
                after_last()

            @pl.when(i >= lag)
            def _():
                backward(i - lag)

            return carry

        lax.fori_loop(0, rows + lag, step, 0)

    @pl.when(is_attention)
    def _():
        out_load.wait()
        transpose(w1, w1t, 3 * dim, ff)
        first_load.wait()

        def late():
            @pl.when(section == 0)
            def _():
                transpose(w1, w1t, 0, 3 * dim)

        @pl.when(section > 0)
        def _():
            transpose(w1, w1t, 0, 3 * dim)

        def relay():
            @pl.when(section == 0)
            def _():
                lax.fori_loop(0, RELAYED, pass_on, 0)

        lag = jnp.where(section == 0, rows, rows // 2)
        run(attention_forward, attention_backward, lag, late, relay)

        @pl.when(section == 0)
        def _():
            ref = w2.at[pl.ds(0, RELAYED * seq), :]
            pltpu.make_async_copy(ref, ref, relay_send).wait()


    @pl.when(jnp.logical_not(is_attention))
    def _():
        out_load.wait()
        first_load.wait()
        second_load.wait()
        transpose(w1, w1t, 0, ff)
        for at in range(0, ff, 2 * PAIR):
            w2t[:, at : at + 2 * PAIR] = w2[at : at + 2 * PAIR, :].T
        lag = jnp.where(section == last, 0, rows - 1)
        run(dense_forward, dense_backward, lag, lambda: None, lambda: None)

    def remote(src, dst, send, recv, to):
        return pltpu.make_async_remote_copy(
            src, dst, send, recv, device_id=to, device_id_type=MESH
        )

    small_mate = remote(
        small.at[0], small.at[1], small_sem.at[0], small_sem.at[1], (section, mate)
    )
    small_line = remote(
        small.at[0], small.at[2], small_sem.at[2], small_sem.at[3], (section, inner)
    )
    small_cross = remote(
        small.at[0], small.at[3], small_sem.at[2], small_sem.at[4], (section, inner)
    )
    small_back = remote(
        small.at[3], small.at[3], small_sem.at[5], small_sem.at[4], (section, outer)
    )


    tokens = rows * seq
    half = ff // 2
    steps = (half // CHUNK) * SUB
    tall, short = dim // SUB, CHUNK // SUB
    mine, theirs = core * half, (1 - core) * half

    def own(k, v):
        if k == 0:
            return w1.at[
                pl.ds(pl.multiple_of((v % SUB) * tall, 16), tall),
                pl.ds(pl.multiple_of(mine + (v // SUB) * CHUNK, CHUNK), CHUNK),
            ]
        return w2.at[pl.ds(pl.multiple_of(mine + v * short, 16), short), :]

    def whole(k, v):
        if k == 0:
            return first_o.at[
                pl.ds(pl.multiple_of((v % SUB) * tall, 16), tall),
                pl.ds(pl.multiple_of(mine + (v // SUB) * CHUNK, CHUNK), CHUNK),
            ]
        return second_o.at[pl.ds(pl.multiple_of(mine + v * short, 16), short), :]

    def slot(ref, k, v):
        if k == 0:
            return ref.at[
                pl.ds(pl.multiple_of((v % SUB) * tall, 16), tall),
                pl.ds(pl.multiple_of((v // SUB) * CHUNK, CHUNK), CHUNK),
            ]
        return ref.at[pl.ds(pl.multiple_of(v * short, 16), short), :]

    line = (sum_b1, sum_b2)

    def part_copy(k, c):
        at = pl.ds(pl.multiple_of(theirs + c * CHUNK, CHUNK), CHUNK)
        to = pl.ds(pl.multiple_of(c * CHUNK, CHUNK), CHUNK)
        src, dst = (w1.at[:, at], sum_a1.at[:, to]) if k == 0 else (w2.at[at, :], sum_a2.at[to, :])
        return remote(src, dst, part_send.at[k], part_recv.at[k, c], (section, mate))

    ring = line_recv.shape[0]

    def line_copy(k, v, p):
        return remote(
            own(k, v), slot(line[k], k, v), line_send.at[k], line_recv.at[p % ring], (section, inner)
        )

    def cross_copy(k, v, p):
        return remote(
            own(k, v), whole(k, v), line_send.at[k], whole_recv.at[p % ring], (section, inner)
        )

    def back_copy(k, v, p):
        ref = whole(k, v)
        return remote(ref, ref, back_send.at[k], whole_recv.at[p % ring], (section, outer))

    shift = jnp.where(section >= 2, NEAR[0] + FAR, 0)

    def given_copy(v):
        to = jnp.where(v < near, helper, nxt)
        w = jnp.where(v < near, v + shift, v)
        return remote(own(1, v), slot(sum_a2, 1, w), line_send.at[1], hand_recv.at[w], (to, dp))

    def return_copy(w, to, v):
        return remote(whole(1, w), whole(1, v), mate_send.at[1], hand_recv.at[v], (to, dp))

    def mate_copy(k, v):
        ref = whole(k, v)
        return remote(ref, ref, mate_send.at[k], mate_recv.at[k], (section, mate))

    def token_sum(matrix):
        return jnp.sum(fold(matrix.astype(F32)), axis=0, keepdims=True)

    def small_start():
        lane = lax.broadcasted_iota(jnp.int32, (1, dim), 1)
        counts = jnp.zeros((1, dim), F32)
        for k, x in enumerate((sq_acc[0], sq_acc[1], val[...].astype(F32))):
            amount = jnp.sum(jnp.sum(x, axis=0, keepdims=True), axis=1, keepdims=True)
            counts = jnp.where(lane == k, amount, counts)
        small[0, 0:1, :] = jnp.sum(norm_acc[0], axis=0, keepdims=True)
        small[0, 1:2, :] = jnp.sum(norm_acc[1], axis=0, keepdims=True)
        small[0, 2 + ff // dim : 3 + ff // dim, :] = token_sum(gin[...].reshape(tokens, dim))
        small[0, 3 + ff // dim : 4 + ff // dim, :] = counts
        small_mate.start()

    def bias_sum(matrix, col):
        third = col // dim
        row = jnp.where(is_attention, third // 2, third) + 2
        at = pl.ds(pl.multiple_of(col - third * dim, CHUNK), CHUNK)

        @pl.when(jnp.logical_not(is_attention) | (third == 0) | (third == 2))
        def _():
            small[0, pl.ds(row, 1), at] = token_sum(matrix)

    def compute(k, c, is_mine):
        base = jnp.where(is_mine, mine, theirs) + c * CHUNK
        at = pl.ds(pl.multiple_of(base, CHUNK), CHUNK)
        if k == 0:
            side = is_attention & (base >= 3 * dim)
            left = pair[side.astype(jnp.int32)].reshape(tokens, dim)
            right = mid[:, :, at].reshape(tokens, CHUNK)
            w1[:, at] = dot(left, right, TN).astype(BF16)
        else:
            left = act[:, :, at].reshape(tokens, CHUNK)
            w2[at, :] = dot(left, gin[...].reshape(tokens, dim), TN).astype(BF16)

        @pl.when(jnp.logical_not(is_mine))
        def _():
            part_copy(k, c).start()

        if k == 0:
            bias_sum(mid[:, :, at].reshape(tokens, CHUNK), base)

    def clear(base):
        at = pl.ds(pl.multiple_of(base, CHUNK), half)
        second_o[at, :] = jnp.zeros((half, dim), BF16)

    def combine(dst, *refs):
        value = refs[0][...].astype(F32)
        for ref in refs[1:]:
            value += ref[...].astype(F32)
        dst[...] = value.astype(BF16)

    def send_in(k, v, p, *refs):
        @pl.when(has_outer)
        def _():
            line_copy(k, v, p).wait_recv()
            combine(own(k, v), *refs, slot(line[k], k, v))

        @pl.when(jnp.logical_not(has_outer))
        def _():
            combine(own(k, v), *refs)

        @pl.when(is_middle)
        def _():
            cross_copy(k, v, p).start()

        @pl.when(jnp.logical_not(is_middle))
        def _():
            line_copy(k, v, p).start()

    def part_wait(k, v):
        @pl.when(v % SUB == 0)
        def _():
            part_copy(k, v // SUB).wait_recv()

    def send_first(v, p):
        part_wait(0, v)
        send_in(0, v, p, own(0, v), slot(sum_a1, 0, v))

    def send_second(v, p):
        part_wait(1, v)
        send_in(1, v, p, own(1, v), slot(sum_a2, 1, v))

    def hand_over(v):
        part_wait(1, v)
        combine(own(1, v), own(1, v), slot(sum_a2, 1, v))
        given_copy(v).start()

    def send_given(w, to, v, p):
        return_copy(w, to, w).wait_recv()
        send_in(1, w, p, slot(sum_a2, 1, w))

    def settle(k, v, p):
        cross_copy(k, v, p).wait_recv()

        @pl.when(is_middle)
        def _():
            combine(whole(k, v), own(k, v), whole(k, v))

        @pl.when(has_outer)
        def _():
            back_copy(k, v, p).start()

    def settle_first(v, p):
        settle(0, v, p)
        mate_copy(0, v).start()

    def settle_second(v, p):
        settle(1, v, p)
        mate_copy(1, v).start()

    def settle_handed(v):
        return_copy(v, helper, v).wait_recv()
        mate_copy(1, v).start()

    def settle_given(w, to, v, p):
        settle(1, w, p)
        return_copy(w, to, v).start()

    def small_in():
        small_mate.wait_recv()
        small_mate.wait_send()
        small[0] += small[1]

        @pl.when(has_outer)
        def _():
            small_line.wait_recv()
            small[0] += small[2]

        @pl.when(is_middle)
        def _():
            small_cross.start()

        @pl.when(jnp.logical_not(is_middle))
        def _():
            small_line.start()

    def small_settle():
        small_cross.wait_recv()

        @pl.when(is_middle)
        def _():
            small[3] += small[0]

        @pl.when(has_outer)
        def _():
            small_back.start()

        small_o[...] = small[3]

    gap = jnp.where(on_left, chips // 2 - 1 - chip, chip - chips // 2)
    lag = 4 + 14 * gap
    blocks = steps // SUB
    early = (blocks * 2 // 3) * SUB
    is_dense = jnp.logical_not(is_attention)
    length = jnp.where(is_attention, steps + near + far, 2 * steps - handed)

    ahead = jnp.where(is_middle, SUB, 0)

    @pl.when(is_dense)
    def _():
        compute(0, 0, False)
        compute(0, 0, True)

    def in_line(u, first_part, second_part, given_part):
        @pl.when((u >= 0) & (u < length) & is_dense)
        def _():
            @pl.when(u < steps)
            def _():
                first_part(u, u)

            @pl.when(u >= steps)
            def _():
                second_part(u - steps + handed, u)

        @pl.when((u >= 0) & (u < length) & is_attention)
        def _():
            @pl.when(u < near)
            def _():
                given_part(u + shift, helper, u, u)

            @pl.when((u >= near) & (u < near + early))
            def _():
                first_part(u - near, u)

            @pl.when((u >= near + early) & (u < near + early + far))
            def _():
                v = NEAR[0] + u - near - early
                given_part(v, prv, v, u)

            @pl.when(u >= near + early + far)
            def _():
                first_part(u - near - far, u)

    def step(u, carry):
        in_line(u - ahead, send_first, send_second, send_given)

        @pl.when((u % SUB >= SUB // 2) & is_dense)
        def _():
            for k in range(2):
                v = u // SUB * SUB + 2 * (u % SUB - SUB // 2) + k

                @pl.when(v < handed)
                def _(v=v):
                    hand_over(v)

        t = u - ahead - lag

        @pl.when(t == length - 1)
        def _():
            small_settle()

        in_line(t, settle_first, settle_second, settle_given)

        @pl.when((t >= length) & (t < length + handed) & is_dense)
        def _():
            settle_handed(t - length)

        c, q = u // SUB, u % SUB // QUARTER
        on_time = (u % QUARTER == 0) & (c < blocks)

        @pl.when(on_time & (q < 2) & is_dense)
        def _():
            compute(1, c, q == 1)

        @pl.when(on_time & jnp.where(is_attention, q < 2, (q >= 2) & (c + 1 < blocks)))
        def _():
            compute(0, jnp.where(is_attention, c, c + 1), q % 2 == 1)

        @pl.when(u == steps - 2)
        def _():
            small_start()

        @pl.when((u == steps) & is_attention)
        def _():
            clear(theirs)

        @pl.when(u - ahead == steps + jnp.where((chip > 0) & (chip < chips - 1), SUB, 0))
        def _():
            small_in()

        return carry

    tail = jnp.where(is_attention, 0, handed)
    lax.fori_loop(0, length + ahead + lag + tail, step, 0)


    @pl.when(section < last)
    def _():
        remote(hout, hin, hs_sem, hr_sem.at[0], (nxt, dp)).wait_send()

    @pl.when(section > 0)
    def _():
        remote(gout, gin, gs_sem, gr_sem.at[0], (prv, dp)).wait_send()

    def taken(k, sem, count):
        if k == 0:
            ref = w1.at[:, pl.ds(0, (count // SUB) * CHUNK)]
        else:
            ref = w2.at[pl.ds(0, count * short), :]
        pltpu.make_async_copy(ref, ref, sem.at[k]).wait()

    taken(0, part_send, steps)
    taken(0, line_send, steps)
    taken(0, mate_send, steps)
    taken(0, mate_recv, steps)

    @pl.when(has_outer)
    def _():
        taken(0, back_send, steps)
        small_back.wait_send()

    @pl.when(jnp.logical_not(is_attention))
    def _():
        taken(1, part_send, steps)
        taken(1, line_send, steps)
        taken(1, mate_send, steps)
        taken(1, mate_recv, steps)

    for which, count in enumerate((NEAR[0], NEAR[0] + FAR, NEAR[1] + FAR, NEAR[1])):
        if which % 2:

            @pl.when((section == which) & has_outer)
            def _(count=count):
                taken(1, back_send, steps - count)

        else:

            @pl.when(section == which)
            def _(count=count):
                taken(1, line_send, count)
                taken(1, mate_send, count)

            @pl.when((section == which) & has_outer)
            def _(count=count):
                taken(1, back_send, count)

    small_line.wait_send()

    @pl.when(is_attention)
    def _():
        clear(mine)


def finish_kernel(
    res, sg, first, second, small,
    res_o, sg_o, first_o, second_o, norm_o, bias_o, rms_o,
    sg_wide, first_wide, second_wide, norm, bias, rms, sem, first_sem, second_sem,
):
    dim = sg.shape[2]
    ff = first.shape[1]
    copies = []

    def write(src, dst, sem):
        copies.append(pltpu.make_async_copy(src, dst, sem))
        copies[-1].start()

    write(res, res_o.at[0], sem.at[0])
    norm[0] = small[0:2, :]
    write(norm, norm_o, sem.at[1])
    count = ff // dim + 1
    for k in range(count):
        bias[0:1, k * dim : (k + 1) * dim] = small[2 + k : 3 + k, :]
    write(bias, bias_o, sem.at[2])
    stat = small[2 + count : 3 + count, :]
    rms[...] = jnp.sqrt(stat[:, 0:2] / (stat[:, 2:3] * dim))
    write(rms, rms_o, sem.at[3])
    sg_wide[...] = sg[...].astype(F32)
    write(sg_wide, sg_o.at[0], sem.at[4])
    for src, wide, dst, sems in (
        (first, first_wide, first_o, first_sem), (second, second_wide, second_o, second_sem),
    ):
        count = src.shape[0] // WRITES
        for k in range(WRITES):
            at = pl.ds(k * count, count)
            wide[at, :] = src[at, :].astype(F32)
            write(wide.at[at], dst.at[0, at], sems.at[k])
    for copy in copies:
        copy.wait()


def run_sublayers(start, cot, first, second, norm, bias, seg, val):
    rows, seq, dim = start.shape
    ff = first.shape[2]
    half = ff // 2
    steps = (half // CHUNK) * SUB
    block = (rows, seq, dim)
    wide = (rows, seq, ff)
    small = (4 + ff // dim, dim)
    ring = RING if lax.axis_size("dp") <= 8 else 2 * steps
    any_space = pl.BlockSpec(memory_space=pl.ANY)
    vmem = pl.BlockSpec(memory_space=pltpu.VMEM)
    out = jax.ShapeDtypeStruct
    dma = pltpu.SemaphoreType.DMA
    return pl.pallas_call(
        sublayer_kernel,
        out_shape=(
            pltpu.VMEM(block, BF16), pltpu.VMEM(block, BF16),
            pltpu.VMEM((dim, ff), BF16), pltpu.VMEM((ff, dim), BF16), pltpu.VMEM(small, F32),
        ),
        in_specs=[any_space] * 8,
        out_specs=(vmem,) * 5,
        scratch_shapes=[
            pltpu.VMEM((dim, ff), BF16), pltpu.VMEM((ff, dim), BF16),
            pltpu.VMEM((ff, dim), BF16), pltpu.VMEM((dim, ff), BF16),
            pltpu.VMEM(block, BF16), pltpu.VMEM((2, *block), BF16),
            pltpu.VMEM(wide, BF16), pltpu.VMEM(wide, BF16),
            pltpu.VMEM(norm.shape, F32), pltpu.VMEM(bias.shape, F32),
            pltpu.VMEM(seg.shape, jnp.int32), pltpu.VMEM(val.shape, jnp.int32),
            pltpu.VMEM((2, 8, dim), F32), pltpu.VMEM((2, 8, dim), F32),
            pltpu.VMEM((4, *small), F32),
            pltpu.VMEM((dim, half), BF16), pltpu.VMEM((dim, half), BF16),
            pltpu.VMEM((half, dim), BF16), pltpu.VMEM((half, dim), BF16),
            dma((10,)), dma, dma((rows,)), dma, dma((rows,)), dma, dma((RELAYED,)), dma((6,)),
            dma((2,)), dma((2, steps // SUB)), dma((sum(NEAR) + FAR,)),
            dma((2,)), dma((ring,)), dma((ring,)), dma((2,)),
            dma((2,)), dma((2,)),
        ],
        compiler_params=pltpu.CompilerParams(
            collective_id=0, has_side_effects=True, vmem_limit_bytes=SUBLAYER_VMEM
        ),
        name="sublayer",
    )(start, cot, first, second, norm, bias, seg, val)


def run_finish(res, sg, first, second, small):
    rows, seq, dim = res.shape
    ff = first.shape[1]
    any_space = pl.BlockSpec(memory_space=pl.ANY)
    vmem = pl.BlockSpec(memory_space=pltpu.VMEM)
    out = jax.ShapeDtypeStruct
    dma = pltpu.SemaphoreType.DMA
    return pl.pallas_call(
        finish_kernel,
        out_shape=(
            out((1, rows, seq, dim), BF16), out((1, rows, seq, dim), F32),
            out((1, dim, ff), F32), out((1, ff, dim), F32),
            out((1, 2, dim), F32), out((1, ff + dim), F32), out((1, 2), F32),
        ),
        in_specs=[vmem] * 5,
        out_specs=(any_space,) * 7,
        scratch_shapes=[
            pltpu.VMEM((rows, seq, dim), F32),
            pltpu.VMEM((dim, ff), F32), pltpu.VMEM((ff, dim), F32),
            pltpu.VMEM((1, 2, dim), F32), pltpu.VMEM((1, ff + dim), F32), pltpu.VMEM((1, 2), F32),
            dma((5,)), dma((WRITES,)), dma((WRITES,)),
        ],
        compiler_params=pltpu.CompilerParams(vmem_limit_bytes=FINISH_VMEM),
        name="finish",
    )(res, sg, first, second, small)


def local(start, cot, first, second, norm, bias, seg, val):
    return run_finish(*run_sublayers(start, cot, first, second, norm, bias, seg, val))


def solution(mesh):
    in_specs = (
        P("dp", None, None),
        P("dp", None, None),
        P("section", None, None),
        P("section", None, None),
        P("section", None, None),
        P("section", None),
        P("dp", None),
        P("dp", None),
    )
    out_specs = (
        P("section", "dp", None, None),
        P("section", "dp", None, None),
        P("section", None, None),
        P("section", None, None),
        P("section", None, None),
        P("section", None),
        P("section", None),
    )
    return jax.shard_map(local, mesh=mesh, in_specs=in_specs, out_specs=out_specs, check_vma=False)
```

```python
import jax
import jax.numpy as jnp
from jax import lax
from jax.experimental import pallas as pl
from jax.experimental.pallas import tpu as pltpu
from jax.sharding import PartitionSpec as P

HEAD_DIM = 64
EPS = 1e-05
NEG_FILL = -1e30
MESH = pl.DeviceIdType.MESH
BF16 = jnp.bfloat16
F32 = jnp.float32
NN = (((1,), (0,)), ((), ()))
NT = (((1,), (1,)), ((), ()))
TN = (((0,), (0,)), ((), ()))
PAIR = 2 * HEAD_DIM
CHUNK = 256
SUB = 8
QUARTER = SUB // 4
NEAR = (11, 12)
FAR = 19
RELAYED = 4
PARTS = 4
RING = 32
LOADS = 4
WRITES = 12
SUBLAYER_VMEM = 50 * 2**20
FINISH_VMEM = 40 * 2**20
GELU_C = 0.7978845608028654
GELU_K = 0.044715


def dot(a, b, dims=NN):
    return lax.dot_general(a, b, dims, preferred_element_type=F32)


def gelu_and_slope(x):
    square = x * x
    t = jnp.tanh(GELU_C * (x + GELU_K * (square * x)))
    half = 0.5 * (1.0 + t)
    slope = half + (0.5 * GELU_C) * x * (1.0 - t * t) * (1.0 + (3.0 * GELU_K) * square)
    return x * half, slope


def fold(x):
    return x.reshape(x.shape[0] // 8, 8, x.shape[1]).sum(axis=0)


def normalize(hidden):
    mean = jnp.mean(hidden, axis=-1, keepdims=True)
    centered = hidden - mean
    variance = jnp.mean(centered * centered, axis=-1, keepdims=True)
    inv_std = lax.rsqrt(variance + EPS)
    return centered * inv_std, inv_std


def sublayer_kernel(
    start, cot, first, second, norm_in, bias_in, seg_in, val_in,
    hout, gout, first_o, second_o, small_o,
    w1, w2, w1t, w2t, hin, pair, act, mid,
    norm, bias, seg, val, sq_acc, norm_acc, small,
    sum_a1, sum_b1, sum_a2, sum_b2,
    load_sem, hs_sem, hr_sem, gs_sem, gr_sem, relay_send, relay_recv, small_sem,
    part_send, part_recv, hand_recv, line_send, line_recv, whole_recv, back_send,
    mate_send, mate_recv,
):
    nrm, gin = pair.at[0], pair.at[1]
    section = lax.axis_index("section")
    dp = lax.axis_index("dp")
    last = lax.axis_size("section") - 1
    rows, seq, dim = start.shape
    ff = first.shape[2]
    pairs = dim // PAIR
    is_attention = section % 2 == 0
    nxt = jnp.minimum(section + 1, last)
    prv = jnp.maximum(section - 1, 0)

    wide, out_cols = 3 * dim, pl.ds(3 * dim, ff - 3 * dim)
    first_load = pltpu.make_async_copy(
        first.at[0, :, pl.ds(0, wide)], w1.at[:, pl.ds(0, wide)], load_sem.at[0]
    )
    out_load = pltpu.make_async_copy(first.at[0, :, out_cols], w1.at[:, out_cols], load_sem.at[8])
    second_load = pltpu.make_async_copy(second.at[0], w2, load_sem.at[1])
    start_load = pltpu.make_async_copy(start.at[0], hin.at[0], load_sem.at[2])
    others = pl.ds(1, rows - 1)
    rest_load = pltpu.make_async_copy(start.at[others], hin.at[others], load_sem.at[9])
    cot_load = pltpu.make_async_copy(cot, gin, load_sem.at[3])
    small_loads = [
        pltpu.make_async_copy(src, dst, load_sem.at[4 + k])
        for k, (src, dst) in enumerate(
            ((norm_in, norm), (bias_in, bias), (seg_in, seg), (val_in, val))
        )
    ]

    def split_load(src, dst, cols, k):
        count = dst.shape[0] // LOADS
        for at in range(0, dst.shape[0], count):
            pltpu.make_async_copy(
                src.at[0, pl.ds(at, count), cols], dst.at[pl.ds(at, count), cols], load_sem.at[k]
            ).start()

    for load in small_loads:
        load.start()

    @pl.when(section == 0)
    def _():
        start_load.start()

    out_load.start()
    split_load(first, w1, pl.ds(0, wide), 0)

    @pl.when(section == 0)
    def _():
        rest_load.start()

    @pl.when(jnp.logical_not(is_attention))
    def _():
        split_load(second, w2, pl.ds(0, dim), 1)

    @pl.when(section == last)
    def _():
        cot_load.start()

    chips = lax.axis_size("dp") // 2
    chip, core = dp // 2, dp % 2
    mate = dp + 1 - 2 * core
    on_left = chip < chips // 2
    is_middle = (chip == chips // 2 - 1) | (chip == chips // 2)
    has_outer = (chip > 0) & (chip < chips - 1)
    inner = jnp.where(on_left, dp + 2, dp - 2)
    outer = jnp.clip(jnp.where(on_left, dp - 2, dp + 2), 0, 2 * chips - 1)
    helper = section + 1 - 2 * (section % 2)
    near = jnp.where(section < 2, NEAR[0], NEAR[1])
    far = jnp.where((section == 1) | (section == 2), FAR, 0)
    handed = near + far

    barrier = pltpu.get_barrier_semaphore()

    def greet(to_section, to_dp):
        pl.semaphore_signal(
            barrier, inc=1, device_id=(to_section, to_dp), device_id_type=MESH
        )

    greet(section, mate)
    greet(section, inner)

    @pl.when(has_outer)
    def _():
        greet(section, outer)

    @pl.when(section > 0)
    def _():
        greet(prv, dp)

    @pl.when(section < last)
    def _():
        greet(nxt, dp)

    @pl.when((section == 0) | (section == 2))
    def _():
        greet(2 - section, dp)

    peers = 3 + has_outer.astype(jnp.int32)
    peers += ((section == 0) | (section == 2)).astype(jnp.int32)
    peers += ((section > 0) & (section < last)).astype(jnp.int32)

    for ref in (sq_acc, norm_acc, small):
        ref[...] = jnp.zeros_like(ref)

    def h_copy(i):
        return pltpu.make_async_remote_copy(
            hout.at[i], hin.at[i], hs_sem, hr_sem.at[i],
            device_id=(nxt, dp), device_id_type=MESH,
        )

    def g_copy(i):
        return pltpu.make_async_remote_copy(
            gout.at[i], gin.at[i], gs_sem, gr_sem.at[i],
            device_id=(prv, dp), device_id_type=MESH,
        )

    part = seq // PARTS

    def via(i, k):
        return w2.at[pl.ds(pl.multiple_of(i * seq + k * part, part), part), :]

    def part_of(ref, i, k):
        return ref.at[i, pl.ds(pl.multiple_of(k * part, part), part)]

    def relay_in(i, k):
        return pltpu.make_async_remote_copy(
            part_of(gout, i, k), via(i, k), gs_sem, relay_recv.at[i, k],
            device_id=(0, dp), device_id_type=MESH,
        )

    def relay_out(i, k):
        return pltpu.make_async_remote_copy(
            via(i, k), part_of(gin, i, k), relay_send, gr_sem.at[i],
            device_id=(nxt, dp), device_id_type=MESH,
        )

    def pass_on(n, carry):
        relay_in(n // PARTS, n % PARTS).wait_recv()
        relay_out(n // PARTS, n % PARTS).start()
        return carry

    eye = lax.broadcasted_iota(jnp.int32, (seq, seq), 0) == lax.broadcasted_iota(
        jnp.int32, (seq, seq), 1
    )

    def column(row):
        return jnp.sum(jnp.where(eye, row, 0.0), axis=1, keepdims=True)

    def valid_row(i):
        return val[pl.ds(i, 1), :].astype(F32)

    def entry(i):
        @pl.when(section > 0)
        def _():
            h_copy(i).wait_recv()

        hidden = hin[i].astype(F32)
        normal, _ = normalize(hidden)
        low = (normal * norm[0, 0:1, :] + norm[0, 1:2, :]).astype(BF16)
        nrm[i] = low
        return hidden, low

    def leave(i, hidden, branch):
        low = (hidden + branch).astype(BF16)
        hout[i] = low

        @pl.when(section < last)
        def _():
            h_copy(i).start()

        weight = column(valid_row(i))
        value = low.astype(F32)
        sq_acc[0] += fold(value * value * weight)
        sq_acc[1] += fold(branch * branch * weight)

    def grad_entry(i):
        @pl.when(section < last)
        def _():
            g_copy(i).wait_recv()

        @pl.when(section == last)
        def _():
            gin[i] = jnp.where(column(valid_row(i)) > 0, gin[i], jnp.zeros((seq, dim), BF16))

        return gin[i]

    def grad_leave(i, grad, normed_grad):
        grad_value = grad.astype(F32)
        normal, inv_std = normalize(hin[i].astype(F32))
        scaled = normed_grad * norm[0, 0:1, :]
        mean_one = jnp.mean(scaled, axis=-1, keepdims=True)
        mean_two = jnp.mean(scaled * normal, axis=-1, keepdims=True)
        low = (grad_value + inv_std * (scaled - mean_one - normal * mean_two)).astype(BF16)
        gout[i] = low

        @pl.when((section == 2) & (i < RELAYED))
        def _():
            for k in range(PARTS):
                relay_in(i, k).start()

        @pl.when((section > 0) & ((section != 2) | (i >= RELAYED)))
        def _():
            g_copy(i).start()

        norm_acc[0] += fold(normed_grad * normal)
        norm_acc[1] += fold(normed_grad)


    def dense_forward(i):
        hidden, low = entry(i)
        value, slope = gelu_and_slope(dot(low, w1[...]) + bias[0:1, :ff])
        value = value.astype(BF16)
        act[i] = value
        mid[i] = slope.astype(BF16)
        leave(i, hidden, dot(value, w2[...]) + bias[0:1, ff:])

    def dense_backward(i):
        grad = grad_entry(i)
        low = (dot(grad, w2t[...]) * mid[i].astype(F32)).astype(BF16)
        mid[i] = low
        grad_leave(i, grad, dot(low, w1t[...]))


    lower = lax.broadcasted_iota(jnp.int32, (seq, PAIR), 1) < HEAD_DIM

    def split_heads(x):
        zero = jnp.zeros_like(x)
        return jnp.concatenate([jnp.where(lower, x, zero), jnp.where(lower, zero, x)], axis=0)

    def join_heads(x):
        return jnp.where(lower, x[:seq], x[seq:])

    def attention_forward(i):
        @pl.when((section == 0) & (i == 1))
        def _():
            rest_load.wait()

        hidden, low = entry(i)
        projected = dot(low, w1[:, : 3 * dim])
        mid[i, :, :dim] = (projected[:, :dim] + bias[0:1, :dim]).astype(BF16)
        mid[i, :, dim : 2 * dim] = projected[:, dim : 2 * dim].astype(BF16)
        mid[i, :, 2 * dim : 3 * dim] = (
            projected[:, 2 * dim :] + bias[0:1, dim : 2 * dim]
        ).astype(BF16)
        seg_row = seg[pl.ds(i, 1), :].astype(F32)
        allowed = (column(seg_row) == seg_row) & ((column(valid_row(i)) > 0) | eye)
        packed = [mid[i, :, k * PAIR : (k + 1) * PAIR] for k in range(3 * pairs)]
        scores = [
            dot(split_heads(packed[pairs + p]), packed[p], NT) * HEAD_DIM**-0.5
            for p in range(pairs)
        ]
        mixed = []
        for p in range(pairs):
            probs = []
            for half in (scores[p][:seq], scores[p][seq:]):
                half = jnp.where(allowed, half, NEG_FILL)
                weight = jnp.exp(half - jnp.max(half, axis=0, keepdims=True))
                probs.append((weight / jnp.sum(weight, axis=0, keepdims=True)).astype(BF16))
                act[i, :, (2 * p + len(probs) - 1) * seq : (2 * p + len(probs)) * seq] = probs[-1]
            prob = jnp.concatenate(probs, axis=0)
            mixed.append(dot(prob, split_heads(packed[2 * pairs + p]), TN).astype(BF16))
        mixed = jnp.concatenate(mixed, axis=1)
        mid[i, :, 3 * dim :] = mixed
        branch = dot(mixed, w1t[3 * dim :, :]) + bias[0:1, ff:]
        leave(i, hidden, branch)

    def attention_backward(i):
        grad = grad_entry(i)
        mixed_grad = dot(grad, w1[:, 3 * dim :]).astype(BF16)
        packed = [mid[i, :, k * PAIR : (k + 1) * PAIR] for k in range(3 * pairs)]
        probs = [act[i, :, k * seq : (k + 1) * seq] for k in range(2 * pairs)]
        grads = [None] * (3 * pairs)
        for p in range(pairs):
            out_grad = mixed_grad[:, p * PAIR : (p + 1) * PAIR]
            prob_grad = dot(split_heads(packed[2 * pairs + p]), out_grad, NT)
            parts = []
            for k in range(2):
                value, grad_of = probs[2 * p + k].astype(F32), prob_grad[k * seq : (k + 1) * seq]
                inner = jnp.sum(value * grad_of, axis=0, keepdims=True)
                parts.append((value * (grad_of - inner)).astype(BF16))
            score_grad = jnp.concatenate(parts, axis=0)
            prob = jnp.concatenate(probs[2 * p : 2 * p + 2], axis=0)
            query_grad = dot(score_grad, split_heads(packed[pairs + p]), TN) * HEAD_DIM**-0.5
            key_grad = join_heads(dot(score_grad, packed[p])) * HEAD_DIM**-0.5
            grads[p] = query_grad.astype(BF16)
            grads[pairs + p] = key_grad.astype(BF16)
            grads[2 * pairs + p] = join_heads(dot(prob, out_grad)).astype(BF16)
        packed_grad = jnp.concatenate(grads, axis=1)
        mid[i, :, : 3 * dim] = packed_grad
        normed_grad = dot(packed_grad, w1t[: 3 * dim, :])
        grad_leave(i, grad, normed_grad)

    for load in small_loads:
        load.wait()

    def transpose(src, dst, low, high):
        for at in range(low, high, 2 * PAIR):
            dst[at : at + 2 * PAIR, :] = src[:, at : at + 2 * PAIR].T

    @pl.when(section == 0)
    def _():
        start_load.wait()

    @pl.when(section == last)
    def _():
        cot_load.wait()

    def run(forward, backward, lag, before_last, after_last):
        pl.semaphore_wait(barrier, peers)

        def step(i, carry):
            @pl.when(i == rows - 1)
            def _():
                before_last()

            @pl.when(i < rows)
            def _():
                forward(i)

            @pl.when(i == rows)
            def _():
                after_last()

            @pl.when(i >= lag)
            def _():
                backward(i - lag)

            return carry

        lax.fori_loop(0, rows + lag, step, 0)

    @pl.when(is_attention)
    def _():
        out_load.wait()
        transpose(w1, w1t, 3 * dim, ff)
        first_load.wait()

        def late():
            @pl.when(section == 0)
            def _():
                transpose(w1, w1t, 0, 3 * dim)

        @pl.when(section > 0)
        def _():
            transpose(w1, w1t, 0, 3 * dim)

        def relay():
            @pl.when(section == 0)
            def _():
                lax.fori_loop(0, PARTS * RELAYED, pass_on, 0)

        lag = jnp.where(section == 0, rows, rows // 2)
        run(attention_forward, attention_backward, lag, late, relay)

        @pl.when(section == 0)
        def _():
            ref = w2.at[pl.ds(0, RELAYED * seq), :]
            pltpu.make_async_copy(ref, ref, relay_send).wait()


    @pl.when(jnp.logical_not(is_attention))
    def _():
        out_load.wait()
        first_load.wait()
        second_load.wait()
        transpose(w1, w1t, 0, ff)
        for at in range(0, ff, 2 * PAIR):
            w2t[:, at : at + 2 * PAIR] = w2[at : at + 2 * PAIR, :].T
        lag = jnp.where(section == last, 0, rows - 1)
        run(dense_forward, dense_backward, lag, lambda: None, lambda: None)

    def remote(src, dst, send, recv, to):
        return pltpu.make_async_remote_copy(
            src, dst, send, recv, device_id=to, device_id_type=MESH
        )

    small_mate = remote(
        small.at[0], small.at[1], small_sem.at[0], small_sem.at[1], (section, mate)
    )
    small_line = remote(
        small.at[0], small.at[2], small_sem.at[2], small_sem.at[3], (section, inner)
    )
    small_cross = remote(
        small.at[0], small.at[3], small_sem.at[2], small_sem.at[4], (section, inner)
    )
    small_back = remote(
        small.at[3], small.at[3], small_sem.at[5], small_sem.at[4], (section, outer)
    )


    tokens = rows * seq
    half = ff // 2
    steps = (half // CHUNK) * SUB
    tall, short = dim // SUB, CHUNK // SUB
    mine, theirs = core * half, (1 - core) * half

    def own(k, v):
        if k == 0:
            return w1.at[
                pl.ds(pl.multiple_of((v % SUB) * tall, 16), tall),
                pl.ds(pl.multiple_of(mine + (v // SUB) * CHUNK, CHUNK), CHUNK),
            ]
        return w2.at[pl.ds(pl.multiple_of(mine + v * short, 16), short), :]

    def whole(k, v):
        if k == 0:
            return first_o.at[
                pl.ds(pl.multiple_of((v % SUB) * tall, 16), tall),
                pl.ds(pl.multiple_of(mine + (v // SUB) * CHUNK, CHUNK), CHUNK),
            ]
        return second_o.at[pl.ds(pl.multiple_of(mine + v * short, 16), short), :]

    def slot(ref, k, v):
        if k == 0:
            return ref.at[
                pl.ds(pl.multiple_of((v % SUB) * tall, 16), tall),
                pl.ds(pl.multiple_of((v // SUB) * CHUNK, CHUNK), CHUNK),
            ]
        return ref.at[pl.ds(pl.multiple_of(v * short, 16), short), :]

    line = (sum_b1, sum_b2)

    def part_copy(k, c):
        at = pl.ds(pl.multiple_of(theirs + c * CHUNK, CHUNK), CHUNK)
        to = pl.ds(pl.multiple_of(c * CHUNK, CHUNK), CHUNK)
        src, dst = (w1.at[:, at], sum_a1.at[:, to]) if k == 0 else (w2.at[at, :], sum_a2.at[to, :])
        return remote(src, dst, part_send.at[k], part_recv.at[k, c], (section, mate))

    ring = line_recv.shape[0]

    def line_copy(k, v, p):
        return remote(
            own(k, v), slot(line[k], k, v), line_send.at[k], line_recv.at[p % ring], (section, inner)
        )

    def cross_copy(k, v, p):
        return remote(
            own(k, v), whole(k, v), line_send.at[k], whole_recv.at[p % ring], (section, inner)
        )

    def back_copy(k, v, p):
        ref = whole(k, v)
        return remote(ref, ref, back_send.at[k], whole_recv.at[p % ring], (section, outer))

    shift = jnp.where(section >= 2, NEAR[0] + FAR, 0)

    def given_copy(v):
        to = jnp.where(v < near, helper, nxt)
        w = jnp.where(v < near, v + shift, v)
        return remote(own(1, v), slot(sum_a2, 1, w), line_send.at[1], hand_recv.at[w], (to, dp))

    def return_copy(w, to, v):
        return remote(whole(1, w), whole(1, v), mate_send.at[1], hand_recv.at[v], (to, dp))

    def mate_copy(k, v):
        ref = whole(k, v)
        return remote(ref, ref, mate_send.at[k], mate_recv.at[k], (section, mate))

    def token_sum(matrix):
        return jnp.sum(fold(matrix.astype(F32)), axis=0, keepdims=True)

    def small_start():
        lane = lax.broadcasted_iota(jnp.int32, (1, dim), 1)
        counts = jnp.zeros((1, dim), F32)
        for k, x in enumerate((sq_acc[0], sq_acc[1], val[...].astype(F32))):
            amount = jnp.sum(jnp.sum(x, axis=0, keepdims=True), axis=1, keepdims=True)
            counts = jnp.where(lane == k, amount, counts)
        small[0, 0:1, :] = jnp.sum(norm_acc[0], axis=0, keepdims=True)
        small[0, 1:2, :] = jnp.sum(norm_acc[1], axis=0, keepdims=True)
        small[0, 2 + ff // dim : 3 + ff // dim, :] = token_sum(gin[...].reshape(tokens, dim))
        small[0, 3 + ff // dim : 4 + ff // dim, :] = counts
        small_mate.start()

    def bias_sum(matrix, col):
        third = col // dim
        row = jnp.where(is_attention, third // 2, third) + 2
        at = pl.ds(pl.multiple_of(col - third * dim, CHUNK), CHUNK)

        @pl.when(jnp.logical_not(is_attention) | (third == 0) | (third == 2))
        def _():
            small[0, pl.ds(row, 1), at] = token_sum(matrix)

    def compute(k, c, is_mine):
        base = jnp.where(is_mine, mine, theirs) + c * CHUNK
        at = pl.ds(pl.multiple_of(base, CHUNK), CHUNK)
        if k == 0:
            side = is_attention & (base >= 3 * dim)
            left = pair[side.astype(jnp.int32)].reshape(tokens, dim)
            right = mid[:, :, at].reshape(tokens, CHUNK)
            w1[:, at] = dot(left, right, TN).astype(BF16)
        else:
            left = act[:, :, at].reshape(tokens, CHUNK)
            w2[at, :] = dot(left, gin[...].reshape(tokens, dim), TN).astype(BF16)

        @pl.when(jnp.logical_not(is_mine))
        def _():
            part_copy(k, c).start()

        if k == 0:
            bias_sum(mid[:, :, at].reshape(tokens, CHUNK), base)

    def clear(base):
        at = pl.ds(pl.multiple_of(base, CHUNK), half)
        second_o[at, :] = jnp.zeros((half, dim), BF16)

    def combine(dst, *refs):
        value = refs[0][...].astype(F32)
        for ref in refs[1:]:
            value += ref[...].astype(F32)
        dst[...] = value.astype(BF16)

    def send_in(k, v, p, *refs):
        @pl.when(has_outer)
        def _():
            line_copy(k, v, p).wait_recv()
            combine(own(k, v), *refs, slot(line[k], k, v))

        @pl.when(jnp.logical_not(has_outer))
        def _():
            combine(own(k, v), *refs)

        @pl.when(is_middle)
        def _():
            cross_copy(k, v, p).start()

        @pl.when(jnp.logical_not(is_middle))
        def _():
            line_copy(k, v, p).start()

    def part_wait(k, v):
        @pl.when(v % SUB == 0)
        def _():
            part_copy(k, v // SUB).wait_recv()

    def send_first(v, p):
        part_wait(0, v)
        send_in(0, v, p, own(0, v), slot(sum_a1, 0, v))

    def send_second(v, p):
        part_wait(1, v)
        send_in(1, v, p, own(1, v), slot(sum_a2, 1, v))

    def hand_over(v):
        part_wait(1, v)
        combine(own(1, v), own(1, v), slot(sum_a2, 1, v))
        given_copy(v).start()

    def send_given(w, to, v, p):
        return_copy(w, to, w).wait_recv()
        send_in(1, w, p, slot(sum_a2, 1, w))

    def settle(k, v, p):
        cross_copy(k, v, p).wait_recv()

        @pl.when(is_middle)
        def _():
            combine(whole(k, v), own(k, v), whole(k, v))

        @pl.when(has_outer)
        def _():
            back_copy(k, v, p).start()

    def settle_first(v, p):
        settle(0, v, p)
        mate_copy(0, v).start()

    def settle_second(v, p):
        settle(1, v, p)
        mate_copy(1, v).start()

    def settle_handed(v):
        return_copy(v, helper, v).wait_recv()
        mate_copy(1, v).start()

    def settle_given(w, to, v, p):
        settle(1, w, p)
        return_copy(w, to, v).start()

    def small_in():
        small_mate.wait_recv()
        small_mate.wait_send()
        small[0] += small[1]

        @pl.when(has_outer)
        def _():
            small_line.wait_recv()
            small[0] += small[2]

        @pl.when(is_middle)
        def _():
            small_cross.start()

        @pl.when(jnp.logical_not(is_middle))
        def _():
            small_line.start()

    def small_settle():
        small_cross.wait_recv()

        @pl.when(is_middle)
        def _():
            small[3] += small[0]

        @pl.when(has_outer)
        def _():
            small_back.start()

        small_o[...] = small[3]

    gap = jnp.where(on_left, chips // 2 - 1 - chip, chip - chips // 2)
    lag = 4 + 14 * gap
    blocks = steps // SUB
    early = (blocks * 2 // 3) * SUB
    is_dense = jnp.logical_not(is_attention)
    length = jnp.where(is_attention, steps + near + far, 2 * steps - handed)

    ahead = jnp.where(is_middle, SUB, 0)

    @pl.when(is_dense)
    def _():
        compute(0, 0, False)
        compute(0, 0, True)

    def in_line(u, first_part, second_part, given_part):
        @pl.when((u >= 0) & (u < length) & is_dense)
        def _():
            @pl.when(u < steps)
            def _():
                first_part(u, u)

            @pl.when(u >= steps)
            def _():
                second_part(u - steps + handed, u)

        @pl.when((u >= 0) & (u < length) & is_attention)
        def _():
            @pl.when(u < near)
            def _():
                given_part(u + shift, helper, u, u)

            @pl.when((u >= near) & (u < near + early))
            def _():
                first_part(u - near, u)

            @pl.when((u >= near + early) & (u < near + early + far))
            def _():
                v = NEAR[0] + u - near - early
                given_part(v, prv, v, u)

            @pl.when(u >= near + early + far)
            def _():
                first_part(u - near - far, u)

    def step(u, carry):
        in_line(u - ahead, send_first, send_second, send_given)

        @pl.when((u % SUB >= SUB // 2) & is_dense)
        def _():
            for k in range(2):
                v = u // SUB * SUB + 2 * (u % SUB - SUB // 2) + k

                @pl.when(v < handed)
                def _(v=v):
                    hand_over(v)

        t = u - ahead - lag

        @pl.when(t == length - 1)
        def _():
            small_settle()

        in_line(t, settle_first, settle_second, settle_given)

        @pl.when((t >= length) & (t < length + handed) & is_dense)
        def _():
            settle_handed(t - length)

        c, q = u // SUB, u % SUB // QUARTER
        on_time = (u % QUARTER == 0) & (c < blocks)

        @pl.when(on_time & (q < 2) & is_dense)
        def _():
            compute(1, c, q == 1)

        @pl.when(on_time & jnp.where(is_attention, q < 2, (q >= 2) & (c + 1 < blocks)))
        def _():
            compute(0, jnp.where(is_attention, c, c + 1), q % 2 == 1)

        @pl.when(u == steps - 2)
        def _():
            small_start()

        @pl.when((u == steps) & is_attention)
        def _():
            clear(theirs)

        @pl.when(u - ahead == steps + jnp.where((chip > 0) & (chip < chips - 1), SUB, 0))
        def _():
            small_in()

        return carry

    tail = jnp.where(is_attention, 0, handed)
    lax.fori_loop(0, length + ahead + lag + tail, step, 0)


    @pl.when(section < last)
    def _():
        remote(hout, hin, hs_sem, hr_sem.at[0], (nxt, dp)).wait_send()

    @pl.when(section > 0)
    def _():
        remote(gout, gin, gs_sem, gr_sem.at[0], (prv, dp)).wait_send()

    def taken(k, sem, count):
        if k == 0:
            ref = w1.at[:, pl.ds(0, (count // SUB) * CHUNK)]
        else:
            ref = w2.at[pl.ds(0, count * short), :]
        pltpu.make_async_copy(ref, ref, sem.at[k]).wait()

    taken(0, part_send, steps)
    taken(0, line_send, steps)
    taken(0, mate_send, steps)
    taken(0, mate_recv, steps)

    @pl.when(has_outer)
    def _():
        taken(0, back_send, steps)
        small_back.wait_send()

    @pl.when(jnp.logical_not(is_attention))
    def _():
        taken(1, part_send, steps)
        taken(1, line_send, steps)
        taken(1, mate_send, steps)
        taken(1, mate_recv, steps)

    for which, count in enumerate((NEAR[0], NEAR[0] + FAR, NEAR[1] + FAR, NEAR[1])):
        if which % 2:

            @pl.when((section == which) & has_outer)
            def _(count=count):
                taken(1, back_send, steps - count)

        else:

            @pl.when(section == which)
            def _(count=count):
                taken(1, line_send, count)
                taken(1, mate_send, count)

            @pl.when((section == which) & has_outer)
            def _(count=count):
                taken(1, back_send, count)

    small_line.wait_send()

    @pl.when(is_attention)
    def _():
        clear(mine)


def finish_kernel(
    res, sg, first, second, small,
    res_o, sg_o, first_o, second_o, norm_o, bias_o, rms_o,
    sg_wide, first_wide, second_wide, norm, bias, rms, sem, first_sem, second_sem,
):
    dim = sg.shape[2]
    ff = first.shape[1]
    copies = []

    def write(src, dst, sem):
        copies.append(pltpu.make_async_copy(src, dst, sem))
        copies[-1].start()

    write(res, res_o.at[0], sem.at[0])
    norm[0] = small[0:2, :]
    write(norm, norm_o, sem.at[1])
    count = ff // dim + 1
    for k in range(count):
        bias[0:1, k * dim : (k + 1) * dim] = small[2 + k : 3 + k, :]
    write(bias, bias_o, sem.at[2])
    stat = small[2 + count : 3 + count, :]
    rms[...] = jnp.sqrt(stat[:, 0:2] / (stat[:, 2:3] * dim))
    write(rms, rms_o, sem.at[3])
    sg_wide[...] = sg[...].astype(F32)
    write(sg_wide, sg_o.at[0], sem.at[4])
    for src, wide, dst, sems in (
        (first, first_wide, first_o, first_sem), (second, second_wide, second_o, second_sem),
    ):
        count = src.shape[0] // WRITES
        for k in range(WRITES):
            at = pl.ds(k * count, count)
            wide[at, :] = src[at, :].astype(F32)
            write(wide.at[at], dst.at[0, at], sems.at[k])
    for copy in copies:
        copy.wait()


def run_sublayers(start, cot, first, second, norm, bias, seg, val):
    rows, seq, dim = start.shape
    ff = first.shape[2]
    half = ff // 2
    steps = (half // CHUNK) * SUB
    block = (rows, seq, dim)
    wide = (rows, seq, ff)
    small = (4 + ff // dim, dim)
    ring = RING if lax.axis_size("dp") <= 8 else 2 * steps
    any_space = pl.BlockSpec(memory_space=pl.ANY)
    vmem = pl.BlockSpec(memory_space=pltpu.VMEM)
    out = jax.ShapeDtypeStruct
    dma = pltpu.SemaphoreType.DMA
    return pl.pallas_call(
        sublayer_kernel,
        out_shape=(
            pltpu.VMEM(block, BF16), pltpu.VMEM(block, BF16),
            pltpu.VMEM((dim, ff), BF16), pltpu.VMEM((ff, dim), BF16), pltpu.VMEM(small, F32),
        ),
        in_specs=[any_space] * 8,
        out_specs=(vmem,) * 5,
        scratch_shapes=[
            pltpu.VMEM((dim, ff), BF16), pltpu.VMEM((ff, dim), BF16),
            pltpu.VMEM((ff, dim), BF16), pltpu.VMEM((dim, ff), BF16),
            pltpu.VMEM(block, BF16), pltpu.VMEM((2, *block), BF16),
            pltpu.VMEM(wide, BF16), pltpu.VMEM(wide, BF16),
            pltpu.VMEM(norm.shape, F32), pltpu.VMEM(bias.shape, F32),
            pltpu.VMEM(seg.shape, jnp.int32), pltpu.VMEM(val.shape, jnp.int32),
            pltpu.VMEM((2, 8, dim), F32), pltpu.VMEM((2, 8, dim), F32),
            pltpu.VMEM((4, *small), F32),
            pltpu.VMEM((dim, half), BF16), pltpu.VMEM((dim, half), BF16),
            pltpu.VMEM((half, dim), BF16), pltpu.VMEM((half, dim), BF16),
            dma((10,)), dma, dma((rows,)), dma, dma((rows,)), dma, dma((RELAYED, PARTS)), dma((6,)),
            dma((2,)), dma((2, steps // SUB)), dma((sum(NEAR) + FAR,)),
            dma((2,)), dma((ring,)), dma((ring,)), dma((2,)),
            dma((2,)), dma((2,)),
        ],
        compiler_params=pltpu.CompilerParams(
            collective_id=0, has_side_effects=True, vmem_limit_bytes=SUBLAYER_VMEM
        ),
        name="sublayer",
    )(start, cot, first, second, norm, bias, seg, val)


def run_finish(res, sg, first, second, small):
    rows, seq, dim = res.shape
    ff = first.shape[1]
    any_space = pl.BlockSpec(memory_space=pl.ANY)
    vmem = pl.BlockSpec(memory_space=pltpu.VMEM)
    out = jax.ShapeDtypeStruct
    dma = pltpu.SemaphoreType.DMA
    return pl.pallas_call(
        finish_kernel,
        out_shape=(
            out((1, rows, seq, dim), BF16), out((1, rows, seq, dim), F32),
            out((1, dim, ff), F32), out((1, ff, dim), F32),
            out((1, 2, dim), F32), out((1, ff + dim), F32), out((1, 2), F32),
        ),
        in_specs=[vmem] * 5,
        out_specs=(any_space,) * 7,
        scratch_shapes=[
            pltpu.VMEM((rows, seq, dim), F32),
            pltpu.VMEM((dim, ff), F32), pltpu.VMEM((ff, dim), F32),
            pltpu.VMEM((1, 2, dim), F32), pltpu.VMEM((1, ff + dim), F32), pltpu.VMEM((1, 2), F32),
            dma((5,)), dma((WRITES,)), dma((WRITES,)),
        ],
        compiler_params=pltpu.CompilerParams(vmem_limit_bytes=FINISH_VMEM),
        name="finish",
    )(res, sg, first, second, small)


def local(start, cot, first, second, norm, bias, seg, val):
    return run_finish(*run_sublayers(start, cot, first, second, norm, bias, seg, val))


def solution(mesh):
    in_specs = (
        P("dp", None, None),
        P("dp", None, None),
        P("section", None, None),
        P("section", None, None),
        P("section", None, None),
        P("section", None),
        P("dp", None),
        P("dp", None),
    )
    out_specs = (
        P("section", "dp", None, None),
        P("section", "dp", None, None),
        P("section", None, None),
        P("section", None, None),
        P("section", None, None),
        P("section", None),
        P("section", None),
    )
    return jax.shard_map(local, mesh=mesh, in_specs=in_specs, out_specs=out_specs, check_vma=False)
```

```python
import jax
import jax.numpy as jnp
from jax import lax
from jax.experimental import pallas as pl
from jax.experimental.pallas import tpu as pltpu
from jax.sharding import PartitionSpec as P

HEAD_DIM = 64
EPS = 1e-05
NEG_FILL = -1e30
MESH = pl.DeviceIdType.MESH
BF16 = jnp.bfloat16
F32 = jnp.float32
NN = (((1,), (0,)), ((), ()))
NT = (((1,), (1,)), ((), ()))
TN = (((0,), (0,)), ((), ()))
PAIR = 2 * HEAD_DIM
CHUNK = 256
SUB = 8
QUARTER = SUB // 4
NEAR = (11, 12)
FAR = 19
RELAYED = 4
PARTS = 4
RING = 24
LOADS = 4
WRITES = 3
SUBLAYER_VMEM = 50 * 2**20
FINISH_VMEM = 40 * 2**20
GELU_C = 0.7978845608028654
GELU_K = 0.044715


def dot(a, b, dims=NN):
    return lax.dot_general(a, b, dims, preferred_element_type=F32)


def gelu_and_slope(x):
    square = x * x
    t = jnp.tanh(GELU_C * (x + GELU_K * (square * x)))
    half = 0.5 * (1.0 + t)
    slope = half + (0.5 * GELU_C) * x * (1.0 - t * t) * (1.0 + (3.0 * GELU_K) * square)
    return x * half, slope


def fold(x):
    return x.reshape(x.shape[0] // 8, 8, x.shape[1]).sum(axis=0)


def normalize(hidden):
    mean = jnp.mean(hidden, axis=-1, keepdims=True)
    centered = hidden - mean
    variance = jnp.mean(centered * centered, axis=-1, keepdims=True)
    inv_std = lax.rsqrt(variance + EPS)
    return centered * inv_std, inv_std


def sublayer_kernel(
    start, cot, first, second, norm_in, bias_in, seg_in, val_in,
    hout, gout, first_o, second_o, small_o,
    w1, w2, w1t, w2t, hin, pair, act, mid,
    norm, bias, seg, val, sq_acc, norm_acc, small,
    sum_a1, sum_b1, sum_a2, sum_b2,
    load_sem, hs_sem, hr_sem, gs_sem, gr_sem, relay_send, relay_recv, small_sem,
    part_send, part_recv, hand_recv, line_send, line_recv, whole_recv, back_send,
    mate_send, mate_recv,
):
    nrm, gin = pair.at[0], pair.at[1]
    section = lax.axis_index("section")
    dp = lax.axis_index("dp")
    last = lax.axis_size("section") - 1
    rows, seq, dim = start.shape
    ff = first.shape[2]
    pairs = dim // PAIR
    is_attention = section % 2 == 0
    nxt = jnp.minimum(section + 1, last)
    prv = jnp.maximum(section - 1, 0)

    wide, out_cols = 3 * dim, pl.ds(3 * dim, ff - 3 * dim)
    first_load = pltpu.make_async_copy(
        first.at[0, :, pl.ds(0, wide)], w1.at[:, pl.ds(0, wide)], load_sem.at[0]
    )
    out_load = pltpu.make_async_copy(first.at[0, :, out_cols], w1.at[:, out_cols], load_sem.at[8])
    second_load = pltpu.make_async_copy(second.at[0], w2, load_sem.at[1])
    start_load = pltpu.make_async_copy(start.at[0], hin.at[0], load_sem.at[2])
    others = pl.ds(1, rows - 1)
    rest_load = pltpu.make_async_copy(start.at[others], hin.at[others], load_sem.at[9])
    cot_load = pltpu.make_async_copy(cot, gin, load_sem.at[3])
    small_loads = [
        pltpu.make_async_copy(src, dst, load_sem.at[4 + k])
        for k, (src, dst) in enumerate(
            ((norm_in, norm), (bias_in, bias), (seg_in, seg), (val_in, val))
        )
    ]

    def split_load(src, dst, cols, k):
        count = dst.shape[0] // LOADS
        for at in range(0, dst.shape[0], count):
            pltpu.make_async_copy(
                src.at[0, pl.ds(at, count), cols], dst.at[pl.ds(at, count), cols], load_sem.at[k]
            ).start()

    for load in small_loads:
        load.start()

    @pl.when(section == 0)
    def _():
        start_load.start()

    out_load.start()
    split_load(first, w1, pl.ds(0, wide), 0)

    @pl.when(section == 0)
    def _():
        rest_load.start()

    @pl.when(jnp.logical_not(is_attention))
    def _():
        split_load(second, w2, pl.ds(0, dim), 1)

    @pl.when(section == last)
    def _():
        cot_load.start()

    chips = lax.axis_size("dp") // 2
    chip, core = dp // 2, dp % 2
    mate = dp + 1 - 2 * core
    on_left = chip < chips // 2
    is_middle = (chip == chips // 2 - 1) | (chip == chips // 2)
    has_outer = (chip > 0) & (chip < chips - 1)
    inner = jnp.where(on_left, dp + 2, dp - 2)
    outer = jnp.clip(jnp.where(on_left, dp - 2, dp + 2), 0, 2 * chips - 1)
    helper = section + 1 - 2 * (section % 2)
    near = jnp.where(section < 2, NEAR[0], NEAR[1])
    far = jnp.where((section == 1) | (section == 2), FAR, 0)
    handed = near + far

    barrier = pltpu.get_barrier_semaphore()

    def greet(to_section, to_dp):
        pl.semaphore_signal(
            barrier, inc=1, device_id=(to_section, to_dp), device_id_type=MESH
        )

    greet(section, mate)
    greet(section, inner)

    @pl.when(has_outer)
    def _():
        greet(section, outer)

    @pl.when(section > 0)
    def _():
        greet(prv, dp)

    @pl.when(section < last)
    def _():
        greet(nxt, dp)

    @pl.when((section == 0) | (section == 2))
    def _():
        greet(2 - section, dp)

    peers = 3 + has_outer.astype(jnp.int32)
    peers += ((section == 0) | (section == 2)).astype(jnp.int32)
    peers += ((section > 0) & (section < last)).astype(jnp.int32)

    for ref in (sq_acc, norm_acc, small):
        ref[...] = jnp.zeros_like(ref)

    def h_copy(i):
        return pltpu.make_async_remote_copy(
            hout.at[i], hin.at[i], hs_sem, hr_sem.at[i],
            device_id=(nxt, dp), device_id_type=MESH,
        )

    def g_copy(i):
        return pltpu.make_async_remote_copy(
            gout.at[i], gin.at[i], gs_sem, gr_sem.at[i],
            device_id=(prv, dp), device_id_type=MESH,
        )

    part = seq // PARTS

    def via(i, k):
        return w2.at[pl.ds(pl.multiple_of(i * seq + k * part, part), part), :]

    def part_of(ref, i, k):
        return ref.at[i, pl.ds(pl.multiple_of(k * part, part), part)]

    def relay_in(i, k):
        return pltpu.make_async_remote_copy(
            part_of(gout, i, k), via(i, k), gs_sem, relay_recv.at[i, k],
            device_id=(0, dp), device_id_type=MESH,
        )

    def relay_out(i, k):
        return pltpu.make_async_remote_copy(
            via(i, k), part_of(gin, i, k), relay_send, gr_sem.at[i],
            device_id=(nxt, dp), device_id_type=MESH,
        )

    def pass_on(n, carry):
        relay_in(n // PARTS, n % PARTS).wait_recv()
        relay_out(n // PARTS, n % PARTS).start()
        return carry

    eye = lax.broadcasted_iota(jnp.int32, (seq, seq), 0) == lax.broadcasted_iota(
        jnp.int32, (seq, seq), 1
    )

    def column(row):
        return jnp.sum(jnp.where(eye, row, 0.0), axis=1, keepdims=True)

    def valid_row(i):
        return val[pl.ds(i, 1), :].astype(F32)

    def entry(i):
        @pl.when(section > 0)
        def _():
            h_copy(i).wait_recv()

        hidden = hin[i].astype(F32)
        normal, _ = normalize(hidden)
        low = (normal * norm[0, 0:1, :] + norm[0, 1:2, :]).astype(BF16)
        nrm[i] = low
        return hidden, low

    def leave(i, hidden, branch):
        low = (hidden + branch).astype(BF16)
        hout[i] = low

        @pl.when(section < last)
        def _():
            h_copy(i).start()

        weight = column(valid_row(i))
        value = low.astype(F32)
        sq_acc[0] += fold(value * value * weight)
        sq_acc[1] += fold(branch * branch * weight)

    def grad_entry(i):
        @pl.when(section < last)
        def _():
            g_copy(i).wait_recv()

        @pl.when(section == last)
        def _():
            gin[i] = jnp.where(column(valid_row(i)) > 0, gin[i], jnp.zeros((seq, dim), BF16))

        return gin[i]

    def grad_leave(i, grad, normed_grad):
        grad_value = grad.astype(F32)
        normal, inv_std = normalize(hin[i].astype(F32))
        scaled = normed_grad * norm[0, 0:1, :]
        mean_one = jnp.mean(scaled, axis=-1, keepdims=True)
        mean_two = jnp.mean(scaled * normal, axis=-1, keepdims=True)
        low = (grad_value + inv_std * (scaled - mean_one - normal * mean_two)).astype(BF16)
        gout[i] = low

        @pl.when((section == 2) & (i < RELAYED))
        def _():
            for k in range(PARTS):
                relay_in(i, k).start()

        @pl.when((section > 0) & ((section != 2) | (i >= RELAYED)))
        def _():
            g_copy(i).start()

        norm_acc[0] += fold(normed_grad * normal)
        norm_acc[1] += fold(normed_grad)


    def dense_forward(i):
        hidden, low = entry(i)
        value, slope = gelu_and_slope(dot(low, w1[...]) + bias[0:1, :ff])
        value = value.astype(BF16)
        act[i] = value
        mid[i] = slope.astype(BF16)
        leave(i, hidden, dot(value, w2[...]) + bias[0:1, ff:])

    def dense_backward(i):
        grad = grad_entry(i)
        low = (dot(grad, w2t[...]) * mid[i].astype(F32)).astype(BF16)
        mid[i] = low
        grad_leave(i, grad, dot(low, w1t[...]))


    lower = lax.broadcasted_iota(jnp.int32, (seq, PAIR), 1) < HEAD_DIM

    def split_heads(x):
        zero = jnp.zeros_like(x)
        return jnp.concatenate([jnp.where(lower, x, zero), jnp.where(lower, zero, x)], axis=0)

    def join_heads(x):
        return jnp.where(lower, x[:seq], x[seq:])

    def attention_forward(i):
        @pl.when((section == 0) & (i == 1))
        def _():
            rest_load.wait()

        hidden, low = entry(i)
        projected = dot(low, w1[:, : 3 * dim])
        mid[i, :, :dim] = (projected[:, :dim] + bias[0:1, :dim]).astype(BF16)
        mid[i, :, dim : 2 * dim] = projected[:, dim : 2 * dim].astype(BF16)
        mid[i, :, 2 * dim : 3 * dim] = (
            projected[:, 2 * dim :] + bias[0:1, dim : 2 * dim]
        ).astype(BF16)
        seg_row = seg[pl.ds(i, 1), :].astype(F32)
        allowed = (column(seg_row) == seg_row) & ((column(valid_row(i)) > 0) | eye)
        packed = [mid[i, :, k * PAIR : (k + 1) * PAIR] for k in range(3 * pairs)]
        scores = [
            dot(split_heads(packed[pairs + p]), packed[p], NT) * HEAD_DIM**-0.5
            for p in range(pairs)
        ]
        mixed = []
        for p in range(pairs):
            probs = []
            for half in (scores[p][:seq], scores[p][seq:]):
                half = jnp.where(allowed, half, NEG_FILL)
                weight = jnp.exp(half - jnp.max(half, axis=0, keepdims=True))
                probs.append((weight / jnp.sum(weight, axis=0, keepdims=True)).astype(BF16))
                act[i, :, (2 * p + len(probs) - 1) * seq : (2 * p + len(probs)) * seq] = probs[-1]
            prob = jnp.concatenate(probs, axis=0)
            mixed.append(dot(prob, split_heads(packed[2 * pairs + p]), TN).astype(BF16))
        mixed = jnp.concatenate(mixed, axis=1)
        mid[i, :, 3 * dim :] = mixed
        branch = dot(mixed, w1t[3 * dim :, :]) + bias[0:1, ff:]
        leave(i, hidden, branch)

    def attention_backward(i):
        grad = grad_entry(i)
        mixed_grad = dot(grad, w1[:, 3 * dim :]).astype(BF16)
        packed = [mid[i, :, k * PAIR : (k + 1) * PAIR] for k in range(3 * pairs)]
        probs = [act[i, :, k * seq : (k + 1) * seq] for k in range(2 * pairs)]
        grads = [None] * (3 * pairs)
        for p in range(pairs):
            out_grad = mixed_grad[:, p * PAIR : (p + 1) * PAIR]
            prob_grad = dot(split_heads(packed[2 * pairs + p]), out_grad, NT)
            parts = []
            for k in range(2):
                value, grad_of = probs[2 * p + k].astype(F32), prob_grad[k * seq : (k + 1) * seq]
                inner = jnp.sum(value * grad_of, axis=0, keepdims=True)
                parts.append((value * (grad_of - inner)).astype(BF16))
            score_grad = jnp.concatenate(parts, axis=0)
            prob = jnp.concatenate(probs[2 * p : 2 * p + 2], axis=0)
            query_grad = dot(score_grad, split_heads(packed[pairs + p]), TN) * HEAD_DIM**-0.5
            key_grad = join_heads(dot(score_grad, packed[p])) * HEAD_DIM**-0.5
            grads[p] = query_grad.astype(BF16)
            grads[pairs + p] = key_grad.astype(BF16)
            grads[2 * pairs + p] = join_heads(dot(prob, out_grad)).astype(BF16)
        packed_grad = jnp.concatenate(grads, axis=1)
        mid[i, :, : 3 * dim] = packed_grad
        normed_grad = dot(packed_grad, w1t[: 3 * dim, :])
        grad_leave(i, grad, normed_grad)

    for load in small_loads:
        load.wait()

    def transpose(src, dst, low, high):
        for at in range(low, high, 2 * PAIR):
            dst[at : at + 2 * PAIR, :] = src[:, at : at + 2 * PAIR].T

    @pl.when(section == 0)
    def _():
        start_load.wait()

    @pl.when(section == last)
    def _():
        cot_load.wait()

    def run(forward, backward, lag, before_last, after_last):
        pl.semaphore_wait(barrier, peers)

        def step(i, carry):
            @pl.when(i == rows - 1)
            def _():
                before_last()

            @pl.when(i < rows)
            def _():
                forward(i)

            @pl.when(i == rows)
            def _():
                after_last()

            @pl.when(i >= lag)
            def _():
                backward(i - lag)

            return carry

        lax.fori_loop(0, rows + lag, step, 0)

    @pl.when(is_attention)
    def _():
        out_load.wait()
        transpose(w1, w1t, 3 * dim, ff)
        first_load.wait()

        def late():
            @pl.when(section == 0)
            def _():
                transpose(w1, w1t, 0, 3 * dim)

        @pl.when(section > 0)
        def _():
            transpose(w1, w1t, 0, 3 * dim)

        def relay():
            @pl.when(section == 0)
            def _():
                lax.fori_loop(0, PARTS * RELAYED, pass_on, 0)

        lag = jnp.where(section == 0, rows, rows // 2)
        run(attention_forward, attention_backward, lag, late, relay)

        @pl.when(section == 0)
        def _():
            ref = w2.at[pl.ds(0, RELAYED * seq), :]
            pltpu.make_async_copy(ref, ref, relay_send).wait()


    @pl.when(jnp.logical_not(is_attention))
    def _():
        out_load.wait()
        first_load.wait()
        second_load.wait()
        transpose(w1, w1t, 0, ff)
        for at in range(0, ff, 2 * PAIR):
            w2t[:, at : at + 2 * PAIR] = w2[at : at + 2 * PAIR, :].T
        lag = jnp.where(section == last, 0, rows - 1)
        run(dense_forward, dense_backward, lag, lambda: None, lambda: None)

    def remote(src, dst, send, recv, to):
        return pltpu.make_async_remote_copy(
            src, dst, send, recv, device_id=to, device_id_type=MESH
        )

    small_mate = remote(
        small.at[0], small.at[1], small_sem.at[0], small_sem.at[1], (section, mate)
    )
    small_line = remote(
        small.at[0], small.at[2], small_sem.at[2], small_sem.at[3], (section, inner)
    )
    small_cross = remote(
        small.at[0], small.at[3], small_sem.at[2], small_sem.at[4], (section, inner)
    )
    small_back = remote(
        small.at[3], small.at[3], small_sem.at[5], small_sem.at[4], (section, outer)
    )


    tokens = rows * seq
    half = ff // 2
    steps = (half // CHUNK) * SUB
    tall, short = dim // SUB, CHUNK // SUB
    mine, theirs = core * half, (1 - core) * half

    def own(k, v):
        if k == 0:
            return w1.at[
                pl.ds(pl.multiple_of((v % SUB) * tall, 16), tall),
                pl.ds(pl.multiple_of(mine + (v // SUB) * CHUNK, CHUNK), CHUNK),
            ]
        return w2.at[pl.ds(pl.multiple_of(mine + v * short, 16), short), :]

    def whole(k, v):
        if k == 0:
            return first_o.at[
                pl.ds(pl.multiple_of((v % SUB) * tall, 16), tall),
                pl.ds(pl.multiple_of(mine + (v // SUB) * CHUNK, CHUNK), CHUNK),
            ]
        return second_o.at[pl.ds(pl.multiple_of(mine + v * short, 16), short), :]

    def slot(ref, k, v):
        if k == 0:
            return ref.at[
                pl.ds(pl.multiple_of((v % SUB) * tall, 16), tall),
                pl.ds(pl.multiple_of((v // SUB) * CHUNK, CHUNK), CHUNK),
            ]
        return ref.at[pl.ds(pl.multiple_of(v * short, 16), short), :]

    line = (sum_b1, sum_b2)

    def part_copy(k, c):
        at = pl.ds(pl.multiple_of(theirs + c * CHUNK, CHUNK), CHUNK)
        to = pl.ds(pl.multiple_of(c * CHUNK, CHUNK), CHUNK)
        src, dst = (w1.at[:, at], sum_a1.at[:, to]) if k == 0 else (w2.at[at, :], sum_a2.at[to, :])
        return remote(src, dst, part_send.at[k], part_recv.at[k, c], (section, mate))

    ring = line_recv.shape[0]

    def line_copy(k, v, p):
        return remote(
            own(k, v), slot(line[k], k, v), line_send.at[k], line_recv.at[p % ring], (section, inner)
        )

    def cross_copy(k, v, p):
        return remote(
            own(k, v), whole(k, v), line_send.at[k], whole_recv.at[p % ring], (section, inner)
        )

    def back_copy(k, v, p):
        ref = whole(k, v)
        return remote(ref, ref, back_send.at[k], whole_recv.at[p % ring], (section, outer))

    shift = jnp.where(section >= 2, NEAR[0] + FAR, 0)

    def given_copy(v):
        to = jnp.where(v < near, helper, nxt)
        w = jnp.where(v < near, v + shift, v)
        return remote(own(1, v), slot(sum_a2, 1, w), line_send.at[1], hand_recv.at[w], (to, dp))

    def return_copy(w, to, v):
        return remote(whole(1, w), whole(1, v), mate_send.at[1], hand_recv.at[v], (to, dp))

    def mate_copy(k, v):
        ref = whole(k, v)
        return remote(ref, ref, mate_send.at[k], mate_recv.at[k], (section, mate))

    def token_sum(matrix):
        return jnp.sum(fold(matrix.astype(F32)), axis=0, keepdims=True)

    def small_start():
        lane = lax.broadcasted_iota(jnp.int32, (1, dim), 1)
        counts = jnp.zeros((1, dim), F32)
        for k, x in enumerate((sq_acc[0], sq_acc[1], val[...].astype(F32))):
            amount = jnp.sum(jnp.sum(x, axis=0, keepdims=True), axis=1, keepdims=True)
            counts = jnp.where(lane == k, amount, counts)
        small[0, 0:1, :] = jnp.sum(norm_acc[0], axis=0, keepdims=True)
        small[0, 1:2, :] = jnp.sum(norm_acc[1], axis=0, keepdims=True)
        small[0, 2 + ff // dim : 3 + ff // dim, :] = token_sum(gin[...].reshape(tokens, dim))
        small[0, 3 + ff // dim : 4 + ff // dim, :] = counts
        small_mate.start()

    def bias_sum(matrix, col):
        third = col // dim
        row = jnp.where(is_attention, third // 2, third) + 2
        at = pl.ds(pl.multiple_of(col - third * dim, CHUNK), CHUNK)

        @pl.when(jnp.logical_not(is_attention) | (third == 0) | (third == 2))
        def _():
            small[0, pl.ds(row, 1), at] = token_sum(matrix)

    def compute(k, c, is_mine):
        base = jnp.where(is_mine, mine, theirs) + c * CHUNK
        at = pl.ds(pl.multiple_of(base, CHUNK), CHUNK)
        if k == 0:
            side = is_attention & (base >= 3 * dim)
            left = pair[side.astype(jnp.int32)].reshape(tokens, dim)
            right = mid[:, :, at].reshape(tokens, CHUNK)
            w1[:, at] = dot(left, right, TN).astype(BF16)
        else:
            left = act[:, :, at].reshape(tokens, CHUNK)
            w2[at, :] = dot(left, gin[...].reshape(tokens, dim), TN).astype(BF16)

        @pl.when(jnp.logical_not(is_mine))
        def _():
            part_copy(k, c).start()

        if k == 0:
            bias_sum(mid[:, :, at].reshape(tokens, CHUNK), base)

    def clear(base):
        at = pl.ds(pl.multiple_of(base, CHUNK), half)
        second_o[at, :] = jnp.zeros((half, dim), BF16)

    def combine(dst, *refs):
        value = refs[0][...].astype(F32)
        for ref in refs[1:]:
            value += ref[...].astype(F32)
        dst[...] = value.astype(BF16)

    def send_in(k, v, p, *refs):
        @pl.when(has_outer)
        def _():
            line_copy(k, v, p).wait_recv()
            combine(own(k, v), *refs, slot(line[k], k, v))

        @pl.when(jnp.logical_not(has_outer))
        def _():
            combine(own(k, v), *refs)

        @pl.when(is_middle)
        def _():
            cross_copy(k, v, p).start()

        @pl.when(jnp.logical_not(is_middle))
        def _():
            line_copy(k, v, p).start()

    def part_wait(k, v):
        @pl.when(v % SUB == 0)
        def _():
            part_copy(k, v // SUB).wait_recv()

    def send_first(v, p):
        part_wait(0, v)
        send_in(0, v, p, own(0, v), slot(sum_a1, 0, v))

    def send_second(v, p):
        part_wait(1, v)
        send_in(1, v, p, own(1, v), slot(sum_a2, 1, v))

    def hand_over(v):
        part_wait(1, v)
        combine(own(1, v), own(1, v), slot(sum_a2, 1, v))
        given_copy(v).start()

    def send_given(w, to, v, p):
        return_copy(w, to, w).wait_recv()
        send_in(1, w, p, slot(sum_a2, 1, w))

    def settle(k, v, p):
        cross_copy(k, v, p).wait_recv()

        @pl.when(is_middle)
        def _():
            combine(whole(k, v), own(k, v), whole(k, v))

        @pl.when(has_outer)
        def _():
            back_copy(k, v, p).start()

    def settle_first(v, p):
        settle(0, v, p)
        mate_copy(0, v).start()

    def settle_second(v, p):
        settle(1, v, p)
        mate_copy(1, v).start()

    def settle_handed(v):
        return_copy(v, helper, v).wait_recv()
        mate_copy(1, v).start()

    def settle_given(w, to, v, p):
        settle(1, w, p)
        return_copy(w, to, v).start()

    def small_in():
        small_mate.wait_recv()
        small_mate.wait_send()
        small[0] += small[1]

        @pl.when(has_outer)
        def _():
            small_line.wait_recv()
            small[0] += small[2]

        @pl.when(is_middle)
        def _():
            small_cross.start()

        @pl.when(jnp.logical_not(is_middle))
        def _():
            small_line.start()

    def small_settle():
        small_cross.wait_recv()

        @pl.when(is_middle)
        def _():
            small[3] += small[0]

        @pl.when(has_outer)
        def _():
            small_back.start()

        small_o[...] = small[3]

    gap = jnp.where(on_left, chips // 2 - 1 - chip, chip - chips // 2)
    lag = 4 + 14 * gap
    blocks = steps // SUB
    early = (blocks * 2 // 3) * SUB
    is_dense = jnp.logical_not(is_attention)
    length = jnp.where(is_attention, steps + near + far, 2 * steps - handed)

    ahead = jnp.where(is_middle, SUB, 0)

    @pl.when(is_dense)
    def _():
        compute(0, 0, False)
        compute(0, 0, True)

    def in_line(u, first_part, second_part, given_part):
        @pl.when((u >= 0) & (u < length) & is_dense)
        def _():
            @pl.when(u < steps)
            def _():
                first_part(u, u)

            @pl.when(u >= steps)
            def _():
                second_part(u - steps + handed, u)

        @pl.when((u >= 0) & (u < length) & is_attention)
        def _():
            @pl.when(u < near)
            def _():
                given_part(u + shift, helper, u, u)

            @pl.when((u >= near) & (u < near + early))
            def _():
                first_part(u - near, u)

            @pl.when((u >= near + early) & (u < near + early + far))
            def _():
                v = NEAR[0] + u - near - early
                given_part(v, prv, v, u)

            @pl.when(u >= near + early + far)
            def _():
                first_part(u - near - far, u)

    def step(u, carry):
        in_line(u - ahead, send_first, send_second, send_given)

        @pl.when((u % SUB >= SUB // 2) & is_dense)
        def _():
            for k in range(2):
                v = u // SUB * SUB + 2 * (u % SUB - SUB // 2) + k

                @pl.when(v < handed)
                def _(v=v):
                    hand_over(v)

        t = u - ahead - lag

        @pl.when(t == length - 1)
        def _():
            small_settle()

        in_line(t, settle_first, settle_second, settle_given)

        @pl.when((t >= length) & (t < length + handed) & is_dense)
        def _():
            settle_handed(t - length)

        c, q = u // SUB, u % SUB // QUARTER
        on_time = (u % QUARTER == 0) & (c < blocks)

        @pl.when(on_time & (q < 2) & is_dense)
        def _():
            compute(1, c, q == 1)

        @pl.when(on_time & jnp.where(is_attention, q < 2, (q >= 2) & (c + 1 < blocks)))
        def _():
            compute(0, jnp.where(is_attention, c, c + 1), q % 2 == 1)

        @pl.when(u == steps - 2)
        def _():
            small_start()

        @pl.when((u == steps) & is_attention)
        def _():
            clear(theirs)

        @pl.when(u - ahead == steps + jnp.where((chip > 0) & (chip < chips - 1), SUB, 0))
        def _():
            small_in()

        return carry

    tail = jnp.where(is_attention, 0, handed)
    lax.fori_loop(0, length + ahead + lag + tail, step, 0)


    @pl.when(section < last)
    def _():
        remote(hout, hin, hs_sem, hr_sem.at[0], (nxt, dp)).wait_send()

    @pl.when(section > 0)
    def _():
        remote(gout, gin, gs_sem, gr_sem.at[0], (prv, dp)).wait_send()

    def taken(k, sem, count):
        if k == 0:
            ref = w1.at[:, pl.ds(0, (count // SUB) * CHUNK)]
        else:
            ref = w2.at[pl.ds(0, count * short), :]
        pltpu.make_async_copy(ref, ref, sem.at[k]).wait()

    taken(0, part_send, steps)
    taken(0, line_send, steps)
    taken(0, mate_send, steps)
    taken(0, mate_recv, steps)

    @pl.when(has_outer)
    def _():
        taken(0, back_send, steps)
        small_back.wait_send()

    @pl.when(jnp.logical_not(is_attention))
    def _():
        taken(1, part_send, steps)
        taken(1, line_send, steps)
        taken(1, mate_send, steps)
        taken(1, mate_recv, steps)

    for which, count in enumerate((NEAR[0], NEAR[0] + FAR, NEAR[1] + FAR, NEAR[1])):
        if which % 2:

            @pl.when((section == which) & has_outer)
            def _(count=count):
                taken(1, back_send, steps - count)

        else:

            @pl.when(section == which)
            def _(count=count):
                taken(1, line_send, count)
                taken(1, mate_send, count)

            @pl.when((section == which) & has_outer)
            def _(count=count):
                taken(1, back_send, count)

    small_line.wait_send()

    @pl.when(is_attention)
    def _():
        clear(mine)


def finish_kernel(
    res, sg, first, second, small,
    res_o, sg_o, first_o, second_o, norm_o, bias_o, rms_o,
    sg_wide, first_wide, second_wide, norm, bias, rms, sem, first_sem, second_sem,
):
    dim = sg.shape[2]
    ff = first.shape[1]
    copies = []

    def write(src, dst, sem):
        copies.append(pltpu.make_async_copy(src, dst, sem))
        copies[-1].start()

    write(res, res_o.at[0], sem.at[0])
    norm[0] = small[0:2, :]
    write(norm, norm_o, sem.at[1])
    count = ff // dim + 1
    for k in range(count):
        bias[0:1, k * dim : (k + 1) * dim] = small[2 + k : 3 + k, :]
    write(bias, bias_o, sem.at[2])
    stat = small[2 + count : 3 + count, :]
    rms[...] = jnp.sqrt(stat[:, 0:2] / (stat[:, 2:3] * dim))
    write(rms, rms_o, sem.at[3])
    sg_wide[...] = sg[...].astype(F32)
    write(sg_wide, sg_o.at[0], sem.at[4])
    for src, wide, dst, sems in (
        (first, first_wide, first_o, first_sem), (second, second_wide, second_o, second_sem),
    ):
        count = src.shape[0] // WRITES
        for k in range(WRITES):
            at = pl.ds(k * count, count)
            wide[at, :] = src[at, :].astype(F32)
            write(wide.at[at], dst.at[0, at], sems.at[k])
    for copy in copies:
        copy.wait()


def run_sublayers(start, cot, first, second, norm, bias, seg, val):
    rows, seq, dim = start.shape
    ff = first.shape[2]
    half = ff // 2
    steps = (half // CHUNK) * SUB
    block = (rows, seq, dim)
    wide = (rows, seq, ff)
    small = (4 + ff // dim, dim)
    ring = RING if lax.axis_size("dp") <= 8 else 2 * steps
    any_space = pl.BlockSpec(memory_space=pl.ANY)
    vmem = pl.BlockSpec(memory_space=pltpu.VMEM)
    out = jax.ShapeDtypeStruct
    dma = pltpu.SemaphoreType.DMA
    return pl.pallas_call(
        sublayer_kernel,
        out_shape=(
            pltpu.VMEM(block, BF16), pltpu.VMEM(block, BF16),
            pltpu.VMEM((dim, ff), BF16), pltpu.VMEM((ff, dim), BF16), pltpu.VMEM(small, F32),
        ),
        in_specs=[any_space] * 8,
        out_specs=(vmem,) * 5,
        scratch_shapes=[
            pltpu.VMEM((dim, ff), BF16), pltpu.VMEM((ff, dim), BF16),
            pltpu.VMEM((ff, dim), BF16), pltpu.VMEM((dim, ff), BF16),
            pltpu.VMEM(block, BF16), pltpu.VMEM((2, *block), BF16),
            pltpu.VMEM(wide, BF16), pltpu.VMEM(wide, BF16),
            pltpu.VMEM(norm.shape, F32), pltpu.VMEM(bias.shape, F32),
            pltpu.VMEM(seg.shape, jnp.int32), pltpu.VMEM(val.shape, jnp.int32),
            pltpu.VMEM((2, 8, dim), F32), pltpu.VMEM((2, 8, dim), F32),
            pltpu.VMEM((4, *small), F32),
            pltpu.VMEM((dim, half), BF16), pltpu.VMEM((dim, half), BF16),
            pltpu.VMEM((half, dim), BF16), pltpu.VMEM((half, dim), BF16),
            dma((10,)), dma, dma((rows,)), dma, dma((rows,)), dma, dma((RELAYED, PARTS)), dma((6,)),
            dma((2,)), dma((2, steps // SUB)), dma((sum(NEAR) + FAR,)),
            dma((2,)), dma((ring,)), dma((ring,)), dma((2,)),
            dma((2,)), dma((2,)),
        ],
        compiler_params=pltpu.CompilerParams(
            collective_id=0, has_side_effects=True, vmem_limit_bytes=SUBLAYER_VMEM
        ),
        name="sublayer",
    )(start, cot, first, second, norm, bias, seg, val)


def run_finish(res, sg, first, second, small):
    rows, seq, dim = res.shape
    ff = first.shape[1]
    any_space = pl.BlockSpec(memory_space=pl.ANY)
    vmem = pl.BlockSpec(memory_space=pltpu.VMEM)
    out = jax.ShapeDtypeStruct
    dma = pltpu.SemaphoreType.DMA
    return pl.pallas_call(
        finish_kernel,
        out_shape=(
            out((1, rows, seq, dim), BF16), out((1, rows, seq, dim), F32),
            out((1, dim, ff), F32), out((1, ff, dim), F32),
            out((1, 2, dim), F32), out((1, ff + dim), F32), out((1, 2), F32),
        ),
        in_specs=[vmem] * 5,
        out_specs=(any_space,) * 7,
        scratch_shapes=[
            pltpu.VMEM((rows, seq, dim), F32),
            pltpu.VMEM((dim, ff), F32), pltpu.VMEM((ff, dim), F32),
            pltpu.VMEM((1, 2, dim), F32), pltpu.VMEM((1, ff + dim), F32), pltpu.VMEM((1, 2), F32),
            dma((5,)), dma((WRITES,)), dma((WRITES,)),
        ],
        compiler_params=pltpu.CompilerParams(vmem_limit_bytes=FINISH_VMEM),
        name="finish",
    )(res, sg, first, second, small)


def local(start, cot, first, second, norm, bias, seg, val):
    return run_finish(*run_sublayers(start, cot, first, second, norm, bias, seg, val))


def solution(mesh):
    in_specs = (
        P("dp", None, None),
        P("dp", None, None),
        P("section", None, None),
        P("section", None, None),
        P("section", None, None),
        P("section", None),
        P("dp", None),
        P("dp", None),
    )
    out_specs = (
        P("section", "dp", None, None),
        P("section", "dp", None, None),
        P("section", None, None),
        P("section", None, None),
        P("section", None, None),
        P("section", None),
        P("section", None),
    )
    return jax.shard_map(local, mesh=mesh, in_specs=in_specs, out_specs=out_specs, check_vma=False)
```

```python
import jax
import jax.numpy as jnp
from jax import lax
from jax.experimental import pallas as pl
from jax.experimental.pallas import tpu as pltpu
from jax.sharding import PartitionSpec as P

HEAD_DIM = 64
EPS = 1e-05
NEG_FILL = -1e30
MESH = pl.DeviceIdType.MESH
BF16 = jnp.bfloat16
F32 = jnp.float32
NN = (((1,), (0,)), ((), ()))
NT = (((1,), (1,)), ((), ()))
TN = (((0,), (0,)), ((), ()))
PAIR = 2 * HEAD_DIM
CHUNK = 256
SUB = 8
QUARTER = SUB // 4
NEAR = (10, 13)
FAR = 19
RELAYED = 4
PARTS = 4
RING = 24
LOADS = 4
WRITES = 3
SUBLAYER_VMEM = 50 * 2**20
FINISH_VMEM = 40 * 2**20
GELU_C = 0.7978845608028654
GELU_K = 0.044715


def dot(a, b, dims=NN):
    return lax.dot_general(a, b, dims, preferred_element_type=F32)


def gelu_and_slope(x):
    square = x * x
    t = jnp.tanh(GELU_C * (x + GELU_K * (square * x)))
    half = 0.5 * (1.0 + t)
    slope = half + (0.5 * GELU_C) * x * (1.0 - t * t) * (1.0 + (3.0 * GELU_K) * square)
    return x * half, slope


def fold(x):
    return x.reshape(x.shape[0] // 8, 8, x.shape[1]).sum(axis=0)


def normalize(hidden):
    mean = jnp.mean(hidden, axis=-1, keepdims=True)
    centered = hidden - mean
    variance = jnp.mean(centered * centered, axis=-1, keepdims=True)
    inv_std = lax.rsqrt(variance + EPS)
    return centered * inv_std, inv_std


def sublayer_kernel(
    start, cot, first, second, norm_in, bias_in, seg_in, val_in,
    hout, gout, first_o, second_o, small_o,
    w1, w2, w1t, w2t, hin, pair, act, mid,
    norm, bias, seg, val, sq_acc, norm_acc, small,
    sum_a1, sum_b1, sum_a2, sum_b2,
    load_sem, hs_sem, hr_sem, gs_sem, gr_sem, relay_send, relay_recv, small_sem,
    part_send, part_recv, hand_recv, line_send, line_recv, whole_recv, back_send,
    mate_send, mate_recv,
):
    nrm, gin = pair.at[0], pair.at[1]
    section = lax.axis_index("section")
    dp = lax.axis_index("dp")
    last = lax.axis_size("section") - 1
    rows, seq, dim = start.shape
    ff = first.shape[2]
    pairs = dim // PAIR
    is_attention = section % 2 == 0
    nxt = jnp.minimum(section + 1, last)
    prv = jnp.maximum(section - 1, 0)

    wide, out_cols = 3 * dim, pl.ds(3 * dim, ff - 3 * dim)
    first_load = pltpu.make_async_copy(
        first.at[0, :, pl.ds(0, wide)], w1.at[:, pl.ds(0, wide)], load_sem.at[0]
    )
    out_load = pltpu.make_async_copy(first.at[0, :, out_cols], w1.at[:, out_cols], load_sem.at[8])
    second_load = pltpu.make_async_copy(second.at[0], w2, load_sem.at[1])
    start_load = pltpu.make_async_copy(start.at[0], hin.at[0], load_sem.at[2])
    others = pl.ds(1, rows - 1)
    rest_load = pltpu.make_async_copy(start.at[others], hin.at[others], load_sem.at[9])
    cot_load = pltpu.make_async_copy(cot, gin, load_sem.at[3])
    small_loads = [
        pltpu.make_async_copy(src, dst, load_sem.at[4 + k])
        for k, (src, dst) in enumerate(
            ((norm_in, norm), (bias_in, bias), (seg_in, seg), (val_in, val))
        )
    ]

    def split_load(src, dst, cols, k):
        count = dst.shape[0] // LOADS
        for at in range(0, dst.shape[0], count):
            pltpu.make_async_copy(
                src.at[0, pl.ds(at, count), cols], dst.at[pl.ds(at, count), cols], load_sem.at[k]
            ).start()

    for load in small_loads:
        load.start()

    @pl.when(section == 0)
    def _():
        start_load.start()

    out_load.start()
    split_load(first, w1, pl.ds(0, wide), 0)

    @pl.when(section == 0)
    def _():
        rest_load.start()

    @pl.when(jnp.logical_not(is_attention))
    def _():
        split_load(second, w2, pl.ds(0, dim), 1)

    @pl.when(section == last)
    def _():
        cot_load.start()

    chips = lax.axis_size("dp") // 2
    chip, core = dp // 2, dp % 2
    mate = dp + 1 - 2 * core
    on_left = chip < chips // 2
    is_middle = (chip == chips // 2 - 1) | (chip == chips // 2)
    has_outer = (chip > 0) & (chip < chips - 1)
    inner = jnp.where(on_left, dp + 2, dp - 2)
    outer = jnp.clip(jnp.where(on_left, dp - 2, dp + 2), 0, 2 * chips - 1)
    helper = section + 1 - 2 * (section % 2)
    near = jnp.where(section < 2, NEAR[0], NEAR[1])
    far = jnp.where((section == 1) | (section == 2), FAR, 0)
    handed = near + far

    barrier = pltpu.get_barrier_semaphore()

    def greet(to_section, to_dp):
        pl.semaphore_signal(
            barrier, inc=1, device_id=(to_section, to_dp), device_id_type=MESH
        )

    greet(section, mate)
    greet(section, inner)

    @pl.when(has_outer)
    def _():
        greet(section, outer)

    @pl.when(section > 0)
    def _():
        greet(prv, dp)

    @pl.when(section < last)
    def _():
        greet(nxt, dp)

    @pl.when((section == 0) | (section == 2))
    def _():
        greet(2 - section, dp)

    peers = 3 + has_outer.astype(jnp.int32)
    peers += ((section == 0) | (section == 2)).astype(jnp.int32)
    peers += ((section > 0) & (section < last)).astype(jnp.int32)

    for ref in (sq_acc, norm_acc, small):
        ref[...] = jnp.zeros_like(ref)

    def h_copy(i):
        return pltpu.make_async_remote_copy(
            hout.at[i], hin.at[i], hs_sem, hr_sem.at[i],
            device_id=(nxt, dp), device_id_type=MESH,
        )

    def g_copy(i):
        return pltpu.make_async_remote_copy(
            gout.at[i], gin.at[i], gs_sem, gr_sem.at[i],
            device_id=(prv, dp), device_id_type=MESH,
        )

    part = seq // PARTS

    def via(i, k):
        return w2.at[pl.ds(pl.multiple_of(i * seq + k * part, part), part), :]

    def part_of(ref, i, k):
        return ref.at[i, pl.ds(pl.multiple_of(k * part, part), part)]

    def relay_in(i, k):
        return pltpu.make_async_remote_copy(
            part_of(gout, i, k), via(i, k), gs_sem, relay_recv.at[i, k],
            device_id=(0, dp), device_id_type=MESH,
        )

    def relay_out(i, k):
        return pltpu.make_async_remote_copy(
            via(i, k), part_of(gin, i, k), relay_send, gr_sem.at[i],
            device_id=(nxt, dp), device_id_type=MESH,
        )

    def pass_on(n, carry):
        relay_in(n // PARTS, n % PARTS).wait_recv()
        relay_out(n // PARTS, n % PARTS).start()
        return carry

    eye = lax.broadcasted_iota(jnp.int32, (seq, seq), 0) == lax.broadcasted_iota(
        jnp.int32, (seq, seq), 1
    )

    def column(row):
        return jnp.sum(jnp.where(eye, row, 0.0), axis=1, keepdims=True)

    def valid_row(i):
        return val[pl.ds(i, 1), :].astype(F32)

    def entry(i):
        @pl.when(section > 0)
        def _():
            h_copy(i).wait_recv()

        hidden = hin[i].astype(F32)
        normal, _ = normalize(hidden)
        low = (normal * norm[0, 0:1, :] + norm[0, 1:2, :]).astype(BF16)
        nrm[i] = low
        return hidden, low

    def leave(i, hidden, branch):
        low = (hidden + branch).astype(BF16)
        hout[i] = low

        @pl.when(section < last)
        def _():
            h_copy(i).start()

        weight = column(valid_row(i))
        value = low.astype(F32)
        sq_acc[0] += fold(value * value * weight)
        sq_acc[1] += fold(branch * branch * weight)

    def grad_entry(i):
        @pl.when(section < last)
        def _():
            g_copy(i).wait_recv()

        @pl.when(section == last)
        def _():
            gin[i] = jnp.where(column(valid_row(i)) > 0, gin[i], jnp.zeros((seq, dim), BF16))

        return gin[i]

    def grad_leave(i, grad, normed_grad):
        grad_value = grad.astype(F32)
        normal, inv_std = normalize(hin[i].astype(F32))
        scaled = normed_grad * norm[0, 0:1, :]
        mean_one = jnp.mean(scaled, axis=-1, keepdims=True)
        mean_two = jnp.mean(scaled * normal, axis=-1, keepdims=True)
        low = (grad_value + inv_std * (scaled - mean_one - normal * mean_two)).astype(BF16)
        gout[i] = low

        @pl.when((section == 2) & (i < RELAYED))
        def _():
            for k in range(PARTS):
                relay_in(i, k).start()

        @pl.when((section > 0) & ((section != 2) | (i >= RELAYED)))
        def _():
            g_copy(i).start()

        norm_acc[0] += fold(normed_grad * normal)
        norm_acc[1] += fold(normed_grad)


    def dense_forward(i):
        hidden, low = entry(i)
        value, slope = gelu_and_slope(dot(low, w1[...]) + bias[0:1, :ff])
        value = value.astype(BF16)
        act[i] = value
        mid[i] = slope.astype(BF16)
        leave(i, hidden, dot(value, w2[...]) + bias[0:1, ff:])

    def dense_backward(i):
        grad = grad_entry(i)
        low = (dot(grad, w2t[...]) * mid[i].astype(F32)).astype(BF16)
        mid[i] = low
        grad_leave(i, grad, dot(low, w1t[...]))


    lower = lax.broadcasted_iota(jnp.int32, (seq, PAIR), 1) < HEAD_DIM

    def split_heads(x):
        zero = jnp.zeros_like(x)
        return jnp.concatenate([jnp.where(lower, x, zero), jnp.where(lower, zero, x)], axis=0)

    def join_heads(x):
        return jnp.where(lower, x[:seq], x[seq:])

    def attention_forward(i):
        @pl.when((section == 0) & (i == 1))
        def _():
            rest_load.wait()

        hidden, low = entry(i)
        projected = dot(low, w1[:, : 3 * dim])
        mid[i, :, :dim] = (projected[:, :dim] + bias[0:1, :dim]).astype(BF16)
        mid[i, :, dim : 2 * dim] = projected[:, dim : 2 * dim].astype(BF16)
        mid[i, :, 2 * dim : 3 * dim] = (
            projected[:, 2 * dim :] + bias[0:1, dim : 2 * dim]
        ).astype(BF16)
        seg_row = seg[pl.ds(i, 1), :].astype(F32)
        allowed = (column(seg_row) == seg_row) & ((column(valid_row(i)) > 0) | eye)
        packed = [mid[i, :, k * PAIR : (k + 1) * PAIR] for k in range(3 * pairs)]
        scores = [
            dot(split_heads(packed[pairs + p]), packed[p], NT) * HEAD_DIM**-0.5
            for p in range(pairs)
        ]
        mixed = []
        for p in range(pairs):
            probs = []
            for half in (scores[p][:seq], scores[p][seq:]):
                half = jnp.where(allowed, half, NEG_FILL)
                weight = jnp.exp(half - jnp.max(half, axis=0, keepdims=True))
                probs.append((weight / jnp.sum(weight, axis=0, keepdims=True)).astype(BF16))
                act[i, :, (2 * p + len(probs) - 1) * seq : (2 * p + len(probs)) * seq] = probs[-1]
            prob = jnp.concatenate(probs, axis=0)
            mixed.append(dot(prob, split_heads(packed[2 * pairs + p]), TN).astype(BF16))
        mixed = jnp.concatenate(mixed, axis=1)
        mid[i, :, 3 * dim :] = mixed
        branch = dot(mixed, w1t[3 * dim :, :]) + bias[0:1, ff:]
        leave(i, hidden, branch)

    def attention_backward(i):
        grad = grad_entry(i)
        mixed_grad = dot(grad, w1[:, 3 * dim :]).astype(BF16)
        packed = [mid[i, :, k * PAIR : (k + 1) * PAIR] for k in range(3 * pairs)]
        probs = [act[i, :, k * seq : (k + 1) * seq] for k in range(2 * pairs)]
        grads = [None] * (3 * pairs)
        for p in range(pairs):
            out_grad = mixed_grad[:, p * PAIR : (p + 1) * PAIR]
            prob_grad = dot(split_heads(packed[2 * pairs + p]), out_grad, NT)
            parts = []
            for k in range(2):
                value, grad_of = probs[2 * p + k].astype(F32), prob_grad[k * seq : (k + 1) * seq]
                inner = jnp.sum(value * grad_of, axis=0, keepdims=True)
                parts.append((value * (grad_of - inner)).astype(BF16))
            score_grad = jnp.concatenate(parts, axis=0)
            prob = jnp.concatenate(probs[2 * p : 2 * p + 2], axis=0)
            query_grad = dot(score_grad, split_heads(packed[pairs + p]), TN) * HEAD_DIM**-0.5
            key_grad = join_heads(dot(score_grad, packed[p])) * HEAD_DIM**-0.5
            grads[p] = query_grad.astype(BF16)
            grads[pairs + p] = key_grad.astype(BF16)
            grads[2 * pairs + p] = join_heads(dot(prob, out_grad)).astype(BF16)
        packed_grad = jnp.concatenate(grads, axis=1)
        mid[i, :, : 3 * dim] = packed_grad
        normed_grad = dot(packed_grad, w1t[: 3 * dim, :])
        grad_leave(i, grad, normed_grad)

    for load in small_loads:
        load.wait()

    def transpose(src, dst, low, high):
        for at in range(low, high, 2 * PAIR):
            dst[at : at + 2 * PAIR, :] = src[:, at : at + 2 * PAIR].T

    @pl.when(section == 0)
    def _():
        start_load.wait()

    @pl.when(section == last)
    def _():
        cot_load.wait()

    def run(forward, backward, lag, before_last, after_last):
        pl.semaphore_wait(barrier, peers)

        def step(i, carry):
            @pl.when(i == rows - 1)
            def _():
                before_last()

            @pl.when(i < rows)
            def _():
                forward(i)

            @pl.when(i == rows)
            def _():
                after_last()

            @pl.when(i >= lag)
            def _():
                backward(i - lag)

            return carry

        lax.fori_loop(0, rows + lag, step, 0)

    @pl.when(is_attention)
    def _():
        out_load.wait()
        transpose(w1, w1t, 3 * dim, ff)
        first_load.wait()

        def late():
            @pl.when(section == 0)
            def _():
                transpose(w1, w1t, 0, 3 * dim)

        @pl.when(section > 0)
        def _():
            transpose(w1, w1t, 0, 3 * dim)

        def relay():
            @pl.when(section == 0)
            def _():
                lax.fori_loop(0, PARTS * RELAYED, pass_on, 0)

        lag = jnp.where(section == 0, rows, rows // 2)
        run(attention_forward, attention_backward, lag, late, relay)

        @pl.when(section == 0)
        def _():
            ref = w2.at[pl.ds(0, RELAYED * seq), :]
            pltpu.make_async_copy(ref, ref, relay_send).wait()


    @pl.when(jnp.logical_not(is_attention))
    def _():
        out_load.wait()
        first_load.wait()
        second_load.wait()
        transpose(w1, w1t, 0, ff)
        for at in range(0, ff, 2 * PAIR):
            w2t[:, at : at + 2 * PAIR] = w2[at : at + 2 * PAIR, :].T
        lag = jnp.where(section == last, 0, rows - 1)
        run(dense_forward, dense_backward, lag, lambda: None, lambda: None)

    def remote(src, dst, send, recv, to):
        return pltpu.make_async_remote_copy(
            src, dst, send, recv, device_id=to, device_id_type=MESH
        )

    small_mate = remote(
        small.at[0], small.at[1], small_sem.at[0], small_sem.at[1], (section, mate)
    )
    small_line = remote(
        small.at[0], small.at[2], small_sem.at[2], small_sem.at[3], (section, inner)
    )
    small_cross = remote(
        small.at[0], small.at[3], small_sem.at[2], small_sem.at[4], (section, inner)
    )
    small_back = remote(
        small.at[3], small.at[3], small_sem.at[5], small_sem.at[4], (section, outer)
    )


    tokens = rows * seq
    half = ff // 2
    steps = (half // CHUNK) * SUB
    tall, short = dim // SUB, CHUNK // SUB
    mine, theirs = core * half, (1 - core) * half

    def own(k, v):
        if k == 0:
            return w1.at[
                pl.ds(pl.multiple_of((v % SUB) * tall, 16), tall),
                pl.ds(pl.multiple_of(mine + (v // SUB) * CHUNK, CHUNK), CHUNK),
            ]
        return w2.at[pl.ds(pl.multiple_of(mine + v * short, 16), short), :]

    def whole(k, v):
        if k == 0:
            return first_o.at[
                pl.ds(pl.multiple_of((v % SUB) * tall, 16), tall),
                pl.ds(pl.multiple_of(mine + (v // SUB) * CHUNK, CHUNK), CHUNK),
            ]
        return second_o.at[pl.ds(pl.multiple_of(mine + v * short, 16), short), :]

    def slot(ref, k, v):
        if k == 0:
            return ref.at[
                pl.ds(pl.multiple_of((v % SUB) * tall, 16), tall),
                pl.ds(pl.multiple_of((v // SUB) * CHUNK, CHUNK), CHUNK),
            ]
        return ref.at[pl.ds(pl.multiple_of(v * short, 16), short), :]

    line = (sum_b1, sum_b2)

    def part_copy(k, c):
        at = pl.ds(pl.multiple_of(theirs + c * CHUNK, CHUNK), CHUNK)
        to = pl.ds(pl.multiple_of(c * CHUNK, CHUNK), CHUNK)
        src, dst = (w1.at[:, at], sum_a1.at[:, to]) if k == 0 else (w2.at[at, :], sum_a2.at[to, :])
        return remote(src, dst, part_send.at[k], part_recv.at[k, c], (section, mate))

    ring = line_recv.shape[0]

    def line_copy(k, v, p):
        return remote(
            own(k, v), slot(line[k], k, v), line_send.at[k], line_recv.at[p % ring], (section, inner)
        )

    def cross_copy(k, v, p):
        return remote(
            own(k, v), whole(k, v), line_send.at[k], whole_recv.at[p % ring], (section, inner)
        )

    def back_copy(k, v, p):
        ref = whole(k, v)
        return remote(ref, ref, back_send.at[k], whole_recv.at[p % ring], (section, outer))

    shift = jnp.where(section >= 2, NEAR[0] + FAR, 0)

    def given_copy(v):
        to = jnp.where(v < near, helper, nxt)
        w = jnp.where(v < near, v + shift, v)
        return remote(own(1, v), slot(sum_a2, 1, w), line_send.at[1], hand_recv.at[w], (to, dp))

    def return_copy(w, to, v):
        return remote(whole(1, w), whole(1, v), mate_send.at[1], hand_recv.at[v], (to, dp))

    def mate_copy(k, v):
        ref = whole(k, v)
        return remote(ref, ref, mate_send.at[k], mate_recv.at[k], (section, mate))

    def token_sum(matrix):
        return jnp.sum(fold(matrix.astype(F32)), axis=0, keepdims=True)

    def small_start():
        lane = lax.broadcasted_iota(jnp.int32, (1, dim), 1)
        counts = jnp.zeros((1, dim), F32)
        for k, x in enumerate((sq_acc[0], sq_acc[1], val[...].astype(F32))):
            amount = jnp.sum(jnp.sum(x, axis=0, keepdims=True), axis=1, keepdims=True)
            counts = jnp.where(lane == k, amount, counts)
        small[0, 0:1, :] = jnp.sum(norm_acc[0], axis=0, keepdims=True)
        small[0, 1:2, :] = jnp.sum(norm_acc[1], axis=0, keepdims=True)
        small[0, 2 + ff // dim : 3 + ff // dim, :] = token_sum(gin[...].reshape(tokens, dim))
        small[0, 3 + ff // dim : 4 + ff // dim, :] = counts
        small_mate.start()

    def bias_sum(matrix, col):
        third = col // dim
        row = jnp.where(is_attention, third // 2, third) + 2
        at = pl.ds(pl.multiple_of(col - third * dim, CHUNK), CHUNK)

        @pl.when(jnp.logical_not(is_attention) | (third == 0) | (third == 2))
        def _():
            small[0, pl.ds(row, 1), at] = token_sum(matrix)

    def compute(k, c, is_mine):
        base = jnp.where(is_mine, mine, theirs) + c * CHUNK
        at = pl.ds(pl.multiple_of(base, CHUNK), CHUNK)
        if k == 0:
            side = is_attention & (base >= 3 * dim)
            left = pair[side.astype(jnp.int32)].reshape(tokens, dim)
            right = mid[:, :, at].reshape(tokens, CHUNK)
            w1[:, at] = dot(left, right, TN).astype(BF16)
        else:
            left = act[:, :, at].reshape(tokens, CHUNK)
            w2[at, :] = dot(left, gin[...].reshape(tokens, dim), TN).astype(BF16)

        @pl.when(jnp.logical_not(is_mine))
        def _():
            part_copy(k, c).start()

        if k == 0:
            bias_sum(mid[:, :, at].reshape(tokens, CHUNK), base)

    def clear(base):
        at = pl.ds(pl.multiple_of(base, CHUNK), half)
        second_o[at, :] = jnp.zeros((half, dim), BF16)

    def combine(dst, *refs):
        value = refs[0][...].astype(F32)
        for ref in refs[1:]:
            value += ref[...].astype(F32)
        dst[...] = value.astype(BF16)

    def send_in(k, v, p, *refs):
        @pl.when(has_outer)
        def _():
            line_copy(k, v, p).wait_recv()
            combine(own(k, v), *refs, slot(line[k], k, v))

        @pl.when(jnp.logical_not(has_outer))
        def _():
            combine(own(k, v), *refs)

        @pl.when(is_middle)
        def _():
            cross_copy(k, v, p).start()

        @pl.when(jnp.logical_not(is_middle))
        def _():
            line_copy(k, v, p).start()

    def part_wait(k, v):
        @pl.when(v % SUB == 0)
        def _():
            part_copy(k, v // SUB).wait_recv()

    def send_first(v, p):
        part_wait(0, v)
        send_in(0, v, p, own(0, v), slot(sum_a1, 0, v))

    def send_second(v, p):
        part_wait(1, v)
        send_in(1, v, p, own(1, v), slot(sum_a2, 1, v))

    def hand_over(v):
        part_wait(1, v)
        combine(own(1, v), own(1, v), slot(sum_a2, 1, v))
        given_copy(v).start()

    def send_given(w, to, v, p):
        return_copy(w, to, w).wait_recv()
        send_in(1, w, p, slot(sum_a2, 1, w))

    def settle(k, v, p):
        cross_copy(k, v, p).wait_recv()

        @pl.when(is_middle)
        def _():
            combine(whole(k, v), own(k, v), whole(k, v))

        @pl.when(has_outer)
        def _():
            back_copy(k, v, p).start()

    def settle_first(v, p):
        settle(0, v, p)
        mate_copy(0, v).start()

    def settle_second(v, p):
        settle(1, v, p)
        mate_copy(1, v).start()

    def settle_handed(v):
        return_copy(v, helper, v).wait_recv()
        mate_copy(1, v).start()

    def settle_given(w, to, v, p):
        settle(1, w, p)
        return_copy(w, to, v).start()

    def small_in():
        small_mate.wait_recv()
        small_mate.wait_send()
        small[0] += small[1]

        @pl.when(has_outer)
        def _():
            small_line.wait_recv()
            small[0] += small[2]

        @pl.when(is_middle)
        def _():
            small_cross.start()

        @pl.when(jnp.logical_not(is_middle))
        def _():
            small_line.start()

    def small_settle():
        small_cross.wait_recv()

        @pl.when(is_middle)
        def _():
            small[3] += small[0]

        @pl.when(has_outer)
        def _():
            small_back.start()

        small_o[...] = small[3]

    gap = jnp.where(on_left, chips // 2 - 1 - chip, chip - chips // 2)
    lag = 3 + 13 * gap
    blocks = steps // SUB
    early = (blocks * 2 // 3) * SUB
    is_dense = jnp.logical_not(is_attention)
    length = jnp.where(is_attention, steps + near + far, 2 * steps - handed)

    ahead = jnp.where(is_middle, SUB // 2, 0)

    @pl.when(is_dense)
    def _():
        compute(0, 0, False)
        compute(0, 0, True)

    def in_line(u, first_part, second_part, given_part):
        @pl.when((u >= 0) & (u < length) & is_dense)
        def _():
            @pl.when(u < steps)
            def _():
                first_part(u, u)

            @pl.when(u >= steps)
            def _():
                second_part(u - steps + handed, u)

        @pl.when((u >= 0) & (u < length) & is_attention)
        def _():
            @pl.when(u < near)
            def _():
                given_part(u + shift, helper, u, u)

            @pl.when((u >= near) & (u < near + early))
            def _():
                first_part(u - near, u)

            @pl.when((u >= near + early) & (u < near + early + far))
            def _():
                v = NEAR[0] + u - near - early
                given_part(v, prv, v, u)

            @pl.when(u >= near + early + far)
            def _():
                first_part(u - near - far, u)

    def step(u, carry):
        in_line(u - ahead, send_first, send_second, send_given)

        @pl.when((u % SUB >= SUB // 2) & is_dense)
        def _():
            for k in range(2):
                v = u // SUB * SUB + 2 * (u % SUB - SUB // 2) + k

                @pl.when(v < handed)
                def _(v=v):
                    hand_over(v)

        t = u - ahead - lag

        @pl.when(t == length - 1)
        def _():
            small_settle()

        in_line(t, settle_first, settle_second, settle_given)

        @pl.when((t >= length) & (t < length + handed) & is_dense)
        def _():
            settle_handed(t - length)

        c, q = u // SUB, u % SUB // QUARTER
        on_time = (u % QUARTER == 0) & (c < blocks)

        @pl.when(on_time & (q < 2) & is_dense)
        def _():
            compute(1, c, q == 1)

        @pl.when(on_time & jnp.where(is_attention, q < 2, (q >= 2) & (c + 1 < blocks)))
        def _():
            compute(0, jnp.where(is_attention, c, c + 1), q % 2 == 1)

        @pl.when(u == steps - 2)
        def _():
            small_start()

        @pl.when((u == steps) & is_attention)
        def _():
            clear(theirs)

        @pl.when(u - ahead == steps + jnp.where((chip > 0) & (chip < chips - 1), SUB, 0))
        def _():
            small_in()

        return carry

    tail = jnp.where(is_attention, 0, handed)
    lax.fori_loop(0, length + ahead + lag + tail, step, 0)


    @pl.when(section < last)
    def _():
        remote(hout, hin, hs_sem, hr_sem.at[0], (nxt, dp)).wait_send()

    @pl.when(section > 0)
    def _():
        remote(gout, gin, gs_sem, gr_sem.at[0], (prv, dp)).wait_send()

    def taken(k, sem, count):
        if k == 0:
            ref = w1.at[:, pl.ds(0, (count // SUB) * CHUNK)]
        else:
            ref = w2.at[pl.ds(0, count * short), :]
        pltpu.make_async_copy(ref, ref, sem.at[k]).wait()

    taken(0, part_send, steps)
    taken(0, line_send, steps)
    taken(0, mate_send, steps)
    taken(0, mate_recv, steps)

    @pl.when(has_outer)
    def _():
        taken(0, back_send, steps)
        small_back.wait_send()

    @pl.when(jnp.logical_not(is_attention))
    def _():
        taken(1, part_send, steps)
        taken(1, line_send, steps)
        taken(1, mate_send, steps)
        taken(1, mate_recv, steps)

    for which, count in enumerate((NEAR[0], NEAR[0] + FAR, NEAR[1] + FAR, NEAR[1])):
        if which % 2:

            @pl.when((section == which) & has_outer)
            def _(count=count):
                taken(1, back_send, steps - count)

        else:

            @pl.when(section == which)
            def _(count=count):
                taken(1, line_send, count)
                taken(1, mate_send, count)

            @pl.when((section == which) & has_outer)
            def _(count=count):
                taken(1, back_send, count)

    small_line.wait_send()

    @pl.when(is_attention)
    def _():
        clear(mine)


def finish_kernel(
    res, sg, first, second, small,
    res_o, sg_o, first_o, second_o, norm_o, bias_o, rms_o,
    sg_wide, first_wide, second_wide, norm, bias, rms, sem, first_sem, second_sem,
):
    dim = sg.shape[2]
    ff = first.shape[1]
    copies = []

    def write(src, dst, sem):
        copies.append(pltpu.make_async_copy(src, dst, sem))
        copies[-1].start()

    write(res, res_o.at[0], sem.at[0])
    norm[0] = small[0:2, :]
    write(norm, norm_o, sem.at[1])
    count = ff // dim + 1
    for k in range(count):
        bias[0:1, k * dim : (k + 1) * dim] = small[2 + k : 3 + k, :]
    write(bias, bias_o, sem.at[2])
    stat = small[2 + count : 3 + count, :]
    rms[...] = jnp.sqrt(stat[:, 0:2] / (stat[:, 2:3] * dim))
    write(rms, rms_o, sem.at[3])
    sg_wide[...] = sg[...].astype(F32)
    write(sg_wide, sg_o.at[0], sem.at[4])
    for src, wide, dst, sems in (
        (first, first_wide, first_o, first_sem), (second, second_wide, second_o, second_sem),
    ):
        count = src.shape[0] // WRITES
        for k in range(WRITES):
            at = pl.ds(k * count, count)
            wide[at, :] = src[at, :].astype(F32)
            write(wide.at[at], dst.at[0, at], sems.at[k])
    for copy in copies:
        copy.wait()


def run_sublayers(start, cot, first, second, norm, bias, seg, val):
    rows, seq, dim = start.shape
    ff = first.shape[2]
    half = ff // 2
    steps = (half // CHUNK) * SUB
    block = (rows, seq, dim)
    wide = (rows, seq, ff)
    small = (4 + ff // dim, dim)
    ring = RING if lax.axis_size("dp") <= 8 else 2 * steps
    any_space = pl.BlockSpec(memory_space=pl.ANY)
    vmem = pl.BlockSpec(memory_space=pltpu.VMEM)
    out = jax.ShapeDtypeStruct
    dma = pltpu.SemaphoreType.DMA
    return pl.pallas_call(
        sublayer_kernel,
        out_shape=(
            pltpu.VMEM(block, BF16), pltpu.VMEM(block, BF16),
            pltpu.VMEM((dim, ff), BF16), pltpu.VMEM((ff, dim), BF16), pltpu.VMEM(small, F32),
        ),
        in_specs=[any_space] * 8,
        out_specs=(vmem,) * 5,
        scratch_shapes=[
            pltpu.VMEM((dim, ff), BF16), pltpu.VMEM((ff, dim), BF16),
            pltpu.VMEM((ff, dim), BF16), pltpu.VMEM((dim, ff), BF16),
            pltpu.VMEM(block, BF16), pltpu.VMEM((2, *block), BF16),
            pltpu.VMEM(wide, BF16), pltpu.VMEM(wide, BF16),
            pltpu.VMEM(norm.shape, F32), pltpu.VMEM(bias.shape, F32),
            pltpu.VMEM(seg.shape, jnp.int32), pltpu.VMEM(val.shape, jnp.int32),
            pltpu.VMEM((2, 8, dim), F32), pltpu.VMEM((2, 8, dim), F32),
            pltpu.VMEM((4, *small), F32),
            pltpu.VMEM((dim, half), BF16), pltpu.VMEM((dim, half), BF16),
            pltpu.VMEM((half, dim), BF16), pltpu.VMEM((half, dim), BF16),
            dma((10,)), dma, dma((rows,)), dma, dma((rows,)), dma, dma((RELAYED, PARTS)), dma((6,)),
            dma((2,)), dma((2, steps // SUB)), dma((sum(NEAR) + FAR,)),
            dma((2,)), dma((ring,)), dma((ring,)), dma((2,)),
            dma((2,)), dma((2,)),
        ],
        compiler_params=pltpu.CompilerParams(
            collective_id=0, has_side_effects=True, vmem_limit_bytes=SUBLAYER_VMEM
        ),
        name="sublayer",
    )(start, cot, first, second, norm, bias, seg, val)


def run_finish(res, sg, first, second, small):
    rows, seq, dim = res.shape
    ff = first.shape[1]
    any_space = pl.BlockSpec(memory_space=pl.ANY)
    vmem = pl.BlockSpec(memory_space=pltpu.VMEM)
    out = jax.ShapeDtypeStruct
    dma = pltpu.SemaphoreType.DMA
    return pl.pallas_call(
        finish_kernel,
        out_shape=(
            out((1, rows, seq, dim), BF16), out((1, rows, seq, dim), F32),
            out((1, dim, ff), F32), out((1, ff, dim), F32),
            out((1, 2, dim), F32), out((1, ff + dim), F32), out((1, 2), F32),
        ),
        in_specs=[vmem] * 5,
        out_specs=(any_space,) * 7,
        scratch_shapes=[
            pltpu.VMEM((rows, seq, dim), F32),
            pltpu.VMEM((dim, ff), F32), pltpu.VMEM((ff, dim), F32),
            pltpu.VMEM((1, 2, dim), F32), pltpu.VMEM((1, ff + dim), F32), pltpu.VMEM((1, 2), F32),
            dma((5,)), dma((WRITES,)), dma((WRITES,)),
        ],
        compiler_params=pltpu.CompilerParams(vmem_limit_bytes=FINISH_VMEM),
        name="finish",
    )(res, sg, first, second, small)


def local(start, cot, first, second, norm, bias, seg, val):
    return run_finish(*run_sublayers(start, cot, first, second, norm, bias, seg, val))


def solution(mesh):
    in_specs = (
        P("dp", None, None),
        P("dp", None, None),
        P("section", None, None),
        P("section", None, None),
        P("section", None, None),
        P("section", None),
        P("dp", None),
        P("dp", None),
    )
    out_specs = (
        P("section", "dp", None, None),
        P("section", "dp", None, None),
        P("section", None, None),
        P("section", None, None),
        P("section", None, None),
        P("section", None),
        P("section", None),
    )
    return jax.shard_map(local, mesh=mesh, in_specs=in_specs, out_specs=out_specs, check_vma=False)
```
